32 devices in a mesh: pipe: 16 (over z, y, core), expert: 2 (over x).
Axes of the slice: x: 2, y: 2, z: 4, core: 2. Of those that a mesh axis runs over, the one named last changes fastest.
Arguments:
- forward_input: bfloat16 [16, 32, 4096], P('pipe', 'expert'), may hold values from -6 to 6
- forward_route: int32 [16, 32, 1], P('pipe', 'expert'), may hold values from 0 to 1, as said below
- forward_gates: float32 [16, 32, 1], P('pipe', 'expert'), may hold values from 0.2 to 2
- backward_cotangent: bfloat16 [16, 32, 4096], P('pipe', 'expert'), may hold values from -6 to 6
- backward_route: int32 [16, 32, 1], P('pipe', 'expert'), may hold values from 0 to 1, as said below
- backward_gates: float32 [16, 32, 1], P('pipe', 'expert'), may hold values from 0.2 to 2
- gate_up_weight: bfloat16 [16, 2, 2048, 512], P('pipe', 'expert'), may hold values from -0.09375 to 0.09375
- down_weight: bfloat16 [16, 2, 1024, 512], P('pipe', 'expert'), may hold values from -0.1875 to 0.1875
- saved_projections: bfloat16 [16, 2, 192, 256], P('pipe', 'expert'), may hold values from -4 to 4
Outputs:
- next_input: bfloat16 [16, 32, 4096], P('pipe', 'expert')
- prior_gradient: bfloat16 [16, 32, 4096], P('pipe', 'expert')
The draws below stay inside these ranges and needn't reach their ends.
Inputs may be any that keep to these rules, and one draw needn't show every extreme that they name: `forward_route`: each token names 1 different experts. In every section one expert, drawn afresh for each section, is named by exactly 12 tokens of every source; each other expert by at most 4 tokens of one source, the remaining choices of a source being spread over the other experts as evenly as possible. `backward_route`: as for forward_route, with its own busiest experts.
All inputs are finite; a program needn't handle non-finite values.
Results may differ from the reference program's by a relative error of at most 0.0058.
Values may be sent and summed in bfloat16 or wider, within the bound.
No kernel may reach another device: no remote copies, remote signals or barrier semaphores. Data moves between devices by JAX's collectives and lax.ppermute only.
A program may use at most 64 MiB of HBM per device.

```python
import math
import jax
import jax.numpy as jnp
from jax import lax

D = 4096
HID = 1024
GROUP = 8
TOK = 16
SECTIONS = 2
EXPERTS = 2
TOPK = 1
CAP = 12
N_PIPE = 16


def route_law(key):
    hot_key, order_key, offset_key, rotation_key, label_key = jax.random.split(key, 5)
    busiest = jnp.repeat(jax.random.randint(hot_key, (SECTIONS,), 0, EXPERTS), GROUP)

    def section_labels(one_key):
        return jax.random.permutation(one_key, EXPERTS - 1)
    others = jax.vmap(section_labels)(jax.random.split(label_key, N_PIPE))
    others = others + (others >= busiest[:, None]).astype(jnp.int32)

    def device_order(one_key):
        return jax.random.permutation(one_key, TOK)
    rank_of = jax.vmap(device_order)(jax.random.split(order_key, N_PIPE * EXPERTS)).reshape(N_PIPE, EXPERTS, TOK)
    offset = jax.random.randint(offset_key, (N_PIPE, EXPERTS, 1), 0, EXPERTS - 1)
    rotation = jax.random.randint(rotation_key, (N_PIPE, EXPERTS, TOK, 1), 0, TOPK)
    is_busy = rank_of < CAP
    first_pick = jnp.where(is_busy, rank_of * (TOPK - 1), CAP * (TOPK - 1) + (rank_of - CAP) * TOPK) + offset
    picked = []
    for column in range(TOPK):
        slot_pick = jnp.where(is_busy, column - 1, column)
        pick_index = (first_pick + slot_pick) % (EXPERTS - 1)
        other_expert = jnp.take_along_axis(others, pick_index.reshape(N_PIPE, EXPERTS * TOK), axis=1).reshape(N_PIPE, EXPERTS, TOK)
        chosen = jnp.where(jnp.logical_and(is_busy, column == 0), busiest[:, None, None], other_expert)
        picked.append(chosen)
    stacked = jnp.stack(picked, axis=-1)
    turned = (lax.broadcasted_iota(jnp.int32, (1, 1, 1, TOPK), 3) + rotation) % TOPK
    stacked = jnp.take_along_axis(stacked, turned, axis=3)
    return stacked.reshape(N_PIPE, EXPERTS * TOK, TOPK).astype(jnp.int32)


def draw_forward_route(key, part):
    key = jax.random.fold_in(key, 11)
    return route_law(key)


def draw_backward_route(key, part):
    key = jax.random.fold_in(key, 12)
    return route_law(key)


def steps_of(stream_key, dims, cuts, least, top_value):
    gain = 1.0
    for axis_at, parts in cuts:
        steps = jax.random.uniform(jax.random.fold_in(jax.random.fold_in(stream_key, 6), axis_at), (parts,), jnp.float32, least / len(cuts), top_value / len(cuts))
        gain = gain * jnp.repeat(jnp.exp(steps), dims[axis_at] // parts).reshape((-1,) + (1,) * (len(dims) - 1 - axis_at))
    return gain


def scatter_about(key, shape, scale, bound, cuts=(), held_as=jnp.bfloat16):
    array = scale * jax.random.normal(key, shape, jnp.float32)
    if cuts:
        array = array * steps_of(key, shape, cuts, -0.22, 0.18)
    return jnp.clip(array, -bound, bound).astype(held_as)


def setup_inputs(seed: int = 0) -> dict:
    key_list = jax.random.split(jax.random.key(seed), 10)
    forward_input = scatter_about(key_list[0], (N_PIPE, EXPERTS * TOK, D), 1.0, 6.0, ((0, 16), (1, 2)))
    forward_route = draw_forward_route(jax.random.fold_in(key_list[9], 71), 0)
    forward_gates = jnp.clip(jnp.exp(math.log(2.0) - 2.3025851 * jax.random.uniform(key_list[2], (N_PIPE, EXPERTS * TOK, TOPK), jnp.float32) ** steps_of(key_list[2], (N_PIPE, EXPERTS * TOK, TOPK), ((0, 16), (1, 2)), -0.2, 0.2)), 0.2, 2.0)
    backward_cotangent = scatter_about(key_list[3], (N_PIPE, EXPERTS * TOK, D), 1.0, 6.0, ((0, 16), (1, 2)))
    backward_route = draw_backward_route(jax.random.fold_in(key_list[9], 71), 0)
    backward_gates = jnp.clip(jnp.exp(math.log(2.0) - 2.3025851 * jax.random.uniform(key_list[5], (N_PIPE, EXPERTS * TOK, TOPK), jnp.float32) ** steps_of(key_list[5], (N_PIPE, EXPERTS * TOK, TOPK), ((0, 16), (1, 2)), -0.2, 0.2)), 0.2, 2.0)
    gate_up_weight = scatter_about(key_list[6], (N_PIPE, EXPERTS, 2 * HID, D // GROUP), D ** -0.5, 0.09375, ((0, 16), (1, 2)))
    down_weight = scatter_about(key_list[7], (N_PIPE, EXPERTS, HID, D // GROUP), HID ** -0.5, 0.1875, ((0, 16), (1, 2)))
    saved_projections = scatter_about(key_list[8], (N_PIPE, EXPERTS, GROUP * EXPERTS * CAP, 2 * HID // GROUP), 1.0, 4.0, ((0, 16), (1, 2)))
    return {"forward_input": forward_input, "forward_route": forward_route, "forward_gates": forward_gates, "backward_cotangent": backward_cotangent, "backward_route": backward_route, "backward_gates": backward_gates, "gate_up_weight": gate_up_weight, "down_weight": down_weight, "saved_projections": saved_projections}


def silu_terms(gate_pre):
    logistic = jax.nn.sigmoid(gate_pre)
    return gate_pre * logistic, logistic * (1.0 + gate_pre * (1.0 - logistic))


def expert_forward(input_row_block, gate_up_product, down_projected_rows):
    hidden_units = down_projected_rows.shape[1]
    projected_rows = jnp.einsum("ahl,atl->aht", input_row_block.astype(jnp.float32), gate_up_product.astype(jnp.float32))
    activated, unused_slope = silu_terms(projected_rows[..., :hidden_units])
    hidden_activation = (activated * projected_rows[..., hidden_units:]).astype(jnp.bfloat16)
    produced_rows = jnp.einsum("yet,ytx->yex", hidden_activation.astype(jnp.float32), down_projected_rows.astype(jnp.float32))
    return produced_rows.astype(jnp.bfloat16)


def expert_backward(gradient_block_rows, stashed, gate_up_product, down_projected_rows):
    hidden_units = down_projected_rows.shape[1]
    hidden_gradient = jnp.einsum("ahl,atl->aht", gradient_block_rows.astype(jnp.float32), down_projected_rows.astype(jnp.float32))
    gate_pre = stashed[..., :hidden_units].astype(jnp.float32)
    up_pre = stashed[..., hidden_units:].astype(jnp.float32)
    activated, slope = silu_terms(gate_pre)
    preactivation_gradient = jnp.concatenate([hidden_gradient * up_pre * slope, hidden_gradient * activated], axis=-1).astype(jnp.bfloat16)
    produced_rows = jnp.einsum("yet,ytx->yex", preactivation_gradient.astype(jnp.float32), gate_up_product.astype(jnp.float32))
    return produced_rows.astype(jnp.bfloat16)


def rank_slots(route, experts):
    labels = lax.broadcasted_iota(jnp.int32, (1, 1, experts), 2)
    hits = (route[:, :, None] == labels).astype(jnp.int32)
    row_hits = jnp.sum(hits, axis=1)
    before = jnp.cumsum(row_hits, axis=0) - row_hits
    return jnp.sum(hits * before[:, None, :], axis=2)


def source_ranks(source_route):
    return rank_slots(source_route, EXPERTS)


def section_routes(route_all):
    sources = GROUP * EXPERTS
    per_source = route_all.reshape(sources, TOK, TOPK)
    slot_rank = jax.vmap(source_ranks)(per_source)
    source_ids = lax.broadcasted_iota(jnp.int32, (sources, TOK, TOPK), 0)
    row_ids = source_ids * TOK + lax.broadcasted_iota(jnp.int32, (sources, TOK, TOPK), 1)
    target = per_source * (sources * CAP) + source_ids * CAP + slot_rank
    source_rows = jnp.full((EXPERTS * sources * CAP,), sources * TOK, jnp.int32)
    source_rows = source_rows.at[target.reshape(-1)].set(row_ids.reshape(-1))
    return source_rows.reshape(EXPERTS, sources * CAP), target.reshape(sources * TOK, TOPK)


def combine_rows(flat_out, position, gates):
    gathered = jnp.take(flat_out, position, axis=0).astype(jnp.float32)
    return jnp.sum(gathered * gates[:, :, None], axis=1).astype(jnp.bfloat16)


def join_columns(slab):
    experts_here = slab.shape[1]
    rows_here = slab.shape[2]
    return jnp.transpose(slab, (1, 2, 0, 3)).reshape(experts_here, rows_here, -1)


def section_work(operands):
    forward_input, forward_route, forward_gates, backward_cotangent, backward_route, backward_gates, gate_up_slab, down_slab, saved_slab = operands
    model_width = forward_input.shape[1]
    gate_up_product = join_columns(gate_up_slab)
    down_projected_rows = join_columns(down_slab)
    units = saved_slab.shape[3] // 2
    slot_rows = saved_slab.shape[2]
    stashed = saved_slab.reshape(GROUP, EXPERTS, slot_rows, 2, units)
    stashed = jnp.transpose(stashed, (1, 2, 3, 0, 4)).reshape(EXPERTS, slot_rows, 2 * GROUP * units)
    source_rows, flat_index = section_routes(forward_route)
    input_row_block = jnp.take(forward_input, source_rows, axis=0, mode="fill", fill_value=0)
    produced_rows = expert_forward(input_row_block, gate_up_product, down_projected_rows).reshape(-1, model_width)
    section_output = combine_rows(produced_rows, flat_index, forward_gates)
    source_rows, flat_index = section_routes(backward_route)
    gradient_block_rows = jnp.take(backward_cotangent, source_rows, axis=0, mode="fill", fill_value=0)
    returned = expert_backward(gradient_block_rows, stashed, gate_up_product, down_projected_rows).reshape(-1, model_width)
    section_gradient = combine_rows(returned, flat_index, backward_gates)
    return section_output, section_gradient


def reference(forward_input, forward_route, forward_gates, backward_cotangent, backward_route, backward_gates, gate_up_weight, down_weight, saved_projections):
    def per_section(values):
        return values.reshape((SECTIONS, GROUP * values.shape[1]) + values.shape[2:])

    def slabs(values):
        return values.reshape((SECTIONS, GROUP) + values.shape[1:])

    outputs, gradients = lax.map(section_work, (per_section(forward_input), per_section(forward_route), per_section(forward_gates), per_section(backward_cotangent), per_section(backward_route), per_section(backward_gates), slabs(gate_up_weight), slabs(down_weight), slabs(saved_projections)))
    outputs = outputs.reshape(forward_input.shape)
    gradients = gradients.reshape(forward_input.shape)
    return jnp.roll(outputs, GROUP, axis=0), jnp.roll(gradients, -GROUP, axis=0)
```

```python
import functools

import jax
import jax.numpy as jnp
from jax import lax
from jax.experimental import pallas as pl
from jax.experimental.pallas import tpu as pltpu
from jax.sharding import PartitionSpec as P

GROUP = 8
CORES = 2
CHIPS = GROUP // CORES
TILE = 16
NT = (((1,), (1,)), ((), ()))
NN = (((1,), (0,)), ((), ()))


def round_up(value, step):
    return (value + step - 1) // step * step


def dot(a, b, dims=NN):
    return lax.dot_general(a, b, dims, preferred_element_type=jnp.float32)


def iota(shape, axis):
    return lax.broadcasted_iota(jnp.int32, shape, axis)


def place():
    pipe = lax.axis_index("pipe")
    core = lax.rem(pipe, CORES)
    chip = lax.rem(lax.div(pipe, CORES), CHIPS)
    return chip, core, lax.axis_index("expert")


def block_of(index, size):
    return pl.ds(pl.multiple_of(index * size, size), size)


def call(kernel, outs, *args, scratch=(), flops=0, name=None):
    size = sum(a.size * a.dtype.itemsize for a in args)
    size += sum(o.size * o.dtype.itemsize for o in jax.tree.leaves(outs))
    spec = pl.BlockSpec(memory_space=pltpu.VMEM)
    return pl.pallas_call(
        kernel,
        out_shape=outs,
        in_specs=[spec] * len(args),
        out_specs=jax.tree.map(lambda _: spec, outs),
        scratch_shapes=scratch,
        compiler_params=pltpu.CompilerParams(vmem_limit_bytes=24 * 2**20),
        cost_estimate=pl.CostEstimate(flops=flops, bytes_accessed=size, transcendentals=0),
        name=name,
    )(*args)


def shape(dims, dtype=jnp.bfloat16):
    return jax.ShapeDtypeStruct(dims, dtype)


def named_and_rank(route, expert):
    tokens = route.shape[1]
    named = jnp.max((route == expert).astype(jnp.float32), axis=0, keepdims=True)
    earlier = (iota((tokens, tokens), 0) < iota((tokens, tokens), 1)).astype(jnp.float32)
    rank = dot(jnp.broadcast_to(named, (8, tokens)), earlier)[:1]
    return named, rank


def dispatch_kernel(experts, route_ref, rows_ref, *outs):
    chip, _, expert = place()
    tokens, width = rows_ref.shape
    wide = width // CHIPS
    route = route_ref[...]
    picks = []
    for de in range(experts):
        named, rank = named_and_rank(route, lax.rem(expert + de, experts))
        slots = iota((TILE, tokens), 0).astype(jnp.float32)
        picks.append(jnp.where(jnp.logical_and(slots == rank, named > 0.0), 1.0, 0.0))
    pick = jnp.concatenate(picks, axis=0).astype(jnp.bfloat16)
    for dk in range(CHIPS):
        columns = rows_ref[:, block_of(chip ^ dk, wide)]
        moved = dot(pick, columns).astype(jnp.bfloat16)
        for de in range(experts):
            outs[dk * experts + de][...] = moved[de * TILE : (de + 1) * TILE]


def dispatch(route, rows, experts):
    wide = rows.shape[1] // CHIPS
    outs = [shape((TILE, wide)) for _ in range(CHIPS * experts)]
    return call(functools.partial(dispatch_kernel, experts), outs, route, rows, name="dispatch")


def slot_rows(experts, capacity):
    return round_up(CHIPS * capacity, TILE)


def squeeze_rows(blocks, chip, experts, capacity):
    rows = slot_rows(experts, capacity)
    stacked = jnp.concatenate([b[...] for b in blocks], axis=0)
    total = len(blocks) * TILE
    column = iota((rows * experts, total), 1)
    source, slot = column // TILE, column % TILE
    target = (source % experts) * rows + ((source // experts) ^ chip) * capacity + slot
    hit = jnp.logical_and(iota((rows * experts, total), 0) == target, slot < capacity)
    return dot(jnp.where(hit, 1.0, 0.0).astype(jnp.bfloat16), stacked).astype(jnp.bfloat16)


def up_kernel(experts, capacity, halves, *refs):
    count = CHIPS * experts
    blocks, (own_w, other_w), outs, held = refs[:count], refs[count : count + 2], refs[count + 2 : -1], refs[-1]
    chip, core, _ = place()
    held[...] = squeeze_rows(blocks, chip, experts, capacity)
    half = held.shape[1] // CORES
    own = held[:, block_of(core, half)]
    other = held[:, block_of(1 - core, half)]
    units = own_w.shape[0] // halves // CHIPS
    for dk in (*range(1, CHIPS), 0):
        for part in range(halves):
            rows = pl.ds(pl.multiple_of((part * CHIPS + (chip ^ dk)) * units, units), units)
            product = dot(own, own_w[rows, :], NT) + dot(other, other_w[rows, :], NT)
            outs[dk][:, part * units : (part + 1) * units] = product.astype(outs[dk].dtype)


def up(blocks, own_w, other_w, experts, capacity, halves, name):
    rows = slot_rows(experts, capacity) * experts
    width = own_w.shape[0] // CHIPS
    outs = [shape((rows, width), jnp.float32 if dk == 0 else jnp.bfloat16) for dk in range(CHIPS)]
    return call(
        functools.partial(up_kernel, experts, capacity, halves),
        outs,
        *blocks,
        own_w,
        other_w,
        scratch=[pltpu.VMEM((rows, blocks[0].shape[1]), jnp.bfloat16)],
        flops=4 * rows * own_w.size,
        name=name,
    )


def down_kernel(experts, halves, *refs):
    parts, (own_w, other_w), outs = refs[:CHIPS], refs[CHIPS : CHIPS + 2], refs[CHIPS + 2 :]
    chip, core, _ = place()
    half = own_w.shape[1]
    units = own_w.shape[0] // halves // CHIPS
    rows = parts[0].shape[0] // experts
    for weight, column in ((own_w, core), (other_w, 1 - core)):
        total = None
        for dk in range(CHIPS):
            for part in range(halves):
                at = pl.ds(pl.multiple_of((part * CHIPS + (chip ^ dk)) * units, units), units)
                term = dot(parts[dk][:, part * units : (part + 1) * units], weight[at, :])
                total = term if total is None else total + term
        total = total.astype(jnp.bfloat16)
        for de in range(experts):
            outs[de][:, block_of(column, half)] = total[de * rows : (de + 1) * rows]


def down(parts, own_w, other_w, experts, halves, name):
    rows = parts[0].shape[0] // experts
    outs = [shape((rows, CORES * own_w.shape[1])) for _ in range(experts)]
    return call(
        functools.partial(down_kernel, experts, halves),
        outs,
        *parts,
        own_w,
        other_w,
        flops=4 * parts[0].shape[0] * own_w.size,
        name=name,
    )


def as_column(row):
    size = row.shape[1]
    same = iota((size, size), 0) == iota((size, size), 1)
    return jnp.sum(jnp.where(same, jnp.broadcast_to(row, (size, size)), 0.0), axis=1, keepdims=True)


def combine_kernel(experts, capacity, topk, first, *refs):
    metas, blocks, outs = refs[:CHIPS], refs[CHIPS : CHIPS + experts], refs[CHIPS + experts :]
    chip, _, expert = place()
    rows = blocks[0].shape[0]
    tokens = outs[0].shape[0]
    gates = [[] for _ in range(topk)]
    picks = [[[] for _ in range(experts)] for _ in range(topk)]
    for dk in range(CHIPS):
        route = metas[dk][first : first + topk, :]
        gate = metas[dk][first + topk : first + 2 * topk, :]
        first_row = ((chip ^ dk) * capacity).astype(jnp.float32)
        for kk in range(topk):
            gates[kk].append(as_column(gate[kk : kk + 1]))
        for de in range(experts):
            here = lax.rem(expert + de, experts).astype(jnp.float32)
            _, rank = named_and_rank(route, here)
            for kk in range(topk):
                target = jnp.where(route[kk : kk + 1] == here, rank + first_row, -1.0)
                picks[kk][de].append(as_column(target))
    slots = iota((CHIPS * tokens, rows), 1).astype(jnp.float32)
    total = None
    for kk in range(topk):
        found = None
        for de in range(experts):
            target = jnp.concatenate(picks[kk][de], axis=0)
            pick = jnp.where(slots == target, 1.0, 0.0).astype(jnp.bfloat16)
            term = dot(pick, blocks[de][...])
            found = term if found is None else found + term
        term = found * jnp.concatenate(gates[kk], axis=0)
        total = term if total is None else total + term
    total = total.astype(jnp.bfloat16)
    for dk in range(CHIPS):
        outs[dk][...] = total[dk * tokens : (dk + 1) * tokens]


def combine(metas, blocks, experts, capacity, topk, first, name):
    tokens = metas[0].shape[1]
    outs = [shape((tokens, blocks[0].shape[1])) for _ in range(CHIPS)]
    return call(
        functools.partial(combine_kernel, experts, capacity, topk, first),
        outs,
        *metas,
        *blocks,
        name=name,
    )


def join_kernel(*refs):
    chip, _, _ = place()
    out = refs[-1]
    for dk in range(CHIPS):
        out[:, block_of(chip ^ dk, refs[dk].shape[1])] = refs[dk][...]


def join(blocks, name):
    tokens, wide = blocks[0].shape
    return call(join_kernel, shape((tokens, CHIPS * wide)), *blocks, name=name)


def stash_kernel(experts, capacity, saved_ref, mine_ref, theirs_ref):
    _, core, expert = place()
    rows = slot_rows(experts, capacity)
    dims = (rows * experts, saved_ref.shape[0])
    row = iota(dims, 0)
    column = iota(dims, 1)
    for target, ref in ((core, mine_ref), (1 - core, theirs_ref)):
        wanted = jnp.full(dims, -1, jnp.int32)
        for de in range(experts):
            for at in range(CHIPS):
                source = (at * CORES + target) * experts + lax.rem(expert + experts - de, experts)
                low = de * rows + at * capacity
                inside = jnp.logical_and(row >= low, row < low + capacity)
                wanted = jnp.where(inside, row + (source * capacity - low), wanted)
        pick = jnp.where(column == wanted, 1.0, 0.0).astype(jnp.bfloat16)
        ref[...] = dot(pick, saved_ref[...]).astype(jnp.bfloat16)


def stash(saved, experts, capacity):
    out = shape((slot_rows(experts, capacity) * experts, saved.shape[1]))
    return call(functools.partial(stash_kernel, experts, capacity), [out, out], saved, name="stash")


def total_of(parts):
    total = parts[0]
    for part in parts[1:]:
        total = total + part.astype(jnp.float32)
    return total


def on_device(
    forward_input,
    forward_route,
    forward_gates,
    backward_cotangent,
    backward_route,
    backward_gates,
    gate_up_weight,
    down_weight,
    saved_projections,
):
    pipes = lax.axis_size("pipe")
    experts = lax.axis_size("expert")
    topk = forward_route.shape[2]
    capacity = saved_projections.shape[2] // (GROUP * experts)
    _, core, _ = place()

    def to_chip(value, dk, by=0):
        pairs = [(i, ((i ^ (dk * CORES)) + by) % pipes) for i in range(pipes)]
        return lax.ppermute(value, "pipe", pairs)

    def to_place(value, dk, de):
        if dk == 0 and de == 0:
            return value
        pairs = [
            (i * experts + j, (i ^ (dk * CORES)) * experts + (j + de) % experts)
            for i in range(pipes)
            for j in range(experts)
        ]
        return lax.ppermute(value, ("pipe", "expert"), pairs)

    def to_core(value):
        return lax.ppermute(value, "pipe", [(i, i ^ 1) for i in range(pipes)])

    def spread(blocks):
        return [to_place(blocks[dk * experts + de], dk, de) for dk in range(CHIPS) for de in range(experts)]

    def reduced(parts):
        return [parts[0]] + [to_chip(parts[dk], dk) for dk in range(1, CHIPS)]

    def gathered(part):
        return [part] + [to_chip(part, dk) for dk in range(1, CHIPS)]

    def returned(blocks):
        return [to_place(blocks[de], 0, (experts - de) % experts) for de in range(experts)]

    rows_ahead, rows_behind = forward_input[0], backward_cotangent[0]
    route_ahead, route_behind = forward_route[0].T, backward_route[0].T
    gu_own, down_own = gate_up_weight[0, 0], down_weight[0, 0]

    gu_other = to_core(gu_own)
    down_other = to_core(down_own)
    ahead = spread(dispatch(route_ahead, rows_ahead, experts))
    behind = spread(dispatch(route_behind, rows_behind, experts))
    meta = jnp.concatenate(
        [
            route_ahead.astype(jnp.float32),
            forward_gates[0].T,
            route_behind.astype(jnp.float32),
            backward_gates[0].T,
        ],
        axis=0,
    )
    metas = gathered(meta)
    stash_mine, stash_theirs = stash(saved_projections[0, 0], experts, capacity)
    stash_other = to_core(stash_theirs)

    parts = reduced(up(ahead, gu_own, gu_other, experts, capacity, 2, "up_ahead"))
    summed = total_of(parts)
    units = summed.shape[1] // 2
    gate_pre = summed[:, :units]
    hidden = (gate_pre * jax.nn.sigmoid(gate_pre) * summed[:, units:]).astype(jnp.bfloat16)
    blocks = returned(down(gathered(hidden), down_own, down_other, experts, 1, "down_ahead"))
    outs = combine(metas, blocks, experts, capacity, topk, 0, "combine_ahead")
    next_input = join([to_chip(outs[dk], dk, GROUP) for dk in range(CHIPS)], "join_ahead")

    parts = reduced(up(behind, down_own, down_other, experts, capacity, 1, "up_behind"))
    hidden_grad = total_of(parts)
    half = stash_mine.shape[1] // 2
    low = jnp.where(core == 0, stash_mine, stash_other).astype(jnp.float32)
    high = jnp.where(core == 0, stash_other, stash_mine).astype(jnp.float32)
    gate_pre = jnp.concatenate([low[:, :half], high[:, :half]], axis=1)
    up_pre = jnp.concatenate([low[:, half:], high[:, half:]], axis=1)
    sig = jax.nn.sigmoid(gate_pre)
    pre_grad = jnp.concatenate(
        [hidden_grad * up_pre * (sig * (1.0 + gate_pre * (1.0 - sig))), hidden_grad * (gate_pre * sig)], axis=1
    ).astype(jnp.bfloat16)
    blocks = returned(down(gathered(pre_grad), gu_own, gu_other, experts, 2, "down_behind"))
    outs = combine(metas, blocks, experts, capacity, topk, 2 * topk, "combine_behind")
    prior_gradient = join([to_chip(outs[dk], dk, -GROUP) for dk in range(CHIPS)], "join_behind")
    return next_input[None], prior_gradient[None]


def solution(mesh):
    rows = P("pipe", "expert", None)
    weights = P("pipe", "expert", None, None)
    return jax.shard_map(
        on_device,
        mesh=mesh,
        in_specs=(rows,) * 6 + (weights,) * 3,
        out_specs=(rows, rows),
        check_vma=False,
    )
```

```python
import functools

import jax
import jax.numpy as jnp
from jax import lax
from jax.experimental import pallas as pl
from jax.experimental.pallas import tpu as pltpu
from jax.sharding import PartitionSpec as P

GROUP = 8
CORES = 2
CHIPS = GROUP // CORES
TILE = 16
NT = (((1,), (1,)), ((), ()))
NN = (((1,), (0,)), ((), ()))


def round_up(value, step):
    return (value + step - 1) // step * step


def dot(a, b, dims=NN):
    return lax.dot_general(a, b, dims, preferred_element_type=jnp.float32)


def iota(shape, axis):
    return lax.broadcasted_iota(jnp.int32, shape, axis)


def place():
    pipe = lax.axis_index("pipe")
    core = lax.rem(pipe, CORES)
    chip = lax.rem(lax.div(pipe, CORES), CHIPS)
    return chip, core, lax.axis_index("expert")


def block_of(index, size):
    return pl.ds(pl.multiple_of(index * size, size), size)


def call(kernel, outs, *args, scratch=(), flops=0, name=None, far=()):
    size = sum(a.size * a.dtype.itemsize for a in args)
    size += sum(o.size * o.dtype.itemsize for o in jax.tree.leaves(outs))
    spec = pl.BlockSpec(memory_space=pltpu.VMEM)
    return pl.pallas_call(
        kernel,
        out_shape=outs,
        in_specs=[pl.BlockSpec(memory_space=pl.ANY) if i in far else spec for i in range(len(args))],
        out_specs=jax.tree.map(lambda _: spec, outs),
        scratch_shapes=scratch,
        compiler_params=pltpu.CompilerParams(vmem_limit_bytes=24 * 2**20),
        cost_estimate=pl.CostEstimate(flops=flops, bytes_accessed=size, transcendentals=0),
        name=name,
    )(*args)


def shape(dims, dtype=jnp.bfloat16):
    return jax.ShapeDtypeStruct(dims, dtype)


def note_lanes(topk, tokens):
    return round_up(4 * topk * tokens, 128)


def dispatch_kernel(experts, tile, refs_in, outs):
    chip, _, expert = place()
    lanes = note_lanes(*refs_in[0][0].shape)
    picks, notes = [], []
    for route_ref, gate_ref, _ in refs_in:
        route, gate = route_ref[...], gate_ref[...]
        topk, tokens = route.shape
        earlier = (iota((tokens, tokens), 0) < iota((tokens, tokens), 1)).astype(jnp.float32)
        pick = []
        for de in range(experts):
            here = lax.rem(expert + de, experts)
            named = jnp.max((route == here).astype(jnp.float32), axis=0, keepdims=True)
            rank = dot(jnp.broadcast_to(named, (8, tokens)), earlier)[:1]
            slots = iota((tile, tokens), 0).astype(jnp.float32)
            pick.append(jnp.where(jnp.logical_and(slots == rank, named > 0.0), 1.0, 0.0))
        picks.append(jnp.concatenate(pick, axis=0).astype(jnp.bfloat16))
        high = gate.astype(jnp.bfloat16).astype(jnp.float32)
        middle = (gate - high).astype(jnp.bfloat16).astype(jnp.float32)
        low = gate - high - middle
        note = jnp.zeros((8, lanes), jnp.float32)
        for part, value in enumerate((route.astype(jnp.float32), high, middle, low)):
            for kk in range(topk):
                first = (part * topk + kk) * tokens
                put = (iota((tokens, lanes), 1) == iota((tokens, lanes), 0) + first).astype(jnp.float32)
                row = jnp.broadcast_to(value[kk : kk + 1], (8, tokens))
                note = note + dot(row.astype(jnp.bfloat16), put.astype(jnp.bfloat16))
        notes.append(jnp.where(iota((tile, lanes), 0) == tile - 1, jnp.broadcast_to(note[:1], (tile, lanes)), 0.0))
    wide = refs_in[0][2].shape[1] // CHIPS
    for dk in (*range(1, CHIPS), 0):
        for at, (_, _, rows_ref) in enumerate(refs_in):
            moved = dot(picks[at], rows_ref[:, block_of(chip ^ dk, wide)])
            for de in range(experts):
                block = moved[de * tile : (de + 1) * tile]
                out = outs[dk * experts + de]
                out[at * tile : (at + 1) * tile, :lanes] = (block[:, :lanes] + notes[at]).astype(jnp.bfloat16)
                out[at * tile : (at + 1) * tile, lanes:] = block[:, lanes:].astype(jnp.bfloat16)


def dispatch(batches, experts, tile):
    wide = batches[0][2].shape[1] // CHIPS
    flat = [a for batch in batches for a in batch]
    outs = [shape((len(batches) * tile, wide)) for _ in range(CHIPS * experts)]

    def kernel(*refs):
        refs_in = [refs[3 * i : 3 * i + 3] for i in range(len(batches))]
        dispatch_kernel(experts, tile, refs_in, refs[len(flat) :])

    return call(kernel, outs, *flat, name="dispatch")


def slot_rows(experts, capacity):
    return round_up(CHIPS * capacity, TILE)


def squeeze_rows(blocks, at, tile, chip, experts, capacity):
    rows = slot_rows(experts, capacity)
    stacked = jnp.concatenate([b[at * tile : (at + 1) * tile] for b in blocks], axis=0)
    total = len(blocks) * tile
    column = iota((rows * experts, total), 1)
    source, slot = column // tile, column % tile
    target = (source % experts) * rows + ((source // experts) ^ chip) * capacity + slot
    hit = jnp.logical_and(iota((rows * experts, total), 0) == target, slot < capacity)
    return dot(jnp.where(hit, 1.0, 0.0).astype(jnp.bfloat16), stacked).astype(jnp.bfloat16)


def unit_rows(part, chip, units):
    return pl.ds(pl.multiple_of((part * CHIPS + chip) * units, units), units)


def up_kernel(experts, capacity, tile, *refs):
    count = CHIPS * experts
    blocks, (gu_own, gu_other, down_own, down_other) = refs[:count], refs[count : count + 4]
    outs, (held, gu_here, arrived) = refs[count + 4 : -3], refs[-3:]
    copy = pltpu.make_async_copy(gu_other, gu_here, arrived)
    copy.start()
    chip, core, _ = place()
    units = down_own.shape[0] // CHIPS
    half = held.shape[2] // CORES
    own, other = block_of(core, half), block_of(1 - core, half)
    for at in range(2):
        held[at] = squeeze_rows(blocks, at, tile, chip, experts, capacity)
    for dk in (*range(1, CHIPS), 0):
        rows = unit_rows(0, chip ^ dk, units)
        product = dot(held[1, :, own], down_own[rows, :], NT) + dot(held[1, :, other], down_other[rows, :], NT)
        outs[dk][:, 2 * units :] = product.astype(outs[dk].dtype)
    copy.wait()
    for dk in (*range(1, CHIPS), 0):
        for part in range(2):
            rows = unit_rows(part, chip ^ dk, units)
            product = dot(held[0, :, own], gu_own[rows, :], NT) + dot(held[0, :, other], gu_here[rows, :], NT)
            outs[dk][:, part * units : (part + 1) * units] = product.astype(outs[dk].dtype)


def up(blocks, weights, experts, capacity, tile):
    rows = slot_rows(experts, capacity) * experts
    gu, down = weights[0], weights[2]
    width = (gu.shape[0] + down.shape[0]) // CHIPS
    outs = [shape((rows, width), jnp.float32 if dk == 0 else jnp.bfloat16) for dk in range(CHIPS)]
    return call(
        functools.partial(up_kernel, experts, capacity, tile),
        outs,
        *blocks,
        *weights,
        scratch=[
            pltpu.VMEM((2, rows, blocks[0].shape[1]), jnp.bfloat16),
            pltpu.VMEM(gu.shape, jnp.bfloat16),
            pltpu.SemaphoreType.DMA,
        ],
        flops=4 * rows * (gu.size + down.size),
        name="up",
        far=(len(blocks) + 1,),
    )


def act_kernel(*refs):
    parts, (mine, theirs, out) = refs[:CHIPS], refs[CHIPS:]
    _, core, _ = place()
    total = parts[0][...]
    for part in parts[1:]:
        total = total + part[...].astype(jnp.float32)
    units = total.shape[1] // 3
    gate_pre, up_pre, hidden_grad = total[:, :units], total[:, units : 2 * units], total[:, 2 * units :]
    out[:, :units] = (gate_pre * jax.nn.sigmoid(gate_pre) * up_pre).astype(jnp.bfloat16)
    own, other = mine[...].astype(jnp.float32), theirs[...].astype(jnp.float32)
    low, high = jnp.where(core == 0, own, other), jnp.where(core == 0, other, own)
    half = units // CORES
    for at, saved in enumerate((low, high)):
        gate_pre, up_pre = saved[:, :half], saved[:, half:]
        sig = jax.nn.sigmoid(gate_pre)
        grad = hidden_grad[:, at * half : (at + 1) * half]
        first = units + at * half
        out[:, first : first + half] = (grad * up_pre * (sig * (1.0 + gate_pre * (1.0 - sig)))).astype(jnp.bfloat16)
        out[:, first + units : first + units + half] = (grad * (gate_pre * sig)).astype(jnp.bfloat16)


def act(parts, mine, theirs):
    return call(act_kernel, shape(parts[0].shape), *parts, mine, theirs, name="act")


def down_kernel(experts, *refs):
    parts, (gu_own, gu_other, down_own, down_other) = refs[:CHIPS], refs[CHIPS : CHIPS + 4]
    outs, (gu_here, arrived) = refs[CHIPS + 4 : -2], refs[-2:]
    copy = pltpu.make_async_copy(gu_other, gu_here, arrived)
    copy.start()
    chip, core, _ = place()
    half = down_own.shape[1]
    units = down_own.shape[0] // CHIPS
    rows = parts[0].shape[0] // experts

    def product(weight, halves, first):
        total = None
        for dk in range(CHIPS):
            for part in range(halves):
                column = (first + part) * units
                term = dot(parts[dk][:, column : column + units], weight[unit_rows(part, chip ^ dk, units), :])
                total = term if total is None else total + term
        return total.astype(jnp.bfloat16)

    jobs = ((down_own, 1, 0, core), (down_other, 1, 0, 1 - core), (gu_own, 2, 1, core), (gu_here, 2, 1, 1 - core))
    for weight, halves, first, column in jobs:
        if weight is gu_here:
            copy.wait()
        total = product(weight, halves, first)
        for de in range(experts):
            outs[de][first * rows : (first + 1) * rows, block_of(column, half)] = total[de * rows : (de + 1) * rows]


def down(parts, weights, experts):
    rows = parts[0].shape[0] // experts
    gu, down = weights[0], weights[2]
    outs = [shape((2 * rows, CORES * down.shape[1])) for _ in range(experts)]
    return call(
        functools.partial(down_kernel, experts),
        outs,
        *parts,
        *weights,
        scratch=[pltpu.VMEM(gu.shape, jnp.bfloat16), pltpu.SemaphoreType.DMA],
        flops=4 * parts[0].shape[0] * (gu.size + down.size),
        name="down",
        far=(len(parts) + 1,),
    )


def as_column(row):
    size = row.shape[1]
    same = iota((size, size), 0) == iota((size, size), 1)
    return jnp.sum(jnp.where(same, jnp.broadcast_to(row, (size, size)), 0.0), axis=1, keepdims=True)


def combine_kernel(experts, capacity, topk, tokens, tile, *refs):
    notes, blocks, outs = refs[:CHIPS], refs[CHIPS : CHIPS + experts], refs[CHIPS + experts :]
    chip, _, expert = place()
    rows = blocks[0].shape[0] // 2
    earlier = iota((tokens, tokens), 1) < iota((tokens, tokens), 0)
    for at in range(2):
        gates = [[] for _ in range(topk)]
        picks = [[[] for _ in range(experts)] for _ in range(topk)]
        for dk in range(CHIPS):
            note = notes[dk][at * tile : (at + 1) * tile, : note_lanes(topk, tokens)].astype(jnp.float32)[tile - 1 :]
            column = as_column(note)

            def piece(part, kk):
                first = (part * topk + kk) * tokens
                return column[first : first + tokens]

            first_row = ((chip ^ dk) * capacity).astype(jnp.float32)
            for kk in range(topk):
                gates[kk].append(piece(1, kk) + piece(2, kk) + piece(3, kk))
            for de in range(experts):
                here = lax.rem(expert + de, experts).astype(jnp.float32)
                rank = jnp.zeros((tokens, 1), jnp.float32)
                for kk in range(topk):
                    named = note[:, kk * tokens : (kk + 1) * tokens] == here
                    named = jnp.where(named, 1.0, 0.0)
                    counted = jnp.where(earlier, jnp.broadcast_to(named, (tokens, tokens)), 0.0)
                    rank = rank + jnp.sum(counted, axis=1, keepdims=True)
                for kk in range(topk):
                    picks[kk][de].append(jnp.where(piece(0, kk) == here, rank + first_row, -1.0))
        slots = iota((CHIPS * tokens, rows), 1).astype(jnp.float32)
        total = None
        for kk in range(topk):
            found = None
            for de in range(experts):
                target = jnp.concatenate(picks[kk][de], axis=0)
                pick = jnp.where(slots == target, 1.0, 0.0).astype(jnp.bfloat16)
                term = dot(pick, blocks[de][at * rows : (at + 1) * rows])
                found = term if found is None else found + term
            term = found * jnp.concatenate(gates[kk], axis=0)
            total = term if total is None else total + term
        total = total.astype(jnp.bfloat16)
        for dk in range(CHIPS):
            outs[dk][at * tokens : (at + 1) * tokens] = total[dk * tokens : (dk + 1) * tokens]


def combine(notes, blocks, experts, capacity, topk, tokens, tile):
    outs = [shape((2 * tokens, blocks[0].shape[1])) for _ in range(CHIPS)]
    return call(
        functools.partial(combine_kernel, experts, capacity, topk, tokens, tile),
        outs,
        *notes,
        *blocks,
        name="combine",
    )


def join_kernel(*refs):
    chip, _, _ = place()
    blocks, outs = refs[: -2], refs[-2:]
    tokens = outs[0].shape[0]
    for at, out in enumerate(outs):
        for dk in range(CHIPS):
            block = blocks[dk + at * (len(blocks) - CHIPS)]
            first = at * tokens if len(blocks) == CHIPS else 0
            out[:, block_of(chip ^ dk, block.shape[1])] = block[first : first + tokens]


def join(blocks, tokens):
    out = shape((tokens, CHIPS * blocks[0].shape[1]))
    return call(join_kernel, [out, out], *blocks, name="join")


def stash_kernel(experts, capacity, saved_ref, mine_ref, theirs_ref):
    _, core, expert = place()
    rows = slot_rows(experts, capacity)
    dims = (rows * experts, saved_ref.shape[0])
    row = iota(dims, 0)
    column = iota(dims, 1)
    for target, ref in ((core, mine_ref), (1 - core, theirs_ref)):
        wanted = jnp.full(dims, -1, jnp.int32)
        for de in range(experts):
            for at in range(CHIPS):
                source = (at * CORES + target) * experts + lax.rem(expert + experts - de, experts)
                low = de * rows + at * capacity
                inside = jnp.logical_and(row >= low, row < low + capacity)
                wanted = jnp.where(inside, row + (source * capacity - low), wanted)
        pick = jnp.where(column == wanted, 1.0, 0.0).astype(jnp.bfloat16)
        ref[...] = dot(pick, saved_ref[...]).astype(jnp.bfloat16)


def stash(saved, experts, capacity):
    out = shape((slot_rows(experts, capacity) * experts, saved.shape[1]))
    return call(functools.partial(stash_kernel, experts, capacity), [out, out], saved, name="stash")


def on_device(
    forward_input,
    forward_route,
    forward_gates,
    backward_cotangent,
    backward_route,
    backward_gates,
    gate_up_weight,
    down_weight,
    saved_projections,
):
    pipes = lax.axis_size("pipe")
    experts = lax.axis_size("expert")
    topk = forward_route.shape[2]
    capacity = saved_projections.shape[2] // (GROUP * experts)
    tokens = forward_route.shape[1]
    tile = round_up(capacity + 1, TILE)

    def to_chip(value, dk, by=0):
        pairs = [(i, ((i ^ (dk * CORES)) + by) % pipes) for i in range(pipes)]
        return lax.ppermute(value, "pipe", pairs)

    def to_place(value, dk, de):
        if dk == 0 and de == 0:
            return value
        pairs = [
            (i * experts + j, (i ^ (dk * CORES)) * experts + (j + de) % experts)
            for i in range(pipes)
            for j in range(experts)
        ]
        return lax.ppermute(value, ("pipe", "expert"), pairs)

    def to_core(value):
        return lax.ppermute(value, "pipe", [(i, i ^ 1) for i in range(pipes)])

    def spread(blocks):
        return [to_place(blocks[dk * experts + de], dk, de) for dk in range(CHIPS) for de in range(experts)]

    def reduced(parts):
        return [parts[0]] + [to_chip(parts[dk], dk) for dk in range(1, CHIPS)]

    def gathered(part):
        return [part] + [to_chip(part, dk) for dk in range(1, CHIPS)]

    def returned(blocks):
        return [to_place(blocks[de], 0, (experts - de) % experts) for de in range(experts)]

    batches = [
        (forward_route[0].T, forward_gates[0].T, forward_input[0]),
        (backward_route[0].T, backward_gates[0].T, backward_cotangent[0]),
    ]
    gu_own, down_own = gate_up_weight[0, 0], down_weight[0, 0]
    weights = (gu_own, to_core(gu_own), down_own, to_core(down_own))
    arrived = spread(dispatch(batches, experts, tile))
    stash_mine, stash_theirs = stash(saved_projections[0, 0], experts, capacity)
    stash_other = to_core(stash_theirs)
    parts = reduced(up(arrived, weights, experts, capacity, tile))
    units = gathered(act(parts, stash_mine, stash_other))
    blocks = returned(down(units, weights, experts))
    outs = combine(arrived[::experts], blocks, experts, capacity, topk, tokens, tile)
    if 2 * GROUP == pipes:
        joined = [to_chip(outs[dk], dk, GROUP) for dk in range(CHIPS)]
    else:
        joined = [to_chip(outs[dk][:tokens], dk, GROUP) for dk in range(CHIPS)]
        joined += [to_chip(outs[dk][tokens:], dk, -GROUP) for dk in range(CHIPS)]
    next_input, prior_gradient = join(joined, tokens)
    return next_input[None], prior_gradient[None]


def solution(mesh):
    rows = P("pipe", "expert", None)
    weights = P("pipe", "expert", None, None)
    return jax.shard_map(
        on_device,
        mesh=mesh,
        in_specs=(rows,) * 6 + (weights,) * 3,
        out_specs=(rows, rows),
        check_vma=False,
    )
```

```python
import functools

import jax
import jax.numpy as jnp
from jax import lax
from jax.experimental import pallas as pl
from jax.experimental.pallas import tpu as pltpu
from jax.sharding import Mesh
from jax.sharding import PartitionSpec as P

GROUP = 8
CORES = 2
CHIPS = GROUP // CORES
TILE = 16
NT = (((1,), (1,)), ((), ()))
NN = (((1,), (0,)), ((), ()))


def round_up(value, step):
    return (value + step - 1) // step * step


def dot(a, b, dims=NN):
    return lax.dot_general(a, b, dims, preferred_element_type=jnp.float32)


def iota(shape, axis):
    return lax.broadcasted_iota(jnp.int32, shape, axis)


def place():
    return lax.axis_index("chip"), lax.axis_index("core"), lax.axis_index("expert")


def block_of(index, size):
    return pl.ds(pl.multiple_of(index * size, size), size)


def call(kernel, outs, *args, scratch=(), flops=0, name=None, far=()):
    size = sum(a.size * a.dtype.itemsize for a in args)
    size += sum(o.size * o.dtype.itemsize for o in jax.tree.leaves(outs))
    spec = pl.BlockSpec(memory_space=pltpu.VMEM)
    return pl.pallas_call(
        kernel,
        out_shape=outs,
        in_specs=[pl.BlockSpec(memory_space=pl.ANY) if i in far else spec for i in range(len(args))],
        out_specs=jax.tree.map(lambda _: spec, outs),
        scratch_shapes=scratch,
        compiler_params=pltpu.CompilerParams(vmem_limit_bytes=16 * 2**20),
        cost_estimate=pl.CostEstimate(flops=flops, bytes_accessed=size, transcendentals=0),
        name=name,
    )(*args)


def shape(dims, dtype=jnp.bfloat16):
    return jax.ShapeDtypeStruct(dims, dtype)


def note_lanes(topk, tokens):
    return round_up(4 * topk * tokens, 128)


def dispatch_kernel(experts, tile, *refs):
    count = (len(refs) - 2) // 2
    far, out, near, arrived = refs[:count], refs[count], refs[count + 1 : -1], refs[-1]
    copies = [pltpu.make_async_copy(far[i], near[i], arrived.at[i]) for i in range(count)]
    for copy in copies:
        copy.start()
    for copy in copies:
        copy.wait()
    for at in range(count // 3):
        route, gate = near[3 * at][...], near[3 * at + 1][...]
        rows_ref = near[3 * at + 2]
        topk, tokens = route.shape
        lanes = note_lanes(topk, tokens)
        earlier = (iota((tokens, tokens), 0) < iota((tokens, tokens), 1)).astype(jnp.float32)
        pick = []
        for e in range(experts):
            named = jnp.max((route == e).astype(jnp.float32), axis=0, keepdims=True)
            rank = dot(jnp.broadcast_to(named, (8, tokens)), earlier)[:1]
            slots = iota((tile, tokens), 0).astype(jnp.float32)
            pick.append(jnp.where(jnp.logical_and(slots == rank, named > 0.0), 1.0, 0.0))
        pick = jnp.concatenate(pick, axis=0).astype(jnp.bfloat16)
        high = gate.astype(jnp.bfloat16).astype(jnp.float32)
        middle = (gate - high).astype(jnp.bfloat16).astype(jnp.float32)
        low = gate - high - middle
        note = jnp.zeros((8, lanes), jnp.float32)
        for part, value in enumerate((route.astype(jnp.float32), high, middle, low)):
            for kk in range(topk):
                first = (part * topk + kk) * tokens
                put = (iota((tokens, lanes), 1) == iota((tokens, lanes), 0) + first).astype(jnp.float32)
                row = jnp.broadcast_to(value[kk : kk + 1], (8, tokens))
                note = note + dot(row.astype(jnp.bfloat16), put.astype(jnp.bfloat16))
        note = jnp.where(iota((tile, lanes), 0) == tile - 1, jnp.broadcast_to(note[:1], (tile, lanes)), 0.0)
        wide = rows_ref.shape[1] // CHIPS
        span = slice(at * tile, (at + 1) * tile)
        for k in range(CHIPS):
            moved = dot(pick, rows_ref[:, k * wide : (k + 1) * wide])
            for e in range(experts):
                block = moved[e * tile : (e + 1) * tile]
                out[k * experts + e, span, :lanes] = (block[:, :lanes] + note).astype(jnp.bfloat16)
                out[k * experts + e, span, lanes:] = block[:, lanes:].astype(jnp.bfloat16)


def dispatch(batches, experts, tile):
    wide = batches[0][2].shape[1] // CHIPS
    flat = [a for batch in batches for a in batch]
    return call(
        functools.partial(dispatch_kernel, experts, tile),
        shape((CHIPS * experts, len(batches) * tile, wide)),
        *flat,
        scratch=[pltpu.VMEM(a.shape, a.dtype) for a in flat] + [pltpu.SemaphoreType.DMA((len(flat),))],
        name="dispatch",
        far=tuple(range(len(flat))),
    )


def bring_kernel(gu_own, gu_other, down_own, down_other, gu, down, arrived):
    half = gu_own.shape[1]
    copies = [
        pltpu.make_async_copy(down_own, down.at[:, :half], arrived.at[0]),
        pltpu.make_async_copy(down_other, down.at[:, half:], arrived.at[1]),
        pltpu.make_async_copy(gu_own, gu.at[:, :half], arrived.at[2]),
        pltpu.make_async_copy(gu_other, gu.at[:, half:], arrived.at[3]),
    ]
    for copy in copies:
        copy.start()
    for copy in copies:
        copy.wait()


def bring(gu_own, gu_other, down_own, down_other):
    outs = [shape((a.shape[0], CORES * a.shape[1])) for a in (gu_own, down_own)]
    scratch = [pltpu.SemaphoreType.DMA((4,))]
    return call(bring_kernel, outs, gu_own, gu_other, down_own, down_other, scratch=scratch, name="bring", far=range(4))


def slot_rows(experts, capacity):
    return round_up(CHIPS * capacity, TILE)


def squeeze_rows(arrived, at, tile, expert, experts, capacity):
    rows = slot_rows(experts, capacity)
    count = CHIPS * experts
    stacked = jnp.concatenate([arrived[j, at * tile : (at + 1) * tile] for j in range(count)], axis=0)
    column = iota((rows * experts, count * tile), 1)
    source, slot = column // tile, column % tile
    target = ((expert + experts - source % experts) % experts) * rows + (source // experts) * capacity + slot
    hit = jnp.logical_and(iota((rows * experts, count * tile), 0) == target, slot < capacity)
    return dot(jnp.where(hit, 1.0, 0.0).astype(jnp.bfloat16), stacked).astype(jnp.bfloat16)


def unit_rows(part, chip, units):
    return pl.ds(pl.multiple_of((part * CHIPS + chip) * units, units), units)


def up_kernel(experts, capacity, tile, arrived, gu, down, *refs):
    outs, held = refs[:-1], refs[-1]
    chip, core, expert = place()
    units = down.shape[0] // CHIPS
    half = held.shape[2] // CORES
    for at in range(2):
        rows = squeeze_rows(arrived, at, tile, expert, experts, capacity)
        held[at, :, :half] = jnp.where(core == 0, rows[:, :half], rows[:, half:])
        held[at, :, half:] = jnp.where(core == 0, rows[:, half:], rows[:, :half])
    for dk in (*range(1, CHIPS), 0):
        for part in range(2):
            product = dot(held[0], gu[unit_rows(part, chip ^ dk, units), :], NT)
            outs[dk][:, part * units : (part + 1) * units] = product.astype(outs[dk].dtype)
        product = dot(held[1], down[unit_rows(0, chip ^ dk, units), :], NT)
        outs[dk][:, 2 * units :] = product.astype(outs[dk].dtype)


def up(arrived, gu, down, experts, capacity, tile):
    rows = slot_rows(experts, capacity) * experts
    width = (gu.shape[0] + down.shape[0]) // CHIPS
    outs = [shape((rows, width), jnp.float32 if dk == 0 else jnp.bfloat16) for dk in range(CHIPS)]
    return call(
        functools.partial(up_kernel, experts, capacity, tile),
        outs,
        arrived,
        gu,
        down,
        scratch=[pltpu.VMEM((2, rows, gu.shape[1]), jnp.bfloat16)],
        flops=2 * rows * (gu.size + down.size),
        name="up",
    )


def act_kernel(*refs):
    parts, (mine, theirs, out) = refs[:CHIPS], refs[CHIPS:]
    _, core, _ = place()
    total = parts[0][...]
    for part in parts[1:]:
        total = total + part[...].astype(jnp.float32)
    units = total.shape[1] // 3
    gate_pre, up_pre, hidden_grad = total[:, :units], total[:, units : 2 * units], total[:, 2 * units :]
    out[:, :units] = (gate_pre * jax.nn.sigmoid(gate_pre) * up_pre).astype(jnp.bfloat16)
    own, other = mine[...].astype(jnp.float32), theirs[...].astype(jnp.float32)
    low, high = jnp.where(core == 0, own, other), jnp.where(core == 0, other, own)
    half = units // CORES
    for at, saved in enumerate((low, high)):
        gate_pre, up_pre = saved[:, :half], saved[:, half:]
        sig = jax.nn.sigmoid(gate_pre)
        grad = hidden_grad[:, at * half : (at + 1) * half]
        first = units + at * half
        out[:, first : first + half] = (grad * up_pre * (sig * (1.0 + gate_pre * (1.0 - sig)))).astype(jnp.bfloat16)
        out[:, first + units : first + units + half] = (grad * (gate_pre * sig)).astype(jnp.bfloat16)


def act(parts, mine, theirs):
    return call(act_kernel, shape(parts[0].shape), *parts, mine, theirs, name="act")


def down_kernel(experts, parts, gu, down, *outs):
    _, core, _ = place()
    half = down.shape[1] // CORES
    units = down.shape[0] // CHIPS
    rows = parts.shape[1] // experts
    for at, weight, halves in ((0, down, 1), (1, gu, 2)):
        total = None
        for k in range(CHIPS):
            for part in range(halves):
                column, first = (at + part) * units, (part * CHIPS + k) * units
                term = dot(parts[k, :, column : column + units], weight[first : first + units, :])
                total = term if total is None else total + term
        total = total.astype(jnp.bfloat16)
        for de in range(experts):
            out, span = outs[de], slice(at * rows, (at + 1) * rows)
            block = total[de * rows : (de + 1) * rows]
            out[span, :half] = jnp.where(core == 0, block[:, :half], block[:, half:])
            out[span, half:] = jnp.where(core == 0, block[:, half:], block[:, :half])


def down(parts, gu, down, experts):
    rows = parts.shape[1] // experts
    outs = [shape((2 * rows, down.shape[1])) for _ in range(experts)]
    flops = 2 * parts.shape[1] * (gu.size + down.size)
    return call(functools.partial(down_kernel, experts), outs, parts, gu, down, flops=flops, name="down")


def as_column(row):
    size = row.shape[1]
    same = iota((size, size), 0) == iota((size, size), 1)
    return jnp.sum(jnp.where(same, jnp.broadcast_to(row, (size, size)), 0.0), axis=1, keepdims=True)


def combine_kernel(experts, capacity, topk, tokens, tile, *refs):
    arrived, blocks, outs = refs[0], refs[1 : 1 + experts], refs[1 + experts :]
    chip, _, expert = place()
    rows = blocks[0].shape[0] // 2
    earlier = iota((tokens, tokens), 1) < iota((tokens, tokens), 0)
    for at in range(2):
        gates = [[] for _ in range(topk)]
        picks = [[[] for _ in range(experts)] for _ in range(topk)]
        for dk in range(CHIPS):
            source = (chip ^ dk) * experts + expert
            note = arrived[source, at * tile : (at + 1) * tile, : note_lanes(topk, tokens)]
            note = note.astype(jnp.float32)[tile - 1 :]
            column = as_column(note)

            def piece(part, kk):
                first = (part * topk + kk) * tokens
                return column[first : first + tokens]

            first_row = ((chip ^ dk) * capacity).astype(jnp.float32)
            for kk in range(topk):
                gates[kk].append(piece(1, kk) + piece(2, kk) + piece(3, kk))
            for de in range(experts):
                here = lax.rem(expert + de, experts).astype(jnp.float32)
                rank = jnp.zeros((tokens, 1), jnp.float32)
                for kk in range(topk):
                    named = note[:, kk * tokens : (kk + 1) * tokens] == here
                    named = jnp.where(named, 1.0, 0.0)
                    counted = jnp.where(earlier, jnp.broadcast_to(named, (tokens, tokens)), 0.0)
                    rank = rank + jnp.sum(counted, axis=1, keepdims=True)
                for kk in range(topk):
                    picks[kk][de].append(jnp.where(piece(0, kk) == here, rank + first_row, -1.0))
        slots = iota((CHIPS * tokens, rows), 1).astype(jnp.float32)
        total = None
        for kk in range(topk):
            found = None
            for de in range(experts):
                target = jnp.concatenate(picks[kk][de], axis=0)
                pick = jnp.where(slots == target, 1.0, 0.0).astype(jnp.bfloat16)
                term = dot(pick, blocks[de][at * rows : (at + 1) * rows])
                found = term if found is None else found + term
            term = found * jnp.concatenate(gates[kk], axis=0)
            total = term if total is None else total + term
        total = total.astype(jnp.bfloat16)
        for dk in range(CHIPS):
            outs[dk][at * tokens : (at + 1) * tokens] = total[dk * tokens : (dk + 1) * tokens]


def combine(arrived, blocks, experts, capacity, topk, tokens, tile):
    outs = [shape((2 * tokens, blocks[0].shape[1])) for _ in range(CHIPS)]
    return call(
        functools.partial(combine_kernel, experts, capacity, topk, tokens, tile),
        outs,
        arrived,
        *blocks,
        name="combine",
    )


def join_kernel(*refs):
    chip, _, _ = place()
    blocks, outs = refs[: -2], refs[-2:]
    tokens = outs[0].shape[0]
    for at, out in enumerate(outs):
        for dk in range(CHIPS):
            block = blocks[dk + at * (len(blocks) - CHIPS)]
            first = at * tokens if len(blocks) == CHIPS else 0
            out[:, block_of(chip ^ dk, block.shape[1])] = block[first : first + tokens]


def join(blocks, tokens):
    out = shape((tokens, CHIPS * blocks[0].shape[1]))
    return call(join_kernel, [out, out], *blocks, name="join")


def stash_kernel(experts, capacity, saved_ref, mine_ref, theirs_ref):
    _, core, expert = place()
    rows = slot_rows(experts, capacity)
    dims = (rows * experts, saved_ref.shape[0])
    row = iota(dims, 0)
    column = iota(dims, 1)
    for target, ref in ((core, mine_ref), (1 - core, theirs_ref)):
        wanted = jnp.full(dims, -1, jnp.int32)
        for de in range(experts):
            for at in range(CHIPS):
                source = (at * CORES + target) * experts + lax.rem(expert + experts - de, experts)
                low = de * rows + at * capacity
                inside = jnp.logical_and(row >= low, row < low + capacity)
                wanted = jnp.where(inside, row + (source * capacity - low), wanted)
        pick = jnp.where(column == wanted, 1.0, 0.0).astype(jnp.bfloat16)
        ref[...] = dot(pick, saved_ref[...]).astype(jnp.bfloat16)


def stash(saved, experts, capacity):
    out = shape((slot_rows(experts, capacity) * experts, saved.shape[1]))
    return call(functools.partial(stash_kernel, experts, capacity), [out, out], saved, name="stash")


def on_device(
    forward_input,
    forward_route,
    forward_gates,
    backward_cotangent,
    backward_route,
    backward_gates,
    gate_up_weight,
    down_weight,
    saved_projections,
):
    sections = lax.axis_size("section")
    experts = lax.axis_size("expert")
    topk = forward_route.shape[2]
    capacity = saved_projections.shape[2] // (GROUP * experts)
    tokens = forward_route.shape[1]
    tile = round_up(capacity + 1, TILE)

    def to_chip(value, dk):
        return lax.ppermute(value, "chip", [(i, i ^ dk) for i in range(CHIPS)])

    def to_section(value, dk, by):
        pairs = [
            (i * CHIPS + j, (i + by) % sections * CHIPS + (j ^ dk)) for i in range(sections) for j in range(CHIPS)
        ]
        return lax.ppermute(value, ("section", "chip"), pairs)

    def to_core(value):
        return lax.ppermute(value, "core", [(i, i ^ 1) for i in range(CORES)])

    def returned(block, de):
        if de == 0:
            return block
        return lax.ppermute(block, "expert", [((i + de) % experts, i) for i in range(experts)])

    batches = [
        (forward_route[0].T, forward_gates[0].T, forward_input[0]),
        (backward_route[0].T, backward_gates[0].T, backward_cotangent[0]),
    ]
    gu_own, down_own = gate_up_weight[0, 0], down_weight[0, 0]
    weights = (gu_own, to_core(gu_own), down_own, to_core(down_own))
    arrived = dispatch(batches, experts, tile)
    arrived = lax.all_to_all(arrived, ("chip", "expert"), split_axis=0, concat_axis=0, tiled=True)
    gu, down_both = bring(*weights)
    stash_mine, stash_theirs = stash(saved_projections[0, 0], experts, capacity)
    stash_other = to_core(stash_theirs)
    parts = up(arrived, gu, down_both, experts, capacity, tile)
    parts = [parts[0]] + [to_chip(parts[dk], dk) for dk in range(1, CHIPS)]
    units = lax.all_gather(act(parts, stash_mine, stash_other), "chip")
    blocks = down(units, gu, down_both, experts)
    blocks = [returned(blocks[de], de) for de in range(experts)]
    outs = combine(arrived, blocks, experts, capacity, topk, tokens, tile)
    if sections == 2:
        joined = [to_section(outs[dk], dk, 1) for dk in range(CHIPS)]
    else:
        joined = [to_section(outs[dk][:tokens], dk, 1) for dk in range(CHIPS)]
        joined += [to_section(outs[dk][tokens:], dk, -1) for dk in range(CHIPS)]
    next_input, prior_gradient = join(joined, tokens)
    return next_input[None], prior_gradient[None]


def solution(mesh):
    pipes, experts = mesh.devices.shape
    axes = ("section", "chip", "core", "expert")
    mesh = Mesh(mesh.devices.reshape(pipes // GROUP, CHIPS, CORES, experts), axes)
    rows = P(axes[:3], "expert", None)
    weights = P(axes[:3], "expert", None, None)
    return jax.shard_map(
        on_device,
        mesh=mesh,
        in_specs=(rows,) * 6 + (weights,) * 3,
        out_specs=(rows, rows),
        check_vma=False,
    )
```

```python
import functools

import jax
import jax.numpy as jnp
from jax import lax
from jax.experimental import pallas as pl
from jax.experimental.pallas import tpu as pltpu
from jax.sharding import Mesh
from jax.sharding import PartitionSpec as P

GROUP = 8
CORES = 2
CHIPS = GROUP // CORES
TILE = 16
NT = (((1,), (1,)), ((), ()))
NN = (((1,), (0,)), ((), ()))


def round_up(value, step):
    return (value + step - 1) // step * step


def dot(a, b, dims=NN):
    return lax.dot_general(a, b, dims, preferred_element_type=jnp.float32)


def iota(shape, axis):
    return lax.broadcasted_iota(jnp.int32, shape, axis)


def place():
    return lax.axis_index("chip"), lax.axis_index("core"), lax.axis_index("expert")


def block_of(index, size):
    return pl.ds(pl.multiple_of(index * size, size), size)


def call(kernel, outs, *args, scratch=(), flops=0, name=None, far=()):
    size = sum(a.size * a.dtype.itemsize for a in args)
    size += sum(o.size * o.dtype.itemsize for o in jax.tree.leaves(outs))
    spec = pl.BlockSpec(memory_space=pltpu.VMEM)
    return pl.pallas_call(
        kernel,
        out_shape=outs,
        in_specs=[pl.BlockSpec(memory_space=pltpu.HBM) if i in far else spec for i in range(len(args))],
        out_specs=jax.tree.map(lambda _: spec, outs),
        scratch_shapes=scratch,
        compiler_params=pltpu.CompilerParams(vmem_limit_bytes=16 * 2**20),
        cost_estimate=pl.CostEstimate(flops=flops, bytes_accessed=size, transcendentals=0),
        name=name,
    )(*args)


def shape(dims, dtype=jnp.bfloat16):
    return jax.ShapeDtypeStruct(dims, dtype)


def note_lanes(topk, tokens):
    return round_up(4 * topk * tokens, 128)


def dispatch_kernel(experts, tile, *refs):
    count = (len(refs) - 2) // 2
    far, out, near, arrived = refs[:count], refs[count], refs[count + 1 : -1], refs[-1]
    copies = [pltpu.make_async_copy(far[i], near[i], arrived.at[i]) for i in range(count)]
    for copy in copies:
        copy.start()
    for copy in copies:
        copy.wait()
    for at in range(count // 3):
        route, gate = near[3 * at][...], near[3 * at + 1][...]
        rows_ref = near[3 * at + 2]
        topk, tokens = route.shape
        lanes = note_lanes(topk, tokens)
        earlier = (iota((tokens, tokens), 0) < iota((tokens, tokens), 1)).astype(jnp.float32)
        pick = []
        for e in range(experts):
            named = jnp.max((route == e).astype(jnp.float32), axis=0, keepdims=True)
            rank = dot(jnp.broadcast_to(named, (8, tokens)), earlier)[:1]
            slots = iota((tile, tokens), 0).astype(jnp.float32)
            pick.append(jnp.where(jnp.logical_and(slots == rank, named > 0.0), 1.0, 0.0))
        pick = jnp.concatenate(pick, axis=0).astype(jnp.bfloat16)
        high = gate.astype(jnp.bfloat16).astype(jnp.float32)
        middle = (gate - high).astype(jnp.bfloat16).astype(jnp.float32)
        low = gate - high - middle
        note = jnp.zeros((8, lanes), jnp.float32)
        for part, value in enumerate((route.astype(jnp.float32), high, middle, low)):
            for kk in range(topk):
                first = (part * topk + kk) * tokens
                put = (iota((tokens, lanes), 1) == iota((tokens, lanes), 0) + first).astype(jnp.float32)
                row = jnp.broadcast_to(value[kk : kk + 1], (8, tokens))
                note = note + dot(row.astype(jnp.bfloat16), put.astype(jnp.bfloat16))
        note = jnp.where(iota((tile, lanes), 0) == tile - 1, jnp.broadcast_to(note[:1], (tile, lanes)), 0.0)
        wide = rows_ref.shape[1] // CHIPS
        span = slice(at * tile, (at + 1) * tile)
        for k in range(CHIPS):
            moved = dot(pick, rows_ref[:, k * wide : (k + 1) * wide])
            for e in range(experts):
                block = moved[e * tile : (e + 1) * tile]
                out[k * experts + e, span, :lanes] = (block[:, :lanes] + note).astype(jnp.bfloat16)
                out[k * experts + e, span, lanes:] = block[:, lanes:].astype(jnp.bfloat16)


def dispatch(batches, experts, tile):
    wide = batches[0][2].shape[1] // CHIPS
    flat = [a for batch in batches for a in batch]
    return call(
        functools.partial(dispatch_kernel, experts, tile),
        shape((CHIPS * experts, len(batches) * tile, wide)),
        *flat,
        scratch=[pltpu.VMEM(a.shape, a.dtype) for a in flat] + [pltpu.SemaphoreType.DMA((len(flat),))],
        name="dispatch",
        far=tuple(range(len(flat))),
    )


def slot_rows(experts, capacity):
    return round_up(CHIPS * capacity, TILE)


def squeeze_rows(arrived, at, tile, expert, experts, capacity):
    rows = slot_rows(experts, capacity)
    count = CHIPS * experts
    stacked = jnp.concatenate([arrived[j, at * tile : (at + 1) * tile] for j in range(count)], axis=0)
    column = iota((rows * experts, count * tile), 1)
    source, slot = column // tile, column % tile
    target = ((expert + experts - source % experts) % experts) * rows + (source // experts) * capacity + slot
    hit = jnp.logical_and(iota((rows * experts, count * tile), 0) == target, slot < capacity)
    return dot(jnp.where(hit, 1.0, 0.0).astype(jnp.bfloat16), stacked).astype(jnp.bfloat16)


def unit_rows(part, chip, units):
    return pl.ds(pl.multiple_of((part * CHIPS + chip) * units, units), units)


def up_kernel(experts, capacity, tile, arrived, gu_own, gu_other, down_own, down_other, gu, down, *refs):
    outs, (held, ready) = refs[:-2], refs[-2:]
    chip, core, expert = place()
    units = down.shape[0] // CHIPS
    half = held.shape[2] // CORES
    order = (*range(1, CHIPS), 0)
    copies = {}
    for dk in order:
        jobs = []
        for part, own, other, both in ((0, gu_own, gu_other, gu), (1, gu_own, gu_other, gu), (0, down_own, down_other, down)):
            rows = unit_rows(part, chip ^ dk, units)
            jobs += [(own.at[rows, :], both.at[rows, :half]), (other.at[rows, :], both.at[rows, half:])]
        copies[dk] = [pltpu.make_async_copy(*job, ready.at[dk, i]) for i, job in enumerate(jobs)]
        for copy in copies[dk]:
            copy.start()
    for at in range(2):
        rows = squeeze_rows(arrived, at, tile, expert, experts, capacity)
        held[at, :, :half] = jnp.where(core == 0, rows[:, :half], rows[:, half:])
        held[at, :, half:] = jnp.where(core == 0, rows[:, half:], rows[:, :half])
    for dk in order:
        for copy in copies[dk]:
            copy.wait()
        for part in range(2):
            product = dot(held[0], gu[unit_rows(part, chip ^ dk, units), :], NT)
            outs[dk][:, part * units : (part + 1) * units] = product.astype(outs[dk].dtype)
        product = dot(held[1], down[unit_rows(0, chip ^ dk, units), :], NT)
        outs[dk][:, 2 * units :] = product.astype(outs[dk].dtype)


def up(arrived, weights, experts, capacity, tile):
    rows = slot_rows(experts, capacity) * experts
    both = [shape((w.shape[0], CORES * w.shape[1])) for w in weights[::2]]
    width = sum(w.shape[0] for w in both) // CHIPS
    outs = [shape((rows, width), jnp.float32 if dk == 0 else jnp.bfloat16) for dk in range(CHIPS)]
    results = call(
        functools.partial(up_kernel, experts, capacity, tile),
        both + outs,
        arrived,
        *weights,
        scratch=[pltpu.VMEM((2, rows, both[0].shape[1]), jnp.bfloat16), pltpu.SemaphoreType.DMA((CHIPS, 6))],
        flops=2 * rows * sum(w.size for w in both),
        name="up",
        far=range(1, 5),
    )
    return results[:2], results[2:]


def act_kernel(*refs):
    parts, (mine, theirs, out) = refs[:CHIPS], refs[CHIPS:]
    _, core, _ = place()
    total = parts[0][...]
    for part in parts[1:]:
        total = total + part[...].astype(jnp.float32)
    units = total.shape[1] // 3
    gate_pre, up_pre, hidden_grad = total[:, :units], total[:, units : 2 * units], total[:, 2 * units :]
    out[:, :units] = (gate_pre * jax.nn.sigmoid(gate_pre) * up_pre).astype(jnp.bfloat16)
    own, other = mine[...].astype(jnp.float32), theirs[...].astype(jnp.float32)
    low, high = jnp.where(core == 0, own, other), jnp.where(core == 0, other, own)
    half = units // CORES
    for at, saved in enumerate((low, high)):
        gate_pre, up_pre = saved[:, :half], saved[:, half:]
        sig = jax.nn.sigmoid(gate_pre)
        grad = hidden_grad[:, at * half : (at + 1) * half]
        first = units + at * half
        out[:, first : first + half] = (grad * up_pre * (sig * (1.0 + gate_pre * (1.0 - sig)))).astype(jnp.bfloat16)
        out[:, first + units : first + units + half] = (grad * (gate_pre * sig)).astype(jnp.bfloat16)


def act(parts, mine, theirs):
    return call(act_kernel, shape(parts[0].shape), *parts, mine, theirs, name="act")


def down_kernel(experts, *refs):
    parts, (gu, down), outs = refs[:CHIPS], refs[CHIPS : CHIPS + 2], refs[CHIPS + 2 :]
    chip, core, _ = place()
    half = down.shape[1] // CORES
    units = down.shape[0] // CHIPS
    rows = parts[0].shape[0] // experts
    for at, weight, halves in ((0, down, 1), (1, gu, 2)):
        total = None
        for dk in range(CHIPS):
            for part in range(halves):
                column = (at + part) * units
                term = dot(parts[dk][:, column : column + units], weight[unit_rows(part, chip ^ dk, units), :])
                total = term if total is None else total + term
        total = total.astype(jnp.bfloat16)
        for de in range(experts):
            out, span = outs[de], slice(at * rows, (at + 1) * rows)
            block = total[de * rows : (de + 1) * rows]
            out[span, :half] = jnp.where(core == 0, block[:, :half], block[:, half:])
            out[span, half:] = jnp.where(core == 0, block[:, half:], block[:, :half])


def down(parts, gu, down, experts):
    rows = parts[0].shape[0] // experts
    outs = [shape((2 * rows, down.shape[1])) for _ in range(experts)]
    flops = 2 * parts[0].shape[0] * (gu.size + down.size)
    return call(functools.partial(down_kernel, experts), outs, *parts, gu, down, flops=flops, name="down")


def as_column(row):
    size = row.shape[1]
    same = iota((size, size), 0) == iota((size, size), 1)
    return jnp.sum(jnp.where(same, jnp.broadcast_to(row, (size, size)), 0.0), axis=1, keepdims=True)


def combine_kernel(experts, capacity, topk, tokens, tile, *refs):
    arrived, blocks, outs = refs[0], refs[1 : 1 + experts], refs[1 + experts :]
    chip, _, expert = place()
    rows = blocks[0].shape[0] // 2
    earlier = iota((tokens, tokens), 1) < iota((tokens, tokens), 0)
    for at in range(2):
        gates = [[] for _ in range(topk)]
        picks = [[[] for _ in range(experts)] for _ in range(topk)]
        for dk in range(CHIPS):
            source = (chip ^ dk) * experts + expert
            note = arrived[source, at * tile : (at + 1) * tile, : note_lanes(topk, tokens)]
            note = note.astype(jnp.float32)[tile - 1 :]
            column = as_column(note)

            def piece(part, kk):
                first = (part * topk + kk) * tokens
                return column[first : first + tokens]

            first_row = ((chip ^ dk) * capacity).astype(jnp.float32)
            for kk in range(topk):
                gates[kk].append(piece(1, kk) + piece(2, kk) + piece(3, kk))
            for de in range(experts):
                here = lax.rem(expert + de, experts).astype(jnp.float32)
                rank = jnp.zeros((tokens, 1), jnp.float32)
                for kk in range(topk):
                    named = note[:, kk * tokens : (kk + 1) * tokens] == here
                    named = jnp.where(named, 1.0, 0.0)
                    counted = jnp.where(earlier, jnp.broadcast_to(named, (tokens, tokens)), 0.0)
                    rank = rank + jnp.sum(counted, axis=1, keepdims=True)
                for kk in range(topk):
                    picks[kk][de].append(jnp.where(piece(0, kk) == here, rank + first_row, -1.0))
        slots = iota((CHIPS * tokens, rows), 1).astype(jnp.float32)
        total = None
        for kk in range(topk):
            found = None
            for de in range(experts):
                target = jnp.concatenate(picks[kk][de], axis=0)
                pick = jnp.where(slots == target, 1.0, 0.0).astype(jnp.bfloat16)
                term = dot(pick, blocks[de][at * rows : (at + 1) * rows])
                found = term if found is None else found + term
            term = found * jnp.concatenate(gates[kk], axis=0)
            total = term if total is None else total + term
        total = total.astype(jnp.bfloat16)
        for dk in range(CHIPS):
            outs[dk][at * tokens : (at + 1) * tokens] = total[dk * tokens : (dk + 1) * tokens]


def combine(arrived, blocks, experts, capacity, topk, tokens, tile):
    outs = [shape((2 * tokens, blocks[0].shape[1])) for _ in range(CHIPS)]
    return call(
        functools.partial(combine_kernel, experts, capacity, topk, tokens, tile),
        outs,
        arrived,
        *blocks,
        name="combine",
    )


def join_kernel(*refs):
    chip, _, _ = place()
    blocks, outs = refs[: -2], refs[-2:]
    tokens = outs[0].shape[0]
    for at, out in enumerate(outs):
        for dk in range(CHIPS):
            block = blocks[dk + at * (len(blocks) - CHIPS)]
            first = at * tokens if len(blocks) == CHIPS else 0
            out[:, block_of(chip ^ dk, block.shape[1])] = block[first : first + tokens]


def join(blocks, tokens):
    out = shape((tokens, CHIPS * blocks[0].shape[1]))
    return call(join_kernel, [out, out], *blocks, name="join")


def stash_kernel(experts, capacity, saved_ref, mine_ref, theirs_ref):
    _, core, expert = place()
    rows = slot_rows(experts, capacity)
    dims = (rows * experts, saved_ref.shape[0])
    row = iota(dims, 0)
    column = iota(dims, 1)
    for target, ref in ((core, mine_ref), (1 - core, theirs_ref)):
        wanted = jnp.full(dims, -1, jnp.int32)
        for de in range(experts):
            for at in range(CHIPS):
                source = (at * CORES + target) * experts + lax.rem(expert + experts - de, experts)
                low = de * rows + at * capacity
                inside = jnp.logical_and(row >= low, row < low + capacity)
                wanted = jnp.where(inside, row + (source * capacity - low), wanted)
        pick = jnp.where(column == wanted, 1.0, 0.0).astype(jnp.bfloat16)
        ref[...] = dot(pick, saved_ref[...]).astype(jnp.bfloat16)


def stash(saved, experts, capacity):
    out = shape((slot_rows(experts, capacity) * experts, saved.shape[1]))
    return call(functools.partial(stash_kernel, experts, capacity), [out, out], saved, name="stash")


def on_device(
    forward_input,
    forward_route,
    forward_gates,
    backward_cotangent,
    backward_route,
    backward_gates,
    gate_up_weight,
    down_weight,
    saved_projections,
):
    sections = lax.axis_size("section")
    experts = lax.axis_size("expert")
    topk = forward_route.shape[2]
    capacity = saved_projections.shape[2] // (GROUP * experts)
    tokens = forward_route.shape[1]
    tile = round_up(capacity + 1, TILE)

    def to_chip(value, dk):
        return lax.ppermute(value, "chip", [(i, i ^ dk) for i in range(CHIPS)])

    def to_section(value, dk, by):
        pairs = [
            (i * CHIPS + j, (i + by) % sections * CHIPS + (j ^ dk)) for i in range(sections) for j in range(CHIPS)
        ]
        return lax.ppermute(value, ("section", "chip"), pairs)

    def to_core(value):
        return lax.ppermute(value, "core", [(i, i ^ 1) for i in range(CORES)])

    def returned(block, de):
        if de == 0:
            return block
        return lax.ppermute(block, "expert", [((i + de) % experts, i) for i in range(experts)])

    batches = [
        (forward_route[0].T, forward_gates[0].T, forward_input[0]),
        (backward_route[0].T, backward_gates[0].T, backward_cotangent[0]),
    ]
    gu_own, down_own = gate_up_weight[0, 0], down_weight[0, 0]
    weights = (gu_own, to_core(gu_own), down_own, to_core(down_own))
    arrived = dispatch(batches, experts, tile)
    arrived = lax.all_to_all(arrived, ("chip", "expert"), split_axis=0, concat_axis=0, tiled=True)
    stash_mine, stash_theirs = stash(saved_projections[0, 0], experts, capacity)
    stash_other = to_core(stash_theirs)
    (gu, down_both), parts = up(arrived, weights, experts, capacity, tile)
    parts = [parts[0]] + [to_chip(parts[dk], dk) for dk in range(1, CHIPS)]
    units = act(parts, stash_mine, stash_other)
    units = [units] + [to_chip(units, dk) for dk in range(1, CHIPS)]
    blocks = down(units, gu, down_both, experts)
    blocks = [returned(blocks[de], de) for de in range(experts)]
    outs = combine(arrived, blocks, experts, capacity, topk, tokens, tile)
    if sections == 2:
        joined = [to_section(outs[dk], dk, 1) for dk in range(CHIPS)]
    else:
        joined = [to_section(outs[dk][:tokens], dk, 1) for dk in range(CHIPS)]
        joined += [to_section(outs[dk][tokens:], dk, -1) for dk in range(CHIPS)]
    next_input, prior_gradient = join(joined, tokens)
    return next_input[None], prior_gradient[None]


def solution(mesh):
    pipes, experts = mesh.devices.shape
    axes = ("section", "chip", "core", "expert")
    mesh = Mesh(mesh.devices.reshape(pipes // GROUP, CHIPS, CORES, experts), axes)
    rows = P(axes[:3], "expert", None)
    weights = P(axes[:3], "expert", None, None)
    return jax.shard_map(
        on_device,
        mesh=mesh,
        in_specs=(rows,) * 6 + (weights,) * 3,
        out_specs=(rows, rows),
        check_vma=False,
    )
```

```python
import functools

import jax
import jax.numpy as jnp
from jax import lax
from jax.experimental import pallas as pl
from jax.experimental.pallas import tpu as pltpu
from jax.sharding import Mesh
from jax.sharding import PartitionSpec as P

GROUP = 8
CORES = 2
CHIPS = GROUP // CORES
TILE = 16
NT = (((1,), (1,)), ((), ()))
NN = (((1,), (0,)), ((), ()))


def round_up(value, step):
    return (value + step - 1) // step * step


def dot(a, b, dims=NN):
    return lax.dot_general(a, b, dims, preferred_element_type=jnp.float32)


def iota(shape, axis):
    return lax.broadcasted_iota(jnp.int32, shape, axis)


def place():
    return lax.axis_index("chip"), lax.axis_index("core"), lax.axis_index("expert")


def block_of(index, size):
    return pl.ds(pl.multiple_of(index * size, size), size)


def call(kernel, outs, *args, scratch=(), flops=0, name=None, far=()):
    size = sum(a.size * a.dtype.itemsize for a in args)
    size += sum(o.size * o.dtype.itemsize for o in jax.tree.leaves(outs))
    spec = pl.BlockSpec(memory_space=pltpu.VMEM)
    return pl.pallas_call(
        kernel,
        out_shape=outs,
        in_specs=[pl.BlockSpec(memory_space=pl.ANY) if i in far else spec for i in range(len(args))],
        out_specs=jax.tree.map(lambda _: spec, outs),
        scratch_shapes=scratch,
        compiler_params=pltpu.CompilerParams(vmem_limit_bytes=16 * 2**20),
        cost_estimate=pl.CostEstimate(flops=flops, bytes_accessed=size, transcendentals=0),
        name=name,
    )(*(pltpu.with_memory_space_constraint(a, pltpu.HBM) if i in far else a for i, a in enumerate(args)))


def shape(dims, dtype=jnp.bfloat16):
    return jax.ShapeDtypeStruct(dims, dtype)


def note_lanes(topk, tokens):
    return round_up(4 * topk * tokens, 128)


def dispatch_kernel(experts, tile, batches, *refs):
    near, arrived = refs[-1 - 3 * batches : -1], refs[-1]
    far, (gu, down), outs = refs[: 3 * batches], refs[3 * batches : 3 * batches + 2], refs[3 * batches + 2 : -1 - 3 * batches]
    held, outs = outs[0], outs[1:]
    copies = [pltpu.make_async_copy(far[i], near[i], arrived.at[i]) for i in range(3 * batches)]
    copies += [
        pltpu.make_async_copy(gu, held.at[: gu.shape[0]], arrived.at[3 * batches]),
        pltpu.make_async_copy(down, held.at[gu.shape[0] :], arrived.at[3 * batches + 1]),
    ]
    for copy in copies:
        copy.start()
    for copy in copies[: 3 * batches]:
        copy.wait()
    chip, _, expert = place()
    for at in range(batches):
        route, gate = near[3 * at][...], near[3 * at + 1][...]
        rows_ref = near[3 * at + 2]
        topk, tokens = route.shape
        lanes = note_lanes(topk, tokens)
        earlier = (iota((tokens, tokens), 0) < iota((tokens, tokens), 1)).astype(jnp.float32)
        pick = []
        for de in range(experts):
            here = lax.rem(expert + de, experts)
            named = jnp.max((route == here).astype(jnp.float32), axis=0, keepdims=True)
            rank = dot(jnp.broadcast_to(named, (8, tokens)), earlier)[:1]
            slots = iota((tile, tokens), 0).astype(jnp.float32)
            pick.append(jnp.where(jnp.logical_and(slots == rank, named > 0.0), 1.0, 0.0))
        pick = jnp.concatenate(pick, axis=0).astype(jnp.bfloat16)
        high = gate.astype(jnp.bfloat16).astype(jnp.float32)
        middle = (gate - high).astype(jnp.bfloat16).astype(jnp.float32)
        low = gate - high - middle
        note = jnp.zeros((8, lanes), jnp.float32)
        for part, value in enumerate((route.astype(jnp.float32), high, middle, low)):
            for kk in range(topk):
                first = (part * topk + kk) * tokens
                put = (iota((tokens, lanes), 1) == iota((tokens, lanes), 0) + first).astype(jnp.float32)
                row = jnp.broadcast_to(value[kk : kk + 1], (8, tokens))
                note = note + dot(row.astype(jnp.bfloat16), put.astype(jnp.bfloat16))
        note = jnp.where(iota((tile, lanes), 0) == tile - 1, jnp.broadcast_to(note[:1], (tile, lanes)), 0.0)
        wide = rows_ref.shape[1] // CHIPS
        span = slice(at * tile, (at + 1) * tile)
        for dk in range(CHIPS):
            moved = dot(pick, rows_ref[:, block_of(chip ^ dk, wide)])
            for de in range(experts):
                block, out = moved[de * tile : (de + 1) * tile], outs[dk * experts + de]
                out[span, :lanes] = (block[:, :lanes] + note).astype(jnp.bfloat16)
                out[span, lanes:] = block[:, lanes:].astype(jnp.bfloat16)
    for copy in copies[3 * batches :]:
        copy.wait()


def dispatch(batches, gu, down, experts, tile):
    wide = batches[0][2].shape[1] // CHIPS
    flat = [a for batch in batches for a in batch]
    held = shape((gu.shape[0] + down.shape[0], gu.shape[1]))
    outs = [shape((len(batches) * tile, wide)) for _ in range(CHIPS * experts)]
    results = call(
        functools.partial(dispatch_kernel, experts, tile, len(batches)),
        [held] + outs,
        *flat,
        gu,
        down,
        scratch=[pltpu.VMEM(a.shape, a.dtype) for a in flat] + [pltpu.SemaphoreType.DMA((len(flat) + 2,))],
        name="dispatch",
        far=range(len(flat) + 2),
    )
    return results[0], results[1:]


def slot_rows(experts, capacity):
    return round_up(CHIPS * capacity, TILE)


def squeeze_rows(blocks, at, tile, chip, experts, capacity):
    rows = slot_rows(experts, capacity)
    stacked = jnp.concatenate([b[at * tile : (at + 1) * tile] for b in blocks], axis=0)
    total = len(blocks) * tile
    column = iota((rows * experts, total), 1)
    source, slot = column // tile, column % tile
    target = (source % experts) * rows + ((source // experts) ^ chip) * capacity + slot
    hit = jnp.logical_and(iota((rows * experts, total), 0) == target, slot < capacity)
    return dot(jnp.where(hit, 1.0, 0.0).astype(jnp.bfloat16), stacked).astype(jnp.bfloat16)


def unit_rows(part, chip, units):
    return pl.ds(pl.multiple_of((part * CHIPS + chip) * units, units), units)


def up_kernel(experts, capacity, tile, *refs):
    count = CHIPS * experts
    blocks, (own, other), outs, held = refs[:count], refs[count : count + 2], refs[count + 2 : -1], refs[-1]
    chip, core, _ = place()
    units = own.shape[0] // 3 // CHIPS
    half = own.shape[1]
    for at in range(2):
        held[at] = squeeze_rows(blocks, at, tile, chip, experts, capacity)
    for dk in (*range(1, CHIPS), 0):
        for part in range(3):
            rows, at = unit_rows(part, chip ^ dk, units), part // 2
            product = dot(held[at, :, block_of(core, half)], own[rows, :], NT)
            product += dot(held[at, :, block_of(1 - core, half)], other[rows, :], NT)
            outs[dk][:, part * units : (part + 1) * units] = product.astype(outs[dk].dtype)


def up(blocks, own, other, experts, capacity, tile):
    rows = slot_rows(experts, capacity) * experts
    width = own.shape[0] // CHIPS
    outs = [shape((rows, width), jnp.float32 if dk == 0 else jnp.bfloat16) for dk in range(CHIPS)]
    return call(
        functools.partial(up_kernel, experts, capacity, tile),
        outs,
        *blocks,
        own,
        other,
        scratch=[pltpu.VMEM((2, rows, blocks[0].shape[1]), jnp.bfloat16)],
        flops=4 * rows * own.size,
        name="up",
    )


def act_kernel(*refs):
    parts, (mine, theirs, out) = refs[:CHIPS], refs[CHIPS:]
    _, core, _ = place()
    total = parts[0][...]
    for part in parts[1:]:
        total = total + part[...].astype(jnp.float32)
    units = total.shape[1] // 3
    gate_pre, up_pre, hidden_grad = total[:, :units], total[:, units : 2 * units], total[:, 2 * units :]
    out[:, :units] = (gate_pre * jax.nn.sigmoid(gate_pre) * up_pre).astype(jnp.bfloat16)
    own, other = mine[...].astype(jnp.float32), theirs[...].astype(jnp.float32)
    low, high = jnp.where(core == 0, own, other), jnp.where(core == 0, other, own)
    half = units // CORES
    for at, saved in enumerate((low, high)):
        gate_pre, up_pre = saved[:, :half], saved[:, half:]
        sig = jax.nn.sigmoid(gate_pre)
        grad = hidden_grad[:, at * half : (at + 1) * half]
        first = units + at * half
        out[:, first : first + half] = (grad * up_pre * (sig * (1.0 + gate_pre * (1.0 - sig)))).astype(jnp.bfloat16)
        out[:, first + units : first + units + half] = (grad * (gate_pre * sig)).astype(jnp.bfloat16)


def act(parts, mine, theirs):
    return call(act_kernel, shape(parts[0].shape), *parts, mine, theirs, name="act")


def down_kernel(experts, *refs):
    parts, (own, other), outs = refs[:CHIPS], refs[CHIPS : CHIPS + 2], refs[CHIPS + 2 :]
    chip, core, _ = place()
    half = own.shape[1]
    units = own.shape[0] // 3 // CHIPS
    rows = parts[0].shape[0] // experts
    for at, terms in ((0, ((0, 2),)), (1, ((1, 0), (2, 1)))):
        for weight, column in ((own, core), (other, 1 - core)):
            total = None
            for dk in range(CHIPS):
                for piece, part in terms:
                    left = parts[dk][:, piece * units : (piece + 1) * units]
                    term = dot(left, weight[unit_rows(part, chip ^ dk, units), :])
                    total = term if total is None else total + term
            total = total.astype(jnp.bfloat16)
            for de in range(experts):
                span = slice(at * rows, (at + 1) * rows)
                outs[de][span, block_of(column, half)] = total[de * rows : (de + 1) * rows]


def down(parts, own, other, experts):
    rows = parts[0].shape[0] // experts
    outs = [shape((2 * rows, CORES * own.shape[1])) for _ in range(experts)]
    flops = 4 * parts[0].shape[0] * own.size
    return call(functools.partial(down_kernel, experts), outs, *parts, own, other, flops=flops, name="down")


def as_column(row):
    size = row.shape[1]
    same = iota((size, size), 0) == iota((size, size), 1)
    return jnp.sum(jnp.where(same, jnp.broadcast_to(row, (size, size)), 0.0), axis=1, keepdims=True)


def combine_kernel(experts, capacity, topk, tokens, tile, *refs):
    notes, blocks, outs = refs[:CHIPS], refs[CHIPS : CHIPS + experts], refs[CHIPS + experts :]
    chip, _, expert = place()
    rows = blocks[0].shape[0] // 2
    earlier = iota((tokens, tokens), 1) < iota((tokens, tokens), 0)
    for at in range(2):
        gates = [[] for _ in range(topk)]
        picks = [[[] for _ in range(experts)] for _ in range(topk)]
        for dk in range(CHIPS):
            note = notes[dk][at * tile : (at + 1) * tile, : note_lanes(topk, tokens)]
            note = note.astype(jnp.float32)[tile - 1 :]
            column = as_column(note)

            def piece(part, kk):
                first = (part * topk + kk) * tokens
                return column[first : first + tokens]

            first_row = ((chip ^ dk) * capacity).astype(jnp.float32)
            for kk in range(topk):
                gates[kk].append(piece(1, kk) + piece(2, kk) + piece(3, kk))
            for de in range(experts):
                here = lax.rem(expert + de, experts).astype(jnp.float32)
                rank = jnp.zeros((tokens, 1), jnp.float32)
                for kk in range(topk):
                    named = note[:, kk * tokens : (kk + 1) * tokens] == here
                    named = jnp.where(named, 1.0, 0.0)
                    counted = jnp.where(earlier, jnp.broadcast_to(named, (tokens, tokens)), 0.0)
                    rank = rank + jnp.sum(counted, axis=1, keepdims=True)
                for kk in range(topk):
                    picks[kk][de].append(jnp.where(piece(0, kk) == here, rank + first_row, -1.0))
        slots = iota((CHIPS * tokens, rows), 1).astype(jnp.float32)
        total = None
        for kk in range(topk):
            found = None
            for de in range(experts):
                target = jnp.concatenate(picks[kk][de], axis=0)
                pick = jnp.where(slots == target, 1.0, 0.0).astype(jnp.bfloat16)
                term = dot(pick, blocks[de][at * rows : (at + 1) * rows])
                found = term if found is None else found + term
            term = found * jnp.concatenate(gates[kk], axis=0)
            total = term if total is None else total + term
        total = total.astype(jnp.bfloat16)
        for dk in range(CHIPS):
            outs[dk][at * tokens : (at + 1) * tokens] = total[dk * tokens : (dk + 1) * tokens]


def combine(notes, blocks, experts, capacity, topk, tokens, tile):
    outs = [shape((2 * tokens, blocks[0].shape[1])) for _ in range(CHIPS)]
    return call(
        functools.partial(combine_kernel, experts, capacity, topk, tokens, tile),
        outs,
        *notes,
        *blocks,
        name="combine",
    )


def join_kernel(*refs):
    chip, _, _ = place()
    blocks, outs = refs[: -2], refs[-2:]
    tokens = outs[0].shape[0]
    for at, out in enumerate(outs):
        for dk in range(CHIPS):
            block = blocks[dk + at * (len(blocks) - CHIPS)]
            first = at * tokens if len(blocks) == CHIPS else 0
            out[:, block_of(chip ^ dk, block.shape[1])] = block[first : first + tokens]


def join(blocks, tokens):
    out = shape((tokens, CHIPS * blocks[0].shape[1]))
    return call(join_kernel, [out, out], *blocks, name="join")


def stash_kernel(experts, capacity, saved_ref, mine_ref, theirs_ref):
    _, core, expert = place()
    rows = slot_rows(experts, capacity)
    dims = (rows * experts, saved_ref.shape[0])
    row = iota(dims, 0)
    column = iota(dims, 1)
    for target, ref in ((core, mine_ref), (1 - core, theirs_ref)):
        wanted = jnp.full(dims, -1, jnp.int32)
        for de in range(experts):
            for at in range(CHIPS):
                source = (at * CORES + target) * experts + lax.rem(expert + experts - de, experts)
                low = de * rows + at * capacity
                inside = jnp.logical_and(row >= low, row < low + capacity)
                wanted = jnp.where(inside, row + (source * capacity - low), wanted)
        pick = jnp.where(column == wanted, 1.0, 0.0).astype(jnp.bfloat16)
        ref[...] = dot(pick, saved_ref[...]).astype(jnp.bfloat16)


def stash(saved, experts, capacity):
    out = shape((slot_rows(experts, capacity) * experts, saved.shape[1]))
    return call(functools.partial(stash_kernel, experts, capacity), [out, out], saved, name="stash")


def on_device(
    forward_input,
    forward_route,
    forward_gates,
    backward_cotangent,
    backward_route,
    backward_gates,
    gate_up_weight,
    down_weight,
    saved_projections,
):
    sections = lax.axis_size("section")
    experts = lax.axis_size("expert")
    topk = forward_route.shape[2]
    capacity = saved_projections.shape[2] // (GROUP * experts)
    tokens = forward_route.shape[1]
    tile = round_up(capacity + 1, TILE)

    def to_chip(value, dk):
        return lax.ppermute(value, "chip", [(i, i ^ dk) for i in range(CHIPS)])

    def to_section(value, dk, by):
        pairs = [
            (i * CHIPS + j, (i + by) % sections * CHIPS + (j ^ dk)) for i in range(sections) for j in range(CHIPS)
        ]
        return lax.ppermute(value, ("section", "chip"), pairs)

    def to_place(value, dk, de):
        if dk == 0 and de == 0:
            return value
        pairs = [
            (i * experts + j, (i ^ dk) * experts + (j + de) % experts) for i in range(CHIPS) for j in range(experts)
        ]
        return lax.ppermute(value, ("chip", "expert"), pairs)

    def to_core(value):
        return lax.ppermute(value, "core", [(i, i ^ 1) for i in range(CORES)])

    def returned(block, de):
        if de == 0:
            return block
        return lax.ppermute(block, "expert", [((i + de) % experts, i) for i in range(experts)])

    batches = [
        (forward_route[0].T, forward_gates[0].T, forward_input[0]),
        (backward_route[0].T, backward_gates[0].T, backward_cotangent[0]),
    ]
    own, sent = dispatch(batches, gate_up_weight[0, 0], down_weight[0, 0], experts, tile)
    arrived = [to_place(sent[dk * experts + de], dk, de) for dk in range(CHIPS) for de in range(experts)]
    other = to_core(own)
    stash_mine, stash_theirs = stash(saved_projections[0, 0], experts, capacity)
    stash_other = to_core(stash_theirs)
    parts = up(arrived, own, other, experts, capacity, tile)
    parts = [parts[0]] + [to_chip(parts[dk], dk) for dk in range(1, CHIPS)]
    units = act(parts, stash_mine, stash_other)
    units = [units] + [to_chip(units, dk) for dk in range(1, CHIPS)]
    blocks = down(units, own, other, experts)
    blocks = [returned(blocks[de], de) for de in range(experts)]
    outs = combine(arrived[::experts], blocks, experts, capacity, topk, tokens, tile)
    if sections == 2:
        joined = [to_section(outs[dk], dk, 1) for dk in range(CHIPS)]
    else:
        joined = [to_section(outs[dk][:tokens], dk, 1) for dk in range(CHIPS)]
        joined += [to_section(outs[dk][tokens:], dk, -1) for dk in range(CHIPS)]
    next_input, prior_gradient = join(joined, tokens)
    return next_input[None], prior_gradient[None]


def solution(mesh):
    pipes, experts = mesh.devices.shape
    axes = ("section", "chip", "core", "expert")
    mesh = Mesh(mesh.devices.reshape(pipes // GROUP, CHIPS, CORES, experts), axes)
    rows = P(axes[:3], "expert", None)
    weights = P(axes[:3], "expert", None, None)
    return jax.shard_map(
        on_device,
        mesh=mesh,
        in_specs=(rows,) * 6 + (weights,) * 3,
        out_specs=(rows, rows),
        check_vma=False,
    )
```

```python
import functools

import jax
import jax.numpy as jnp
from jax import lax
from jax.experimental import pallas as pl
from jax.experimental.pallas import tpu as pltpu
from jax.sharding import Mesh
from jax.sharding import PartitionSpec as P

GROUP = 8
CORES = 2
CHIPS = GROUP // CORES
TILE = 16
NT = (((1,), (1,)), ((), ()))
NN = (((1,), (0,)), ((), ()))
TN = (((0,), (0,)), ((), ()))


def round_up(value, step):
    return (value + step - 1) // step * step


def dot(a, b, dims=NN):
    return lax.dot_general(a, b, dims, preferred_element_type=jnp.float32)


def iota(shape, axis):
    return lax.broadcasted_iota(jnp.int32, shape, axis)


def place():
    return lax.axis_index("chip"), lax.axis_index("core"), lax.axis_index("expert")


def block_of(index, size):
    return pl.ds(pl.multiple_of(index * size, size), size)


def call(kernel, outs, *args, scratch=(), flops=0, name=None, far=()):
    size = sum(a.size * a.dtype.itemsize for a in args)
    size += sum(o.size * o.dtype.itemsize for o in jax.tree.leaves(outs))
    spec = pl.BlockSpec(memory_space=pltpu.VMEM)
    return pl.pallas_call(
        kernel,
        out_shape=outs,
        in_specs=[pl.BlockSpec(memory_space=pl.ANY) if i in far else spec for i in range(len(args))],
        out_specs=jax.tree.map(lambda _: spec, outs),
        scratch_shapes=scratch,
        compiler_params=pltpu.CompilerParams(vmem_limit_bytes=16 * 2**20),
        cost_estimate=pl.CostEstimate(flops=flops, bytes_accessed=size, transcendentals=0),
        name=name,
    )(*(pltpu.with_memory_space_constraint(a, pltpu.HBM) if i in far else a for i, a in enumerate(args)))


def shape(dims, dtype=jnp.bfloat16):
    return jax.ShapeDtypeStruct(dims, dtype)


def slot_rows(experts, capacity):
    return round_up(CHIPS * capacity, TILE)


def dispatch_kernel(experts, capacity, *refs):
    far, held, outs, near, ready = refs[:9], refs[9], refs[10 : 10 + CHIPS], refs[10 + CHIPS : -1], refs[-1]
    gu, down, saved = far[6:]
    near_saved = near[4]
    chip, core, expert = place()
    tokens, width = far[4].shape
    wide = width // CHIPS
    units = gu.shape[0] + down.shape[0]
    jobs = [(far[i], near[i]) for i in range(4)]
    for dk in range(CHIPS):
        for at in range(2):
            block = outs[dk].at[at * tokens : (at + 1) * tokens, :wide]
            jobs.append((far[4 + at].at[:, block_of(chip ^ dk, wide)], block))
    jobs += [(saved, near_saved), (gu, held.at[: gu.shape[0]]), (down, held.at[gu.shape[0] : units])]
    copies = [pltpu.make_async_copy(*job, ready.at[i]) for i, job in enumerate(jobs)]
    for copy in copies:
        copy.start()
    for copy in copies[:4]:
        copy.wait()
    for at in range(2):
        route, gate = near[2 * at][...], near[2 * at + 1][...]
        topk = route.shape[0]
        earlier = (iota((tokens, tokens), 0) < iota((tokens, tokens), 1)).astype(jnp.float32)
        rank = jnp.zeros((topk, tokens), jnp.float32)
        for e in range(experts):
            named = (route == e).astype(jnp.float32)
            count = jnp.broadcast_to(jnp.sum(named, axis=0, keepdims=True), (8, tokens))
            rank = rank + named * dot(count, earlier)[:1]
        high = gate.astype(jnp.bfloat16).astype(jnp.float32)
        middle = (gate - high).astype(jnp.bfloat16).astype(jnp.float32)
        low = gate - high - middle
        table = jnp.zeros((128, tokens), jnp.float32)
        for part, value in enumerate((route.astype(jnp.float32), rank, high, middle, low)):
            for kk in range(topk):
                row = jnp.broadcast_to(value[kk : kk + 1], (128, tokens))
                table = jnp.where(iota((128, tokens), 0) == part * topk + kk, row, table)
        same = (iota((tokens, tokens), 0) == iota((tokens, tokens), 1)).astype(jnp.bfloat16)
        note = dot(same, table.astype(jnp.bfloat16), NT).astype(jnp.bfloat16)
        for dk in range(CHIPS):
            outs[dk][at * tokens : (at + 1) * tokens, wide:] = note
    for copy in copies[4:-2]:
        copy.wait()
    stash(experts, capacity, core, expert, near_saved, held, units)
    for copy in copies[-2:]:
        copy.wait()


def stash(experts, capacity, core, expert, saved, held, first):
    rows = slot_rows(experts, capacity)
    dims = (rows * experts, saved.shape[0])
    width = saved.shape[1]
    row, column = iota(dims, 0), iota(dims, 1)
    for target, lane in ((1 - core, 0), (core, width)):
        wanted = jnp.full(dims, -1, jnp.int32)
        for de in range(experts):
            for at in range(CHIPS):
                source = (at * CORES + target) * experts + lax.rem(expert + experts - de, experts)
                low = de * rows + at * capacity
                inside = jnp.logical_and(row >= low, row < low + capacity)
                wanted = jnp.where(inside, row + (source * capacity - low), wanted)
        pick = jnp.where(column == wanted, 1.0, 0.0).astype(jnp.bfloat16)
        held[first : first + dims[0], lane : lane + width] = dot(pick, saved[...]).astype(jnp.bfloat16)


def dispatch(args, experts, capacity):
    rows, gu, down, saved = args[4], *args[6:]
    tokens, wide = rows.shape[0], rows.shape[1] // CHIPS
    held = shape((gu.shape[0] + down.shape[0] + slot_rows(experts, capacity) * experts, gu.shape[1]))
    outs = [shape((2 * tokens, wide + 128)) for _ in range(CHIPS)]
    near = [*args[:4], saved]
    results = call(
        functools.partial(dispatch_kernel, experts, capacity),
        [held] + outs,
        *args,
        scratch=[pltpu.VMEM(a.shape, a.dtype) for a in near] + [pltpu.SemaphoreType.DMA((7 + 2 * CHIPS,))],
        name="dispatch",
        far=range(9),
    )
    return results[0], results[1:]


def slot_choice(blocks, at, tokens, wide, topk, capacity, rows, chip, here):
    lane = iota((CHIPS * tokens, rows), 1).astype(jnp.float32)
    notes = [b[at * tokens : (at + 1) * tokens, wide:].astype(jnp.float32) for b in blocks]
    choices = []
    for kk in range(topk):
        targets = []
        for dk, note in enumerate(notes):
            route, rank = note[:, kk : kk + 1], note[:, topk + kk : topk + kk + 1]
            first = ((chip ^ dk) * capacity).astype(jnp.float32)
            targets.append(jnp.where(route == here, rank + first, -1.0))
        choices.append(jnp.where(lane == jnp.concatenate(targets, axis=0), 1.0, 0.0))
    return choices


def pick_kernel(experts, capacity, topk, *refs):
    blocks, outs = refs[:CHIPS], refs[CHIPS:]
    chip, _, expert = place()
    wide = outs[0].shape[1]
    rows = outs[0].shape[0] // 2
    tokens = blocks[0].shape[0] // 2
    for at in range(2):
        left = jnp.concatenate([b[at * tokens : (at + 1) * tokens, :wide] for b in blocks], axis=0)
        for de in (*range(1, experts), 0):
            here = lax.rem(expert + de, experts).astype(jnp.float32)
            choice = sum(slot_choice(blocks, at, tokens, wide, topk, capacity, rows, chip, here))
            picked = dot(choice.astype(jnp.bfloat16), left, TN)
            outs[de][at * rows : (at + 1) * rows] = picked.astype(jnp.bfloat16)


def pick(blocks, experts, capacity, topk):
    wide = blocks[0].shape[1] - 128
    outs = [shape((2 * slot_rows(experts, capacity), wide)) for _ in range(experts)]
    return call(functools.partial(pick_kernel, experts, capacity, topk), outs, *blocks, name="pick")


def unit_rows(part, chip, units):
    return pl.ds(pl.multiple_of((part * CHIPS + chip) * units, units), units)


def up_kernel(experts, unit_count, *refs):
    blocks, (own, other), outs = refs[:experts], refs[experts : experts + 2], refs[experts + 2 :]
    chip, core, _ = place()
    units = unit_count // 3 // CHIPS
    half = own.shape[1]
    rows = blocks[0].shape[0] // 2

    def left(at, side):
        return jnp.concatenate([b[at * rows : (at + 1) * rows, block_of(side, half)] for b in blocks], axis=0)

    near, far = [left(at, core) for at in range(2)], [left(at, 1 - core) for at in range(2)]
    for dk in (*range(1, CHIPS), 0):
        for part in range(3):
            at, span = part // 2, unit_rows(part, chip ^ dk, units)
            product = dot(near[at], own[span, :], NT) + dot(far[at], other[span, :], NT)
            outs[dk][:, part * units : (part + 1) * units] = product.astype(outs[dk].dtype)


def up(blocks, own, other, unit_count):
    experts = len(blocks)
    rows = blocks[0].shape[0] // 2 * experts
    width = unit_count // CHIPS
    outs = [shape((rows, width), jnp.float32 if dk == 0 else jnp.bfloat16) for dk in range(CHIPS)]
    flops = 4 * rows * unit_count * own.shape[1]
    return call(functools.partial(up_kernel, experts, unit_count), outs, *blocks, own, other, flops=flops, name="up")


def act_kernel(*refs):
    parts, (held, arrived, out) = refs[:CHIPS], refs[CHIPS:]
    _, core, _ = place()
    total = parts[0][...]
    for part in parts[1:]:
        total = total + part[...].astype(jnp.float32)
    units = total.shape[1] // 3
    gate_pre, up_pre, hidden_grad = total[:, :units], total[:, units : 2 * units], total[:, 2 * units :]
    out[:, :units] = (gate_pre * jax.nn.sigmoid(gate_pre) * up_pre).astype(jnp.bfloat16)
    half = units // CORES
    first = held.shape[0] - total.shape[0]
    own = held[first:, 2 * half : 4 * half].astype(jnp.float32)
    other = arrived[first:, : 2 * half].astype(jnp.float32)
    low, high = jnp.where(core == 0, own, other), jnp.where(core == 0, other, own)
    for at, saved in enumerate((low, high)):
        gate_pre, up_pre = saved[:, :half], saved[:, half:]
        sig = jax.nn.sigmoid(gate_pre)
        grad = hidden_grad[:, at * half : (at + 1) * half]
        first = units + at * half
        out[:, first : first + half] = (grad * up_pre * (sig * (1.0 + gate_pre * (1.0 - sig)))).astype(jnp.bfloat16)
        out[:, first + units : first + units + half] = (grad * (gate_pre * sig)).astype(jnp.bfloat16)


def act(parts, own, other):
    return call(act_kernel, shape(parts[0].shape), *parts, own, other, name="act")


def down_kernel(experts, unit_count, *refs):
    parts, (own, other), outs = refs[:CHIPS], refs[CHIPS : CHIPS + 2], refs[CHIPS + 2 :]
    chip, core, _ = place()
    half = own.shape[1]
    units = unit_count // 3 // CHIPS
    rows = parts[0].shape[0] // experts
    for at, terms in ((0, ((0, 2),)), (1, ((1, 0), (2, 1)))):
        for weight, column in ((own, core), (other, 1 - core)):
            total = None
            for dk in range(CHIPS):
                for piece, part in terms:
                    left = parts[dk][:, piece * units : (piece + 1) * units]
                    term = dot(left, weight[unit_rows(part, chip ^ dk, units), :])
                    total = term if total is None else total + term
            total = total.astype(jnp.bfloat16)
            for de in range(experts):
                span = slice(at * rows, (at + 1) * rows)
                outs[de][span, block_of(column, half)] = total[de * rows : (de + 1) * rows]


def down(parts, own, other, experts, unit_count):
    rows = parts[0].shape[0] // experts
    outs = [shape((2 * rows, CORES * own.shape[1])) for _ in range(experts)]
    flops = 4 * parts[0].shape[0] * unit_count * own.shape[1]
    return call(functools.partial(down_kernel, experts, unit_count), outs, *parts, own, other, flops=flops, name="down")


def combine_kernel(experts, capacity, topk, *refs):
    blocks, results, outs = refs[:CHIPS], refs[CHIPS : CHIPS + experts], refs[CHIPS + experts :]
    chip, _, expert = place()
    rows, wide = results[0].shape[0] // 2, results[0].shape[1]
    tokens = outs[0].shape[0] // 2
    for at in range(2):
        found = [None] * topk
        for de in range(experts):
            here = lax.rem(expert + de, experts).astype(jnp.float32)
            choices = slot_choice(blocks, at, tokens, wide, topk, capacity, rows, chip, here)
            for kk in range(topk):
                term = dot(choices[kk].astype(jnp.bfloat16), results[de][at * rows : (at + 1) * rows])
                found[kk] = term if de == 0 else found[kk] + term
        for dk in range(CHIPS):
            note = blocks[dk][at * tokens : (at + 1) * tokens, wide:].astype(jnp.float32)
            total = None
            for kk in range(topk):
                terms = [note[:, part * topk + kk : part * topk + kk + 1] for part in (2, 3, 4)]
                gate = terms[0] + terms[1] + terms[2]
                term = found[kk][dk * tokens : (dk + 1) * tokens] * gate
                total = term if total is None else total + term
            outs[dk][at * tokens : (at + 1) * tokens] = total.astype(jnp.bfloat16)


def combine(blocks, results, capacity, topk):
    experts = len(results)
    outs = [shape((blocks[0].shape[0], results[0].shape[1])) for _ in range(CHIPS)]
    kernel = functools.partial(combine_kernel, experts, capacity, topk)
    return call(kernel, outs, *blocks, *results, name="combine")


def join_kernel(*refs):
    chip, _, _ = place()
    blocks, outs = refs[: -2], refs[-2:]
    tokens = outs[0].shape[0]
    for at, out in enumerate(outs):
        for dk in range(CHIPS):
            block = blocks[dk + at * (len(blocks) - CHIPS)]
            first = at * tokens if len(blocks) == CHIPS else 0
            out[:, block_of(chip ^ dk, block.shape[1])] = block[first : first + tokens]


def join(blocks, tokens):
    out = shape((tokens, CHIPS * blocks[0].shape[1]))
    return call(join_kernel, [out, out], *blocks, name="join")


def on_device(
    forward_input,
    forward_route,
    forward_gates,
    backward_cotangent,
    backward_route,
    backward_gates,
    gate_up_weight,
    down_weight,
    saved_projections,
):
    sections = lax.axis_size("section")
    experts = lax.axis_size("expert")
    topk = forward_route.shape[2]
    capacity = saved_projections.shape[2] // (GROUP * experts)
    tokens = forward_route.shape[1]

    def to_chip(value, dk):
        return lax.ppermute(value, "chip", [(i, i ^ dk) for i in range(CHIPS)])

    def to_section(value, dk, by):
        pairs = [
            (i * CHIPS + j, (i + by) % sections * CHIPS + (j ^ dk)) for i in range(sections) for j in range(CHIPS)
        ]
        return lax.ppermute(value, ("section", "chip"), pairs)

    def to_expert(block, de):
        if de == 0:
            return block
        return lax.ppermute(block, "expert", [(i, (i + de) % experts) for i in range(experts)])

    def to_core(value):
        return lax.ppermute(value, "core", [(i, i ^ 1) for i in range(CORES)])

    def from_expert(block, de):
        if de == 0:
            return block
        return lax.ppermute(block, "expert", [((i + de) % experts, i) for i in range(experts)])

    def to_chips(blocks):
        return [blocks[0]] + [to_chip(blocks[dk], dk) for dk in range(1, CHIPS)]

    args = [a[0].T for a in (forward_route, forward_gates, backward_route, backward_gates)]
    args += [forward_input[0], backward_cotangent[0], gate_up_weight[0, 0], down_weight[0, 0], saved_projections[0, 0]]
    unit_count = args[6].shape[0] + args[7].shape[0]
    own, sent = dispatch(args, experts, capacity)
    other = to_core(own)
    tokens_here = to_chips(sent)
    picked = pick(tokens_here, experts, capacity, topk)
    rows_here = [to_expert(picked[de], de) for de in range(experts)]
    parts = to_chips(up(rows_here, own, other, unit_count))
    units = to_chips([act(parts, own, other)] * CHIPS)
    results = down(units, own, other, experts, unit_count)
    results = [from_expert(results[de], de) for de in range(experts)]
    outs = combine(tokens_here, results, capacity, topk)
    if sections == 2:
        joined = [to_section(outs[dk], dk, 1) for dk in range(CHIPS)]
    else:
        joined = [to_section(outs[dk][:tokens], dk, 1) for dk in range(CHIPS)]
        joined += [to_section(outs[dk][tokens:], dk, -1) for dk in range(CHIPS)]
    next_input, prior_gradient = join(joined, tokens)
    return next_input[None], prior_gradient[None]


def solution(mesh):
    pipes, experts = mesh.devices.shape
    axes = ("section", "chip", "core", "expert")
    mesh = Mesh(mesh.devices.reshape(pipes // GROUP, CHIPS, CORES, experts), axes)
    rows = P(axes[:3], "expert", None)
    weights = P(axes[:3], "expert", None, None)
    return jax.shard_map(
        on_device,
        mesh=mesh,
        in_specs=(rows,) * 6 + (weights,) * 3,
        out_specs=(rows, rows),
        check_vma=False,
    )
```

```python
import functools

import jax
import jax.numpy as jnp
from jax import lax
from jax.experimental import pallas as pl
from jax.experimental.pallas import tpu as pltpu
from jax.sharding import Mesh
from jax.sharding import PartitionSpec as P

GROUP = 8
CORES = 2
CHIPS = GROUP // CORES
TILE = 16
NT = (((1,), (1,)), ((), ()))
NN = (((1,), (0,)), ((), ()))
TN = (((0,), (0,)), ((), ()))


def round_up(value, step):
    return (value + step - 1) // step * step


def dot(a, b, dims=NN):
    return lax.dot_general(a, b, dims, preferred_element_type=jnp.float32)


def iota(shape, axis):
    return lax.broadcasted_iota(jnp.int32, shape, axis)


def place():
    return lax.axis_index("chip"), lax.axis_index("core"), lax.axis_index("expert")


def block_of(index, size):
    return pl.ds(pl.multiple_of(index * size, size), size)


def call(kernel, outs, *args, scratch=(), flops=0, name=None, far=()):
    size = sum(a.size * a.dtype.itemsize for a in args)
    size += sum(o.size * o.dtype.itemsize for o in jax.tree.leaves(outs))
    spec = pl.BlockSpec(memory_space=pltpu.VMEM)
    return pl.pallas_call(
        kernel,
        out_shape=outs,
        in_specs=[pl.BlockSpec(memory_space=pl.ANY) if i in far else spec for i in range(len(args))],
        out_specs=jax.tree.map(lambda _: spec, outs),
        scratch_shapes=scratch,
        compiler_params=pltpu.CompilerParams(vmem_limit_bytes=16 * 2**20),
        cost_estimate=pl.CostEstimate(flops=flops, bytes_accessed=size, transcendentals=0),
        name=name,
    )(*(pltpu.with_memory_space_constraint(a, pltpu.HBM) if i in far else a for i, a in enumerate(args)))


def shape(dims, dtype=jnp.bfloat16):
    return jax.ShapeDtypeStruct(dims, dtype)


def slot_rows(experts, capacity):
    return round_up(CHIPS * capacity, TILE)


def dispatch_kernel(experts, *refs):
    far, outs, near, ready = refs[:6], refs[6 : 6 + CHIPS], refs[6 + CHIPS : -1], refs[-1]
    chip, _, _ = place()
    tokens, width = far[4].shape
    wide = width // CHIPS
    jobs = [(far[i], near[i]) for i in range(4)]
    for dk in range(CHIPS):
        for at in range(2):
            block = outs[dk].at[at * tokens : (at + 1) * tokens, :wide]
            jobs.append((far[4 + at].at[:, block_of(chip ^ dk, wide)], block))
    copies = [pltpu.make_async_copy(*job, ready.at[i]) for i, job in enumerate(jobs)]
    for copy in copies:
        copy.start()
    for copy in copies[:4]:
        copy.wait()
    for at in range(2):
        route, gate = near[2 * at][...], near[2 * at + 1][...]
        topk = route.shape[0]
        earlier = (iota((tokens, tokens), 0) < iota((tokens, tokens), 1)).astype(jnp.float32)
        rank = jnp.zeros((topk, tokens), jnp.float32)
        for e in range(experts):
            named = (route == e).astype(jnp.float32)
            count = jnp.broadcast_to(jnp.sum(named, axis=0, keepdims=True), (8, tokens))
            rank = rank + named * dot(count, earlier)[:1]
        high = gate.astype(jnp.bfloat16).astype(jnp.float32)
        middle = (gate - high).astype(jnp.bfloat16).astype(jnp.float32)
        low = gate - high - middle
        table = jnp.zeros((128, tokens), jnp.float32)
        for part, value in enumerate((route.astype(jnp.float32), rank, high, middle, low)):
            for kk in range(topk):
                row = jnp.broadcast_to(value[kk : kk + 1], (128, tokens))
                table = jnp.where(iota((128, tokens), 0) == part * topk + kk, row, table)
        same = (iota((tokens, tokens), 0) == iota((tokens, tokens), 1)).astype(jnp.bfloat16)
        note = dot(same, table.astype(jnp.bfloat16), NT).astype(jnp.bfloat16)
        for dk in range(CHIPS):
            outs[dk][at * tokens : (at + 1) * tokens, wide:] = note
    for copy in copies[4:]:
        copy.wait()


def hold_kernel(experts, capacity, gu, down, saved, _, held, near_saved, ready):
    _, core, expert = place()
    units = gu.shape[0] + down.shape[0]
    jobs = ((saved, near_saved), (gu, held.at[: gu.shape[0]]), (down, held.at[gu.shape[0] : units]))
    copies = [pltpu.make_async_copy(*job, ready.at[i]) for i, job in enumerate(jobs)]
    for copy in copies:
        copy.start()
    copies[0].wait()
    stash(experts, capacity, core, expert, near_saved, held, units)
    for copy in copies[1:]:
        copy.wait()


def stash(experts, capacity, core, expert, saved, held, first):
    rows = slot_rows(experts, capacity)
    dims = (rows * experts, saved.shape[0])
    width = saved.shape[1]
    row, column = iota(dims, 0), iota(dims, 1)
    for target, lane in ((1 - core, 0), (core, width)):
        wanted = jnp.full(dims, -1, jnp.int32)
        for de in range(experts):
            for at in range(CHIPS):
                source = (at * CORES + target) * experts + lax.rem(expert + experts - de, experts)
                low = de * rows + at * capacity
                inside = jnp.logical_and(row >= low, row < low + capacity)
                wanted = jnp.where(inside, row + (source * capacity - low), wanted)
        pick = jnp.where(column == wanted, 1.0, 0.0).astype(jnp.bfloat16)
        held[first : first + dims[0], lane : lane + width] = dot(pick, saved[...]).astype(jnp.bfloat16)


def dispatch(args, experts):
    tokens, wide = args[4].shape[0], args[4].shape[1] // CHIPS
    return call(
        functools.partial(dispatch_kernel, experts),
        [shape((2 * tokens, wide + 128)) for _ in range(CHIPS)],
        *args,
        scratch=[pltpu.VMEM(a.shape, a.dtype) for a in args[:4]] + [pltpu.SemaphoreType.DMA((4 + 2 * CHIPS,))],
        name="dispatch",
        far=range(6),
    )


def hold(gu, down, saved, after, experts, capacity):
    rows = slot_rows(experts, capacity) * experts
    return call(
        functools.partial(hold_kernel, experts, capacity),
        shape((gu.shape[0] + down.shape[0] + rows, gu.shape[1])),
        gu,
        down,
        saved,
        after,
        scratch=[pltpu.VMEM(saved.shape, saved.dtype), pltpu.SemaphoreType.DMA((3,))],
        name="hold",
        far=range(3),
    )


def slot_choice(blocks, at, tokens, wide, topk, capacity, rows, chip, here):
    lane = iota((CHIPS * tokens, rows), 1).astype(jnp.float32)
    notes = [b[at * tokens : (at + 1) * tokens, wide:].astype(jnp.float32) for b in blocks]
    choices = []
    for kk in range(topk):
        targets = []
        for dk, note in enumerate(notes):
            route, rank = note[:, kk : kk + 1], note[:, topk + kk : topk + kk + 1]
            first = ((chip ^ dk) * capacity).astype(jnp.float32)
            targets.append(jnp.where(route == here, rank + first, -1.0))
        choices.append(jnp.where(lane == jnp.concatenate(targets, axis=0), 1.0, 0.0))
    return choices


def pick_kernel(experts, capacity, topk, *refs):
    blocks, outs = refs[:CHIPS], refs[CHIPS:]
    chip, _, expert = place()
    wide = outs[0].shape[1]
    rows = outs[0].shape[0] // 2
    tokens = blocks[0].shape[0] // 2
    for at in range(2):
        left = jnp.concatenate([b[at * tokens : (at + 1) * tokens, :wide] for b in blocks], axis=0)
        for de in (*range(1, experts), 0):
            here = lax.rem(expert + de, experts).astype(jnp.float32)
            choice = sum(slot_choice(blocks, at, tokens, wide, topk, capacity, rows, chip, here))
            picked = dot(choice.astype(jnp.bfloat16), left, TN)
            outs[de][at * rows : (at + 1) * rows] = picked.astype(jnp.bfloat16)


def pick(blocks, experts, capacity, topk):
    wide = blocks[0].shape[1] - 128
    outs = [shape((2 * slot_rows(experts, capacity), wide)) for _ in range(experts)]
    return call(functools.partial(pick_kernel, experts, capacity, topk), outs, *blocks, name="pick")


def unit_rows(part, chip, units):
    return pl.ds(pl.multiple_of((part * CHIPS + chip) * units, units), units)


def up_kernel(experts, unit_count, *refs):
    blocks, (own, other), outs = refs[:experts], refs[experts : experts + 2], refs[experts + 2 :]
    chip, core, _ = place()
    units = unit_count // 3 // CHIPS
    half = own.shape[1]
    rows = blocks[0].shape[0] // 2

    def left(at, side):
        return jnp.concatenate([b[at * rows : (at + 1) * rows, block_of(side, half)] for b in blocks], axis=0)

    near, far = [left(at, core) for at in range(2)], [left(at, 1 - core) for at in range(2)]
    for dk in (*range(1, CHIPS), 0):
        for part in range(3):
            at, span = part // 2, unit_rows(part, chip ^ dk, units)
            product = dot(near[at], own[span, :], NT) + dot(far[at], other[span, :], NT)
            outs[dk][:, part * units : (part + 1) * units] = product.astype(outs[dk].dtype)


def up(blocks, own, other, unit_count):
    experts = len(blocks)
    rows = blocks[0].shape[0] // 2 * experts
    width = unit_count // CHIPS
    outs = [shape((rows, width), jnp.float32 if dk == 0 else jnp.bfloat16) for dk in range(CHIPS)]
    flops = 4 * rows * unit_count * own.shape[1]
    return call(functools.partial(up_kernel, experts, unit_count), outs, *blocks, own, other, flops=flops, name="up")


def act_kernel(*refs):
    parts, (held, arrived, out) = refs[:CHIPS], refs[CHIPS:]
    _, core, _ = place()
    total = parts[0][...]
    for part in parts[1:]:
        total = total + part[...].astype(jnp.float32)
    units = total.shape[1] // 3
    gate_pre, up_pre, hidden_grad = total[:, :units], total[:, units : 2 * units], total[:, 2 * units :]
    out[:, :units] = (gate_pre * jax.nn.sigmoid(gate_pre) * up_pre).astype(jnp.bfloat16)
    half = units // CORES
    first = held.shape[0] - total.shape[0]
    own = held[first:, 2 * half : 4 * half].astype(jnp.float32)
    other = arrived[first:, : 2 * half].astype(jnp.float32)
    low, high = jnp.where(core == 0, own, other), jnp.where(core == 0, other, own)
    for at, saved in enumerate((low, high)):
        gate_pre, up_pre = saved[:, :half], saved[:, half:]
        sig = jax.nn.sigmoid(gate_pre)
        grad = hidden_grad[:, at * half : (at + 1) * half]
        first = units + at * half
        out[:, first : first + half] = (grad * up_pre * (sig * (1.0 + gate_pre * (1.0 - sig)))).astype(jnp.bfloat16)
        out[:, first + units : first + units + half] = (grad * (gate_pre * sig)).astype(jnp.bfloat16)


def act(parts, own, other):
    return call(act_kernel, shape(parts[0].shape), *parts, own, other, name="act")


def down_kernel(experts, unit_count, *refs):
    parts, (own, other), outs = refs[:CHIPS], refs[CHIPS : CHIPS + 2], refs[CHIPS + 2 :]
    chip, core, _ = place()
    half = own.shape[1]
    units = unit_count // 3 // CHIPS
    rows = parts[0].shape[0] // experts
    for at, terms in ((0, ((0, 2),)), (1, ((1, 0), (2, 1)))):
        for weight, column in ((own, core), (other, 1 - core)):
            total = None
            for dk in range(CHIPS):
                for piece, part in terms:
                    left = parts[dk][:, piece * units : (piece + 1) * units]
                    term = dot(left, weight[unit_rows(part, chip ^ dk, units), :])
                    total = term if total is None else total + term
            total = total.astype(jnp.bfloat16)
            for de in range(experts):
                span = slice(at * rows, (at + 1) * rows)
                outs[de][span, block_of(column, half)] = total[de * rows : (de + 1) * rows]


def down(parts, own, other, experts, unit_count):
    rows = parts[0].shape[0] // experts
    outs = [shape((2 * rows, CORES * own.shape[1])) for _ in range(experts)]
    flops = 4 * parts[0].shape[0] * unit_count * own.shape[1]
    return call(functools.partial(down_kernel, experts, unit_count), outs, *parts, own, other, flops=flops, name="down")


def combine_kernel(experts, capacity, topk, *refs):
    blocks, results, outs = refs[:CHIPS], refs[CHIPS : CHIPS + experts], refs[CHIPS + experts :]
    chip, _, expert = place()
    rows, wide = results[0].shape[0] // 2, results[0].shape[1]
    tokens = outs[0].shape[0] // 2
    for at in range(2):
        found = [None] * topk
        for de in range(experts):
            here = lax.rem(expert + de, experts).astype(jnp.float32)
            choices = slot_choice(blocks, at, tokens, wide, topk, capacity, rows, chip, here)
            for kk in range(topk):
                term = dot(choices[kk].astype(jnp.bfloat16), results[de][at * rows : (at + 1) * rows])
                found[kk] = term if de == 0 else found[kk] + term
        for dk in range(CHIPS):
            note = blocks[dk][at * tokens : (at + 1) * tokens, wide:].astype(jnp.float32)
            total = None
            for kk in range(topk):
                terms = [note[:, part * topk + kk : part * topk + kk + 1] for part in (2, 3, 4)]
                gate = terms[0] + terms[1] + terms[2]
                term = found[kk][dk * tokens : (dk + 1) * tokens] * gate
                total = term if total is None else total + term
            outs[dk][at * tokens : (at + 1) * tokens] = total.astype(jnp.bfloat16)


def combine(blocks, results, capacity, topk):
    experts = len(results)
    outs = [shape((blocks[0].shape[0], results[0].shape[1])) for _ in range(CHIPS)]
    kernel = functools.partial(combine_kernel, experts, capacity, topk)
    return call(kernel, outs, *blocks, *results, name="combine")


def join_kernel(*refs):
    chip, _, _ = place()
    blocks, outs = refs[: -2], refs[-2:]
    tokens = outs[0].shape[0]
    for at, out in enumerate(outs):
        for dk in range(CHIPS):
            block = blocks[dk + at * (len(blocks) - CHIPS)]
            first = at * tokens if len(blocks) == CHIPS else 0
            out[:, block_of(chip ^ dk, block.shape[1])] = block[first : first + tokens]


def join(blocks, tokens):
    out = shape((tokens, CHIPS * blocks[0].shape[1]))
    return call(join_kernel, [out, out], *blocks, name="join")


def on_device(
    forward_input,
    forward_route,
    forward_gates,
    backward_cotangent,
    backward_route,
    backward_gates,
    gate_up_weight,
    down_weight,
    saved_projections,
):
    sections = lax.axis_size("section")
    experts = lax.axis_size("expert")
    topk = forward_route.shape[2]
    capacity = saved_projections.shape[2] // (GROUP * experts)
    tokens = forward_route.shape[1]

    def to_chip(value, dk):
        return lax.ppermute(value, "chip", [(i, i ^ dk) for i in range(CHIPS)])

    def to_section(value, dk, by):
        pairs = [
            (i * CHIPS + j, (i + by) % sections * CHIPS + (j ^ dk)) for i in range(sections) for j in range(CHIPS)
        ]
        return lax.ppermute(value, ("section", "chip"), pairs)

    def to_expert(block, de):
        if de == 0:
            return block
        return lax.ppermute(block, "expert", [(i, (i + de) % experts) for i in range(experts)])

    def to_core(value):
        return lax.ppermute(value, "core", [(i, i ^ 1) for i in range(CORES)])

    def from_expert(block, de):
        if de == 0:
            return block
        return lax.ppermute(block, "expert", [((i + de) % experts, i) for i in range(experts)])

    def to_chips(blocks):
        return [blocks[0]] + [to_chip(blocks[dk], dk) for dk in range(1, CHIPS)]

    args = [a[0].T for a in (forward_route, forward_gates, backward_route, backward_gates)]
    sent = dispatch(args + [forward_input[0], backward_cotangent[0]], experts)
    gu, down_rows = gate_up_weight[0, 0], down_weight[0, 0]
    unit_count = gu.shape[0] + down_rows.shape[0]
    tokens_here = to_chips(sent)
    own = hold(gu, down_rows, saved_projections[0, 0], tokens_here[1], experts, capacity)
    other = to_core(own)
    picked = pick(tokens_here, experts, capacity, topk)
    rows_here = [to_expert(picked[de], de) for de in range(experts)]
    parts = to_chips(up(rows_here, own, other, unit_count))
    units = to_chips([act(parts, own, other)] * CHIPS)
    results = down(units, own, other, experts, unit_count)
    results = [from_expert(results[de], de) for de in range(experts)]
    outs = combine(tokens_here, results, capacity, topk)
    if sections == 2:
        joined = [to_section(outs[dk], dk, 1) for dk in range(CHIPS)]
    else:
        joined = [to_section(outs[dk][:tokens], dk, 1) for dk in range(CHIPS)]
        joined += [to_section(outs[dk][tokens:], dk, -1) for dk in range(CHIPS)]
    next_input, prior_gradient = join(joined, tokens)
    return next_input[None], prior_gradient[None]


def solution(mesh):
    pipes, experts = mesh.devices.shape
    axes = ("section", "chip", "core", "expert")
    mesh = Mesh(mesh.devices.reshape(pipes // GROUP, CHIPS, CORES, experts), axes)
    rows = P(axes[:3], "expert", None)
    weights = P(axes[:3], "expert", None, None)
    return jax.shard_map(
        on_device,
        mesh=mesh,
        in_specs=(rows,) * 6 + (weights,) * 3,
        out_specs=(rows, rows),
        check_vma=False,
    )
```

```python
import functools

import jax
import jax.numpy as jnp
from jax import lax
from jax.experimental import pallas as pl
from jax.experimental.pallas import tpu as pltpu
from jax.sharding import Mesh
from jax.sharding import PartitionSpec as P

GROUP = 8
CORES = 2
CHIPS = GROUP // CORES
ORDER = (*range(1, CHIPS), 0)
TILE = 16
NT = (((1,), (1,)), ((), ()))
NN = (((1,), (0,)), ((), ()))
TN = (((0,), (0,)), ((), ()))


def round_up(value, step):
    return (value + step - 1) // step * step


def dot(a, b, dims=NN):
    return lax.dot_general(a, b, dims, preferred_element_type=jnp.float32)


def iota(shape, axis):
    return lax.broadcasted_iota(jnp.int32, shape, axis)


def place():
    return lax.axis_index("chip"), lax.axis_index("core"), lax.axis_index("expert")


def peer(chip, core, j):
    if isinstance(core, int):
        return chip ^ (CHIPS - 1 - j if core == 1 and 0 < j < CHIPS - 1 else j)
    return chip ^ (jnp.where(core == 1, CHIPS - 1 - j, j) if 0 < j < CHIPS - 1 else j)


def block_of(index, size):
    return pl.ds(pl.multiple_of(index * size, size), size)


def pinned(array, memory):
    return array if memory is None else pltpu.with_memory_space_constraint(array, memory)


def call(kernel, outs, *args, scratch=(), flops=0, name=None, far=(), near=()):
    size = sum(a.size * a.dtype.itemsize for a in args)
    size += sum(o.size * o.dtype.itemsize for o in jax.tree.leaves(outs))
    spec = pl.BlockSpec(memory_space=pltpu.VMEM)
    return pl.pallas_call(
        kernel,
        out_shape=outs,
        in_specs=[pl.BlockSpec(memory_space=pl.ANY) if i in far else spec for i in range(len(args))],
        out_specs=jax.tree.map(lambda _: spec, outs),
        scratch_shapes=scratch,
        compiler_params=pltpu.CompilerParams(vmem_limit_bytes=16 * 2**20),
        cost_estimate=pl.CostEstimate(flops=flops, bytes_accessed=size, transcendentals=0),
        name=name,
    )(*(pinned(a, pltpu.HBM if i in far else pltpu.VMEM if i in near else None) for i, a in enumerate(args)))


def shape(dims, dtype=jnp.bfloat16):
    return jax.ShapeDtypeStruct(dims, dtype)


def slot_rows(experts, capacity):
    return round_up(CHIPS * capacity, TILE)


def dispatch_kernel(experts, *refs):
    far, outs, near, ready = refs[:6], refs[6 : 6 + CHIPS], refs[6 + CHIPS : -1], refs[-1]
    chip, core, _ = place()
    tokens, width = far[4].shape
    wide = width // CHIPS
    jobs = [(far[i], near[i]) for i in range(4)]
    for dk in range(CHIPS):
        for at in range(2):
            block = outs[dk].at[at * tokens : (at + 1) * tokens, :wide]
            jobs.append((far[4 + at].at[:, block_of(peer(chip, core, dk), wide)], block))
    copies = [pltpu.make_async_copy(*job, ready.at[i]) for i, job in enumerate(jobs)]
    for copy in copies:
        copy.start()
    for copy in copies[:4]:
        copy.wait()
    for at in range(2):
        route, gate = near[2 * at][...], near[2 * at + 1][...]
        topk = route.shape[0]
        earlier = (iota((tokens, tokens), 0) < iota((tokens, tokens), 1)).astype(jnp.float32)
        rank = jnp.zeros((topk, tokens), jnp.float32)
        for e in range(experts):
            named = (route == e).astype(jnp.float32)
            count = jnp.broadcast_to(jnp.sum(named, axis=0, keepdims=True), (8, tokens))
            rank = rank + named * dot(count, earlier)[:1]
        high = gate.astype(jnp.bfloat16).astype(jnp.float32)
        middle = (gate - high).astype(jnp.bfloat16).astype(jnp.float32)
        low = gate - high - middle
        table = jnp.zeros((128, tokens), jnp.float32)
        for part, value in enumerate((route.astype(jnp.float32), rank, high, middle, low)):
            for kk in range(topk):
                row = jnp.broadcast_to(value[kk : kk + 1], (128, tokens))
                table = jnp.where(iota((128, tokens), 0) == part * topk + kk, row, table)
        same = (iota((tokens, tokens), 0) == iota((tokens, tokens), 1)).astype(jnp.bfloat16)
        note = dot(same, table.astype(jnp.bfloat16), NT).astype(jnp.bfloat16)
        for dk in range(CHIPS):
            outs[dk][at * tokens : (at + 1) * tokens, wide:] = note
    for copy in copies[4:]:
        copy.wait()


def stash(experts, capacity, core, expert, saved, mine, theirs):
    rows = slot_rows(experts, capacity)
    dims = (rows * experts, saved.shape[0])
    row, column = iota(dims, 0), iota(dims, 1)
    for target, ref in ((1 - core, theirs), (core, mine)):
        wanted = jnp.full(dims, -1, jnp.int32)
        for de in range(experts):
            for at in range(CHIPS):
                source = (at * CORES + target) * experts + lax.rem(expert + experts - de, experts)
                low = de * rows + at * capacity
                inside = jnp.logical_and(row >= low, row < low + capacity)
                wanted = jnp.where(inside, row + (source * capacity - low), wanted)
        pick = jnp.where(column == wanted, 1.0, 0.0).astype(jnp.bfloat16)
        ref[...] = dot(pick, saved[...]).astype(jnp.bfloat16)


def dispatch(args, experts):
    tokens, wide = args[4].shape[0], args[4].shape[1] // CHIPS
    return call(
        functools.partial(dispatch_kernel, experts),
        [shape((2 * tokens, wide + 128)) for _ in range(CHIPS)],
        *args,
        scratch=[pltpu.VMEM(a.shape, a.dtype) for a in args[:4]] + [pltpu.SemaphoreType.DMA((4 + 2 * CHIPS,))],
        name="dispatch",
        far=range(6),
    )


def slot_choice(blocks, at, tokens, wide, topk, capacity, rows, chip, core, here):
    lane = iota((CHIPS * tokens, rows), 1).astype(jnp.float32)
    notes = [b[at * tokens : (at + 1) * tokens, wide:].astype(jnp.float32) for b in blocks]
    choices = []
    for kk in range(topk):
        targets = []
        for dk, note in enumerate(notes):
            route, rank = note[:, kk : kk + 1], note[:, topk + kk : topk + kk + 1]
            first = ((peer(chip, core, dk)) * capacity).astype(jnp.float32)
            targets.append(jnp.where(route == here, rank + first, -1.0))
        choices.append(jnp.where(lane == jnp.concatenate(targets, axis=0), 1.0, 0.0))
    return choices


def pick_kernel(experts, capacity, topk, *refs):
    blocks, outs = refs[:CHIPS], refs[CHIPS:]
    chip, core, expert = place()
    wide = outs[0].shape[1]
    rows = outs[0].shape[0] // 2
    tokens = blocks[0].shape[0] // 2
    for at in range(2):
        left = jnp.concatenate([b[at * tokens : (at + 1) * tokens, :wide] for b in blocks], axis=0)
        for de in (*range(1, experts), 0):
            here = lax.rem(expert + de, experts).astype(jnp.float32)
            choice = sum(slot_choice(blocks, at, tokens, wide, topk, capacity, rows, chip, core, here))
            picked = dot(choice.astype(jnp.bfloat16), left, TN)
            outs[de][at * rows : (at + 1) * rows] = picked.astype(jnp.bfloat16)


def pick(blocks, experts, capacity, topk):
    wide = blocks[0].shape[1] - 128
    outs = [shape((2 * slot_rows(experts, capacity), wide)) for _ in range(experts)]
    return call(functools.partial(pick_kernel, experts, capacity, topk), outs, *blocks, name="pick")


def unit_rows(part, chip, units):
    return pl.ds(pl.multiple_of((part * CHIPS + chip) * units, units), units)


def product_rows(blocks, outs, near, far, arrive):
    chip, core, _ = place()
    half = near[0].shape[1]
    units = near[1].shape[0] // CHIPS
    rows = blocks[0].shape[0] // 2

    def left(at, side):
        return jnp.concatenate([b[at * rows : (at + 1) * rows, block_of(side, half)] for b in blocks], axis=0)

    own, other = [left(at, core) for at in range(2)], [left(at, 1 - core) for at in range(2)]
    for dk in ORDER:
        totals = []
        for part in range(3):
            which, piece = divmod(part, 2)
            totals.append(dot(other[which], far[which][unit_rows(piece, peer(chip, core, dk), units), :], NT))
        arrive(dk)
        for part in range(3):
            which, piece = divmod(part, 2)
            total = totals[part] + dot(own[which], near[which][unit_rows(piece, peer(chip, core, dk), units), :], NT)
            outs[dk][:, part * units : (part + 1) * units] = total.astype(outs[dk].dtype)


def up_kernel(experts, capacity, *refs):
    blocks, (gu, down, gu_far, down_far, saved), refs = refs[:experts], refs[experts : experts + 5], refs[experts + 5 :]
    outs, near, (mine, theirs), (near_saved, ready) = refs[:CHIPS], refs[CHIPS : CHIPS + 2], refs[-4:-2], refs[-2:]
    chip, core, expert = place()
    units = down.shape[0] // CHIPS
    copies = {}
    for dk in ORDER:
        copies[dk] = []
        for i, (source, target, piece) in enumerate(((gu, near[0], 0), (gu, near[0], 1), (down, near[1], 0))):
            span = unit_rows(piece, peer(chip, core, dk), units)
            copies[dk].append(pltpu.make_async_copy(source.at[span, :], target.at[span, :], ready.at[3 * dk + i]))
            copies[dk][-1].start()
    last = pltpu.make_async_copy(saved, near_saved, ready.at[3 * CHIPS])
    last.start()

    def arrive(dk):
        for copy in copies[dk]:
            copy.wait()

    product_rows(blocks, outs, near, (gu_far, down_far), arrive)
    last.wait()
    stash(experts, capacity, core, expert, near_saved, mine, theirs)


def up(blocks, gu, down, gu_far, down_far, saved, capacity):
    experts = len(blocks)
    rows = blocks[0].shape[0] // 2 * experts
    width = (gu.shape[0] + down.shape[0]) // CHIPS
    outs = [shape((rows, width), jnp.float32 if j == 0 else jnp.bfloat16) for j in range(CHIPS)]
    stashed = shape((rows, saved.shape[1]))
    results = call(
        functools.partial(up_kernel, experts, capacity),
        outs + [shape(gu.shape), shape(down.shape), stashed, stashed],
        *blocks,
        gu,
        down,
        gu_far,
        down_far,
        saved,
        scratch=[pltpu.VMEM(saved.shape, saved.dtype), pltpu.SemaphoreType.DMA((3 * CHIPS + 1,))],
        flops=4 * rows * (gu.size + down.size),
        name="up",
        far=(experts, experts + 1, experts + 4),
        near=(experts + 2, experts + 3),
    )
    return results[:CHIPS], results[CHIPS : CHIPS + 2], results[CHIPS + 2 :]


def act_kernel(*refs):
    parts, (mine, theirs, out) = refs[:CHIPS], refs[CHIPS:]
    _, core, _ = place()
    total = parts[0][...]
    for part in parts[1:]:
        total = total + part[...].astype(jnp.float32)
    units = total.shape[1] // 3
    gate_pre, up_pre, hidden_grad = total[:, :units], total[:, units : 2 * units], total[:, 2 * units :]
    out[:, :units] = (gate_pre * jax.nn.sigmoid(gate_pre) * up_pre).astype(jnp.bfloat16)
    half = units // CORES
    own, other = mine[...].astype(jnp.float32), theirs[...].astype(jnp.float32)
    low, high = jnp.where(core == 0, own, other), jnp.where(core == 0, other, own)
    for at, saved in enumerate((low, high)):
        gate_pre, up_pre = saved[:, :half], saved[:, half:]
        sig = jax.nn.sigmoid(gate_pre)
        grad = hidden_grad[:, at * half : (at + 1) * half]
        first = units + at * half
        out[:, first : first + half] = (grad * up_pre * (sig * (1.0 + gate_pre * (1.0 - sig)))).astype(jnp.bfloat16)
        out[:, first + units : first + units + half] = (grad * (gate_pre * sig)).astype(jnp.bfloat16)


def act(parts, mine, theirs):
    return call(act_kernel, shape(parts[0].shape), *parts, mine, theirs, name="act")


def down_kernel(*refs):
    parts, near, far, outs = refs[:CHIPS], refs[CHIPS : CHIPS + 2], refs[CHIPS + 2 : CHIPS + 4], refs[CHIPS + 4 :]
    chip, core, _ = place()
    half = near[0].shape[1]
    units = near[1].shape[0] // CHIPS
    rows = parts[0].shape[0] // len(outs)
    for at, which, terms in ((0, 1, ((0, 0),)), (1, 0, ((1, 0), (2, 1)))):
        for weight, column in ((near[which], core), (far[which], 1 - core)):
            total = None
            for dk in range(CHIPS):
                for piece, part in terms:
                    left = parts[dk][:, piece * units : (piece + 1) * units]
                    term = dot(left, weight[unit_rows(part, peer(chip, core, dk), units), :])
                    total = term if total is None else total + term
            total = total.astype(jnp.bfloat16)
            for i, out in enumerate(outs):
                out[at * rows : (at + 1) * rows, block_of(column, half)] = total[i * rows : (i + 1) * rows]


def down(parts, near, far, count):
    rows = parts[0].shape[0] // count
    outs = [shape((2 * rows, CORES * near[0].shape[1])) for _ in range(count)]
    flops = 4 * parts[0].shape[0] * (near[0].size + near[1].size)
    return call(down_kernel, outs, *parts, *near, *far, flops=flops, name="down", near=(CHIPS + 2, CHIPS + 3))


def combine_kernel(experts, capacity, topk, *refs):
    blocks, results, outs = refs[:CHIPS], refs[CHIPS : CHIPS + experts], refs[CHIPS + experts :]
    chip, core, expert = place()
    rows, wide = results[0].shape[0] // 2, results[0].shape[1]
    tokens = outs[0].shape[0] // 2
    for at in range(2):
        found = [None] * topk
        for de in range(experts):
            here = lax.rem(expert + de, experts).astype(jnp.float32)
            choices = slot_choice(blocks, at, tokens, wide, topk, capacity, rows, chip, core, here)
            for kk in range(topk):
                term = dot(choices[kk].astype(jnp.bfloat16), results[de][at * rows : (at + 1) * rows])
                found[kk] = term if de == 0 else found[kk] + term
        for dk in range(CHIPS):
            note = blocks[dk][at * tokens : (at + 1) * tokens, wide:].astype(jnp.float32)
            total = None
            for kk in range(topk):
                terms = [note[:, part * topk + kk : part * topk + kk + 1] for part in (2, 3, 4)]
                gate = terms[0] + terms[1] + terms[2]
                term = found[kk][dk * tokens : (dk + 1) * tokens] * gate
                total = term if total is None else total + term
            outs[dk][at * tokens : (at + 1) * tokens] = total.astype(jnp.bfloat16)


def combine(blocks, results, capacity, topk):
    experts = len(results)
    outs = [shape((blocks[0].shape[0], results[0].shape[1])) for _ in range(CHIPS)]
    kernel = functools.partial(combine_kernel, experts, capacity, topk)
    return call(kernel, outs, *blocks, *results, name="combine")


def join_kernel(*refs):
    chip, core, _ = place()
    blocks, outs = refs[: -2], refs[-2:]
    tokens = outs[0].shape[0]
    for at, out in enumerate(outs):
        for dk in range(CHIPS):
            block = blocks[dk + at * (len(blocks) - CHIPS)]
            first = at * tokens if len(blocks) == CHIPS else 0
            out[:, block_of(peer(chip, core, dk), block.shape[1])] = block[first : first + tokens]


def join(blocks, tokens):
    out = shape((tokens, CHIPS * blocks[0].shape[1]))
    return call(join_kernel, [out, out], *blocks, name="join")


def on_device(
    forward_input,
    forward_route,
    forward_gates,
    backward_cotangent,
    backward_route,
    backward_gates,
    gate_up_weight,
    down_weight,
    saved_projections,
):
    sections = lax.axis_size("section")
    experts = lax.axis_size("expert")
    topk = forward_route.shape[2]
    capacity = saved_projections.shape[2] // (GROUP * experts)
    tokens = forward_route.shape[1]

    def to_section(value, j, by):
        pairs = [
            ((i * CHIPS + k) * CORES + c, ((i + by) % sections * CHIPS + peer(k, c, j)) * CORES + c)
            for i in range(sections)
            for k in range(CHIPS)
            for c in range(CORES)
        ]
        return lax.ppermute(value, ("section", "chip", "core"), pairs)

    def to_chip(value, j):
        return to_section(value, j, 0)

    def to_expert(block, de):
        if de == 0:
            return block
        return lax.ppermute(block, "expert", [(i, (i + de) % experts) for i in range(experts)])

    def to_core(value):
        return lax.ppermute(value, "core", [(i, i ^ 1) for i in range(CORES)])

    def from_expert(block, de):
        if de == 0:
            return block
        return lax.ppermute(block, "expert", [((i + de) % experts, i) for i in range(experts)])

    def to_chips(blocks):
        return [blocks[0]] + [to_chip(blocks[dk], dk) for dk in range(1, CHIPS)]

    args = [a[0].T for a in (forward_route, forward_gates, backward_route, backward_gates)]
    gu, down_rows, saved = gate_up_weight[0, 0], down_weight[0, 0], saved_projections[0, 0]
    far = [to_core(gu), to_core(down_rows)]
    tokens_here = to_chips(dispatch(args + [forward_input[0], backward_cotangent[0]], experts))
    picked = pick(tokens_here, experts, capacity, topk)
    rows_here = [to_expert(picked[de], de) for de in range(experts)]
    parts, near, (mine, theirs) = up(rows_here, gu, down_rows, *far, saved, capacity)
    units = act(to_chips(parts), mine, to_core(theirs))
    results = down(to_chips([units] * CHIPS), near, far, experts)
    results = [from_expert(results[de], de) for de in range(experts)]
    outs = combine(tokens_here, results, capacity, topk)
    if sections == 2:
        joined = [to_section(outs[dk], dk, 1) for dk in range(CHIPS)]
    else:
        joined = [to_section(outs[dk][:tokens], dk, 1) for dk in range(CHIPS)]
        joined += [to_section(outs[dk][tokens:], dk, -1) for dk in range(CHIPS)]
    next_input, prior_gradient = join(joined, tokens)
    return next_input[None], prior_gradient[None]


def solution(mesh):
    pipes, experts = mesh.devices.shape
    axes = ("section", "chip", "core", "expert")
    mesh = Mesh(mesh.devices.reshape(pipes // GROUP, CHIPS, CORES, experts), axes)
    rows = P(axes[:3], "expert", None)
    weights = P(axes[:3], "expert", None, None)
    return jax.shard_map(
        on_device,
        mesh=mesh,
        in_specs=(rows,) * 6 + (weights,) * 3,
        out_specs=(rows, rows),
        check_vma=False,
    )
```

```python
import functools

import jax
import jax.numpy as jnp
from jax import lax
from jax.experimental import pallas as pl
from jax.experimental.pallas import tpu as pltpu
from jax.sharding import Mesh
from jax.sharding import PartitionSpec as P

GROUP = 8
CORES = 2
CHIPS = GROUP // CORES
COLUMNS = 2
ROWS = CHIPS // COLUMNS
ORDER = (*range(1, CHIPS), 0)
TILE = 16
NT = (((1,), (1,)), ((), ()))
NN = (((1,), (0,)), ((), ()))
TN = (((0,), (0,)), ((), ()))


def round_up(value, step):
    return (value + step - 1) // step * step


def dot(a, b, dims=NN):
    return lax.dot_general(a, b, dims, preferred_element_type=jnp.float32)


def iota(shape, axis):
    return lax.broadcasted_iota(jnp.int32, shape, axis)


def place():
    return lax.axis_index("chip"), lax.axis_index("core"), lax.axis_index("expert")


def peer(chip, core, j):
    if isinstance(core, int):
        return chip ^ (CHIPS - 1 - j if core == 1 and 0 < j < CHIPS - 1 else j)
    return chip ^ (jnp.where(core == 1, CHIPS - 1 - j, j) if 0 < j < CHIPS - 1 else j)


def block_of(index, size):
    return pl.ds(pl.multiple_of(index * size, size), size)


def pinned(array, memory):
    return array if memory is None else pltpu.with_memory_space_constraint(array, memory)


def call(kernel, outs, *args, scratch=(), flops=0, name=None, far=(), near=()):
    size = sum(a.size * a.dtype.itemsize for a in args)
    size += sum(o.size * o.dtype.itemsize for o in jax.tree.leaves(outs))
    spec = pl.BlockSpec(memory_space=pltpu.VMEM)
    return pl.pallas_call(
        kernel,
        out_shape=outs,
        in_specs=[pl.BlockSpec(memory_space=pl.ANY) if i in far else spec for i in range(len(args))],
        out_specs=jax.tree.map(lambda _: spec, outs),
        scratch_shapes=scratch,
        compiler_params=pltpu.CompilerParams(vmem_limit_bytes=16 * 2**20),
        cost_estimate=pl.CostEstimate(flops=flops, bytes_accessed=size, transcendentals=0),
        name=name,
    )(*(pinned(a, pltpu.HBM if i in far else pltpu.VMEM if i in near else None) for i, a in enumerate(args)))


def shape(dims, dtype=jnp.bfloat16):
    return jax.ShapeDtypeStruct(dims, dtype)


def group_rows(capacity):
    return round_up(ROWS * capacity, 8)


def slot_rows(capacity):
    return COLUMNS * group_rows(capacity)


def first_row(chip, capacity):
    return (chip % COLUMNS) * group_rows(capacity) + (chip // COLUMNS) * capacity


def dispatch_kernel(experts, *refs):
    far, outs, near, ready = refs[:6], refs[6 : 6 + CHIPS], refs[6 + CHIPS : -1], refs[-1]
    chip, core, _ = place()
    tokens, width = far[4].shape
    wide = width // CHIPS
    jobs = [(far[i], near[i]) for i in range(4)]
    for dk in range(CHIPS):
        for at in range(2):
            block = outs[dk].at[at * tokens : (at + 1) * tokens, :wide]
            jobs.append((far[4 + at].at[:, block_of(peer(chip, core, dk), wide)], block))
    copies = [pltpu.make_async_copy(*job, ready.at[i]) for i, job in enumerate(jobs)]
    for copy in copies:
        copy.start()
    for copy in copies[:4]:
        copy.wait()
    for at in range(2):
        route, gate = near[2 * at][...], near[2 * at + 1][...]
        topk = route.shape[0]
        earlier = (iota((tokens, tokens), 0) < iota((tokens, tokens), 1)).astype(jnp.float32)
        rank = jnp.zeros((topk, tokens), jnp.float32)
        for e in range(experts):
            named = (route == e).astype(jnp.float32)
            count = jnp.broadcast_to(jnp.sum(named, axis=0, keepdims=True), (8, tokens))
            rank = rank + named * dot(count, earlier)[:1]
        high = gate.astype(jnp.bfloat16).astype(jnp.float32)
        middle = (gate - high).astype(jnp.bfloat16).astype(jnp.float32)
        low = gate - high - middle
        table = jnp.zeros((128, tokens), jnp.float32)
        for part, value in enumerate((route.astype(jnp.float32), rank, high, middle, low)):
            for kk in range(topk):
                row = jnp.broadcast_to(value[kk : kk + 1], (128, tokens))
                table = jnp.where(iota((128, tokens), 0) == part * topk + kk, row, table)
        same = (iota((tokens, tokens), 0) == iota((tokens, tokens), 1)).astype(jnp.bfloat16)
        note = dot(same, table.astype(jnp.bfloat16), NT).astype(jnp.bfloat16)
        for dk in range(CHIPS):
            outs[dk][at * tokens : (at + 1) * tokens, wide:] = note
    for copy in copies[4:]:
        copy.wait()


def stash(experts, capacity, core, expert, saved, mine, theirs):
    rows = slot_rows(capacity)
    dims = (rows * experts, saved.shape[0])
    row, column = iota(dims, 0), iota(dims, 1)
    for target, ref in ((1 - core, theirs), (core, mine)):
        wanted = jnp.full(dims, -1, jnp.int32)
        for de in range(experts):
            for at in range(CHIPS):
                source = (at * CORES + target) * experts + lax.rem(expert + experts - de, experts)
                low = de * rows + first_row(at, capacity)
                inside = jnp.logical_and(row >= low, row < low + capacity)
                wanted = jnp.where(inside, row + (source * capacity - low), wanted)
        pick = jnp.where(column == wanted, 1.0, 0.0).astype(jnp.bfloat16)
        ref[...] = dot(pick, saved[...]).astype(jnp.bfloat16)


def dispatch(args, experts):
    tokens, wide = args[4].shape[0], args[4].shape[1] // CHIPS
    return call(
        functools.partial(dispatch_kernel, experts),
        [shape((2 * tokens, wide + 128)) for _ in range(CHIPS)],
        *args,
        scratch=[pltpu.VMEM(a.shape, a.dtype) for a in args[:4]] + [pltpu.SemaphoreType.DMA((4 + 2 * CHIPS,))],
        name="dispatch",
        far=range(6),
    )


def pick_kernel(experts, capacity, topk, *refs):
    blocks, outs = refs[:CHIPS], refs[CHIPS:]
    chip, core, expert = place()
    wide = outs[0].shape[1]
    rows = outs[0].shape[0] // 2
    tokens = blocks[0].shape[0] // 2
    lane = iota((CHIPS * tokens, rows), 1).astype(jnp.float32)
    for at in range(2):
        span = slice(at * tokens, (at + 1) * tokens)
        left = jnp.concatenate([b[span, :wide] for b in blocks], axis=0)
        notes = [b[span, wide:].astype(jnp.float32) for b in blocks]
        for de in (*range(1, experts), 0):
            here = lax.rem(expert + de, experts).astype(jnp.float32)
            choice = jnp.zeros((CHIPS * tokens, rows), jnp.float32)
            for kk in range(topk):
                targets = []
                for j, note in enumerate(notes):
                    route, rank = note[:, kk : kk + 1], note[:, topk + kk : topk + kk + 1]
                    first = first_row(peer(chip, core, j), capacity).astype(jnp.float32)
                    targets.append(jnp.where(route == here, rank + first, -1.0))
                choice += jnp.where(lane == jnp.concatenate(targets, axis=0), 1.0, 0.0)
            picked = dot(choice.astype(jnp.bfloat16), left, TN)
            outs[de][at * rows : (at + 1) * rows] = picked.astype(jnp.bfloat16)


def pick(blocks, experts, capacity, topk):
    wide = blocks[0].shape[1] - 128
    outs = [shape((2 * slot_rows(capacity), wide)) for _ in range(experts)]
    return call(functools.partial(pick_kernel, experts, capacity, topk), outs, *blocks, name="pick")


def hold_kernel(experts, capacity, gu, down, saved, gu_near, down_near, mine, theirs, near_saved, ready):
    _, core, expert = place()
    jobs = ((saved, near_saved), (gu, gu_near), (down, down_near))
    copies = [pltpu.make_async_copy(*job, ready.at[i]) for i, job in enumerate(jobs)]
    for copy in copies:
        copy.start()
    copies[0].wait()
    stash(experts, capacity, core, expert, near_saved, mine, theirs)
    for copy in copies[1:]:
        copy.wait()


def hold(gu, down, saved, experts, capacity):
    stashed = shape((slot_rows(capacity) * experts, saved.shape[1]))
    return call(
        functools.partial(hold_kernel, experts, capacity),
        [shape(gu.shape), shape(down.shape), stashed, stashed],
        gu,
        down,
        saved,
        scratch=[pltpu.VMEM(saved.shape, saved.dtype), pltpu.SemaphoreType.DMA((3,))],
        name="hold",
        far=range(3),
    )


def unit_rows(part, chip, units):
    return pl.ds(pl.multiple_of((part * CHIPS + chip) * units, units), units)


def up_kernel(experts, *refs):
    blocks, near, far = refs[:experts], refs[experts : experts + 2], refs[experts + 2 : experts + 4]
    outs = refs[experts + 4 :]
    chip, core, _ = place()
    half = near[0].shape[1]
    units = near[1].shape[0] // CHIPS
    rows = blocks[0].shape[0] // 2

    def left(at, side):
        return jnp.concatenate([b[at * rows : (at + 1) * rows, block_of(side, half)] for b in blocks], axis=0)

    own, other = [left(at, core) for at in range(2)], [left(at, 1 - core) for at in range(2)]
    for j in ORDER:
        for part in range(3):
            which, piece = divmod(part, 2)
            span = unit_rows(piece, peer(chip, core, j), units)
            total = dot(own[which], near[which][span, :], NT) + dot(other[which], far[which][span, :], NT)
            outs[j][:, part * units : (part + 1) * units] = total.astype(outs[j].dtype)


def up(blocks, near, far):
    experts = len(blocks)
    rows = blocks[0].shape[0] // 2 * experts
    size = near[0].size + near[1].size
    width = (near[0].shape[0] + near[1].shape[0]) // CHIPS
    outs = [shape((rows, width), jnp.float32 if j == 0 else jnp.bfloat16) for j in range(CHIPS)]
    kernel = functools.partial(up_kernel, experts)
    pins = (experts + 2, experts + 3)
    return call(kernel, outs, *blocks, *near, *far, flops=4 * rows * size, name="up", near=pins)


def act_kernel(*refs):
    parts, (mine, theirs, out) = refs[:CHIPS], refs[CHIPS:]
    _, core, _ = place()
    total = parts[0][...]
    for part in parts[1:]:
        total = total + part[...].astype(jnp.float32)
    units = total.shape[1] // 3
    gate_pre, up_pre, hidden_grad = total[:, :units], total[:, units : 2 * units], total[:, 2 * units :]
    out[:, :units] = (gate_pre * jax.nn.sigmoid(gate_pre) * up_pre).astype(jnp.bfloat16)
    half = units // CORES
    own, other = mine[...].astype(jnp.float32), theirs[...].astype(jnp.float32)
    low, high = jnp.where(core == 0, own, other), jnp.where(core == 0, other, own)
    for at, saved in enumerate((low, high)):
        gate_pre, up_pre = saved[:, :half], saved[:, half:]
        sig = jax.nn.sigmoid(gate_pre)
        grad = hidden_grad[:, at * half : (at + 1) * half]
        first = units + at * half
        out[:, first : first + half] = (grad * up_pre * (sig * (1.0 + gate_pre * (1.0 - sig)))).astype(jnp.bfloat16)
        out[:, first + units : first + units + half] = (grad * (gate_pre * sig)).astype(jnp.bfloat16)


def act(parts, mine, theirs):
    return call(act_kernel, shape(parts[0].shape), *parts, mine, theirs, name="act")


def down_kernel(experts, *refs):
    parts, near, far, outs = refs[:CHIPS], refs[CHIPS : CHIPS + 2], refs[CHIPS + 2 : CHIPS + 4], refs[CHIPS + 4 :]
    chip, core, _ = place()
    half = near[0].shape[1]
    units = near[1].shape[0] // CHIPS
    rows = parts[0].shape[0] // experts
    group = rows // COLUMNS
    low = chip % COLUMNS == 0
    for side, column in ((0, core), (1, 1 - core)):
        totals = []
        for which, terms in ((1, ((0, 0),)), (0, ((1, 0), (2, 1)))):
            weight = (near, far)[side][which]
            total = None
            for j in range(CHIPS):
                for piece, part in terms:
                    left = parts[j][:, piece * units : (piece + 1) * units]
                    term = dot(left, weight[unit_rows(part, peer(chip, core, j), units), :])
                    total = term if total is None else total + term
            totals.append(total)
        for de in range(experts):
            first = de * rows
            lower = jnp.concatenate([t[first : first + group] for t in totals], axis=0).astype(jnp.bfloat16)
            upper = jnp.concatenate([t[first + group : first + rows] for t in totals], axis=0).astype(jnp.bfloat16)
            outs[de][:, block_of(column, half)] = jnp.where(low, lower, upper)
            outs[experts + de][:, block_of(column, half)] = jnp.where(low, upper, lower)


def down(parts, near, far, experts):
    rows = parts[0].shape[0] // experts
    outs = [shape((2 * rows // COLUMNS, CORES * near[0].shape[1])) for _ in range(COLUMNS * experts)]
    flops = 4 * parts[0].shape[0] * (near[0].size + near[1].size)
    kernel = functools.partial(down_kernel, experts)
    return call(kernel, outs, *parts, *near, *far, flops=flops, name="down", near=(CHIPS + 2, CHIPS + 3))


def combine_kernel(experts, capacity, topk, *refs):
    blocks, results, outs = refs[:CHIPS], refs[CHIPS : CHIPS + COLUMNS * experts], refs[CHIPS + COLUMNS * experts :]
    chip, core, expert = place()
    group, wide = results[0].shape[0] // 2, results[0].shape[1]
    tokens = outs[0].shape[0] // 2
    lane = iota((2 * ROWS * tokens, 2 * group), 1).astype(jnp.float32)
    own = blocks[0][:, wide:].astype(jnp.float32)
    other = jnp.where(core == 0, blocks[2][:, wide:].astype(jnp.float32), blocks[1][:, wide:].astype(jnp.float32))
    notes, firsts = [], []
    for dz, note in enumerate((own, other)):
        for at in range(2):
            notes.append(note[at * tokens : (at + 1) * tokens])
            firsts.append((((chip // COLUMNS) ^ dz) * capacity + at * group).astype(jnp.float32))
    for dy in range(COLUMNS):
        total = None
        for kk in range(topk):
            found = None
            for de in range(experts):
                here = lax.rem(expert + de, experts).astype(jnp.float32)
                targets = []
                for note, first in zip(notes, firsts):
                    route, rank = note[:, kk : kk + 1], note[:, topk + kk : topk + kk + 1]
                    targets.append(jnp.where(route == here, rank + first, -1.0))
                choice = jnp.where(lane == jnp.concatenate(targets, axis=0), 1.0, 0.0).astype(jnp.bfloat16)
                term = dot(choice, results[dy * experts + de][...])
                found = term if found is None else found + term
            gates = []
            for note in notes:
                terms = [note[:, part * topk + kk : part * topk + kk + 1] for part in (2, 3, 4)]
                gates.append(terms[0] + terms[1] + terms[2])
            term = found * jnp.concatenate(gates, axis=0)
            total = term if total is None else total + term
        total = total.astype(jnp.bfloat16)
        for dz in range(ROWS):
            span = slice(dz * 2 * tokens, (dz + 1) * 2 * tokens)
            outs[dz][:, block_of((chip % COLUMNS) ^ dy, wide)] = total[span]


def combine(blocks, results, capacity, topk):
    experts = len(results) // COLUMNS
    outs = [shape((blocks[0].shape[0], COLUMNS * results[0].shape[1])) for _ in range(ROWS)]
    kernel = functools.partial(combine_kernel, experts, capacity, topk)
    return call(kernel, outs, *blocks, *results, name="combine")


def join_kernel(*refs):
    chip, _, _ = place()
    blocks, outs = refs[:-2], refs[-2:]
    tokens = outs[0].shape[0]
    for at, out in enumerate(outs):
        for dz in range(ROWS):
            block = blocks[dz + at * (len(blocks) - ROWS)]
            first = at * tokens if len(blocks) == ROWS else 0
            out[:, block_of((chip // COLUMNS) ^ dz, block.shape[1])] = block[first : first + tokens]


def join(blocks, tokens):
    out = shape((tokens, ROWS * blocks[0].shape[1]))
    return call(join_kernel, [out, out], *blocks, name="join")


def on_device(
    forward_input,
    forward_route,
    forward_gates,
    backward_cotangent,
    backward_route,
    backward_gates,
    gate_up_weight,
    down_weight,
    saved_projections,
):
    sections = lax.axis_size("section")
    experts = lax.axis_size("expert")
    topk = forward_route.shape[2]
    capacity = saved_projections.shape[2] // (GROUP * experts)
    tokens = forward_route.shape[1]

    def to_chip(value, j):
        places = [(k, c) for k in range(CHIPS) for c in range(CORES)]
        pairs = [(k * CORES + c, peer(k, c, j) * CORES + c) for k, c in places]
        return lax.ppermute(value, ("chip", "core"), pairs)

    def to_section(value, dz, by):
        places = [(i, k) for i in range(sections) for k in range(CHIPS)]
        pairs = [(i * CHIPS + k, (i + by) % sections * CHIPS + (k ^ (dz * COLUMNS))) for i, k in places]
        return lax.ppermute(value, ("section", "chip"), pairs)

    def to_expert(block, de):
        if de == 0:
            return block
        return lax.ppermute(block, "expert", [(i, (i + de) % experts) for i in range(experts)])

    def to_core(value):
        return lax.ppermute(value, "core", [(i, i ^ 1) for i in range(CORES)])

    def returned(block, dy, de):
        if dy == 0 and de == 0:
            return block
        places = [(k, e) for k in range(CHIPS) for e in range(experts)]
        pairs = [(k * experts + (e + de) % experts, (k ^ dy) * experts + e) for k, e in places]
        return lax.ppermute(block, ("chip", "expert"), pairs)

    def to_chips(blocks):
        return [blocks[0]] + [to_chip(blocks[dk], dk) for dk in range(1, CHIPS)]

    args = [a[0].T for a in (forward_route, forward_gates, backward_route, backward_gates)]
    gu, down_rows, saved = gate_up_weight[0, 0], down_weight[0, 0], saved_projections[0, 0]
    far = [to_core(gu), to_core(down_rows)]
    tokens_here = to_chips(dispatch(args + [forward_input[0], backward_cotangent[0]], experts))
    picked = pick(tokens_here, experts, capacity, topk)
    rows_here = [to_expert(picked[de], de) for de in range(experts)]
    *near, mine, theirs = hold(gu, down_rows, saved, experts, capacity)
    parts = up(rows_here, near, far)
    units = act(to_chips(parts), mine, to_core(theirs))
    results = down(to_chips([units] * CHIPS), near, far, experts)
    results = [returned(results[dy * experts + de], dy, de) for dy in range(COLUMNS) for de in range(experts)]
    outs = combine(tokens_here, results, capacity, topk)
    if sections == 2:
        joined = [to_section(outs[dz], dz, 1) for dz in range(ROWS)]
    else:
        joined = [to_section(outs[dz][:tokens], dz, 1) for dz in range(ROWS)]
        joined += [to_section(outs[dz][tokens:], dz, -1) for dz in range(ROWS)]
    next_input, prior_gradient = join(joined, tokens)
    return next_input[None], prior_gradient[None]


def solution(mesh):
    pipes, experts = mesh.devices.shape
    axes = ("section", "chip", "core", "expert")
    mesh = Mesh(mesh.devices.reshape(pipes // GROUP, CHIPS, CORES, experts), axes)
    rows = P(axes[:3], "expert", None)
    weights = P(axes[:3], "expert", None, None)
    return jax.shard_map(
        on_device,
        mesh=mesh,
        in_specs=(rows,) * 6 + (weights,) * 3,
        out_specs=(rows, rows),
        check_vma=False,
    )
```

```python
import functools

import jax
import jax.numpy as jnp
from jax import lax
from jax.experimental import pallas as pl
from jax.experimental.pallas import tpu as pltpu
from jax.sharding import Mesh
from jax.sharding import PartitionSpec as P

GROUP = 8
CORES = 2
CHIPS = GROUP // CORES
COLUMNS = 2
ROWS = CHIPS // COLUMNS
ORDER = (*range(1, CHIPS), 0)
TILE = 16
NT = (((1,), (1,)), ((), ()))
NN = (((1,), (0,)), ((), ()))
TN = (((0,), (0,)), ((), ()))


def round_up(value, step):
    return (value + step - 1) // step * step


def dot(a, b, dims=NN):
    return lax.dot_general(a, b, dims, preferred_element_type=jnp.float32)


def iota(shape, axis):
    return lax.broadcasted_iota(jnp.int32, shape, axis)


def place():
    return lax.axis_index("chip"), lax.axis_index("core"), lax.axis_index("expert")


def peer(chip, core, j):
    if isinstance(core, int):
        return chip ^ (CHIPS - 1 - j if core == 1 and 0 < j < CHIPS - 1 else j)
    return chip ^ (jnp.where(core == 1, CHIPS - 1 - j, j) if 0 < j < CHIPS - 1 else j)


def block_of(index, size):
    return pl.ds(pl.multiple_of(index * size, size), size)


def pinned(array, memory):
    return array if memory is None else pltpu.with_memory_space_constraint(array, memory)


def call(kernel, outs, *args, scratch=(), flops=0, name=None, far=(), near=()):
    size = sum(a.size * a.dtype.itemsize for a in args)
    size += sum(o.size * o.dtype.itemsize for o in jax.tree.leaves(outs))
    spec = pl.BlockSpec(memory_space=pltpu.VMEM)
    return pl.pallas_call(
        kernel,
        out_shape=outs,
        in_specs=[pl.BlockSpec(memory_space=pl.ANY) if i in far else spec for i in range(len(args))],
        out_specs=jax.tree.map(lambda _: spec, outs),
        scratch_shapes=scratch,
        compiler_params=pltpu.CompilerParams(vmem_limit_bytes=16 * 2**20),
        cost_estimate=pl.CostEstimate(flops=flops, bytes_accessed=size, transcendentals=0),
        name=name,
    )(*(pinned(a, pltpu.HBM if i in far else pltpu.VMEM if i in near else None) for i, a in enumerate(args)))


def shape(dims, dtype=jnp.bfloat16):
    return jax.ShapeDtypeStruct(dims, dtype)


def group_rows(capacity):
    return round_up(ROWS * capacity, 8)


def slot_rows(capacity):
    return COLUMNS * group_rows(capacity)


def first_row(chip, capacity):
    return (chip % COLUMNS) * group_rows(capacity) + (chip // COLUMNS) * capacity


def dispatch_kernel(experts, *refs):
    far, outs, near, ready = refs[:6], refs[6 : 6 + CHIPS], refs[6 + CHIPS : -1], refs[-1]
    chip, core, _ = place()
    tokens, width = far[4].shape
    wide = width // CHIPS
    jobs = [(far[i], near[i]) for i in range(4)]
    for dk in range(CHIPS):
        for at in range(2):
            block = outs[dk].at[at * tokens : (at + 1) * tokens, :wide]
            jobs.append((far[4 + at].at[:, block_of(peer(chip, core, dk), wide)], block))
    copies = [pltpu.make_async_copy(*job, ready.at[i]) for i, job in enumerate(jobs)]
    for copy in copies:
        copy.start()
    for copy in copies[:4]:
        copy.wait()
    for at in range(2):
        route, gate = near[2 * at][...], near[2 * at + 1][...]
        topk = route.shape[0]
        earlier = (iota((tokens, tokens), 0) < iota((tokens, tokens), 1)).astype(jnp.float32)
        rank = jnp.zeros((topk, tokens), jnp.float32)
        for e in range(experts):
            named = (route == e).astype(jnp.float32)
            count = jnp.broadcast_to(jnp.sum(named, axis=0, keepdims=True), (8, tokens))
            rank = rank + named * dot(count, earlier)[:1]
        high = gate.astype(jnp.bfloat16).astype(jnp.float32)
        middle = (gate - high).astype(jnp.bfloat16).astype(jnp.float32)
        low = gate - high - middle
        table = jnp.zeros((128, tokens), jnp.float32)
        for part, value in enumerate((route.astype(jnp.float32), rank, high, middle, low)):
            for kk in range(topk):
                row = jnp.broadcast_to(value[kk : kk + 1], (128, tokens))
                table = jnp.where(iota((128, tokens), 0) == part * topk + kk, row, table)
        same = (iota((tokens, tokens), 0) == iota((tokens, tokens), 1)).astype(jnp.bfloat16)
        note = dot(same, table.astype(jnp.bfloat16), NT).astype(jnp.bfloat16)
        for dk in range(CHIPS):
            outs[dk][at * tokens : (at + 1) * tokens, wide:] = note
    for copy in copies[4:]:
        copy.wait()


def stash(experts, capacity, core, expert, saved, mine, theirs):
    rows = slot_rows(capacity)
    dims = (rows * experts, saved.shape[0])
    row, column = iota(dims, 0), iota(dims, 1)
    for target, ref in ((1 - core, theirs), (core, mine)):
        wanted = jnp.full(dims, -1, jnp.int32)
        for de in range(experts):
            for at in range(CHIPS):
                source = (at * CORES + target) * experts + lax.rem(expert + experts - de, experts)
                low = de * rows + first_row(at, capacity)
                inside = jnp.logical_and(row >= low, row < low + capacity)
                wanted = jnp.where(inside, row + (source * capacity - low), wanted)
        pick = jnp.where(column == wanted, 1.0, 0.0).astype(jnp.bfloat16)
        ref[...] = dot(pick, saved[...]).astype(jnp.bfloat16)


def dispatch(args, experts):
    tokens, wide = args[4].shape[0], args[4].shape[1] // CHIPS
    return call(
        functools.partial(dispatch_kernel, experts),
        [shape((2 * tokens, wide + 128)) for _ in range(CHIPS)],
        *args,
        scratch=[pltpu.VMEM(a.shape, a.dtype) for a in args[:4]] + [pltpu.SemaphoreType.DMA((4 + 2 * CHIPS,))],
        name="dispatch",
        far=range(6),
    )


def pick_kernel(experts, capacity, topk, *refs):
    blocks, outs = refs[:CHIPS], refs[CHIPS:]
    chip, core, expert = place()
    wide = outs[0].shape[1]
    rows = outs[0].shape[0] // 2
    tokens = blocks[0].shape[0] // 2
    lane = iota((CHIPS * tokens, rows), 1).astype(jnp.float32)
    for at in range(2):
        span = slice(at * tokens, (at + 1) * tokens)
        left = jnp.concatenate([b[span, :wide] for b in blocks], axis=0)
        notes = [b[span, wide:].astype(jnp.float32) for b in blocks]
        for de in (*range(1, experts), 0):
            here = lax.rem(expert + de, experts).astype(jnp.float32)
            choice = jnp.zeros((CHIPS * tokens, rows), jnp.float32)
            for kk in range(topk):
                targets = []
                for j, note in enumerate(notes):
                    route, rank = note[:, kk : kk + 1], note[:, topk + kk : topk + kk + 1]
                    first = first_row(peer(chip, core, j), capacity).astype(jnp.float32)
                    targets.append(jnp.where(route == here, rank + first, -1.0))
                choice += jnp.where(lane == jnp.concatenate(targets, axis=0), 1.0, 0.0)
            picked = dot(choice.astype(jnp.bfloat16), left, TN)
            outs[de][at * rows : (at + 1) * rows] = picked.astype(jnp.bfloat16)


def pick(blocks, experts, capacity, topk):
    wide = blocks[0].shape[1] - 128
    outs = [shape((2 * slot_rows(capacity), wide)) for _ in range(experts)]
    return call(functools.partial(pick_kernel, experts, capacity, topk), outs, *blocks, name="pick")


def hold_kernel(experts, capacity, gu, down, saved, gu_near, down_near, mine, theirs, near_saved, ready):
    _, core, expert = place()
    jobs = ((saved, near_saved), (gu, gu_near), (down, down_near))
    copies = [pltpu.make_async_copy(*job, ready.at[i]) for i, job in enumerate(jobs)]
    for copy in copies:
        copy.start()
    copies[0].wait()
    stash(experts, capacity, core, expert, near_saved, mine, theirs)
    for copy in copies[1:]:
        copy.wait()


def hold(gu, down, saved, experts, capacity):
    stashed = shape((slot_rows(capacity) * experts, saved.shape[1]))
    return call(
        functools.partial(hold_kernel, experts, capacity),
        [shape(gu.shape), shape(down.shape), stashed, stashed],
        gu,
        down,
        saved,
        scratch=[pltpu.VMEM(saved.shape, saved.dtype), pltpu.SemaphoreType.DMA((3,))],
        name="hold",
        far=range(3),
    )


def unit_rows(part, chip, units):
    return pl.ds(pl.multiple_of((part * CHIPS + chip) * units, units), units)


def up_kernel(experts, *refs):
    blocks, near, far = refs[:experts], refs[experts : experts + 2], refs[experts + 2 : experts + 4]
    outs = refs[experts + 4 :]
    chip, core, _ = place()
    half = near[0].shape[1]
    units = near[1].shape[0] // CHIPS
    rows = blocks[0].shape[0] // 2

    def left(at, side):
        return jnp.concatenate([b[at * rows : (at + 1) * rows, block_of(side, half)] for b in blocks], axis=0)

    own, other = [left(at, core) for at in range(2)], [left(at, 1 - core) for at in range(2)]
    for j in ORDER:
        for part in range(3):
            which, piece = divmod(part, 2)
            span = unit_rows(piece, peer(chip, core, j), units)
            total = dot(own[which], near[which][span, :], NT) + dot(other[which], far[which][span, :], NT)
            outs[j][:, part * units : (part + 1) * units] = total.astype(outs[j].dtype)


def up(blocks, near, far):
    experts = len(blocks)
    rows = blocks[0].shape[0] // 2 * experts
    size = near[0].size + near[1].size
    width = (near[0].shape[0] + near[1].shape[0]) // CHIPS
    outs = [shape((rows, width), jnp.float32 if j == 0 else jnp.bfloat16) for j in range(CHIPS)]
    kernel = functools.partial(up_kernel, experts)
    pins = (experts + 2, experts + 3)
    return call(kernel, outs, *blocks, *near, *far, flops=4 * rows * size, name="up", near=pins)


def act_kernel(*refs):
    parts, (mine, theirs, out) = refs[:CHIPS], refs[CHIPS:]
    _, core, _ = place()
    total = parts[0][...]
    for part in parts[1:]:
        total = total + part[...].astype(jnp.float32)
    units = total.shape[1] // 3
    gate_pre, up_pre, hidden_grad = total[:, :units], total[:, units : 2 * units], total[:, 2 * units :]
    out[:, :units] = (gate_pre * jax.nn.sigmoid(gate_pre) * up_pre).astype(jnp.bfloat16)
    half = units // CORES
    own, other = mine[...].astype(jnp.float32), theirs[...].astype(jnp.float32)
    low, high = jnp.where(core == 0, own, other), jnp.where(core == 0, other, own)
    for at, saved in enumerate((low, high)):
        gate_pre, up_pre = saved[:, :half], saved[:, half:]
        sig = jax.nn.sigmoid(gate_pre)
        grad = hidden_grad[:, at * half : (at + 1) * half]
        first = units + at * half
        out[:, first : first + half] = (grad * up_pre * (sig * (1.0 + gate_pre * (1.0 - sig)))).astype(jnp.bfloat16)
        out[:, first + units : first + units + half] = (grad * (gate_pre * sig)).astype(jnp.bfloat16)


def act(parts, mine, theirs):
    return call(act_kernel, shape(parts[0].shape), *parts, mine, theirs, name="act")


def down_kernel(experts, terms, *refs):
    parts, near, far, outs = refs[:CHIPS], refs[CHIPS], refs[CHIPS + 1], refs[CHIPS + 2 :]
    chip, core, _ = place()
    half = near.shape[1]
    units = near.shape[0] // CHIPS // len(terms)
    rows = parts[0].shape[0] // experts
    group = rows // COLUMNS
    low = chip % COLUMNS == 0
    for weight, column in ((near, core), (far, 1 - core)):
        total = None
        for j in range(CHIPS):
            for part, piece in enumerate(terms):
                left = parts[j][:, piece * units : (piece + 1) * units]
                term = dot(left, weight[unit_rows(part, peer(chip, core, j), units), :])
                total = term if total is None else total + term
        for de in range(experts):
            first = de * rows
            lower, upper = total[first : first + group], total[first + group : first + rows]
            outs[de][:, block_of(column, half)] = jnp.where(low, lower, upper).astype(jnp.bfloat16)
            outs[experts + de][:, block_of(column, half)] = jnp.where(low, upper, lower).astype(jnp.bfloat16)


def down(parts, near, far, experts, terms, name):
    group = parts[0].shape[0] // experts // COLUMNS
    outs = [shape((group, CORES * near.shape[1])) for _ in range(COLUMNS * experts)]
    flops = 4 * parts[0].shape[0] * near.size
    kernel = functools.partial(down_kernel, experts, terms)
    return call(kernel, outs, *parts, near, far, flops=flops, name=name, near=(CHIPS + 1,))


def combine_kernel(experts, capacity, topk, at, *refs):
    blocks, results, outs = refs[:CHIPS], refs[CHIPS : CHIPS + COLUMNS * experts], refs[CHIPS + COLUMNS * experts :]
    chip, core, expert = place()
    group, wide = results[0].shape
    tokens = outs[0].shape[0]
    lane = iota((ROWS * tokens, group), 1).astype(jnp.float32)
    own, one, two = [blocks[j][at * tokens : (at + 1) * tokens, wide:].astype(jnp.float32) for j in range(3)]
    notes = (own, jnp.where(core == 0, two, one))
    firsts = [(((chip // COLUMNS) ^ dz) * capacity).astype(jnp.float32) for dz in range(ROWS)]
    for dy in range(COLUMNS):
        total = None
        for kk in range(topk):
            found = None
            for de in range(experts):
                here = lax.rem(expert + de, experts).astype(jnp.float32)
                targets = []
                for note, first in zip(notes, firsts):
                    route, rank = note[:, kk : kk + 1], note[:, topk + kk : topk + kk + 1]
                    targets.append(jnp.where(route == here, rank + first, -1.0))
                choice = jnp.where(lane == jnp.concatenate(targets, axis=0), 1.0, 0.0).astype(jnp.bfloat16)
                term = dot(choice, results[dy * experts + de][...])
                found = term if found is None else found + term
            gates = []
            for note in notes:
                terms = [note[:, part * topk + kk : part * topk + kk + 1] for part in (2, 3, 4)]
                gates.append(terms[0] + terms[1] + terms[2])
            term = found * jnp.concatenate(gates, axis=0)
            total = term if total is None else total + term
        total = total.astype(jnp.bfloat16)
        for dz in range(ROWS):
            outs[dz][:, block_of((chip % COLUMNS) ^ dy, wide)] = total[dz * tokens : (dz + 1) * tokens]


def combine(blocks, results, capacity, topk, at, name):
    experts = len(results) // COLUMNS
    outs = [shape((blocks[0].shape[0] // 2, COLUMNS * results[0].shape[1])) for _ in range(ROWS)]
    kernel = functools.partial(combine_kernel, experts, capacity, topk, at)
    return call(kernel, outs, *blocks, *results, name=name)


def join_kernel(*refs):
    chip, _, _ = place()
    blocks, out = refs[:-1], refs[-1]
    for dz, block in enumerate(blocks):
        out[:, block_of((chip // COLUMNS) ^ dz, block.shape[1])] = block[...]


def join(blocks, name):
    tokens, wide = blocks[0].shape
    return call(join_kernel, shape((tokens, ROWS * wide)), *blocks, name=name)


def on_device(
    forward_input,
    forward_route,
    forward_gates,
    backward_cotangent,
    backward_route,
    backward_gates,
    gate_up_weight,
    down_weight,
    saved_projections,
):
    sections = lax.axis_size("section")
    experts = lax.axis_size("expert")
    topk = forward_route.shape[2]
    capacity = saved_projections.shape[2] // (GROUP * experts)

    def to_chip(value, j):
        places = [(k, c) for k in range(CHIPS) for c in range(CORES)]
        pairs = [(k * CORES + c, peer(k, c, j) * CORES + c) for k, c in places]
        return lax.ppermute(value, ("chip", "core"), pairs)

    def to_section(value, dz, by):
        places = [(i, k) for i in range(sections) for k in range(CHIPS)]
        pairs = [(i * CHIPS + k, (i + by) % sections * CHIPS + (k ^ (dz * COLUMNS))) for i, k in places]
        return lax.ppermute(value, ("section", "chip"), pairs)

    def to_expert(block, de):
        if de == 0:
            return block
        return lax.ppermute(block, "expert", [(i, (i + de) % experts) for i in range(experts)])

    def to_core(value):
        return lax.ppermute(value, "core", [(i, i ^ 1) for i in range(CORES)])

    def returned(block, dy, de):
        if dy == 0 and de == 0:
            return block
        places = [(k, e) for k in range(CHIPS) for e in range(experts)]
        pairs = [(k * experts + (e + de) % experts, (k ^ dy) * experts + e) for k, e in places]
        return lax.ppermute(block, ("chip", "expert"), pairs)

    def to_chips(blocks):
        return [blocks[0]] + [to_chip(blocks[dk], dk) for dk in range(1, CHIPS)]

    args = [a[0].T for a in (forward_route, forward_gates, backward_route, backward_gates)]
    gu, down_rows, saved = gate_up_weight[0, 0], down_weight[0, 0], saved_projections[0, 0]
    far = [to_core(gu), to_core(down_rows)]
    tokens_here = to_chips(dispatch(args + [forward_input[0], backward_cotangent[0]], experts))
    picked = pick(tokens_here, experts, capacity, topk)
    rows_here = [to_expert(picked[de], de) for de in range(experts)]
    *near, mine, theirs = hold(gu, down_rows, saved, experts, capacity)
    parts = up(rows_here, near, far)
    units = act(to_chips(parts), mine, to_core(theirs))
    units = to_chips([units] * CHIPS)
    outputs = []
    for at, which, terms, by, name in ((0, 1, (0,), 1, "ahead"), (1, 0, (1, 2), -1, "behind")):
        results = down(units, near[which], far[which], experts, terms, "down_" + name)
        results = [returned(results[dy * experts + de], dy, de) for dy in range(COLUMNS) for de in range(experts)]
        outs = combine(tokens_here, results, capacity, topk, at, "combine_" + name)
        outputs.append(join([to_section(outs[dz], dz, by) for dz in range(ROWS)], "join_" + name)[None])
    return tuple(outputs)


def solution(mesh):
    pipes, experts = mesh.devices.shape
    axes = ("section", "chip", "core", "expert")
    mesh = Mesh(mesh.devices.reshape(pipes // GROUP, CHIPS, CORES, experts), axes)
    rows = P(axes[:3], "expert", None)
    weights = P(axes[:3], "expert", None, None)
    return jax.shard_map(
        on_device,
        mesh=mesh,
        in_specs=(rows,) * 6 + (weights,) * 3,
        out_specs=(rows, rows),
        check_vma=False,
    )
```

```python
import functools

import jax
import jax.numpy as jnp
from jax import lax
from jax.experimental import pallas as pl
from jax.experimental.pallas import tpu as pltpu
from jax.sharding import Mesh
from jax.sharding import PartitionSpec as P

GROUP = 8
CORES = 2
CHIPS = GROUP // CORES
COLUMNS = 2
ROWS = CHIPS // COLUMNS
ORDER = (*range(1, CHIPS), 0)
TILE = 16
NT = (((1,), (1,)), ((), ()))
NN = (((1,), (0,)), ((), ()))
TN = (((0,), (0,)), ((), ()))


def round_up(value, step):
    return (value + step - 1) // step * step


def dot(a, b, dims=NN):
    return lax.dot_general(a, b, dims, preferred_element_type=jnp.float32)


def iota(shape, axis):
    return lax.broadcasted_iota(jnp.int32, shape, axis)


def place():
    return lax.axis_index("chip"), lax.axis_index("core"), lax.axis_index("expert")


def peer(chip, core, j):
    if isinstance(core, int):
        return chip ^ (CHIPS - 1 - j if core == 1 and 0 < j < CHIPS - 1 else j)
    return chip ^ (jnp.where(core == 1, CHIPS - 1 - j, j) if 0 < j < CHIPS - 1 else j)


def block_of(index, size):
    return pl.ds(pl.multiple_of(index * size, size), size)


def pinned(array, memory):
    return array if memory is None else pltpu.with_memory_space_constraint(array, memory)


def call(kernel, outs, *args, scratch=(), flops=0, name=None, far=(), near=()):
    size = sum(a.size * a.dtype.itemsize for a in args)
    size += sum(o.size * o.dtype.itemsize for o in jax.tree.leaves(outs))
    spec = pl.BlockSpec(memory_space=pltpu.VMEM)
    return pl.pallas_call(
        kernel,
        out_shape=outs,
        in_specs=[pl.BlockSpec(memory_space=pl.ANY) if i in far else spec for i in range(len(args))],
        out_specs=jax.tree.map(lambda _: spec, outs),
        scratch_shapes=scratch,
        compiler_params=pltpu.CompilerParams(vmem_limit_bytes=16 * 2**20),
        cost_estimate=pl.CostEstimate(flops=flops, bytes_accessed=size, transcendentals=0),
        name=name,
    )(*(pinned(a, pltpu.HBM if i in far else pltpu.VMEM if i in near else None) for i, a in enumerate(args)))


def shape(dims, dtype=jnp.bfloat16):
    return jax.ShapeDtypeStruct(dims, dtype)


def chip_rows(capacity):
    return round_up(CORES * capacity, 8)


def position(chip):
    return (chip % COLUMNS) * ROWS + chip // COLUMNS


def lane_shift(lanes, by):
    return (iota((lanes, lanes), 1) == iota((lanes, lanes), 0) + by).astype(jnp.bfloat16)


def pack_kernel(experts, *refs):
    far, out, near, ready = refs[:6], refs[6], refs[7:-1], refs[-1]
    tokens, width = far[4].shape
    jobs = [(far[i], near[i]) for i in range(4)]
    jobs += [(far[4 + at], out.at[at * tokens : (at + 1) * tokens, :width]) for at in range(2)]
    copies = [pltpu.make_async_copy(*job, ready.at[i]) for i, job in enumerate(jobs)]
    for copy in copies:
        copy.start()
    for copy in copies[:4]:
        copy.wait()
    for at in range(2):
        route, gate = near[2 * at][...], near[2 * at + 1][...]
        topk = route.shape[0]
        earlier = (iota((tokens, tokens), 0) < iota((tokens, tokens), 1)).astype(jnp.float32)
        rank = jnp.zeros((topk, tokens), jnp.float32)
        for e in range(experts):
            named = (route == e).astype(jnp.float32)
            count = jnp.broadcast_to(jnp.sum(named, axis=0, keepdims=True), (8, tokens))
            rank = rank + named * dot(count, earlier)[:1]
        high = gate.astype(jnp.bfloat16).astype(jnp.float32)
        middle = (gate - high).astype(jnp.bfloat16).astype(jnp.float32)
        low = gate - high - middle
        table = jnp.zeros((128, tokens), jnp.float32)
        for part, value in enumerate((route.astype(jnp.float32), rank, high, middle, low)):
            for kk in range(topk):
                row = jnp.broadcast_to(value[kk : kk + 1], (128, tokens))
                table = jnp.where(iota((128, tokens), 0) == part * topk + kk, row, table)
        same = (iota((tokens, tokens), 0) == iota((tokens, tokens), 1)).astype(jnp.bfloat16)
        note = dot(same, table.astype(jnp.bfloat16), NT).astype(jnp.bfloat16)
        out[at * tokens : (at + 1) * tokens, width:] = note
    for copy in copies[4:]:
        copy.wait()


def pack(args, experts):
    tokens, width = args[4].shape
    return call(
        functools.partial(pack_kernel, experts),
        shape((2 * tokens, width + 128)),
        *args,
        scratch=[pltpu.VMEM(a.shape, a.dtype) for a in args[:4]] + [pltpu.SemaphoreType.DMA((6,))],
        name="pack",
        far=range(6),
    )


def targets_of(note, kk, topk, tokens, here, firsts):
    route, rank = note[:, kk : kk + 1], note[:, topk + kk : topk + kk + 1]
    ahead = iota(route.shape, 0) < tokens
    first = jnp.where(ahead, firsts[0].astype(jnp.float32), firsts[1].astype(jnp.float32))
    return jnp.where(route == here, rank + first, -1.0)


def pick_kernel(experts, capacity, topk, own, other, *outs):
    chip, core, expert = place()
    tokens, width = own.shape[0] // 2, own.shape[1] - 128
    wide, rows = width // CHIPS, chip_rows(capacity)
    span = 2 * rows
    lane = iota((4 * tokens, span), 1).astype(jnp.float32)
    notes = [own[:, width:], other[:, width:]]
    firsts = [(side * capacity, rows + side * capacity) for side in (core, 1 - core)]
    first_core = jnp.where(core == 0, notes[0].astype(jnp.float32), notes[1].astype(jnp.float32))
    second_core = jnp.where(core == 0, notes[1].astype(jnp.float32), notes[0].astype(jnp.float32))
    both = first_core + dot(second_core.astype(jnp.bfloat16), lane_shift(128, 64))
    both = jnp.concatenate([both, jnp.zeros((span - 2 * tokens, 128), jnp.float32)], axis=0).astype(jnp.bfloat16)
    for i in range(experts // CORES):
        here = lax.rem(expert + core * (experts // CORES) + i, experts).astype(jnp.float32)
        choice = jnp.zeros((4 * tokens, span), jnp.float32)
        for kk in range(topk):
            targets = [
                targets_of(note.astype(jnp.float32), kk, topk, tokens, here, first) for note, first in zip(notes, firsts)
            ]
            choice += jnp.where(lane == jnp.concatenate(targets, axis=0), 1.0, 0.0)
        choice = choice.astype(jnp.bfloat16)
        for dk in range(CHIPS):
            at = block_of(chip ^ dk, wide)
            left = jnp.concatenate([own[:, at], other[:, at]], axis=0)
            out = outs[i * CHIPS + dk]
            out[:, :wide] = dot(choice, left, TN).astype(jnp.bfloat16)
            out[:, wide:] = both


def pick(own, other, experts, capacity, topk):
    wide = (own.shape[1] - 128) // CHIPS
    outs = [shape((2 * chip_rows(capacity), wide + 128)) for _ in range(CHIPS * experts // CORES)]
    return call(functools.partial(pick_kernel, experts, capacity, topk), outs, own, other, name="pick")


def hold_kernel(experts, capacity, gu, down, saved, gu_near, down_near, mine, theirs, near_saved, ready):
    _, core, expert = place()
    jobs = ((saved, near_saved), (gu, gu_near), (down, down_near))
    copies = [pltpu.make_async_copy(*job, ready.at[i]) for i, job in enumerate(jobs)]
    for copy in copies:
        copy.start()
    copies[0].wait()
    stash(experts, capacity, core, expert, near_saved, mine, theirs)
    for copy in copies[1:]:
        copy.wait()


def stash(experts, capacity, core, expert, saved, mine, theirs):
    rows = chip_rows(capacity)
    dims = (rows * CHIPS * experts // CORES, saved.shape[0])
    row, column = iota(dims, 0), iota(dims, 1)
    for target, ref in ((1 - core, theirs), (core, mine)):
        wanted = jnp.full(dims, -1, jnp.int32)
        for i in range(experts // CORES):
            column_of = lax.rem(expert + experts - target * (experts // CORES) - i, experts)
            for at in range(CHIPS):
                for side in range(CORES):
                    source = (at * CORES + side) * experts + column_of
                    low = (i * CHIPS + position(at)) * rows + side * capacity
                    inside = jnp.logical_and(row >= low, row < low + capacity)
                    wanted = jnp.where(inside, row + (source * capacity - low), wanted)
        choice = jnp.where(column == wanted, 1.0, 0.0).astype(jnp.bfloat16)
        ref[...] = dot(choice, saved[...]).astype(jnp.bfloat16)


def hold(gu, down, saved, experts, capacity):
    stashed = shape((chip_rows(capacity) * CHIPS * experts // CORES, saved.shape[1]))
    return call(
        functools.partial(hold_kernel, experts, capacity),
        [shape(gu.shape), shape(down.shape), stashed, stashed],
        gu,
        down,
        saved,
        scratch=[pltpu.VMEM(saved.shape, saved.dtype), pltpu.SemaphoreType.DMA((3,))],
        name="hold",
        far=range(3),
    )


def unit_rows(part, chip, units):
    return pl.ds(pl.multiple_of((part * CHIPS + chip) * units, units), units)


def up_kernel(count, *refs):
    blocks, near, far, outs = refs[:count], refs[count : count + 2], refs[count + 2 : count + 4], refs[count + 4 : -1]
    note = refs[-1]
    chip, core, _ = place()
    half = near[0].shape[1]
    wide = CORES * half
    units = near[1].shape[0] // CHIPS
    rows = blocks[0].shape[0] // 2
    note[...] = blocks[COLUMNS][: note.shape[0], wide:]
    lefts = [[], []]
    for i in range(count // CHIPS):
        here = [blocks[i * CHIPS + dk][:, :wide].astype(jnp.float32) for dk in range(CHIPS)]
        here = [jnp.where(chip % COLUMNS == 0, here[k], here[k ^ 1]) for k in range(CHIPS)]
        here = [jnp.where(chip // COLUMNS == 0, here[k], here[k ^ COLUMNS]) for k in range(CHIPS)]
        for at in range(2):
            for k in sorted(range(CHIPS), key=position):
                lefts[at].append(here[k][at * rows : (at + 1) * rows])
    lefts = [jnp.concatenate(left, axis=0).astype(jnp.bfloat16) for left in lefts]
    own = [jnp.where(core == 0, left[:, :half], left[:, half:]) for left in lefts]
    other = [jnp.where(core == 0, left[:, half:], left[:, :half]) for left in lefts]
    for j in ORDER:
        for part in range(3):
            which, piece = divmod(part, 2)
            span = unit_rows(piece, peer(chip, core, j), units)
            total = dot(own[which], near[which][span, :], NT) + dot(other[which], far[which][span, :], NT)
            outs[j][:, part * units : (part + 1) * units] = total.astype(outs[j].dtype)


def up(blocks, near, far, tokens):
    count = len(blocks)
    rows = blocks[0].shape[0] // 2 * count
    size = near[0].size + near[1].size
    width = (near[0].shape[0] + near[1].shape[0]) // CHIPS
    outs = [shape((rows, width), jnp.float32 if j == 0 else jnp.bfloat16) for j in range(CHIPS)]
    outs.append(shape((2 * tokens, 128)))
    kernel = functools.partial(up_kernel, count)
    pins = (count + 2, count + 3)
    results = call(kernel, outs, *blocks, *near, *far, flops=4 * rows * size, name="up", near=pins)
    return results[:-1], results[-1]


def act_kernel(*refs):
    parts, (mine, theirs, out) = refs[:CHIPS], refs[CHIPS:]
    _, core, _ = place()
    total = parts[0][...]
    for part in parts[1:]:
        total = total + part[...].astype(jnp.float32)
    units = total.shape[1] // 3
    gate_pre, up_pre, hidden_grad = total[:, :units], total[:, units : 2 * units], total[:, 2 * units :]
    out[:, :units] = (gate_pre * jax.nn.sigmoid(gate_pre) * up_pre).astype(jnp.bfloat16)
    half = units // CORES
    own, other = mine[...].astype(jnp.float32), theirs[...].astype(jnp.float32)
    low, high = jnp.where(core == 0, own, other), jnp.where(core == 0, other, own)
    for at, saved in enumerate((low, high)):
        gate_pre, up_pre = saved[:, :half], saved[:, half:]
        sig = jax.nn.sigmoid(gate_pre)
        grad = hidden_grad[:, at * half : (at + 1) * half]
        first = units + at * half
        out[:, first : first + half] = (grad * up_pre * (sig * (1.0 + gate_pre * (1.0 - sig)))).astype(jnp.bfloat16)
        out[:, first + units : first + units + half] = (grad * (gate_pre * sig)).astype(jnp.bfloat16)


def act(parts, mine, theirs):
    return call(act_kernel, shape(parts[0].shape), *parts, mine, theirs, name="act")


def down_kernel(experts, *refs):
    parts, near, far, outs = refs[:CHIPS], refs[CHIPS : CHIPS + 2], refs[CHIPS + 2 : CHIPS + 4], refs[CHIPS + 4 :]
    chip, core, _ = place()
    half = near[0].shape[1]
    units = near[1].shape[0] // CHIPS
    rows = parts[0].shape[0] // experts
    group = rows // COLUMNS
    low = chip % COLUMNS == 0
    for side, column in ((0, core), (1, 1 - core)):
        totals = []
        for which, terms in ((1, ((0, 0),)), (0, ((1, 0), (2, 1)))):
            weight = (near, far)[side][which]
            total = None
            for j in range(CHIPS):
                for piece, part in terms:
                    left = parts[j][:, piece * units : (piece + 1) * units]
                    term = dot(left, weight[unit_rows(part, peer(chip, core, j), units), :])
                    total = term if total is None else total + term
            totals.append(total)
        for de in range(experts):
            first = de * rows
            lower = jnp.concatenate([t[first : first + group] for t in totals], axis=0).astype(jnp.bfloat16)
            upper = jnp.concatenate([t[first + group : first + rows] for t in totals], axis=0).astype(jnp.bfloat16)
            outs[de][:, block_of(column, half)] = jnp.where(low, lower, upper)
            outs[experts + de][:, block_of(column, half)] = jnp.where(low, upper, lower)


def down(parts, near, far, experts):
    rows = parts[0].shape[0] // experts
    outs = [shape((2 * rows // COLUMNS, CORES * near[0].shape[1])) for _ in range(COLUMNS * experts)]
    flops = 4 * parts[0].shape[0] * (near[0].size + near[1].size)
    kernel = functools.partial(down_kernel, experts)
    return call(kernel, outs, *parts, *near, *far, flops=flops, name="down", near=(CHIPS + 2, CHIPS + 3))


def combine_kernel(experts, capacity, topk, own, other, note_here, note_there, *refs):
    results, (keep, send) = refs[:-2], refs[-2:]
    chip, core, expert = place()
    count = experts // CORES
    group, wide = results[0].shape[0] // 2, results[0].shape[1]
    tokens, width = own.shape[0] // 2, own.shape[1] - 128
    rows = chip_rows(capacity)
    lane = iota((2 * ROWS * tokens, 2 * group), 1).astype(jnp.float32)
    near = [own[:, width:].astype(jnp.float32), other[:, width:].astype(jnp.float32)]
    remote = jnp.where(core == 0, note_here[...].astype(jnp.float32), note_there[...].astype(jnp.float32))
    shifted = dot(remote.astype(jnp.bfloat16), lane_shift(128, -64))
    remotes = [jnp.where(core == 0, remote, shifted), jnp.where(core == 0, shifted, remote)]
    for out, side, notes in ((send, 1 - core, (near[1], remotes[1])), (keep, core, (near[0], remotes[0]))):
        firsts = [((chip // COLUMNS) ^ dz) * rows + side * capacity for dz in range(ROWS)]
        for dy in range(COLUMNS):
            total = None
            for kk in range(topk):
                found = None
                for i in range(count):
                    here = lax.rem(expert + core * count + i, experts).astype(jnp.float32)
                    targets = [
                        targets_of(note, kk, topk, tokens, here, (first, first + group))
                        for note, first in zip(notes, firsts)
                    ]
                    choice = jnp.where(lane == jnp.concatenate(targets, axis=0), 1.0, 0.0).astype(jnp.bfloat16)
                    term = dot(choice, results[dy * count + i][...])
                    found = term if found is None else found + term
                gates = []
                for note in notes:
                    terms = [note[:, part * topk + kk : part * topk + kk + 1] for part in (2, 3, 4)]
                    gates.append(terms[0] + terms[1] + terms[2])
                term = found * jnp.concatenate(gates, axis=0)
                total = term if total is None else total + term
            out[:, block_of((chip % COLUMNS) ^ dy, wide)] = total.astype(jnp.bfloat16)


def combine(own, other, note_here, note_there, results, experts, capacity, topk):
    out = shape((ROWS * own.shape[0], COLUMNS * results[0].shape[1]))
    kernel = functools.partial(combine_kernel, experts, capacity, topk)
    return call(kernel, [out, out], own, other, note_here, note_there, *results, name="combine")


def merge_kernel(keep, got, *outs):
    rows = outs[0].shape[0]
    for dz, out in enumerate(outs):
        span = slice(dz * rows, (dz + 1) * rows)
        out[...] = (keep[span].astype(jnp.float32) + got[span].astype(jnp.float32)).astype(jnp.bfloat16)


def merge(keep, got):
    outs = [shape((keep.shape[0] // ROWS, keep.shape[1])) for _ in range(ROWS)]
    return call(merge_kernel, outs, keep, got, name="merge")


def join_kernel(*refs):
    chip, _, _ = place()
    blocks, outs = refs[:-2], refs[-2:]
    tokens = outs[0].shape[0]
    for at, out in enumerate(outs):
        for dz in range(ROWS):
            block = blocks[dz + at * (len(blocks) - ROWS)]
            first = at * tokens if len(blocks) == ROWS else 0
            out[:, block_of((chip // COLUMNS) ^ dz, block.shape[1])] = block[first : first + tokens]


def join(blocks, tokens):
    out = shape((tokens, ROWS * blocks[0].shape[1]))
    return call(join_kernel, [out, out], *blocks, name="join")


def on_device(
    forward_input,
    forward_route,
    forward_gates,
    backward_cotangent,
    backward_route,
    backward_gates,
    gate_up_weight,
    down_weight,
    saved_projections,
):
    sections = lax.axis_size("section")
    experts = lax.axis_size("expert")
    topk = forward_route.shape[2]
    capacity = saved_projections.shape[2] // (GROUP * experts)
    tokens = forward_route.shape[1]

    def to_chip(value, j):
        places = [(k, c) for k in range(CHIPS) for c in range(CORES)]
        pairs = [(k * CORES + c, peer(k, c, j) * CORES + c) for k, c in places]
        return lax.ppermute(value, ("chip", "core"), pairs)

    def to_section(value, dz, by):
        places = [(i, k) for i in range(sections) for k in range(CHIPS)]
        pairs = [(i * CHIPS + k, (i + by) % sections * CHIPS + (k ^ (dz * COLUMNS))) for i, k in places]
        return lax.ppermute(value, ("section", "chip"), pairs)

    def to_core(value):
        return lax.ppermute(value, "core", [(i, i ^ 1) for i in range(CORES)])

    half = experts // CORES
    everyone = [(k, c, e) for k in range(CHIPS) for c in range(CORES) for e in range(experts)]

    def moved(value, dk, i, way):
        pairs = [
            ((k * CORES + c) * experts + e, ((k ^ dk) * CORES + c) * experts + (e + way * (c * half + i)) % experts)
            for k, c, e in everyone
        ]
        return lax.ppermute(value, ("chip", "core", "expert"), pairs)

    def to_chips(blocks):
        return [blocks[0]] + [to_chip(blocks[dk], dk) for dk in range(1, CHIPS)]

    args = [a[0].T for a in (forward_route, forward_gates, backward_route, backward_gates)]
    gu, down_rows, saved = gate_up_weight[0, 0], down_weight[0, 0], saved_projections[0, 0]
    far = [to_core(gu), to_core(down_rows)]
    own = pack(args + [forward_input[0], backward_cotangent[0]], experts)
    other = to_core(own)
    picked = pick(own, other, experts, capacity, topk)
    arrived = [moved(picked[i * CHIPS + dk], dk, i, 1) for i in range(half) for dk in range(CHIPS)]
    *near, mine, theirs = hold(gu, down_rows, saved, experts, capacity)
    parts, note = up(arrived, near, far, tokens)
    units = act(to_chips(parts), mine, to_core(theirs))
    note_there = to_core(note)
    results = down(to_chips([units] * CHIPS), near, far, half)
    results = [moved(results[dy * half + i], dy, i, -1) for dy in range(COLUMNS) for i in range(half)]
    keep, send = combine(own, other, note, note_there, results, experts, capacity, topk)
    outs = merge(keep, to_core(send))
    if sections == 2:
        joined = [to_section(outs[dz], dz, 1) for dz in range(ROWS)]
    else:
        joined = [to_section(outs[dz][:tokens], dz, 1) for dz in range(ROWS)]
        joined += [to_section(outs[dz][tokens:], dz, -1) for dz in range(ROWS)]
    next_input, prior_gradient = join(joined, tokens)
    return next_input[None], prior_gradient[None]


def solution(mesh):
    pipes, experts = mesh.devices.shape
    axes = ("section", "chip", "core", "expert")
    mesh = Mesh(mesh.devices.reshape(pipes // GROUP, CHIPS, CORES, experts), axes)
    rows = P(axes[:3], "expert", None)
    weights = P(axes[:3], "expert", None, None)
    return jax.shard_map(
        on_device,
        mesh=mesh,
        in_specs=(rows,) * 6 + (weights,) * 3,
        out_specs=(rows, rows),
        check_vma=False,
    )
```

```python
import functools

import jax
import jax.numpy as jnp
from jax import lax
from jax.experimental import pallas as pl
from jax.experimental.pallas import tpu as pltpu
from jax.sharding import Mesh
from jax.sharding import PartitionSpec as P

GROUP = 8
CORES = 2
CHIPS = GROUP // CORES
COLUMNS = 2
ROWS = CHIPS // COLUMNS
ORDER = (*range(1, CHIPS), 0)
TILE = 16
NT = (((1,), (1,)), ((), ()))
NN = (((1,), (0,)), ((), ()))
TN = (((0,), (0,)), ((), ()))


def round_up(value, step):
    return (value + step - 1) // step * step


def dot(a, b, dims=NN):
    return lax.dot_general(a, b, dims, preferred_element_type=jnp.float32)


def iota(shape, axis):
    return lax.broadcasted_iota(jnp.int32, shape, axis)


def place():
    return lax.axis_index("chip"), lax.axis_index("core"), lax.axis_index("expert")


def peer(chip, core, j):
    if isinstance(core, int):
        return chip ^ (CHIPS - 1 - j if core == 1 and 0 < j < CHIPS - 1 else j)
    return chip ^ (jnp.where(core == 1, CHIPS - 1 - j, j) if 0 < j < CHIPS - 1 else j)


def block_of(index, size):
    return pl.ds(pl.multiple_of(index * size, size), size)


def pinned(array, memory):
    return array if memory is None else pltpu.with_memory_space_constraint(array, memory)


def call(kernel, outs, *args, scratch=(), flops=0, name=None, far=(), near=()):
    size = sum(a.size * a.dtype.itemsize for a in args)
    size += sum(o.size * o.dtype.itemsize for o in jax.tree.leaves(outs))
    spec = pl.BlockSpec(memory_space=pltpu.VMEM)
    return pl.pallas_call(
        kernel,
        out_shape=outs,
        in_specs=[pl.BlockSpec(memory_space=pl.ANY) if i in far else spec for i in range(len(args))],
        out_specs=jax.tree.map(lambda _: spec, outs),
        scratch_shapes=scratch,
        compiler_params=pltpu.CompilerParams(vmem_limit_bytes=16 * 2**20),
        cost_estimate=pl.CostEstimate(flops=flops, bytes_accessed=size, transcendentals=0),
        name=name,
    )(*(pinned(a, pltpu.HBM if i in far else pltpu.VMEM if i in near else None) for i, a in enumerate(args)))


def shape(dims, dtype=jnp.bfloat16):
    return jax.ShapeDtypeStruct(dims, dtype)


def group_rows(capacity):
    return round_up(ROWS * capacity, 8)


def slot_rows(capacity):
    return COLUMNS * group_rows(capacity)


def first_row(chip, capacity):
    return (chip % COLUMNS) * group_rows(capacity) + (chip // COLUMNS) * capacity


def dispatch_kernel(experts, *refs):
    far, outs, near, ready = refs[:6], refs[6 : 6 + CHIPS], refs[6 + CHIPS : -1], refs[-1]
    chip, core, _ = place()
    tokens, width = far[4].shape
    wide = width // CHIPS
    jobs = [(far[i], near[i]) for i in range(4)]
    for dk in range(CHIPS):
        for at in range(2):
            block = outs[dk].at[at * tokens : (at + 1) * tokens, :wide]
            jobs.append((far[4 + at].at[:, block_of(peer(chip, core, dk), wide)], block))
    copies = [pltpu.make_async_copy(*job, ready.at[i]) for i, job in enumerate(jobs)]
    for copy in copies:
        copy.start()
    for copy in copies[:4]:
        copy.wait()
    for at in range(2):
        route, gate = near[2 * at][...], near[2 * at + 1][...]
        topk = route.shape[0]
        earlier = (iota((tokens, tokens), 0) < iota((tokens, tokens), 1)).astype(jnp.float32)
        rank = jnp.zeros((topk, tokens), jnp.float32)
        for e in range(experts):
            named = (route == e).astype(jnp.float32)
            count = jnp.broadcast_to(jnp.sum(named, axis=0, keepdims=True), (8, tokens))
            rank = rank + named * dot(count, earlier)[:1]
        high = gate.astype(jnp.bfloat16).astype(jnp.float32)
        middle = (gate - high).astype(jnp.bfloat16).astype(jnp.float32)
        low = gate - high - middle
        table = jnp.zeros((128, tokens), jnp.float32)
        for part, value in enumerate((route.astype(jnp.float32), rank, high, middle, low)):
            for kk in range(topk):
                row = jnp.broadcast_to(value[kk : kk + 1], (128, tokens))
                table = jnp.where(iota((128, tokens), 0) == part * topk + kk, row, table)
        same = (iota((tokens, tokens), 0) == iota((tokens, tokens), 1)).astype(jnp.bfloat16)
        note = dot(same, table.astype(jnp.bfloat16), NT).astype(jnp.bfloat16)
        for dk in range(CHIPS):
            outs[dk][at * tokens : (at + 1) * tokens, wide:] = note
    for copy in copies[4:]:
        copy.wait()


def stash(experts, capacity, core, expert, saved, mine, theirs):
    rows = slot_rows(capacity)
    dims = (rows * experts, saved.shape[0])
    row, column = iota(dims, 0), iota(dims, 1)
    for target, ref in ((1 - core, theirs), (core, mine)):
        wanted = jnp.full(dims, -1, jnp.int32)
        for de in range(experts):
            for at in range(CHIPS):
                source = (at * CORES + target) * experts + lax.rem(expert + experts - de, experts)
                low = de * rows + first_row(at, capacity)
                inside = jnp.logical_and(row >= low, row < low + capacity)
                wanted = jnp.where(inside, row + (source * capacity - low), wanted)
        pick = jnp.where(column == wanted, 1.0, 0.0).astype(jnp.bfloat16)
        ref[...] = dot(pick, saved[...]).astype(jnp.bfloat16)


def dispatch(args, experts):
    tokens, wide = args[4].shape[0], args[4].shape[1] // CHIPS
    return call(
        functools.partial(dispatch_kernel, experts),
        [shape((2 * tokens, wide + 128)) for _ in range(CHIPS)],
        *args,
        scratch=[pltpu.VMEM(a.shape, a.dtype) for a in args[:4]] + [pltpu.SemaphoreType.DMA((4 + 2 * CHIPS,))],
        name="dispatch",
        far=range(6),
    )


def pick_kernel(shifts, experts, capacity, topk, *refs):
    blocks, outs = refs[:CHIPS], refs[CHIPS:]
    chip, core, expert = place()
    wide = outs[0].shape[1]
    rows = outs[0].shape[0] // 2
    tokens = blocks[0].shape[0] // 2
    lane = iota((CHIPS * tokens, rows), 1).astype(jnp.float32)
    for at in range(2):
        span = slice(at * tokens, (at + 1) * tokens)
        left = jnp.concatenate([b[span, :wide] for b in blocks], axis=0)
        notes = [b[span, wide:].astype(jnp.float32) for b in blocks]
        for out, de in zip(outs, shifts):
            here = lax.rem(expert + de, experts).astype(jnp.float32)
            choice = jnp.zeros((CHIPS * tokens, rows), jnp.float32)
            for kk in range(topk):
                targets = []
                for j, note in enumerate(notes):
                    route, rank = note[:, kk : kk + 1], note[:, topk + kk : topk + kk + 1]
                    first = first_row(peer(chip, core, j), capacity).astype(jnp.float32)
                    targets.append(jnp.where(route == here, rank + first, -1.0))
                choice += jnp.where(lane == jnp.concatenate(targets, axis=0), 1.0, 0.0)
            picked = dot(choice.astype(jnp.bfloat16), left, TN)
            out[at * rows : (at + 1) * rows] = picked.astype(jnp.bfloat16)


def pick(blocks, shifts, experts, capacity, topk, name):
    wide = blocks[0].shape[1] - 128
    outs = [shape((2 * slot_rows(capacity), wide)) for _ in shifts]
    kernel = functools.partial(pick_kernel, shifts, experts, capacity, topk)
    return call(kernel, outs, *blocks, name=name)


def hold_kernel(experts, capacity, gu, down, saved, gu_far, down_far, *refs):
    gu_near, down_near, gu_turned, down_turned, mine, theirs, near_saved, ready = refs
    _, core, expert = place()
    jobs = ((saved, near_saved), (gu, gu_near), (down, down_near))
    copies = [pltpu.make_async_copy(*job, ready.at[i]) for i, job in enumerate(jobs)]
    for copy in copies:
        copy.start()

    def turn(source, target, first):
        step = source.shape[0] // 8
        for i in range(8):
            span = slice(i * step, (i + 1) * step)
            target[first : first + source.shape[1], span] = source[span, :].T

    half = gu.shape[1]
    turn(gu_far, gu_turned, half)
    turn(down_far, down_turned, half)
    copies[0].wait()
    stash(experts, capacity, core, expert, near_saved, mine, theirs)
    copies[1].wait()
    turn(gu_near, gu_turned, 0)
    copies[2].wait()
    turn(down_near, down_turned, 0)


def hold(gu, down, saved, far, experts, capacity):
    stashed = shape((slot_rows(capacity) * experts, saved.shape[1]))
    turned = [shape((CORES * w.shape[1], w.shape[0])) for w in (gu, down)]
    results = call(
        functools.partial(hold_kernel, experts, capacity),
        [shape(gu.shape), shape(down.shape), *turned, stashed, stashed],
        gu,
        down,
        saved,
        *far,
        scratch=[pltpu.VMEM(saved.shape, saved.dtype), pltpu.SemaphoreType.DMA((3,))],
        name="hold",
        far=range(3),
        near=(3, 4),
    )
    return results[:2], results[2:4], results[4:]


def unit_rows(part, chip, units):
    return pl.ds(pl.multiple_of((part * CHIPS + chip) * units, units), units)


def up_kernel(experts, steps, *refs):
    blocks, turned, outs = refs[:experts], refs[experts : experts + 2], refs[experts + 2 :]
    chip, core, _ = place()
    half = turned[0].shape[0] // CORES
    units = turned[1].shape[1] // CHIPS
    rows = blocks[0].shape[0] // 2

    def left(at):
        sides = [
            jnp.concatenate([b[at * rows : (at + 1) * rows, block_of(side, half)] for b in blocks], axis=0)
            for side in (core, 1 - core)
        ]
        return jnp.concatenate(sides, axis=1)

    lefts = [left(at) for at in range(2)]
    for out, j in zip(outs, steps):
        for part in range(3):
            which, piece = divmod(part, 2)
            span = unit_rows(piece, peer(chip, core, j), units)
            out[:, part * units : (part + 1) * units] = dot(lefts[which], turned[which][:, span]).astype(out.dtype)


def up(blocks, turned, steps, dtype, name):
    experts = len(blocks)
    rows = blocks[0].shape[0] // 2 * experts
    width = (turned[0].shape[1] + turned[1].shape[1]) // CHIPS
    outs = [shape((rows, width), dtype) for _ in steps]
    flops = 2 * rows * width * turned[0].shape[0] * len(steps)
    return call(functools.partial(up_kernel, experts, steps), outs, *blocks, *turned, flops=flops, name=name)


def act_kernel(*refs):
    parts, (mine, theirs, out) = refs[:CHIPS], refs[CHIPS:]
    _, core, _ = place()
    total = parts[0][...]
    for part in parts[1:]:
        total = total + part[...].astype(jnp.float32)
    units = total.shape[1] // 3
    gate_pre, up_pre, hidden_grad = total[:, :units], total[:, units : 2 * units], total[:, 2 * units :]
    out[:, :units] = (gate_pre * jax.nn.sigmoid(gate_pre) * up_pre).astype(jnp.bfloat16)
    half = units // CORES
    own, other = mine[...].astype(jnp.float32), theirs[...].astype(jnp.float32)
    low, high = jnp.where(core == 0, own, other), jnp.where(core == 0, other, own)
    for at, saved in enumerate((low, high)):
        gate_pre, up_pre = saved[:, :half], saved[:, half:]
        sig = jax.nn.sigmoid(gate_pre)
        grad = hidden_grad[:, at * half : (at + 1) * half]
        first = units + at * half
        out[:, first : first + half] = (grad * up_pre * (sig * (1.0 + gate_pre * (1.0 - sig)))).astype(jnp.bfloat16)
        out[:, first + units : first + units + half] = (grad * (gate_pre * sig)).astype(jnp.bfloat16)


def act(parts, mine, theirs):
    return call(act_kernel, shape(parts[0].shape), *parts, mine, theirs, name="act")


def down_kernel(experts, *refs):
    parts, near, far, outs = refs[:CHIPS], refs[CHIPS : CHIPS + 2], refs[CHIPS + 2 : CHIPS + 4], refs[CHIPS + 4 :]
    chip, core, _ = place()
    half = near[0].shape[1]
    units = near[1].shape[0] // CHIPS
    rows = parts[0].shape[0] // experts
    group = rows // COLUMNS
    low = chip % COLUMNS == 0
    for side, column in ((0, core), (1, 1 - core)):
        totals = []
        for which, terms in ((1, ((0, 0),)), (0, ((1, 0), (2, 1)))):
            weight = (near, far)[side][which]
            total = None
            for j in range(CHIPS):
                for piece, part in terms:
                    left = parts[j][:, piece * units : (piece + 1) * units]
                    term = dot(left, weight[unit_rows(part, peer(chip, core, j), units), :])
                    total = term if total is None else total + term
            totals.append(total)
        for de in range(experts):
            first = de * rows
            lower = jnp.concatenate([t[first : first + group] for t in totals], axis=0).astype(jnp.bfloat16)
            upper = jnp.concatenate([t[first + group : first + rows] for t in totals], axis=0).astype(jnp.bfloat16)
            outs[de][:, block_of(column, half)] = jnp.where(low, lower, upper)
            outs[experts + de][:, block_of(column, half)] = jnp.where(low, upper, lower)


def down(parts, near, far, experts):
    rows = parts[0].shape[0] // experts
    outs = [shape((2 * rows // COLUMNS, CORES * near[0].shape[1])) for _ in range(COLUMNS * experts)]
    flops = 4 * parts[0].shape[0] * (near[0].size + near[1].size)
    kernel = functools.partial(down_kernel, experts)
    return call(kernel, outs, *parts, *near, *far, flops=flops, name="down", near=(CHIPS + 2, CHIPS + 3))


def combine_kernel(experts, capacity, topk, *refs):
    blocks, results, outs = refs[:CHIPS], refs[CHIPS : CHIPS + COLUMNS * experts], refs[CHIPS + COLUMNS * experts :]
    chip, core, expert = place()
    group, wide = results[0].shape[0] // 2, results[0].shape[1]
    tokens = outs[0].shape[0] // 2
    lane = iota((2 * ROWS * tokens, 2 * group), 1).astype(jnp.float32)
    own = blocks[0][:, wide:].astype(jnp.float32)
    other = jnp.where(core == 0, blocks[2][:, wide:].astype(jnp.float32), blocks[1][:, wide:].astype(jnp.float32))
    notes, firsts = [], []
    for dz, note in enumerate((own, other)):
        for at in range(2):
            notes.append(note[at * tokens : (at + 1) * tokens])
            firsts.append((((chip // COLUMNS) ^ dz) * capacity + at * group).astype(jnp.float32))
    for dy in range(COLUMNS):
        total = None
        for kk in range(topk):
            found = None
            for de in range(experts):
                here = lax.rem(expert + de, experts).astype(jnp.float32)
                targets = []
                for note, first in zip(notes, firsts):
                    route, rank = note[:, kk : kk + 1], note[:, topk + kk : topk + kk + 1]
                    targets.append(jnp.where(route == here, rank + first, -1.0))
                choice = jnp.where(lane == jnp.concatenate(targets, axis=0), 1.0, 0.0).astype(jnp.bfloat16)
                term = dot(choice, results[dy * experts + de][...])
                found = term if found is None else found + term
            gates = []
            for note in notes:
                terms = [note[:, part * topk + kk : part * topk + kk + 1] for part in (2, 3, 4)]
                gates.append(terms[0] + terms[1] + terms[2])
            term = found * jnp.concatenate(gates, axis=0)
            total = term if total is None else total + term
        total = total.astype(jnp.bfloat16)
        for dz in range(ROWS):
            span = slice(dz * 2 * tokens, (dz + 1) * 2 * tokens)
            outs[dz][:, block_of((chip % COLUMNS) ^ dy, wide)] = total[span]


def combine(blocks, results, capacity, topk):
    experts = len(results) // COLUMNS
    outs = [shape((blocks[0].shape[0], COLUMNS * results[0].shape[1])) for _ in range(ROWS)]
    kernel = functools.partial(combine_kernel, experts, capacity, topk)
    return call(kernel, outs, *blocks, *results, name="combine")


def join_kernel(*refs):
    chip, _, _ = place()
    blocks, outs = refs[:-2], refs[-2:]
    tokens = outs[0].shape[0]
    for at, out in enumerate(outs):
        for dz in range(ROWS):
            block = blocks[dz + at * (len(blocks) - ROWS)]
            first = at * tokens if len(blocks) == ROWS else 0
            out[:, block_of((chip // COLUMNS) ^ dz, block.shape[1])] = block[first : first + tokens]


def join(blocks, tokens):
    out = shape((tokens, ROWS * blocks[0].shape[1]))
    return call(join_kernel, [out, out], *blocks, name="join")


def on_device(
    forward_input,
    forward_route,
    forward_gates,
    backward_cotangent,
    backward_route,
    backward_gates,
    gate_up_weight,
    down_weight,
    saved_projections,
):
    sections = lax.axis_size("section")
    experts = lax.axis_size("expert")
    topk = forward_route.shape[2]
    capacity = saved_projections.shape[2] // (GROUP * experts)
    tokens = forward_route.shape[1]

    def to_chip(value, j):
        places = [(k, c) for k in range(CHIPS) for c in range(CORES)]
        pairs = [(k * CORES + c, peer(k, c, j) * CORES + c) for k, c in places]
        return lax.ppermute(value, ("chip", "core"), pairs)

    def to_section(value, dz, by):
        places = [(i, k) for i in range(sections) for k in range(CHIPS)]
        pairs = [(i * CHIPS + k, (i + by) % sections * CHIPS + (k ^ (dz * COLUMNS))) for i, k in places]
        return lax.ppermute(value, ("section", "chip"), pairs)

    def to_expert(block, de):
        if de == 0:
            return block
        return lax.ppermute(block, "expert", [(i, (i + de) % experts) for i in range(experts)])

    def to_core(value):
        return lax.ppermute(value, "core", [(i, i ^ 1) for i in range(CORES)])

    def returned(block, dy, de):
        if dy == 0 and de == 0:
            return block
        places = [(k, e) for k in range(CHIPS) for e in range(experts)]
        pairs = [(k * experts + (e + de) % experts, (k ^ dy) * experts + e) for k, e in places]
        return lax.ppermute(block, ("chip", "expert"), pairs)

    def to_chips(blocks):
        return [blocks[0]] + [to_chip(blocks[dk], dk) for dk in range(1, CHIPS)]

    args = [a[0].T for a in (forward_route, forward_gates, backward_route, backward_gates)]
    gu, down_rows, saved = gate_up_weight[0, 0], down_weight[0, 0], saved_projections[0, 0]
    far = [to_core(gu), to_core(down_rows)]
    tokens_here = to_chips(dispatch(args + [forward_input[0], backward_cotangent[0]], experts))
    others = pick(tokens_here, (*range(1, experts),), experts, capacity, topk, "pick_others")
    rows_here = [to_expert(others[de - 1], de) for de in range(1, experts)]
    rows_here = [*pick(tokens_here, (0,), experts, capacity, topk, "pick_own"), *rows_here]
    near, turned, (mine, theirs) = hold(gu, down_rows, saved, far, experts, capacity)
    parts = [to_chip(part, j) for j, part in enumerate(up(rows_here, turned, ORDER[:-1], jnp.bfloat16, "up_others"), 1)]
    parts = [*up(rows_here, turned, (0,), jnp.float32, "up_own"), *parts]
    units = act(parts, mine, to_core(theirs))
    results = down(to_chips([units] * CHIPS), near, far, experts)
    results = [returned(results[dy * experts + de], dy, de) for dy in range(COLUMNS) for de in range(experts)]
    outs = combine(tokens_here, results, capacity, topk)
    if sections == 2:
        joined = [to_section(outs[dz], dz, 1) for dz in range(ROWS)]
    else:
        joined = [to_section(outs[dz][:tokens], dz, 1) for dz in range(ROWS)]
        joined += [to_section(outs[dz][tokens:], dz, -1) for dz in range(ROWS)]
    next_input, prior_gradient = join(joined, tokens)
    return next_input[None], prior_gradient[None]


def solution(mesh):
    pipes, experts = mesh.devices.shape
    axes = ("section", "chip", "core", "expert")
    mesh = Mesh(mesh.devices.reshape(pipes // GROUP, CHIPS, CORES, experts), axes)
    rows = P(axes[:3], "expert", None)
    weights = P(axes[:3], "expert", None, None)
    return jax.shard_map(
        on_device,
        mesh=mesh,
        in_specs=(rows,) * 6 + (weights,) * 3,
        out_specs=(rows, rows),
        check_vma=False,
    )
```

```python
import functools

import jax
import jax.numpy as jnp
from jax import lax
from jax.experimental import pallas as pl
from jax.experimental.pallas import tpu as pltpu
from jax.sharding import Mesh
from jax.sharding import PartitionSpec as P

GROUP = 8
CORES = 2
CHIPS = GROUP // CORES
COLUMNS = 2
ROWS = CHIPS // COLUMNS
ORDER = (*range(1, CHIPS), 0)
TILE = 16
NT = (((1,), (1,)), ((), ()))
NN = (((1,), (0,)), ((), ()))
TN = (((0,), (0,)), ((), ()))


def round_up(value, step):
    return (value + step - 1) // step * step


def dot(a, b, dims=NN):
    return lax.dot_general(a, b, dims, preferred_element_type=jnp.float32)


def iota(shape, axis):
    return lax.broadcasted_iota(jnp.int32, shape, axis)


def place():
    return lax.axis_index("chip"), lax.axis_index("core"), lax.axis_index("expert")


def peer(chip, core, j):
    far = CHIPS - 1
    if j in (0, 1):
        return chip ^ (far * j)
    if isinstance(core, int):
        return chip ^ (far - j + 1 if core == 1 else j - 1)
    return chip ^ jnp.where(core == 1, far - j + 1, j - 1)


def block_of(index, size):
    return pl.ds(pl.multiple_of(index * size, size), size)


def pinned(array, memory):
    return array if memory is None else pltpu.with_memory_space_constraint(array, memory)


def call(kernel, outs, *args, scratch=(), flops=0, name=None, far=(), near=()):
    size = sum(a.size * a.dtype.itemsize for a in args)
    size += sum(o.size * o.dtype.itemsize for o in jax.tree.leaves(outs))
    spec = pl.BlockSpec(memory_space=pltpu.VMEM)
    return pl.pallas_call(
        kernel,
        out_shape=outs,
        in_specs=[pl.BlockSpec(memory_space=pl.ANY) if i in far else spec for i in range(len(args))],
        out_specs=jax.tree.map(lambda _: spec, outs),
        scratch_shapes=scratch,
        compiler_params=pltpu.CompilerParams(vmem_limit_bytes=16 * 2**20),
        cost_estimate=pl.CostEstimate(flops=flops, bytes_accessed=size, transcendentals=0),
        name=name,
    )(*(pinned(a, pltpu.HBM if i in far else pltpu.VMEM if i in near else None) for i, a in enumerate(args)))


def shape(dims, dtype=jnp.bfloat16):
    return jax.ShapeDtypeStruct(dims, dtype)


def group_rows(capacity):
    return round_up(ROWS * capacity, 8)


def slot_rows(capacity):
    return COLUMNS * group_rows(capacity)


def first_row(chip, capacity):
    return (chip % COLUMNS) * group_rows(capacity) + (chip // COLUMNS) * capacity


def dispatch_kernel(experts, *refs):
    far, outs, near, ready = refs[:6], refs[6 : 6 + CHIPS], refs[6 + CHIPS : -1], refs[-1]
    chip, core, _ = place()
    tokens, width = far[4].shape
    wide = width // CHIPS
    jobs = [(far[i], near[i]) for i in range(4)]
    for dk in range(CHIPS):
        for at in range(2):
            block = outs[dk].at[at * tokens : (at + 1) * tokens, :wide]
            jobs.append((far[4 + at].at[:, block_of(peer(chip, core, dk), wide)], block))
    copies = [pltpu.make_async_copy(*job, ready.at[i]) for i, job in enumerate(jobs)]
    for copy in copies:
        copy.start()
    for copy in copies[:4]:
        copy.wait()
    for at in range(2):
        route, gate = near[2 * at][...], near[2 * at + 1][...]
        topk = route.shape[0]
        earlier = (iota((tokens, tokens), 0) < iota((tokens, tokens), 1)).astype(jnp.float32)
        rank = jnp.zeros((topk, tokens), jnp.float32)
        for e in range(experts):
            named = (route == e).astype(jnp.float32)
            count = jnp.broadcast_to(jnp.sum(named, axis=0, keepdims=True), (8, tokens))
            rank = rank + named * dot(count, earlier)[:1]
        high = gate.astype(jnp.bfloat16).astype(jnp.float32)
        middle = (gate - high).astype(jnp.bfloat16).astype(jnp.float32)
        low = gate - high - middle
        table = jnp.zeros((128, tokens), jnp.float32)
        for part, value in enumerate((route.astype(jnp.float32), rank, high, middle, low)):
            for kk in range(topk):
                row = jnp.broadcast_to(value[kk : kk + 1], (128, tokens))
                table = jnp.where(iota((128, tokens), 0) == part * topk + kk, row, table)
        same = (iota((tokens, tokens), 0) == iota((tokens, tokens), 1)).astype(jnp.bfloat16)
        note = dot(same, table.astype(jnp.bfloat16), NT).astype(jnp.bfloat16)
        for dk in range(CHIPS):
            outs[dk][at * tokens : (at + 1) * tokens, wide:] = note
    for copy in copies[4:]:
        copy.wait()


def stash(experts, capacity, core, expert, saved, mine, theirs):
    rows = slot_rows(capacity)
    dims = (rows * experts, saved.shape[0])
    row, column = iota(dims, 0), iota(dims, 1)
    for target, ref in ((1 - core, theirs), (core, mine)):
        wanted = jnp.full(dims, -1, jnp.int32)
        for de in range(experts):
            for at in range(CHIPS):
                source = (at * CORES + target) * experts + lax.rem(expert + experts - de, experts)
                low = de * rows + first_row(at, capacity)
                inside = jnp.logical_and(row >= low, row < low + capacity)
                wanted = jnp.where(inside, row + (source * capacity - low), wanted)
        pick = jnp.where(column == wanted, 1.0, 0.0).astype(jnp.bfloat16)
        ref[...] = dot(pick, saved[...]).astype(jnp.bfloat16)


def dispatch(args, experts):
    tokens, wide = args[4].shape[0], args[4].shape[1] // CHIPS
    return call(
        functools.partial(dispatch_kernel, experts),
        [shape((2 * tokens, wide + 128)) for _ in range(CHIPS)],
        *args,
        scratch=[pltpu.VMEM(a.shape, a.dtype) for a in args[:4]] + [pltpu.SemaphoreType.DMA((4 + 2 * CHIPS,))],
        name="dispatch",
        far=range(6),
    )


def pick_kernel(shifts, experts, capacity, topk, *refs):
    blocks, outs = refs[:CHIPS], refs[CHIPS:]
    chip, core, expert = place()
    wide = outs[0].shape[1]
    rows = outs[0].shape[0] // 2
    tokens = blocks[0].shape[0] // 2
    lane = iota((CHIPS * tokens, rows), 1).astype(jnp.float32)
    for at in range(2):
        span = slice(at * tokens, (at + 1) * tokens)
        left = jnp.concatenate([b[span, :wide] for b in blocks], axis=0)
        notes = [b[span, wide:].astype(jnp.float32) for b in blocks]
        for out, de in zip(outs, shifts):
            here = lax.rem(expert + de, experts).astype(jnp.float32)
            choice = jnp.zeros((CHIPS * tokens, rows), jnp.float32)
            for kk in range(topk):
                targets = []
                for j, note in enumerate(notes):
                    route, rank = note[:, kk : kk + 1], note[:, topk + kk : topk + kk + 1]
                    first = first_row(peer(chip, core, j), capacity).astype(jnp.float32)
                    targets.append(jnp.where(route == here, rank + first, -1.0))
                choice += jnp.where(lane == jnp.concatenate(targets, axis=0), 1.0, 0.0)
            picked = dot(choice.astype(jnp.bfloat16), left, TN)
            out[at * rows : (at + 1) * rows] = picked.astype(jnp.bfloat16)


def pick(blocks, shifts, experts, capacity, topk, name):
    wide = blocks[0].shape[1] - 128
    outs = [shape((2 * slot_rows(capacity), wide)) for _ in shifts]
    kernel = functools.partial(pick_kernel, shifts, experts, capacity, topk)
    return call(kernel, outs, *blocks, name=name)


def hold_kernel(experts, capacity, gu, down, saved, gu_far, down_far, *refs):
    gu_near, down_near, gu_turned, down_turned, mine, theirs, near_saved, ready = refs
    _, core, expert = place()
    jobs = ((saved, near_saved), (gu, gu_near), (down, down_near))
    copies = [pltpu.make_async_copy(*job, ready.at[i]) for i, job in enumerate(jobs)]
    for copy in copies:
        copy.start()

    def turn(source, target, first):
        step = source.shape[0] // 8
        for i in range(8):
            span = slice(i * step, (i + 1) * step)
            target[first : first + source.shape[1], span] = source[span, :].T

    half = gu.shape[1]
    turn(gu_far, gu_turned, half)
    turn(down_far, down_turned, half)
    copies[0].wait()
    stash(experts, capacity, core, expert, near_saved, mine, theirs)
    copies[1].wait()
    turn(gu_near, gu_turned, 0)
    copies[2].wait()
    turn(down_near, down_turned, 0)


def hold(gu, down, saved, far, experts, capacity):
    stashed = shape((slot_rows(capacity) * experts, saved.shape[1]))
    turned = [shape((CORES * w.shape[1], w.shape[0])) for w in (gu, down)]
    results = call(
        functools.partial(hold_kernel, experts, capacity),
        [shape(gu.shape), shape(down.shape), *turned, stashed, stashed],
        gu,
        down,
        saved,
        *far,
        scratch=[pltpu.VMEM(saved.shape, saved.dtype), pltpu.SemaphoreType.DMA((3,))],
        name="hold",
        far=range(3),
        near=(3, 4),
    )
    return results[:2], results[2:4], results[4:]


def unit_rows(part, chip, units):
    return pl.ds(pl.multiple_of((part * CHIPS + chip) * units, units), units)


def up_kernel(experts, steps, *refs):
    blocks, turned, outs = refs[:experts], refs[experts : experts + 2], refs[experts + 2 :]
    chip, core, _ = place()
    half = turned[0].shape[0] // CORES
    units = turned[1].shape[1] // CHIPS
    rows = blocks[0].shape[0] // 2

    def left(at):
        sides = [
            jnp.concatenate([b[at * rows : (at + 1) * rows, block_of(side, half)] for b in blocks], axis=0)
            for side in (core, 1 - core)
        ]
        return jnp.concatenate(sides, axis=1)

    lefts = [left(at) for at in range(2)]
    for out, j in zip(outs, steps):
        for part in range(3):
            which, piece = divmod(part, 2)
            span = unit_rows(piece, peer(chip, core, j), units)
            out[:, part * units : (part + 1) * units] = dot(lefts[which], turned[which][:, span]).astype(out.dtype)


def up(blocks, turned, steps, dtype, name):
    experts = len(blocks)
    rows = blocks[0].shape[0] // 2 * experts
    width = (turned[0].shape[1] + turned[1].shape[1]) // CHIPS
    outs = [shape((rows, width), dtype) for _ in steps]
    flops = 2 * rows * width * turned[0].shape[0] * len(steps)
    return call(functools.partial(up_kernel, experts, steps), outs, *blocks, *turned, flops=flops, name=name)


def act_kernel(*refs):
    parts, (mine, theirs, out) = refs[:CHIPS], refs[CHIPS:]
    _, core, _ = place()
    total = parts[0][...]
    for part in parts[1:]:
        total = total + part[...].astype(jnp.float32)
    units = total.shape[1] // 3
    gate_pre, up_pre, hidden_grad = total[:, :units], total[:, units : 2 * units], total[:, 2 * units :]
    out[:, :units] = (gate_pre * jax.nn.sigmoid(gate_pre) * up_pre).astype(jnp.bfloat16)
    half = units // CORES
    own, other = mine[...].astype(jnp.float32), theirs[...].astype(jnp.float32)
    low, high = jnp.where(core == 0, own, other), jnp.where(core == 0, other, own)
    for at, saved in enumerate((low, high)):
        gate_pre, up_pre = saved[:, :half], saved[:, half:]
        sig = jax.nn.sigmoid(gate_pre)
        grad = hidden_grad[:, at * half : (at + 1) * half]
        first = units + at * half
        out[:, first : first + half] = (grad * up_pre * (sig * (1.0 + gate_pre * (1.0 - sig)))).astype(jnp.bfloat16)
        out[:, first + units : first + units + half] = (grad * (gate_pre * sig)).astype(jnp.bfloat16)


def act(parts, mine, theirs):
    return call(act_kernel, shape(parts[0].shape), *parts, mine, theirs, name="act")


def down_kernel(experts, *refs):
    parts, near, far = refs[:CHIPS][::-1], refs[CHIPS : CHIPS + 2], refs[CHIPS + 2 : CHIPS + 4]
    outs = refs[CHIPS + 4 :][::-1]
    chip, core, _ = place()
    half = near[0].shape[1]
    units = near[1].shape[0] // CHIPS
    rows = parts[0].shape[0] // experts
    group = rows // COLUMNS
    low = chip % COLUMNS == 0
    for side, column in ((0, core), (1, 1 - core)):
        totals = []
        for which, terms in ((1, ((0, 0),)), (0, ((1, 0), (2, 1)))):
            weight = (near, far)[side][which]
            total = None
            for j in range(CHIPS):
                for piece, part in terms:
                    left = parts[j][:, piece * units : (piece + 1) * units]
                    term = dot(left, weight[unit_rows(part, peer(chip, core, j), units), :])
                    total = term if total is None else total + term
            totals.append(total)
        for de in range(experts):
            first = de * rows
            lower = jnp.concatenate([t[first : first + group] for t in totals], axis=0).astype(jnp.bfloat16)
            upper = jnp.concatenate([t[first + group : first + rows] for t in totals], axis=0).astype(jnp.bfloat16)
            outs[de][:, block_of(column, half)] = jnp.where(low, lower, upper)
            outs[experts + de][:, block_of(column, half)] = jnp.where(low, upper, lower)


def down(parts, near, far, experts):
    rows = parts[0].shape[0] // experts
    outs = [shape((2 * rows // COLUMNS, CORES * near[0].shape[1])) for _ in range(COLUMNS * experts)]
    flops = 4 * parts[0].shape[0] * (near[0].size + near[1].size)
    kernel = functools.partial(down_kernel, experts)
    return call(kernel, outs, *parts[::-1], *near, *far, flops=flops, name="down", near=(CHIPS + 2, CHIPS + 3))


def combine_kernel(experts, capacity, topk, *refs):
    blocks, results, outs = refs[:CHIPS], refs[CHIPS : CHIPS + COLUMNS * experts], refs[CHIPS + COLUMNS * experts :]
    results = results[::-1]
    chip, core, expert = place()
    group, wide = results[0].shape[0] // 2, results[0].shape[1]
    tokens = outs[0].shape[0] // 2
    lane = iota((2 * ROWS * tokens, 2 * group), 1).astype(jnp.float32)
    own = blocks[0][:, wide:].astype(jnp.float32)
    other = jnp.where(core == 0, blocks[3][:, wide:].astype(jnp.float32), blocks[2][:, wide:].astype(jnp.float32))
    notes, firsts = [], []
    for dz, note in enumerate((own, other)):
        for at in range(2):
            notes.append(note[at * tokens : (at + 1) * tokens])
            firsts.append((((chip // COLUMNS) ^ dz) * capacity + at * group).astype(jnp.float32))
    for dy in range(COLUMNS):
        total = None
        for kk in range(topk):
            found = None
            for de in range(experts):
                here = lax.rem(expert + de, experts).astype(jnp.float32)
                targets = []
                for note, first in zip(notes, firsts):
                    route, rank = note[:, kk : kk + 1], note[:, topk + kk : topk + kk + 1]
                    targets.append(jnp.where(route == here, rank + first, -1.0))
                choice = jnp.where(lane == jnp.concatenate(targets, axis=0), 1.0, 0.0).astype(jnp.bfloat16)
                term = dot(choice, results[dy * experts + de][...])
                found = term if found is None else found + term
            gates = []
            for note in notes:
                terms = [note[:, part * topk + kk : part * topk + kk + 1] for part in (2, 3, 4)]
                gates.append(terms[0] + terms[1] + terms[2])
            term = found * jnp.concatenate(gates, axis=0)
            total = term if total is None else total + term
        total = total.astype(jnp.bfloat16)
        for dz in range(ROWS):
            span = slice(dz * 2 * tokens, (dz + 1) * 2 * tokens)
            outs[dz][:, block_of((chip % COLUMNS) ^ dy, wide)] = total[span]


def combine(blocks, results, capacity, topk):
    experts = len(results) // COLUMNS
    outs = [shape((blocks[0].shape[0], COLUMNS * results[0].shape[1])) for _ in range(ROWS)]
    kernel = functools.partial(combine_kernel, experts, capacity, topk)
    return call(kernel, outs, *blocks, *results, name="combine")


def join_kernel(*refs):
    chip, _, _ = place()
    blocks, outs = refs[:-2], refs[-2:]
    tokens = outs[0].shape[0]
    for at, out in enumerate(outs):
        for dz in range(ROWS):
            block = blocks[dz + at * (len(blocks) - ROWS)]
            first = at * tokens if len(blocks) == ROWS else 0
            out[:, block_of((chip // COLUMNS) ^ dz, block.shape[1])] = block[first : first + tokens]


def join(blocks, tokens):
    out = shape((tokens, ROWS * blocks[0].shape[1]))
    return call(join_kernel, [out, out], *blocks, name="join")


def on_device(
    forward_input,
    forward_route,
    forward_gates,
    backward_cotangent,
    backward_route,
    backward_gates,
    gate_up_weight,
    down_weight,
    saved_projections,
):
    sections = lax.axis_size("section")
    experts = lax.axis_size("expert")
    topk = forward_route.shape[2]
    capacity = saved_projections.shape[2] // (GROUP * experts)
    tokens = forward_route.shape[1]

    def to_chip(value, j):
        places = [(k, c) for k in range(CHIPS) for c in range(CORES)]
        pairs = [(k * CORES + c, peer(k, c, j) * CORES + c) for k, c in places]
        return lax.ppermute(value, ("chip", "core"), pairs)

    def to_section(value, dz, by):
        places = [(i, k) for i in range(sections) for k in range(CHIPS)]
        pairs = [(i * CHIPS + k, (i + by) % sections * CHIPS + (k ^ (dz * COLUMNS))) for i, k in places]
        return lax.ppermute(value, ("section", "chip"), pairs)

    def to_expert(block, de):
        if de == 0:
            return block
        return lax.ppermute(block, "expert", [(i, (i + de) % experts) for i in range(experts)])

    def to_core(value):
        return lax.ppermute(value, "core", [(i, i ^ 1) for i in range(CORES)])

    def returned(block, dy, de):
        if dy == 0 and de == 0:
            return block
        places = [(k, e) for k in range(CHIPS) for e in range(experts)]
        pairs = [(k * experts + (e + de) % experts, (k ^ dy) * experts + e) for k, e in places]
        return lax.ppermute(block, ("chip", "expert"), pairs)

    def to_chips(blocks):
        return [blocks[0]] + [to_chip(blocks[dk], dk) for dk in range(1, CHIPS)]

    args = [a[0].T for a in (forward_route, forward_gates, backward_route, backward_gates)]
    gu, down_rows, saved = gate_up_weight[0, 0], down_weight[0, 0], saved_projections[0, 0]
    far = [to_core(gu), to_core(down_rows)]
    tokens_here = to_chips(dispatch(args + [forward_input[0], backward_cotangent[0]], experts))
    others = pick(tokens_here, (*range(1, experts),), experts, capacity, topk, "pick_others")
    rows_here = [to_expert(others[de - 1], de) for de in range(1, experts)]
    rows_here = [*pick(tokens_here, (0,), experts, capacity, topk, "pick_own"), *rows_here]
    near, turned, (mine, theirs) = hold(gu, down_rows, saved, far, experts, capacity)
    parts = [to_chip(part, j) for j, part in enumerate(up(rows_here, turned, ORDER[:-1], jnp.bfloat16, "up_others"), 1)]
    parts = [*up(rows_here, turned, (0,), jnp.float32, "up_own"), *parts]
    units = act(parts, mine, to_core(theirs))
    results = down(to_chips([units] * CHIPS), near, far, experts)
    steps = [(dy, de) for dy in range(COLUMNS) for de in range(experts)][::-1]
    results = [returned(result, *step) for result, step in zip(results, steps)]
    outs = combine(tokens_here, results, capacity, topk)
    if sections == 2:
        joined = [to_section(outs[dz], dz, 1) for dz in range(ROWS)]
    else:
        joined = [to_section(outs[dz][:tokens], dz, 1) for dz in range(ROWS)]
        joined += [to_section(outs[dz][tokens:], dz, -1) for dz in range(ROWS)]
    next_input, prior_gradient = join(joined, tokens)
    return next_input[None], prior_gradient[None]


def solution(mesh):
    pipes, experts = mesh.devices.shape
    axes = ("section", "chip", "core", "expert")
    mesh = Mesh(mesh.devices.reshape(pipes // GROUP, CHIPS, CORES, experts), axes)
    rows = P(axes[:3], "expert", None)
    weights = P(axes[:3], "expert", None, None)
    return jax.shard_map(
        on_device,
        mesh=mesh,
        in_specs=(rows,) * 6 + (weights,) * 3,
        out_specs=(rows, rows),
        check_vma=False,
    )
```

```python
import functools

import jax
import jax.numpy as jnp
from jax import lax
from jax.experimental import pallas as pl
from jax.experimental.pallas import tpu as pltpu
from jax.sharding import Mesh
from jax.sharding import PartitionSpec as P

GROUP = 8
CORES = 2
CHIPS = GROUP // CORES
COLUMNS = 2
ROWS = CHIPS // COLUMNS
ORDER = (*range(1, CHIPS), 0)
TILE = 16
NT = (((1,), (1,)), ((), ()))
NN = (((1,), (0,)), ((), ()))
TN = (((0,), (0,)), ((), ()))


def round_up(value, step):
    return (value + step - 1) // step * step


def dot(a, b, dims=NN):
    return lax.dot_general(a, b, dims, preferred_element_type=jnp.float32)


def iota(shape, axis):
    return lax.broadcasted_iota(jnp.int32, shape, axis)


def place():
    return lax.axis_index("chip"), lax.axis_index("core"), lax.axis_index("expert")


def peer(chip, core, j):
    if isinstance(core, int):
        return chip ^ (CHIPS - 1 - j if core == 1 and 0 < j < CHIPS - 1 else j)
    return chip ^ (jnp.where(core == 1, CHIPS - 1 - j, j) if 0 < j < CHIPS - 1 else j)


def block_of(index, size):
    return pl.ds(pl.multiple_of(index * size, size), size)


def pinned(array, memory):
    return array if memory is None else pltpu.with_memory_space_constraint(array, memory)


def call(kernel, outs, *args, scratch=(), flops=0, name=None, far=(), near=()):
    size = sum(a.size * a.dtype.itemsize for a in args)
    size += sum(o.size * o.dtype.itemsize for o in jax.tree.leaves(outs))
    spec = pl.BlockSpec(memory_space=pltpu.VMEM)
    return pl.pallas_call(
        kernel,
        out_shape=outs,
        in_specs=[pl.BlockSpec(memory_space=pl.ANY) if i in far else spec for i in range(len(args))],
        out_specs=jax.tree.map(lambda _: spec, outs),
        scratch_shapes=scratch,
        compiler_params=pltpu.CompilerParams(vmem_limit_bytes=16 * 2**20),
        cost_estimate=pl.CostEstimate(flops=flops, bytes_accessed=size, transcendentals=0),
        name=name,
    )(*(pinned(a, pltpu.HBM if i in far else pltpu.VMEM if i in near else None) for i, a in enumerate(args)))


def shape(dims, dtype=jnp.bfloat16):
    return jax.ShapeDtypeStruct(dims, dtype)


def group_rows(capacity):
    return round_up(ROWS * capacity, 8)


def slot_rows(capacity):
    return COLUMNS * group_rows(capacity)


def first_row(chip, capacity):
    return (chip % COLUMNS) * group_rows(capacity) + (chip // COLUMNS) * capacity


def dispatch_kernel(experts, *refs):
    far, outs, near, ready = refs[:6], refs[6 : 6 + CHIPS], refs[6 + CHIPS : -1], refs[-1]
    chip, core, _ = place()
    tokens, width = far[4].shape
    wide = width // CHIPS
    jobs = [(far[i], near[i]) for i in range(4)]
    for dk in range(CHIPS):
        for at in range(2):
            block = outs[dk].at[at * tokens : (at + 1) * tokens, :wide]
            jobs.append((far[4 + at].at[:, block_of(peer(chip, core, dk), wide)], block))
    copies = [pltpu.make_async_copy(*job, ready.at[i]) for i, job in enumerate(jobs)]
    for copy in copies:
        copy.start()
    for copy in copies[:4]:
        copy.wait()
    for at in range(2):
        route, gate = near[2 * at][...], near[2 * at + 1][...]
        topk = route.shape[0]
        earlier = (iota((tokens, tokens), 0) < iota((tokens, tokens), 1)).astype(jnp.float32)
        rank = jnp.zeros((topk, tokens), jnp.float32)
        for e in range(experts):
            named = (route == e).astype(jnp.float32)
            count = jnp.broadcast_to(jnp.sum(named, axis=0, keepdims=True), (8, tokens))
            rank = rank + named * dot(count, earlier)[:1]
        high = gate.astype(jnp.bfloat16).astype(jnp.float32)
        middle = (gate - high).astype(jnp.bfloat16).astype(jnp.float32)
        low = gate - high - middle
        table = jnp.zeros((128, tokens), jnp.float32)
        for part, value in enumerate((route.astype(jnp.float32), rank, high, middle, low)):
            for kk in range(topk):
                row = jnp.broadcast_to(value[kk : kk + 1], (128, tokens))
                table = jnp.where(iota((128, tokens), 0) == part * topk + kk, row, table)
        same = (iota((tokens, tokens), 0) == iota((tokens, tokens), 1)).astype(jnp.bfloat16)
        note = dot(same, table.astype(jnp.bfloat16), NT).astype(jnp.bfloat16)
        for dk in range(CHIPS):
            outs[dk][at * tokens : (at + 1) * tokens, wide:] = note
    for copy in copies[4:]:
        copy.wait()


def stash(experts, capacity, core, expert, saved, mine, theirs):
    rows = slot_rows(capacity)
    dims = (rows * experts, saved.shape[0])
    row, column = iota(dims, 0), iota(dims, 1)
    for target, ref in ((1 - core, theirs), (core, mine)):
        wanted = jnp.full(dims, -1, jnp.int32)
        for de in range(experts):
            for at in range(CHIPS):
                source = (at * CORES + target) * experts + lax.rem(expert + experts - de, experts)
                low = de * rows + first_row(at, capacity)
                inside = jnp.logical_and(row >= low, row < low + capacity)
                wanted = jnp.where(inside, row + (source * capacity - low), wanted)
        pick = jnp.where(column == wanted, 1.0, 0.0).astype(jnp.bfloat16)
        ref[...] = dot(pick, saved[...]).astype(jnp.bfloat16)


def dispatch(args, experts):
    tokens, wide = args[4].shape[0], args[4].shape[1] // CHIPS
    return call(
        functools.partial(dispatch_kernel, experts),
        [shape((2 * tokens, wide + 128)) for _ in range(CHIPS)],
        *args,
        scratch=[pltpu.VMEM(a.shape, a.dtype) for a in args[:4]] + [pltpu.SemaphoreType.DMA((4 + 2 * CHIPS,))],
        name="dispatch",
        far=range(6),
    )


def pick_kernel(shifts, experts, capacity, topk, *refs):
    blocks, outs = refs[:CHIPS], refs[CHIPS:]
    chip, core, expert = place()
    wide = outs[0].shape[1]
    rows = outs[0].shape[0] // 2
    tokens = blocks[0].shape[0] // 2
    lane = iota((CHIPS * tokens, rows), 1).astype(jnp.float32)
    for at in range(2):
        span = slice(at * tokens, (at + 1) * tokens)
        left = jnp.concatenate([b[span, :wide] for b in blocks], axis=0)
        notes = [b[span, wide:].astype(jnp.float32) for b in blocks]
        for out, de in zip(outs, shifts):
            here = lax.rem(expert + de, experts).astype(jnp.float32)
            choice = jnp.zeros((CHIPS * tokens, rows), jnp.float32)
            for kk in range(topk):
                targets = []
                for j, note in enumerate(notes):
                    route, rank = note[:, kk : kk + 1], note[:, topk + kk : topk + kk + 1]
                    first = first_row(peer(chip, core, j), capacity).astype(jnp.float32)
                    targets.append(jnp.where(route == here, rank + first, -1.0))
                choice += jnp.where(lane == jnp.concatenate(targets, axis=0), 1.0, 0.0)
            picked = dot(choice.astype(jnp.bfloat16), left, TN)
            out[at * rows : (at + 1) * rows] = picked.astype(jnp.bfloat16)


def pick(blocks, shifts, experts, capacity, topk, name):
    wide = blocks[0].shape[1] - 128
    outs = [shape((2 * slot_rows(capacity), wide)) for _ in shifts]
    kernel = functools.partial(pick_kernel, shifts, experts, capacity, topk)
    return call(kernel, outs, *blocks, name=name)


def hold_kernel(experts, capacity, gu, down, saved, gu_far, down_far, *refs):
    gu_near, down_near, gu_turned, down_turned, mine, theirs, near_saved, ready = refs
    _, core, expert = place()
    jobs = ((saved, near_saved), (gu, gu_near), (down, down_near))
    copies = [pltpu.make_async_copy(*job, ready.at[i]) for i, job in enumerate(jobs)]
    for copy in copies:
        copy.start()

    def turn(source, target, first):
        step = source.shape[0] // 8
        for i in range(8):
            span = slice(i * step, (i + 1) * step)
            target[first : first + source.shape[1], span] = source[span, :].T

    half = gu.shape[1]
    turn(gu_far, gu_turned, half)
    turn(down_far, down_turned, half)
    copies[0].wait()
    stash(experts, capacity, core, expert, near_saved, mine, theirs)
    copies[1].wait()
    turn(gu_near, gu_turned, 0)
    copies[2].wait()
    turn(down_near, down_turned, 0)


def hold(gu, down, saved, far, experts, capacity):
    stashed = shape((slot_rows(capacity) * experts, saved.shape[1]))
    turned = [shape((CORES * w.shape[1], w.shape[0])) for w in (gu, down)]
    results = call(
        functools.partial(hold_kernel, experts, capacity),
        [shape(gu.shape), shape(down.shape), *turned, stashed, stashed],
        gu,
        down,
        saved,
        *far,
        scratch=[pltpu.VMEM(saved.shape, saved.dtype), pltpu.SemaphoreType.DMA((3,))],
        name="hold",
        far=range(3),
        near=(3, 4),
    )
    return results[:2], results[2:4], results[4:]


def unit_rows(part, chip, units):
    return pl.ds(pl.multiple_of((part * CHIPS + chip) * units, units), units)


def up_kernel(experts, steps, *refs):
    blocks, turned, outs = refs[:experts], refs[experts : experts + 2], refs[experts + 2 :]
    chip, core, _ = place()
    half = turned[0].shape[0] // CORES
    units = turned[1].shape[1] // CHIPS
    rows = blocks[0].shape[0] // 2

    def left(at):
        sides = [
            jnp.concatenate([b[at * rows : (at + 1) * rows, block_of(side, half)] for b in blocks], axis=0)
            for side in (core, 1 - core)
        ]
        return jnp.concatenate(sides, axis=1)

    lefts = [left(at) for at in range(2)]
    for out, j in zip(outs, steps):
        for part in range(3):
            which, piece = divmod(part, 2)
            span = unit_rows(piece, peer(chip, core, j), units)
            out[:, part * units : (part + 1) * units] = dot(lefts[which], turned[which][:, span]).astype(out.dtype)


def up(blocks, turned, steps, dtype, name):
    experts = len(blocks)
    rows = blocks[0].shape[0] // 2 * experts
    width = (turned[0].shape[1] + turned[1].shape[1]) // CHIPS
    outs = [shape((rows, width), dtype) for _ in steps]
    flops = 2 * rows * width * turned[0].shape[0] * len(steps)
    return call(functools.partial(up_kernel, experts, steps), outs, *blocks, *turned, flops=flops, name=name)


def act_kernel(*refs):
    parts, (mine, theirs, out) = refs[:CHIPS], refs[CHIPS:]
    _, core, _ = place()
    total = parts[0][...]
    for part in parts[1:]:
        total = total + part[...].astype(jnp.float32)
    units = total.shape[1] // 3
    gate_pre, up_pre, hidden_grad = total[:, :units], total[:, units : 2 * units], total[:, 2 * units :]
    out[:, :units] = (gate_pre * jax.nn.sigmoid(gate_pre) * up_pre).astype(jnp.bfloat16)
    half = units // CORES
    own, other = mine[...].astype(jnp.float32), theirs[...].astype(jnp.float32)
    low, high = jnp.where(core == 0, own, other), jnp.where(core == 0, other, own)
    for at, saved in enumerate((low, high)):
        gate_pre, up_pre = saved[:, :half], saved[:, half:]
        sig = jax.nn.sigmoid(gate_pre)
        grad = hidden_grad[:, at * half : (at + 1) * half]
        first = units + at * half
        out[:, first : first + half] = (grad * up_pre * (sig * (1.0 + gate_pre * (1.0 - sig)))).astype(jnp.bfloat16)
        out[:, first + units : first + units + half] = (grad * (gate_pre * sig)).astype(jnp.bfloat16)


def act(parts, mine, theirs):
    return call(act_kernel, shape(parts[0].shape), *parts, mine, theirs, name="act")


def down_kernel(experts, *refs):
    parts, near, far = refs[:CHIPS], refs[CHIPS : CHIPS + 2], refs[CHIPS + 2 : CHIPS + 4]
    outs = refs[CHIPS + 4 :][::-1]
    chip, core, _ = place()
    half = near[0].shape[1]
    units = near[1].shape[0] // CHIPS
    rows = parts[0].shape[0] // experts
    group = rows // COLUMNS
    low = chip % COLUMNS == 0
    for side, column in ((0, core), (1, 1 - core)):
        totals = []
        for which, terms in ((1, ((0, 0),)), (0, ((1, 0), (2, 1)))):
            weight = (near, far)[side][which]
            total = None
            for j in range(CHIPS):
                for piece, part in terms:
                    left = parts[j][:, piece * units : (piece + 1) * units]
                    term = dot(left, weight[unit_rows(part, peer(chip, core, j), units), :])
                    total = term if total is None else total + term
            totals.append(total)
        for de in range(experts):
            first = de * rows
            lower = jnp.concatenate([t[first : first + group] for t in totals], axis=0).astype(jnp.bfloat16)
            upper = jnp.concatenate([t[first + group : first + rows] for t in totals], axis=0).astype(jnp.bfloat16)
            outs[de][:, block_of(column, half)] = jnp.where(low, lower, upper)
            outs[experts + de][:, block_of(column, half)] = jnp.where(low, upper, lower)


def down(parts, near, far, experts):
    rows = parts[0].shape[0] // experts
    outs = [shape((2 * rows // COLUMNS, CORES * near[0].shape[1])) for _ in range(COLUMNS * experts)]
    flops = 4 * parts[0].shape[0] * (near[0].size + near[1].size)
    kernel = functools.partial(down_kernel, experts)
    return call(kernel, outs, *parts, *near, *far, flops=flops, name="down", near=(CHIPS + 2, CHIPS + 3))


def combine_kernel(experts, capacity, topk, *refs):
    blocks, results, outs = refs[:CHIPS], refs[CHIPS : CHIPS + COLUMNS * experts], refs[CHIPS + COLUMNS * experts :]
    results = results[::-1]
    chip, core, expert = place()
    group, wide = results[0].shape[0] // 2, results[0].shape[1]
    tokens = outs[0].shape[0] // 2
    lane = iota((2 * ROWS * tokens, 2 * group), 1).astype(jnp.float32)
    own = blocks[0][:, wide:].astype(jnp.float32)
    other = jnp.where(core == 0, blocks[2][:, wide:].astype(jnp.float32), blocks[1][:, wide:].astype(jnp.float32))
    notes, firsts = [], []
    for dz, note in enumerate((own, other)):
        for at in range(2):
            notes.append(note[at * tokens : (at + 1) * tokens])
            firsts.append((((chip // COLUMNS) ^ dz) * capacity + at * group).astype(jnp.float32))
    for dy in range(COLUMNS):
        total = None
        for kk in range(topk):
            found = None
            for de in range(experts):
                here = lax.rem(expert + de, experts).astype(jnp.float32)
                targets = []
                for note, first in zip(notes, firsts):
                    route, rank = note[:, kk : kk + 1], note[:, topk + kk : topk + kk + 1]
                    targets.append(jnp.where(route == here, rank + first, -1.0))
                choice = jnp.where(lane == jnp.concatenate(targets, axis=0), 1.0, 0.0).astype(jnp.bfloat16)
                term = dot(choice, results[dy * experts + de][...])
                found = term if found is None else found + term
            gates = []
            for note in notes:
                terms = [note[:, part * topk + kk : part * topk + kk + 1] for part in (2, 3, 4)]
                gates.append(terms[0] + terms[1] + terms[2])
            term = found * jnp.concatenate(gates, axis=0)
            total = term if total is None else total + term
        total = total.astype(jnp.bfloat16)
        for dz in range(ROWS):
            span = slice(dz * 2 * tokens, (dz + 1) * 2 * tokens)
            outs[dz][:, block_of((chip % COLUMNS) ^ dy, wide)] = total[span]


def combine(blocks, results, capacity, topk):
    experts = len(results) // COLUMNS
    outs = [shape((blocks[0].shape[0], COLUMNS * results[0].shape[1])) for _ in range(ROWS)]
    kernel = functools.partial(combine_kernel, experts, capacity, topk)
    return call(kernel, outs, *blocks, *results, name="combine")


def join_kernel(*refs):
    chip, _, _ = place()
    blocks, outs = refs[:-2], refs[-2:]
    tokens = outs[0].shape[0]
    for at, out in enumerate(outs):
        for dz in range(ROWS):
            block = blocks[dz + at * (len(blocks) - ROWS)]
            first = at * tokens if len(blocks) == ROWS else 0
            out[:, block_of((chip // COLUMNS) ^ dz, block.shape[1])] = block[first : first + tokens]


def join(blocks, tokens):
    out = shape((tokens, ROWS * blocks[0].shape[1]))
    return call(join_kernel, [out, out], *blocks, name="join")


def on_device(
    forward_input,
    forward_route,
    forward_gates,
    backward_cotangent,
    backward_route,
    backward_gates,
    gate_up_weight,
    down_weight,
    saved_projections,
):
    sections = lax.axis_size("section")
    experts = lax.axis_size("expert")
    topk = forward_route.shape[2]
    capacity = saved_projections.shape[2] // (GROUP * experts)
    tokens = forward_route.shape[1]

    def to_chip(value, j):
        places = [(k, c) for k in range(CHIPS) for c in range(CORES)]
        pairs = [(k * CORES + c, peer(k, c, j) * CORES + c) for k, c in places]
        return lax.ppermute(value, ("chip", "core"), pairs)

    def to_section(value, dz, by):
        places = [(i, k) for i in range(sections) for k in range(CHIPS)]
        pairs = [(i * CHIPS + k, (i + by) % sections * CHIPS + (k ^ (dz * COLUMNS))) for i, k in places]
        return lax.ppermute(value, ("section", "chip"), pairs)

    def to_expert(block, de):
        if de == 0:
            return block
        return lax.ppermute(block, "expert", [(i, (i + de) % experts) for i in range(experts)])

    def to_core(value):
        return lax.ppermute(value, "core", [(i, i ^ 1) for i in range(CORES)])

    def returned(block, dy, de):
        if dy == 0 and de == 0:
            return block
        places = [(k, e) for k in range(CHIPS) for e in range(experts)]
        pairs = [(k * experts + (e + de) % experts, (k ^ dy) * experts + e) for k, e in places]
        return lax.ppermute(block, ("chip", "expert"), pairs)

    def to_chips(blocks):
        return [blocks[0]] + [to_chip(blocks[dk], dk) for dk in range(1, CHIPS)]

    args = [a[0].T for a in (forward_route, forward_gates, backward_route, backward_gates)]
    gu, down_rows, saved = gate_up_weight[0, 0], down_weight[0, 0], saved_projections[0, 0]
    far = [to_core(gu), to_core(down_rows)]
    tokens_here = to_chips(dispatch(args + [forward_input[0], backward_cotangent[0]], experts))
    others = pick(tokens_here, (*range(1, experts),), experts, capacity, topk, "pick_others")
    rows_here = [to_expert(others[de - 1], de) for de in range(1, experts)]
    rows_here = [*pick(tokens_here, (0,), experts, capacity, topk, "pick_own"), *rows_here]
    near, turned, (mine, theirs) = hold(gu, down_rows, saved, far, experts, capacity)
    parts = [to_chip(part, j) for j, part in enumerate(up(rows_here, turned, ORDER[:-1], jnp.bfloat16, "up_others"), 1)]
    parts = [*up(rows_here, turned, (0,), jnp.float32, "up_own"), *parts]
    units = act(parts, mine, to_core(theirs))
    results = down(to_chips([units] * CHIPS), near, far, experts)
    steps = [(dy, de) for dy in range(COLUMNS) for de in range(experts)][::-1]
    results = [returned(result, *step) for result, step in zip(results, steps)]
    outs = combine(tokens_here, results, capacity, topk)
    if sections == 2:
        joined = [to_section(outs[dz], dz, 1) for dz in range(ROWS)]
    else:
        joined = [to_section(outs[dz][:tokens], dz, 1) for dz in range(ROWS)]
        joined += [to_section(outs[dz][tokens:], dz, -1) for dz in range(ROWS)]
    next_input, prior_gradient = join(joined, tokens)
    return next_input[None], prior_gradient[None]


def solution(mesh):
    pipes, experts = mesh.devices.shape
    axes = ("section", "chip", "core", "expert")
    mesh = Mesh(mesh.devices.reshape(pipes // GROUP, CHIPS, CORES, experts), axes)
    rows = P(axes[:3], "expert", None)
    weights = P(axes[:3], "expert", None, None)
    return jax.shard_map(
        on_device,
        mesh=mesh,
        in_specs=(rows,) * 6 + (weights,) * 3,
        out_specs=(rows, rows),
        check_vma=False,
    )
```

```python
import functools

import jax
import jax.numpy as jnp
from jax import lax
from jax.experimental import pallas as pl
from jax.experimental.pallas import tpu as pltpu
from jax.sharding import Mesh
from jax.sharding import PartitionSpec as P

GROUP = 8
CORES = 2
CHIPS = GROUP // CORES
COLUMNS = 2
ROWS = CHIPS // COLUMNS
FAR_FIRST = (CHIPS - 1, *range(1, CHIPS - 1))
TILE = 16
NT = (((1,), (1,)), ((), ()))
NN = (((1,), (0,)), ((), ()))
TN = (((0,), (0,)), ((), ()))


def round_up(value, step):
    return (value + step - 1) // step * step


def dot(a, b, dims=NN):
    return lax.dot_general(a, b, dims, preferred_element_type=jnp.float32)


def iota(shape, axis):
    return lax.broadcasted_iota(jnp.int32, shape, axis)


def place():
    return lax.axis_index("chip"), lax.axis_index("core"), lax.axis_index("expert")


def peer(chip, core, j):
    if isinstance(core, int):
        return chip ^ (CHIPS - 1 - j if core == 1 and 0 < j < CHIPS - 1 else j)
    return chip ^ (jnp.where(core == 1, CHIPS - 1 - j, j) if 0 < j < CHIPS - 1 else j)


def block_of(index, size):
    return pl.ds(pl.multiple_of(index * size, size), size)


def pinned(array, memory):
    return array if memory is None else pltpu.with_memory_space_constraint(array, memory)


def call(kernel, outs, *args, scratch=(), flops=0, name=None, far=(), near=()):
    size = sum(a.size * a.dtype.itemsize for a in args)
    size += sum(o.size * o.dtype.itemsize for o in jax.tree.leaves(outs))
    spec = pl.BlockSpec(memory_space=pltpu.VMEM)
    return pl.pallas_call(
        kernel,
        out_shape=outs,
        in_specs=[pl.BlockSpec(memory_space=pl.ANY) if i in far else spec for i in range(len(args))],
        out_specs=jax.tree.map(lambda _: spec, outs),
        scratch_shapes=scratch,
        compiler_params=pltpu.CompilerParams(vmem_limit_bytes=16 * 2**20),
        cost_estimate=pl.CostEstimate(flops=flops, bytes_accessed=size, transcendentals=0),
        name=name,
    )(*(pinned(a, pltpu.HBM if i in far else pltpu.VMEM if i in near else None) for i, a in enumerate(args)))


def shape(dims, dtype=jnp.bfloat16):
    return jax.ShapeDtypeStruct(dims, dtype)


def group_rows(capacity):
    return round_up(ROWS * capacity, 8)


def slot_rows(capacity):
    return COLUMNS * group_rows(capacity)


def first_row(chip, capacity):
    return (chip % COLUMNS) * group_rows(capacity) + (chip // COLUMNS) * capacity


def dispatch_kernel(experts, *refs):
    far, outs, near, ready = refs[:6], refs[6 : 6 + CHIPS], refs[6 + CHIPS : -1], refs[-1]
    chip, core, _ = place()
    tokens, width = far[4].shape
    wide = width // CHIPS
    jobs = [(far[i], near[i]) for i in range(4)]
    for dk in range(CHIPS):
        for at in range(2):
            block = outs[dk].at[at * tokens : (at + 1) * tokens, :wide]
            jobs.append((far[4 + at].at[:, block_of(peer(chip, core, dk), wide)], block))
    copies = [pltpu.make_async_copy(*job, ready.at[i]) for i, job in enumerate(jobs)]
    for copy in copies:
        copy.start()
    for copy in copies[:4]:
        copy.wait()
    for at in range(2):
        route, gate = near[2 * at][...], near[2 * at + 1][...]
        topk = route.shape[0]
        earlier = (iota((tokens, tokens), 0) < iota((tokens, tokens), 1)).astype(jnp.float32)
        rank = jnp.zeros((topk, tokens), jnp.float32)
        for e in range(experts):
            named = (route == e).astype(jnp.float32)
            count = jnp.broadcast_to(jnp.sum(named, axis=0, keepdims=True), (8, tokens))
            rank = rank + named * dot(count, earlier)[:1]
        high = gate.astype(jnp.bfloat16).astype(jnp.float32)
        middle = (gate - high).astype(jnp.bfloat16).astype(jnp.float32)
        low = gate - high - middle
        table = jnp.zeros((128, tokens), jnp.float32)
        for part, value in enumerate((route.astype(jnp.float32), rank, high, middle, low)):
            for kk in range(topk):
                row = jnp.broadcast_to(value[kk : kk + 1], (128, tokens))
                table = jnp.where(iota((128, tokens), 0) == part * topk + kk, row, table)
        same = (iota((tokens, tokens), 0) == iota((tokens, tokens), 1)).astype(jnp.bfloat16)
        note = dot(same, table.astype(jnp.bfloat16), NT).astype(jnp.bfloat16)
        for dk in range(CHIPS):
            outs[dk][at * tokens : (at + 1) * tokens, wide:] = note
    for copy in copies[4:]:
        copy.wait()


def stash(experts, capacity, core, expert, saved, mine, theirs):
    rows = slot_rows(capacity)
    dims = (rows * experts, saved.shape[0])
    row, column = iota(dims, 0), iota(dims, 1)
    for target, ref in ((1 - core, theirs), (core, mine)):
        wanted = jnp.full(dims, -1, jnp.int32)
        for de in range(experts):
            for at in range(CHIPS):
                source = (at * CORES + target) * experts + lax.rem(expert + experts - de, experts)
                low = de * rows + first_row(at, capacity)
                inside = jnp.logical_and(row >= low, row < low + capacity)
                wanted = jnp.where(inside, row + (source * capacity - low), wanted)
        pick = jnp.where(column == wanted, 1.0, 0.0).astype(jnp.bfloat16)
        ref[...] = dot(pick, saved[...]).astype(jnp.bfloat16)


def dispatch(args, experts):
    tokens, wide = args[4].shape[0], args[4].shape[1] // CHIPS
    return call(
        functools.partial(dispatch_kernel, experts),
        [shape((2 * tokens, wide + 128)) for _ in range(CHIPS)],
        *args,
        scratch=[pltpu.VMEM(a.shape, a.dtype) for a in args[:4]] + [pltpu.SemaphoreType.DMA((4 + 2 * CHIPS,))],
        name="dispatch",
        far=range(6),
    )


def pick_kernel(shifts, experts, capacity, topk, *refs):
    blocks, outs = refs[:CHIPS], refs[CHIPS:]
    chip, core, expert = place()
    wide = outs[0].shape[1]
    rows = outs[0].shape[0] // 2
    tokens = blocks[0].shape[0] // 2
    lane = iota((CHIPS * tokens, rows), 1).astype(jnp.float32)
    for at in range(2):
        span = slice(at * tokens, (at + 1) * tokens)
        left = jnp.concatenate([b[span, :wide] for b in blocks], axis=0)
        notes = [b[span, wide:].astype(jnp.float32) for b in blocks]
        for out, de in zip(outs, shifts):
            here = lax.rem(expert + de, experts).astype(jnp.float32)
            choice = jnp.zeros((CHIPS * tokens, rows), jnp.float32)
            for kk in range(topk):
                targets = []
                for j, note in enumerate(notes):
                    route, rank = note[:, kk : kk + 1], note[:, topk + kk : topk + kk + 1]
                    first = first_row(peer(chip, core, j), capacity).astype(jnp.float32)
                    targets.append(jnp.where(route == here, rank + first, -1.0))
                choice += jnp.where(lane == jnp.concatenate(targets, axis=0), 1.0, 0.0)
            picked = dot(choice.astype(jnp.bfloat16), left, TN)
            out[at * rows : (at + 1) * rows] = picked.astype(jnp.bfloat16)


def pick(blocks, shifts, experts, capacity, topk, name):
    wide = blocks[0].shape[1] - 128
    outs = [shape((2 * slot_rows(capacity), wide)) for _ in shifts]
    kernel = functools.partial(pick_kernel, shifts, experts, capacity, topk)
    return call(kernel, outs, *blocks, name=name)


def hold_kernel(experts, capacity, gu, down, saved, gu_far, down_far, *refs):
    gu_near, down_near, gu_turned, down_turned, mine, theirs, near_saved, ready = refs
    _, core, expert = place()
    jobs = ((saved, near_saved), (gu, gu_near), (down, down_near))
    copies = [pltpu.make_async_copy(*job, ready.at[i]) for i, job in enumerate(jobs)]
    for copy in copies:
        copy.start()

    def turn(source, target, first):
        step = source.shape[0] // 8
        for i in range(8):
            span = slice(i * step, (i + 1) * step)
            target[first : first + source.shape[1], span] = source[span, :].T

    half = gu.shape[1]
    turn(gu_far, gu_turned, half)
    turn(down_far, down_turned, half)
    copies[0].wait()
    stash(experts, capacity, core, expert, near_saved, mine, theirs)
    copies[1].wait()
    turn(gu_near, gu_turned, 0)
    copies[2].wait()
    turn(down_near, down_turned, 0)


def hold(gu, down, saved, far, experts, capacity):
    stashed = shape((slot_rows(capacity) * experts, saved.shape[1]))
    turned = [shape((CORES * w.shape[1], w.shape[0])) for w in (gu, down)]
    results = call(
        functools.partial(hold_kernel, experts, capacity),
        [shape(gu.shape), shape(down.shape), *turned, stashed, stashed],
        gu,
        down,
        saved,
        *far,
        scratch=[pltpu.VMEM(saved.shape, saved.dtype), pltpu.SemaphoreType.DMA((3,))],
        name="hold",
        far=range(3),
        near=(3, 4),
    )
    return results[:2], results[2:4], results[4:]


def unit_rows(part, chip, units):
    return pl.ds(pl.multiple_of((part * CHIPS + chip) * units, units), units)


def up_kernel(experts, steps, *refs):
    blocks, turned, outs = refs[:experts], refs[experts : experts + 2], refs[experts + 2 :]
    chip, core, _ = place()
    half = turned[0].shape[0] // CORES
    units = turned[1].shape[1] // CHIPS
    rows = blocks[0].shape[0] // 2

    def left(at):
        sides = [
            jnp.concatenate([b[at * rows : (at + 1) * rows, block_of(side, half)] for b in blocks], axis=0)
            for side in (core, 1 - core)
        ]
        return jnp.concatenate(sides, axis=1)

    lefts = [left(at) for at in range(2)]
    for out, j in zip(outs, steps):
        for part in range(3):
            which, piece = divmod(part, 2)
            span = unit_rows(piece, peer(chip, core, j), units)
            out[:, part * units : (part + 1) * units] = dot(lefts[which], turned[which][:, span]).astype(out.dtype)


def up(blocks, turned, steps, dtype, name):
    experts = len(blocks)
    rows = blocks[0].shape[0] // 2 * experts
    width = (turned[0].shape[1] + turned[1].shape[1]) // CHIPS
    outs = [shape((rows, width), dtype) for _ in steps]
    flops = 2 * rows * width * turned[0].shape[0] * len(steps)
    return call(functools.partial(up_kernel, experts, steps), outs, *blocks, *turned, flops=flops, name=name)


def act_kernel(*refs):
    parts, (mine, theirs, out) = refs[:CHIPS], refs[CHIPS:]
    _, core, _ = place()
    total = parts[0][...]
    for part in parts[1:]:
        total = total + part[...].astype(jnp.float32)
    units = total.shape[1] // 3
    gate_pre, up_pre, hidden_grad = total[:, :units], total[:, units : 2 * units], total[:, 2 * units :]
    out[:, :units] = (gate_pre * jax.nn.sigmoid(gate_pre) * up_pre).astype(jnp.bfloat16)
    half = units // CORES
    own, other = mine[...].astype(jnp.float32), theirs[...].astype(jnp.float32)
    low, high = jnp.where(core == 0, own, other), jnp.where(core == 0, other, own)
    for at, saved in enumerate((low, high)):
        gate_pre, up_pre = saved[:, :half], saved[:, half:]
        sig = jax.nn.sigmoid(gate_pre)
        grad = hidden_grad[:, at * half : (at + 1) * half]
        first = units + at * half
        out[:, first : first + half] = (grad * up_pre * (sig * (1.0 + gate_pre * (1.0 - sig)))).astype(jnp.bfloat16)
        out[:, first + units : first + units + half] = (grad * (gate_pre * sig)).astype(jnp.bfloat16)


def act(parts, mine, theirs):
    return call(act_kernel, shape(parts[0].shape), *parts, mine, theirs, name="act")


def down_kernel(experts, *refs):
    parts, near, far = refs[:CHIPS], refs[CHIPS : CHIPS + 2], refs[CHIPS + 2 : CHIPS + 4]
    outs = refs[CHIPS + 4 :][::-1]
    chip, core, _ = place()
    half = near[0].shape[1]
    units = near[1].shape[0] // CHIPS
    rows = parts[0].shape[0] // experts
    group = rows // COLUMNS
    low = chip % COLUMNS == 0
    for side, column in ((0, core), (1, 1 - core)):
        totals = []
        for which, terms in ((1, ((0, 0),)), (0, ((1, 0), (2, 1)))):
            weight = (near, far)[side][which]
            total = None
            for j in range(CHIPS):
                for piece, part in terms:
                    left = parts[j][:, piece * units : (piece + 1) * units]
                    term = dot(left, weight[unit_rows(part, peer(chip, core, j), units), :])
                    total = term if total is None else total + term
            totals.append(total)
        for de in range(experts):
            first = de * rows
            lower = jnp.concatenate([t[first : first + group] for t in totals], axis=0).astype(jnp.bfloat16)
            upper = jnp.concatenate([t[first + group : first + rows] for t in totals], axis=0).astype(jnp.bfloat16)
            outs[de][:, block_of(column, half)] = jnp.where(low, lower, upper)
            outs[experts + de][:, block_of(column, half)] = jnp.where(low, upper, lower)


def down(parts, near, far, experts):
    rows = parts[0].shape[0] // experts
    outs = [shape((2 * rows // COLUMNS, CORES * near[0].shape[1])) for _ in range(COLUMNS * experts)]
    flops = 4 * parts[0].shape[0] * (near[0].size + near[1].size)
    kernel = functools.partial(down_kernel, experts)
    return call(kernel, outs, *parts, *near, *far, flops=flops, name="down", near=(CHIPS + 2, CHIPS + 3))


def combine_kernel(experts, capacity, topk, *refs):
    blocks, results, outs = refs[:CHIPS], refs[CHIPS : CHIPS + COLUMNS * experts], refs[CHIPS + COLUMNS * experts :]
    results = results[::-1]
    chip, core, expert = place()
    group, wide = results[0].shape[0] // 2, results[0].shape[1]
    tokens = outs[0].shape[0] // 2
    lane = iota((2 * ROWS * tokens, 2 * group), 1).astype(jnp.float32)
    own = blocks[0][:, wide:].astype(jnp.float32)
    other = jnp.where(core == 0, blocks[2][:, wide:].astype(jnp.float32), blocks[1][:, wide:].astype(jnp.float32))
    notes, firsts = [], []
    for dz, note in enumerate((own, other)):
        for at in range(2):
            notes.append(note[at * tokens : (at + 1) * tokens])
            firsts.append((((chip // COLUMNS) ^ dz) * capacity + at * group).astype(jnp.float32))
    for dy in range(COLUMNS):
        total = None
        for kk in range(topk):
            found = None
            for de in range(experts):
                here = lax.rem(expert + de, experts).astype(jnp.float32)
                targets = []
                for note, first in zip(notes, firsts):
                    route, rank = note[:, kk : kk + 1], note[:, topk + kk : topk + kk + 1]
                    targets.append(jnp.where(route == here, rank + first, -1.0))
                choice = jnp.where(lane == jnp.concatenate(targets, axis=0), 1.0, 0.0).astype(jnp.bfloat16)
                term = dot(choice, results[dy * experts + de][...])
                found = term if found is None else found + term
            gates = []
            for note in notes:
                terms = [note[:, part * topk + kk : part * topk + kk + 1] for part in (2, 3, 4)]
                gates.append(terms[0] + terms[1] + terms[2])
            term = found * jnp.concatenate(gates, axis=0)
            total = term if total is None else total + term
        total = total.astype(jnp.bfloat16)
        for dz in range(ROWS):
            span = slice(dz * 2 * tokens, (dz + 1) * 2 * tokens)
            outs[ROWS - 1 - dz][:, block_of((chip % COLUMNS) ^ dy, wide)] = total[span]


def combine(blocks, results, capacity, topk):
    experts = len(results) // COLUMNS
    outs = [shape((blocks[0].shape[0], COLUMNS * results[0].shape[1])) for _ in range(ROWS)]
    kernel = functools.partial(combine_kernel, experts, capacity, topk)
    return call(kernel, outs, *blocks, *results, name="combine")


def join_kernel(count, *refs):
    chip, _, _ = place()
    blocks, outs, ready = refs[:count], refs[count:-1], refs[-1]
    tokens, wide = outs[0].shape[0], blocks[0].shape[1]
    copies = []
    for at, out in enumerate(outs):
        for dz in range(ROWS):
            block = blocks[ROWS - 1 - dz + at * (count - ROWS)]
            first = at * tokens if count == ROWS else 0
            target = out.at[:, block_of((chip // COLUMNS) ^ dz, wide)]
            copies.append(pltpu.make_async_copy(block.at[first : first + tokens], target, ready.at[at, dz]))
            copies[-1].start()
    for copy in copies:
        copy.wait()


def join(blocks, tokens):
    out = shape((tokens, ROWS * blocks[0].shape[1]))
    count = len(blocks)
    return pl.pallas_call(
        functools.partial(join_kernel, count),
        out_shape=[out, out],
        in_specs=[pl.BlockSpec(memory_space=pltpu.VMEM)] * count,
        out_specs=[pl.BlockSpec(memory_space=pl.ANY)] * 2,
        scratch_shapes=[pltpu.SemaphoreType.DMA((2, ROWS))],
        compiler_params=pltpu.CompilerParams(vmem_limit_bytes=16 * 2**20),
        cost_estimate=pl.CostEstimate(flops=0, bytes_accessed=8 * out.size, transcendentals=0),
        name="join",
    )(*blocks)


def on_device(
    forward_input,
    forward_route,
    forward_gates,
    backward_cotangent,
    backward_route,
    backward_gates,
    gate_up_weight,
    down_weight,
    saved_projections,
):
    sections = lax.axis_size("section")
    experts = lax.axis_size("expert")
    topk = forward_route.shape[2]
    capacity = saved_projections.shape[2] // (GROUP * experts)
    tokens = forward_route.shape[1]

    def to_chip(value, j):
        places = [(k, c) for k in range(CHIPS) for c in range(CORES)]
        pairs = [(k * CORES + c, peer(k, c, j) * CORES + c) for k, c in places]
        return lax.ppermute(value, ("chip", "core"), pairs)

    def to_section(value, dz, by):
        places = [(i, k) for i in range(sections) for k in range(CHIPS)]
        pairs = [(i * CHIPS + k, (i + by) % sections * CHIPS + (k ^ (dz * COLUMNS))) for i, k in places]
        return lax.ppermute(value, ("section", "chip"), pairs)

    def to_expert(block, de):
        if de == 0:
            return block
        return lax.ppermute(block, "expert", [(i, (i + de) % experts) for i in range(experts)])

    def to_core(value):
        return lax.ppermute(value, "core", [(i, i ^ 1) for i in range(CORES)])

    def returned(block, dy, de):
        if dy == 0 and de == 0:
            return block
        places = [(k, e) for k in range(CHIPS) for e in range(experts)]
        pairs = [(k * experts + (e + de) % experts, (k ^ dy) * experts + e) for k, e in places]
        return lax.ppermute(block, ("chip", "expert"), pairs)

    def to_chips(blocks):
        return [blocks[0]] + [to_chip(blocks[dk], dk) for dk in range(1, CHIPS)]

    args = [a[0].T for a in (forward_route, forward_gates, backward_route, backward_gates)]
    gu, down_rows, saved = gate_up_weight[0, 0], down_weight[0, 0], saved_projections[0, 0]
    far = [to_core(gu), to_core(down_rows)]
    tokens_here = to_chips(dispatch(args + [forward_input[0], backward_cotangent[0]], experts))
    others = pick(tokens_here, (*range(1, experts),), experts, capacity, topk, "pick_others")
    rows_here = [to_expert(others[de - 1], de) for de in range(1, experts)]
    rows_here = [*pick(tokens_here, (0,), experts, capacity, topk, "pick_own"), *rows_here]
    near, turned, (mine, theirs) = hold(gu, down_rows, saved, far, experts, capacity)
    parts = [to_chip(part, j) for j, part in zip(FAR_FIRST, up(rows_here, turned, FAR_FIRST, jnp.bfloat16, "up_others"))]
    parts = [*up(rows_here, turned, (0,), jnp.float32, "up_own"), *parts]
    units = act(parts, mine, to_core(theirs))
    results = down(to_chips([units] * CHIPS), near, far, experts)
    steps = [(dy, de) for dy in range(COLUMNS) for de in range(experts)][::-1]
    results = [returned(result, *step) for result, step in zip(results, steps)]
    outs = combine(tokens_here, results, capacity, topk)
    steps = [*range(ROWS)][::-1]
    if sections == 2:
        joined = [to_section(out, dz, 1) for out, dz in zip(outs, steps)]
    else:
        joined = [to_section(out[:tokens], dz, 1) for out, dz in zip(outs, steps)]
        joined += [to_section(out[tokens:], dz, -1) for out, dz in zip(outs, steps)]
    next_input, prior_gradient = join(joined, tokens)
    return next_input[None], prior_gradient[None]


def solution(mesh):
    pipes, experts = mesh.devices.shape
    axes = ("section", "chip", "core", "expert")
    mesh = Mesh(mesh.devices.reshape(pipes // GROUP, CHIPS, CORES, experts), axes)
    rows = P(axes[:3], "expert", None)
    weights = P(axes[:3], "expert", None, None)
    return jax.shard_map(
        on_device,
        mesh=mesh,
        in_specs=(rows,) * 6 + (weights,) * 3,
        out_specs=(rows, rows),
        check_vma=False,
    )
```

```python
import functools

import jax
import jax.numpy as jnp
from jax import lax
from jax.experimental import pallas as pl
from jax.experimental.pallas import tpu as pltpu
from jax.sharding import Mesh
from jax.sharding import PartitionSpec as P

GROUP = 8
CORES = 2
CHIPS = GROUP // CORES
COLUMNS = 2
ROWS = CHIPS // COLUMNS
FAR_FIRST = (CHIPS - 1, *range(1, CHIPS - 1))
TILE = 16
NT = (((1,), (1,)), ((), ()))
NN = (((1,), (0,)), ((), ()))
TN = (((0,), (0,)), ((), ()))


def round_up(value, step):
    return (value + step - 1) // step * step


def dot(a, b, dims=NN):
    return lax.dot_general(a, b, dims, preferred_element_type=jnp.float32)


def iota(shape, axis):
    return lax.broadcasted_iota(jnp.int32, shape, axis)


def place():
    return lax.axis_index("chip"), lax.axis_index("core"), lax.axis_index("expert")


def peer(chip, core, j):
    if isinstance(core, int):
        return chip ^ (CHIPS - 1 - j if core == 1 and 0 < j < CHIPS - 1 else j)
    return chip ^ (jnp.where(core == 1, CHIPS - 1 - j, j) if 0 < j < CHIPS - 1 else j)


def block_of(index, size):
    return pl.ds(pl.multiple_of(index * size, size), size)


def pinned(array, memory):
    return array if memory is None else pltpu.with_memory_space_constraint(array, memory)


def call(kernel, outs, *args, scratch=(), flops=0, name=None, far=(), near=()):
    size = sum(a.size * a.dtype.itemsize for a in args)
    size += sum(o.size * o.dtype.itemsize for o in jax.tree.leaves(outs))
    spec = pl.BlockSpec(memory_space=pltpu.VMEM)
    return pl.pallas_call(
        kernel,
        out_shape=outs,
        in_specs=[pl.BlockSpec(memory_space=pl.ANY) if i in far else spec for i in range(len(args))],
        out_specs=jax.tree.map(lambda _: spec, outs),
        scratch_shapes=scratch,
        compiler_params=pltpu.CompilerParams(vmem_limit_bytes=16 * 2**20),
        cost_estimate=pl.CostEstimate(flops=flops, bytes_accessed=size, transcendentals=0),
        name=name,
    )(*(pinned(a, pltpu.HBM if i in far else pltpu.VMEM if i in near else None) for i, a in enumerate(args)))


def shape(dims, dtype=jnp.bfloat16):
    return jax.ShapeDtypeStruct(dims, dtype)


def group_rows(capacity):
    return round_up(ROWS * capacity, 8)


def slot_rows(capacity):
    return COLUMNS * group_rows(capacity)


def first_row(chip, capacity):
    return (chip % COLUMNS) * group_rows(capacity) + (chip // COLUMNS) * capacity


def dispatch_kernel(experts, *refs):
    far, outs, near, ready = refs[:6], refs[6 : 6 + CHIPS], refs[6 + CHIPS : -1], refs[-1]
    chip, core, _ = place()
    tokens, width = far[4].shape
    wide = width // CHIPS
    jobs = [(far[i], near[i]) for i in range(4)]
    for dk in range(CHIPS):
        for at in range(2):
            block = outs[dk].at[at * tokens : (at + 1) * tokens, :wide]
            jobs.append((far[4 + at].at[:, block_of(peer(chip, core, dk), wide)], block))
    copies = [pltpu.make_async_copy(*job, ready.at[i]) for i, job in enumerate(jobs)]
    for copy in copies:
        copy.start()
    for copy in copies[:4]:
        copy.wait()
    for at in range(2):
        route, gate = near[2 * at][...], near[2 * at + 1][...]
        topk = route.shape[0]
        earlier = (iota((tokens, tokens), 0) < iota((tokens, tokens), 1)).astype(jnp.float32)
        rank = jnp.zeros((topk, tokens), jnp.float32)
        for e in range(experts):
            named = (route == e).astype(jnp.float32)
            count = jnp.broadcast_to(jnp.sum(named, axis=0, keepdims=True), (8, tokens))
            rank = rank + named * dot(count, earlier)[:1]
        high = gate.astype(jnp.bfloat16).astype(jnp.float32)
        middle = (gate - high).astype(jnp.bfloat16).astype(jnp.float32)
        low = gate - high - middle
        table = jnp.zeros((128, tokens), jnp.float32)
        for part, value in enumerate((route.astype(jnp.float32), rank, high, middle, low)):
            for kk in range(topk):
                row = jnp.broadcast_to(value[kk : kk + 1], (128, tokens))
                table = jnp.where(iota((128, tokens), 0) == part * topk + kk, row, table)
        same = (iota((tokens, tokens), 0) == iota((tokens, tokens), 1)).astype(jnp.bfloat16)
        note = dot(same, table.astype(jnp.bfloat16), NT).astype(jnp.bfloat16)
        for dk in range(CHIPS):
            outs[dk][at * tokens : (at + 1) * tokens, wide:] = note
    for copy in copies[4:]:
        copy.wait()


def stash(experts, capacity, core, expert, saved, mine, theirs):
    rows = slot_rows(capacity)
    dims = (rows * experts, saved.shape[0])
    row, column = iota(dims, 0), iota(dims, 1)
    for target, ref in ((1 - core, theirs), (core, mine)):
        wanted = jnp.full(dims, -1, jnp.int32)
        for de in range(experts):
            for at in range(CHIPS):
                source = (at * CORES + target) * experts + lax.rem(expert + experts - de, experts)
                low = de * rows + first_row(at, capacity)
                inside = jnp.logical_and(row >= low, row < low + capacity)
                wanted = jnp.where(inside, row + (source * capacity - low), wanted)
        pick = jnp.where(column == wanted, 1.0, 0.0).astype(jnp.bfloat16)
        ref[...] = dot(pick, saved[...]).astype(jnp.bfloat16)


def dispatch(args, experts):
    tokens, wide = args[4].shape[0], args[4].shape[1] // CHIPS
    return call(
        functools.partial(dispatch_kernel, experts),
        [shape((2 * tokens, wide + 128)) for _ in range(CHIPS)],
        *args,
        scratch=[pltpu.VMEM(a.shape, a.dtype) for a in args[:4]] + [pltpu.SemaphoreType.DMA((4 + 2 * CHIPS,))],
        name="dispatch",
        far=range(6),
    )


def pick_kernel(shifts, experts, capacity, topk, *refs):
    blocks, outs = refs[:CHIPS], refs[CHIPS:]
    chip, core, expert = place()
    wide = outs[0].shape[1]
    rows = outs[0].shape[0] // 2
    tokens = blocks[0].shape[0] // 2
    lane = iota((CHIPS * tokens, rows), 1).astype(jnp.float32)
    for at in range(2):
        span = slice(at * tokens, (at + 1) * tokens)
        left = jnp.concatenate([b[span, :wide] for b in blocks], axis=0)
        notes = [b[span, wide:].astype(jnp.float32) for b in blocks]
        for out, de in zip(outs, shifts):
            here = lax.rem(expert + de, experts).astype(jnp.float32)
            choice = jnp.zeros((CHIPS * tokens, rows), jnp.float32)
            for kk in range(topk):
                targets = []
                for j, note in enumerate(notes):
                    route, rank = note[:, kk : kk + 1], note[:, topk + kk : topk + kk + 1]
                    first = first_row(peer(chip, core, j), capacity).astype(jnp.float32)
                    targets.append(jnp.where(route == here, rank + first, -1.0))
                choice += jnp.where(lane == jnp.concatenate(targets, axis=0), 1.0, 0.0)
            picked = dot(choice.astype(jnp.bfloat16), left, TN)
            out[at * rows : (at + 1) * rows] = picked.astype(jnp.bfloat16)


def pick(blocks, shifts, experts, capacity, topk, name):
    wide = blocks[0].shape[1] - 128
    outs = [shape((2 * slot_rows(capacity), wide)) for _ in shifts]
    kernel = functools.partial(pick_kernel, shifts, experts, capacity, topk)
    return call(kernel, outs, *blocks, name=name)


def hold_kernel(experts, capacity, gu, down, saved, gu_far, down_far, *refs):
    gu_near, down_near, gu_turned, down_turned, mine, theirs, near_saved, ready = refs
    _, core, expert = place()
    jobs = ((saved, near_saved), (gu, gu_near), (down, down_near))
    copies = [pltpu.make_async_copy(*job, ready.at[i]) for i, job in enumerate(jobs)]
    for copy in copies:
        copy.start()

    def turn(source, target, first):
        step = source.shape[0] // 8
        for i in range(8):
            span = slice(i * step, (i + 1) * step)
            target[first : first + source.shape[1], span] = source[span, :].T

    half = gu.shape[1]
    turn(gu_far, gu_turned, half)
    turn(down_far, down_turned, half)
    copies[0].wait()
    stash(experts, capacity, core, expert, near_saved, mine, theirs)
    copies[1].wait()
    turn(gu_near, gu_turned, 0)
    copies[2].wait()
    turn(down_near, down_turned, 0)


def hold(gu, down, saved, far, experts, capacity):
    stashed = shape((slot_rows(capacity) * experts, saved.shape[1]))
    turned = [shape((CORES * w.shape[1], w.shape[0])) for w in (gu, down)]
    results = call(
        functools.partial(hold_kernel, experts, capacity),
        [shape(gu.shape), shape(down.shape), *turned, stashed, stashed],
        gu,
        down,
        saved,
        *far,
        scratch=[pltpu.VMEM(saved.shape, saved.dtype), pltpu.SemaphoreType.DMA((3,))],
        name="hold",
        far=range(3),
        near=(3, 4),
    )
    return results[:2], results[2:4], results[4:]


def unit_rows(part, chip, units):
    return pl.ds(pl.multiple_of((part * CHIPS + chip) * units, units), units)


def up_kernel(experts, steps, *refs):
    blocks, turned, outs = refs[:experts], refs[experts : experts + 2], refs[experts + 2 :]
    chip, core, _ = place()
    half = turned[0].shape[0] // CORES
    units = turned[1].shape[1] // CHIPS
    rows = blocks[0].shape[0] // 2

    def left(at):
        sides = [
            jnp.concatenate([b[at * rows : (at + 1) * rows, block_of(side, half)] for b in blocks], axis=0)
            for side in (core, 1 - core)
        ]
        return jnp.concatenate(sides, axis=1)

    lefts = [left(at) for at in range(2)]
    for out, j in zip(outs, steps):
        for part in range(3):
            which, piece = divmod(part, 2)
            span = unit_rows(piece, peer(chip, core, j), units)
            out[:, part * units : (part + 1) * units] = dot(lefts[which], turned[which][:, span]).astype(out.dtype)


def up(blocks, turned, steps, dtype, name):
    experts = len(blocks)
    rows = blocks[0].shape[0] // 2 * experts
    width = (turned[0].shape[1] + turned[1].shape[1]) // CHIPS
    outs = [shape((rows, width), dtype) for _ in steps]
    flops = 2 * rows * width * turned[0].shape[0] * len(steps)
    return call(functools.partial(up_kernel, experts, steps), outs, *blocks, *turned, flops=flops, name=name)


def act_kernel(*refs):
    parts, (mine, theirs, out) = refs[:CHIPS], refs[CHIPS:]
    _, core, _ = place()
    total = parts[0][...]
    for part in parts[1:]:
        total = total + part[...].astype(jnp.float32)
    units = total.shape[1] // 3
    gate_pre, up_pre, hidden_grad = total[:, :units], total[:, units : 2 * units], total[:, 2 * units :]
    out[:, :units] = (gate_pre * jax.nn.sigmoid(gate_pre) * up_pre).astype(jnp.bfloat16)
    half = units // CORES
    own, other = mine[...].astype(jnp.float32), theirs[...].astype(jnp.float32)
    low, high = jnp.where(core == 0, own, other), jnp.where(core == 0, other, own)
    for at, saved in enumerate((low, high)):
        gate_pre, up_pre = saved[:, :half], saved[:, half:]
        sig = jax.nn.sigmoid(gate_pre)
        grad = hidden_grad[:, at * half : (at + 1) * half]
        first = units + at * half
        out[:, first : first + half] = (grad * up_pre * (sig * (1.0 + gate_pre * (1.0 - sig)))).astype(jnp.bfloat16)
        out[:, first + units : first + units + half] = (grad * (gate_pre * sig)).astype(jnp.bfloat16)


def act(parts, mine, theirs):
    return call(act_kernel, shape(parts[0].shape), *parts, mine, theirs, name="act")


def down_kernel(experts, *refs):
    parts, near, far = refs[:CHIPS], refs[CHIPS : CHIPS + 2], refs[CHIPS + 2 : CHIPS + 4]
    outs = refs[CHIPS + 4 :][::-1]
    chip, core, _ = place()
    half = near[0].shape[1]
    units = near[1].shape[0] // CHIPS
    rows = parts[0].shape[0] // experts
    group = rows // COLUMNS
    low = chip % COLUMNS == 0
    for side, column in ((0, core), (1, 1 - core)):
        totals = []
        for which, terms in ((1, ((0, 0),)), (0, ((1, 0), (2, 1)))):
            weight = (near, far)[side][which]
            total = None
            for j in range(CHIPS):
                for piece, part in terms:
                    left = parts[j][:, piece * units : (piece + 1) * units]
                    term = dot(left, weight[unit_rows(part, peer(chip, core, j), units), :])
                    total = term if total is None else total + term
            totals.append(total)
        for de in range(experts):
            first = de * rows
            lower = jnp.concatenate([t[first : first + group] for t in totals], axis=0).astype(jnp.bfloat16)
            upper = jnp.concatenate([t[first + group : first + rows] for t in totals], axis=0).astype(jnp.bfloat16)
            outs[de][:, block_of(column, half)] = jnp.where(low, lower, upper)
            outs[experts + de][:, block_of(column, half)] = jnp.where(low, upper, lower)


def down(parts, near, far, experts):
    rows = parts[0].shape[0] // experts
    outs = [shape((2 * rows // COLUMNS, CORES * near[0].shape[1])) for _ in range(COLUMNS * experts)]
    flops = 4 * parts[0].shape[0] * (near[0].size + near[1].size)
    kernel = functools.partial(down_kernel, experts)
    return call(kernel, outs, *parts, *near, *far, flops=flops, name="down", near=(CHIPS + 2, CHIPS + 3))


def plan_kernel(experts, capacity, topk, group, *refs):
    blocks, (choices, gates) = refs[:CHIPS], refs[CHIPS:]
    chip, core, expert = place()
    tokens, wide = blocks[0].shape[0] // 2, blocks[0].shape[1] - 128
    count = 2 * ROWS * tokens
    lane = iota((count, 2 * group), 1).astype(jnp.float32)
    own = blocks[0][:, wide:].astype(jnp.float32)
    other = jnp.where(core == 0, blocks[2][:, wide:].astype(jnp.float32), blocks[1][:, wide:].astype(jnp.float32))
    notes, firsts = [], []
    for dz, note in enumerate((own, other)):
        for at in range(2):
            notes.append(note[at * tokens : (at + 1) * tokens])
            firsts.append((((chip // COLUMNS) ^ dz) * capacity + at * group).astype(jnp.float32))
    for kk in range(topk):
        for de in range(experts):
            here = lax.rem(expert + de, experts).astype(jnp.float32)
            targets = []
            for note, first in zip(notes, firsts):
                route, rank = note[:, kk : kk + 1], note[:, topk + kk : topk + kk + 1]
                targets.append(jnp.where(route == here, rank + first, -1.0))
            choice = jnp.where(lane == jnp.concatenate(targets, axis=0), 1.0, 0.0)
            choices[kk * experts + de] = choice.astype(jnp.bfloat16)
        terms = []
        for note in notes:
            part = [note[:, i * topk + kk : i * topk + kk + 1] for i in (2, 3, 4)]
            terms.append(part[0] + part[1] + part[2])
        gates[kk] = jnp.broadcast_to(jnp.concatenate(terms, axis=0), (count, 128))


def plan(blocks, experts, capacity, topk):
    group = group_rows(capacity)
    count = ROWS * blocks[0].shape[0]
    outs = [shape((topk * experts, count, 2 * group)), shape((topk, count, 128), jnp.float32)]
    return call(functools.partial(plan_kernel, experts, capacity, topk, group), outs, *blocks, name="plan")


def combine_kernel(experts, choices, gates, *refs):
    results, outs = refs[: COLUMNS * experts][::-1], refs[COLUMNS * experts :]
    chip, _, _ = place()
    wide = results[0].shape[1]
    rows = outs[0].shape[0]
    for dy in range(COLUMNS):
        total = None
        for kk in range(gates.shape[0]):
            found = None
            for de in range(experts):
                term = dot(choices[kk * experts + de], results[dy * experts + de][...])
                found = term if found is None else found + term
            term = found * gates[kk][:, :1]
            total = term if total is None else total + term
        total = total.astype(jnp.bfloat16)
        for dz in range(ROWS):
            outs[dz][:, block_of((chip % COLUMNS) ^ dy, wide)] = total[dz * rows : (dz + 1) * rows]


def combine(choices, gates, results):
    experts = len(results) // COLUMNS
    outs = [shape((choices.shape[1] // ROWS, COLUMNS * results[0].shape[1])) for _ in range(ROWS)]
    return call(functools.partial(combine_kernel, experts), outs, choices, gates, *results, name="combine")


def join_kernel(count, *refs):
    chip, _, _ = place()
    blocks, outs, ready = refs[:count], refs[count:-1], refs[-1]
    tokens, wide = outs[0].shape[0], blocks[0].shape[1]
    copies = []
    for at, out in enumerate(outs):
        for dz in range(ROWS):
            block = blocks[dz + at * (count - ROWS)]
            first = at * tokens if count == ROWS else 0
            target = out.at[:, block_of((chip // COLUMNS) ^ dz, wide)]
            copies.append(pltpu.make_async_copy(block.at[first : first + tokens], target, ready.at[at, dz]))
            copies[-1].start()
    for copy in copies:
        copy.wait()


def join(blocks, tokens):
    out = shape((tokens, ROWS * blocks[0].shape[1]))
    count = len(blocks)
    return pl.pallas_call(
        functools.partial(join_kernel, count),
        out_shape=[out, out],
        in_specs=[pl.BlockSpec(memory_space=pltpu.VMEM)] * count,
        out_specs=[pl.BlockSpec(memory_space=pl.ANY)] * 2,
        scratch_shapes=[pltpu.SemaphoreType.DMA((2, ROWS))],
        compiler_params=pltpu.CompilerParams(vmem_limit_bytes=16 * 2**20),
        cost_estimate=pl.CostEstimate(flops=0, bytes_accessed=8 * out.size, transcendentals=0),
        name="join",
    )(*blocks)


def on_device(
    forward_input,
    forward_route,
    forward_gates,
    backward_cotangent,
    backward_route,
    backward_gates,
    gate_up_weight,
    down_weight,
    saved_projections,
):
    sections = lax.axis_size("section")
    experts = lax.axis_size("expert")
    topk = forward_route.shape[2]
    capacity = saved_projections.shape[2] // (GROUP * experts)
    tokens = forward_route.shape[1]

    def to_chip(value, j):
        places = [(k, c) for k in range(CHIPS) for c in range(CORES)]
        pairs = [(k * CORES + c, peer(k, c, j) * CORES + c) for k, c in places]
        return lax.ppermute(value, ("chip", "core"), pairs)

    def to_section(value, dz, by):
        places = [(i, k) for i in range(sections) for k in range(CHIPS)]
        pairs = [(i * CHIPS + k, (i + by) % sections * CHIPS + (k ^ (dz * COLUMNS))) for i, k in places]
        return lax.ppermute(value, ("section", "chip"), pairs)

    def to_expert(block, de):
        if de == 0:
            return block
        return lax.ppermute(block, "expert", [(i, (i + de) % experts) for i in range(experts)])

    def to_core(value):
        return lax.ppermute(value, "core", [(i, i ^ 1) for i in range(CORES)])

    def returned(block, dy, de):
        if dy == 0 and de == 0:
            return block
        places = [(k, e) for k in range(CHIPS) for e in range(experts)]
        pairs = [(k * experts + (e + de) % experts, (k ^ dy) * experts + e) for k, e in places]
        return lax.ppermute(block, ("chip", "expert"), pairs)

    def to_chips(blocks):
        return [blocks[0]] + [to_chip(blocks[dk], dk) for dk in range(1, CHIPS)]

    args = [a[0].T for a in (forward_route, forward_gates, backward_route, backward_gates)]
    gu, down_rows, saved = gate_up_weight[0, 0], down_weight[0, 0], saved_projections[0, 0]
    far = [to_core(gu), to_core(down_rows)]
    tokens_here = to_chips(dispatch(args + [forward_input[0], backward_cotangent[0]], experts))
    others = pick(tokens_here, (*range(1, experts),), experts, capacity, topk, "pick_others")
    rows_here = [to_expert(others[de - 1], de) for de in range(1, experts)]
    rows_here = [*pick(tokens_here, (0,), experts, capacity, topk, "pick_own"), *rows_here]
    near, turned, (mine, theirs) = hold(gu, down_rows, saved, far, experts, capacity)
    parts = [to_chip(part, j) for j, part in zip(FAR_FIRST, up(rows_here, turned, FAR_FIRST, jnp.bfloat16, "up_others"))]
    parts = [*up(rows_here, turned, (0,), jnp.float32, "up_own"), *parts]
    units = act(parts, mine, to_core(theirs))
    results = down(to_chips([units] * CHIPS), near, far, experts)
    steps = [(dy, de) for dy in range(COLUMNS) for de in range(experts)][::-1]
    results = [returned(result, *step) for result, step in zip(results, steps)]
    outs = combine(*plan(tokens_here, experts, capacity, topk), results)
    steps = range(ROWS)
    if sections == 2:
        joined = [to_section(out, dz, 1) for out, dz in zip(outs, steps)]
    else:
        joined = [to_section(out[:tokens], dz, 1) for out, dz in zip(outs, steps)]
        joined += [to_section(out[tokens:], dz, -1) for out, dz in zip(outs, steps)]
    next_input, prior_gradient = join(joined, tokens)
    return next_input[None], prior_gradient[None]


def solution(mesh):
    pipes, experts = mesh.devices.shape
    axes = ("section", "chip", "core", "expert")
    mesh = Mesh(mesh.devices.reshape(pipes // GROUP, CHIPS, CORES, experts), axes)
    rows = P(axes[:3], "expert", None)
    weights = P(axes[:3], "expert", None, None)
    return jax.shard_map(
        on_device,
        mesh=mesh,
        in_specs=(rows,) * 6 + (weights,) * 3,
        out_specs=(rows, rows),
        check_vma=False,
    )
```

```python
import functools

import jax
import jax.numpy as jnp
from jax import lax
from jax.experimental import pallas as pl
from jax.experimental.pallas import tpu as pltpu
from jax.sharding import Mesh
from jax.sharding import PartitionSpec as P

GROUP = 8
CORES = 2
CHIPS = GROUP // CORES
COLUMNS = 2
ROWS = CHIPS // COLUMNS
FAR_FIRST = (CHIPS - 1, *range(1, CHIPS - 1))
TILE = 16
NT = (((1,), (1,)), ((), ()))
NN = (((1,), (0,)), ((), ()))
TN = (((0,), (0,)), ((), ()))


def round_up(value, step):
    return (value + step - 1) // step * step


def dot(a, b, dims=NN):
    return lax.dot_general(a, b, dims, preferred_element_type=jnp.float32)


def iota(shape, axis):
    return lax.broadcasted_iota(jnp.int32, shape, axis)


def place():
    return lax.axis_index("chip"), lax.axis_index("core"), lax.axis_index("expert")


def peer(chip, core, j):
    if isinstance(core, int):
        return chip ^ (CHIPS - 1 - j if core == 1 and 0 < j < CHIPS - 1 else j)
    return chip ^ (jnp.where(core == 1, CHIPS - 1 - j, j) if 0 < j < CHIPS - 1 else j)


def block_of(index, size):
    return pl.ds(pl.multiple_of(index * size, size), size)


def pinned(array, memory):
    return array if memory is None else pltpu.with_memory_space_constraint(array, memory)


def call(kernel, outs, *args, scratch=(), flops=0, name=None, far=(), near=()):
    size = sum(a.size * a.dtype.itemsize for a in args)
    size += sum(o.size * o.dtype.itemsize for o in jax.tree.leaves(outs))
    spec = pl.BlockSpec(memory_space=pltpu.VMEM)
    return pl.pallas_call(
        kernel,
        out_shape=outs,
        in_specs=[pl.BlockSpec(memory_space=pl.ANY) if i in far else spec for i in range(len(args))],
        out_specs=jax.tree.map(lambda _: spec, outs),
        scratch_shapes=scratch,
        compiler_params=pltpu.CompilerParams(vmem_limit_bytes=16 * 2**20),
        cost_estimate=pl.CostEstimate(flops=flops, bytes_accessed=size, transcendentals=0),
        name=name,
    )(*(pinned(a, pltpu.HBM if i in far else pltpu.VMEM if i in near else None) for i, a in enumerate(args)))


def shape(dims, dtype=jnp.bfloat16):
    return jax.ShapeDtypeStruct(dims, dtype)


def group_rows(capacity):
    return round_up(ROWS * capacity, 8)


def slot_rows(capacity):
    return COLUMNS * group_rows(capacity)


def first_row(chip, capacity):
    return (chip % COLUMNS) * group_rows(capacity) + (chip // COLUMNS) * capacity


def dispatch_kernel(experts, *refs):
    far, outs, near, ready = refs[:6], refs[6 : 6 + CHIPS], refs[6 + CHIPS : -1], refs[-1]
    chip, core, _ = place()
    tokens, width = far[4].shape
    wide = width // CHIPS
    jobs = [(far[i], near[i]) for i in range(4)]
    for dk in range(CHIPS):
        for at in range(2):
            block = outs[dk].at[at * tokens : (at + 1) * tokens, :wide]
            jobs.append((far[4 + at].at[:, block_of(peer(chip, core, dk), wide)], block))
    copies = [pltpu.make_async_copy(*job, ready.at[i]) for i, job in enumerate(jobs)]
    for copy in copies:
        copy.start()
    for copy in copies[:4]:
        copy.wait()
    for at in range(2):
        route, gate = near[2 * at][...], near[2 * at + 1][...]
        topk = route.shape[0]
        earlier = (iota((tokens, tokens), 0) < iota((tokens, tokens), 1)).astype(jnp.float32)
        rank = jnp.zeros((topk, tokens), jnp.float32)
        for e in range(experts):
            named = (route == e).astype(jnp.float32)
            count = jnp.broadcast_to(jnp.sum(named, axis=0, keepdims=True), (8, tokens))
            rank = rank + named * dot(count, earlier)[:1]
        high = gate.astype(jnp.bfloat16).astype(jnp.float32)
        middle = (gate - high).astype(jnp.bfloat16).astype(jnp.float32)
        low = gate - high - middle
        table = jnp.zeros((128, tokens), jnp.float32)
        for part, value in enumerate((route.astype(jnp.float32), rank, high, middle, low)):
            for kk in range(topk):
                row = jnp.broadcast_to(value[kk : kk + 1], (128, tokens))
                table = jnp.where(iota((128, tokens), 0) == part * topk + kk, row, table)
        same = (iota((tokens, tokens), 0) == iota((tokens, tokens), 1)).astype(jnp.bfloat16)
        note = dot(same, table.astype(jnp.bfloat16), NT).astype(jnp.bfloat16)
        for dk in range(CHIPS):
            outs[dk][at * tokens : (at + 1) * tokens, wide:] = note
    for copy in copies[4:]:
        copy.wait()


def stash(experts, capacity, core, expert, saved, mine, theirs):
    rows = slot_rows(capacity)
    dims = (rows * experts, saved.shape[0])
    row, column = iota(dims, 0), iota(dims, 1)
    for target, ref in ((1 - core, theirs), (core, mine)):
        wanted = jnp.full(dims, -1, jnp.int32)
        for de in range(experts):
            for at in range(CHIPS):
                source = (at * CORES + target) * experts + lax.rem(expert + experts - de, experts)
                low = de * rows + first_row(at, capacity)
                inside = jnp.logical_and(row >= low, row < low + capacity)
                wanted = jnp.where(inside, row + (source * capacity - low), wanted)
        pick = jnp.where(column == wanted, 1.0, 0.0).astype(jnp.bfloat16)
        ref[...] = dot(pick, saved[...]).astype(jnp.bfloat16)


def dispatch(args, experts):
    tokens, wide = args[4].shape[0], args[4].shape[1] // CHIPS
    return call(
        functools.partial(dispatch_kernel, experts),
        [shape((2 * tokens, wide + 128)) for _ in range(CHIPS)],
        *args,
        scratch=[pltpu.VMEM(a.shape, a.dtype) for a in args[:4]] + [pltpu.SemaphoreType.DMA((4 + 2 * CHIPS,))],
        name="dispatch",
        far=range(6),
    )


def pick_kernel(shifts, experts, capacity, topk, *refs):
    blocks, outs = refs[:CHIPS], refs[CHIPS:]
    chip, core, expert = place()
    wide = outs[0].shape[1]
    rows = outs[0].shape[0] // 2
    tokens = blocks[0].shape[0] // 2
    lane = iota((CHIPS * tokens, rows), 1).astype(jnp.float32)
    for at in range(2):
        span = slice(at * tokens, (at + 1) * tokens)
        left = jnp.concatenate([b[span, :wide] for b in blocks], axis=0)
        notes = [b[span, wide:].astype(jnp.float32) for b in blocks]
        for out, de in zip(outs, shifts):
            here = lax.rem(expert + de, experts).astype(jnp.float32)
            choice = jnp.zeros((CHIPS * tokens, rows), jnp.float32)
            for kk in range(topk):
                targets = []
                for j, note in enumerate(notes):
                    route, rank = note[:, kk : kk + 1], note[:, topk + kk : topk + kk + 1]
                    first = first_row(peer(chip, core, j), capacity).astype(jnp.float32)
                    targets.append(jnp.where(route == here, rank + first, -1.0))
                choice += jnp.where(lane == jnp.concatenate(targets, axis=0), 1.0, 0.0)
            picked = dot(choice.astype(jnp.bfloat16), left, TN)
            out[at * rows : (at + 1) * rows] = picked.astype(jnp.bfloat16)


def pick(blocks, shifts, experts, capacity, topk, name):
    wide = blocks[0].shape[1] - 128
    outs = [shape((2 * slot_rows(capacity), wide)) for _ in shifts]
    kernel = functools.partial(pick_kernel, shifts, experts, capacity, topk)
    return call(kernel, outs, *blocks, name=name)


def hold_kernel(experts, capacity, gu, down, saved, gu_far, down_far, *refs):
    gu_near, down_near, gu_turned, down_turned, mine, theirs, near_saved, ready = refs
    _, core, expert = place()
    jobs = ((saved, near_saved), (gu, gu_near), (down, down_near))
    copies = [pltpu.make_async_copy(*job, ready.at[i]) for i, job in enumerate(jobs)]
    for copy in copies:
        copy.start()

    def turn(source, target, first):
        step = source.shape[0] // 8
        for i in range(8):
            span = slice(i * step, (i + 1) * step)
            target[first : first + source.shape[1], span] = source[span, :].T

    half = gu.shape[1]
    turn(gu_far, gu_turned, half)
    turn(down_far, down_turned, half)
    copies[0].wait()
    stash(experts, capacity, core, expert, near_saved, mine, theirs)
    copies[1].wait()
    turn(gu_near, gu_turned, 0)
    copies[2].wait()
    turn(down_near, down_turned, 0)


def hold(gu, down, saved, far, experts, capacity):
    stashed = shape((slot_rows(capacity) * experts, saved.shape[1]))
    turned = [shape((CORES * w.shape[1], w.shape[0])) for w in (gu, down)]
    results = call(
        functools.partial(hold_kernel, experts, capacity),
        [shape(gu.shape), shape(down.shape), *turned, stashed, stashed],
        gu,
        down,
        saved,
        *far,
        scratch=[pltpu.VMEM(saved.shape, saved.dtype), pltpu.SemaphoreType.DMA((3,))],
        name="hold",
        far=range(3),
        near=(3, 4),
    )
    return results[:2], results[2:4], results[4:]


def unit_rows(part, chip, units):
    return pl.ds(pl.multiple_of((part * CHIPS + chip) * units, units), units)


def up_kernel(experts, steps, *refs):
    blocks, turned, outs = refs[:experts], refs[experts : experts + 2], refs[experts + 2 :]
    chip, core, _ = place()
    half = turned[0].shape[0] // CORES
    units = turned[1].shape[1] // CHIPS
    rows = blocks[0].shape[0] // 2

    def left(at):
        sides = [
            jnp.concatenate([b[at * rows : (at + 1) * rows, block_of(side, half)] for b in blocks], axis=0)
            for side in (core, 1 - core)
        ]
        return jnp.concatenate(sides, axis=1)

    lefts = [left(at) for at in range(2)]
    for out, j in zip(outs, steps):
        for part in range(3):
            which, piece = divmod(part, 2)
            span = unit_rows(piece, peer(chip, core, j), units)
            out[:, part * units : (part + 1) * units] = dot(lefts[which], turned[which][:, span]).astype(out.dtype)


def up(blocks, turned, steps, dtype, name):
    experts = len(blocks)
    rows = blocks[0].shape[0] // 2 * experts
    width = (turned[0].shape[1] + turned[1].shape[1]) // CHIPS
    outs = [shape((rows, width), dtype) for _ in steps]
    flops = 2 * rows * width * turned[0].shape[0] * len(steps)
    return call(functools.partial(up_kernel, experts, steps), outs, *blocks, *turned, flops=flops, name=name)


def act_kernel(*refs):
    parts, (mine, theirs, out) = refs[:CHIPS], refs[CHIPS:]
    _, core, _ = place()
    total = parts[0][...]
    for part in parts[1:]:
        total = total + part[...].astype(jnp.float32)
    units = total.shape[1] // 3
    gate_pre, up_pre, hidden_grad = total[:, :units], total[:, units : 2 * units], total[:, 2 * units :]
    out[:, :units] = (gate_pre * jax.nn.sigmoid(gate_pre) * up_pre).astype(jnp.bfloat16)
    half = units // CORES
    own, other = mine[...].astype(jnp.float32), theirs[...].astype(jnp.float32)
    low, high = jnp.where(core == 0, own, other), jnp.where(core == 0, other, own)
    for at, saved in enumerate((low, high)):
        gate_pre, up_pre = saved[:, :half], saved[:, half:]
        sig = jax.nn.sigmoid(gate_pre)
        grad = hidden_grad[:, at * half : (at + 1) * half]
        first = units + at * half
        out[:, first : first + half] = (grad * up_pre * (sig * (1.0 + gate_pre * (1.0 - sig)))).astype(jnp.bfloat16)
        out[:, first + units : first + units + half] = (grad * (gate_pre * sig)).astype(jnp.bfloat16)


def act(parts, mine, theirs):
    return call(act_kernel, shape(parts[0].shape), *parts, mine, theirs, name="act")


DOWN_TERMS = ((1, ((0, 0),)), (0, ((1, 0), (2, 1))))


def down_terms(parts, peers, weights, at, total):
    which, terms = DOWN_TERMS[at]
    weight = weights[which]
    units = weights[1].shape[0] // CHIPS
    for part_ref, chip in zip(parts, peers):
        for piece, part in terms:
            left = part_ref[:, piece * units : (piece + 1) * units]
            term = dot(left, weight[unit_rows(part, chip, units), :])
            total = term if total is None else total + term
    return total


def down_own_kernel(part, *refs):
    sides, out = (refs[:2], refs[2:4]), refs[4]
    chip, _, _ = place()
    for side, weights in enumerate(sides):
        for at in range(2):
            out[2 * side + at] = down_terms((part,), (chip,), weights, at, None)


def down_own(part, near, far):
    out = shape((4, part.shape[0], near[0].shape[1]), jnp.float32)
    flops = part.shape[0] * (near[0].size + near[1].size)
    return call(down_own_kernel, out, part, *near, *far, flops=flops, name="down_own", near=(3, 4))


def down_kernel(experts, own, *refs):
    parts, sides, outs = refs[: CHIPS - 1], (refs[CHIPS - 1 : CHIPS + 1], refs[CHIPS + 1 : CHIPS + 3]), refs[CHIPS + 3 :]
    outs = outs[::-1]
    chip, core, _ = place()
    half = sides[0][0].shape[1]
    rows = parts[0].shape[0] // experts
    group = rows // COLUMNS
    low = chip % COLUMNS == 0
    peers = [peer(chip, core, j) for j in range(1, CHIPS)]
    for side, column in ((0, core), (1, 1 - core)):
        totals = [down_terms(parts, peers, sides[side], at, own[2 * side + at]) for at in range(2)]
        for de in range(experts):
            first = de * rows
            lower = jnp.concatenate([t[first : first + group] for t in totals], axis=0).astype(jnp.bfloat16)
            upper = jnp.concatenate([t[first + group : first + rows] for t in totals], axis=0).astype(jnp.bfloat16)
            outs[de][:, block_of(column, half)] = jnp.where(low, lower, upper)
            outs[experts + de][:, block_of(column, half)] = jnp.where(low, upper, lower)


def down(own, parts, near, far, experts):
    rows = parts[0].shape[0] // experts
    outs = [shape((2 * rows // COLUMNS, CORES * near[0].shape[1])) for _ in range(COLUMNS * experts)]
    flops = 3 * parts[0].shape[0] * (near[0].size + near[1].size)
    kernel = functools.partial(down_kernel, experts)
    return call(kernel, outs, own, *parts, *near, *far, flops=flops, name="down", near=(CHIPS + 2, CHIPS + 3))


def plan_kernel(experts, capacity, topk, group, *refs):
    blocks, (choices, gates) = refs[:CHIPS], refs[CHIPS:]
    chip, core, expert = place()
    tokens, wide = blocks[0].shape[0] // 2, blocks[0].shape[1] - 128
    count = 2 * ROWS * tokens
    lane = iota((count, 2 * group), 1).astype(jnp.float32)
    own = blocks[0][:, wide:].astype(jnp.float32)
    other = jnp.where(core == 0, blocks[2][:, wide:].astype(jnp.float32), blocks[1][:, wide:].astype(jnp.float32))
    notes, firsts = [], []
    for dz, note in enumerate((own, other)):
        for at in range(2):
            notes.append(note[at * tokens : (at + 1) * tokens])
            firsts.append((((chip // COLUMNS) ^ dz) * capacity + at * group).astype(jnp.float32))
    for kk in range(topk):
        for de in range(experts):
            here = lax.rem(expert + de, experts).astype(jnp.float32)
            targets = []
            for note, first in zip(notes, firsts):
                route, rank = note[:, kk : kk + 1], note[:, topk + kk : topk + kk + 1]
                targets.append(jnp.where(route == here, rank + first, -1.0))
            choice = jnp.where(lane == jnp.concatenate(targets, axis=0), 1.0, 0.0)
            choices[kk * experts + de] = choice.astype(jnp.bfloat16)
        terms = []
        for note in notes:
            part = [note[:, i * topk + kk : i * topk + kk + 1] for i in (2, 3, 4)]
            terms.append(part[0] + part[1] + part[2])
        gates[kk] = jnp.broadcast_to(jnp.concatenate(terms, axis=0), (count, 128))


def plan(blocks, experts, capacity, topk):
    group = group_rows(capacity)
    count = ROWS * blocks[0].shape[0]
    outs = [shape((topk * experts, count, 2 * group)), shape((topk, count, 128), jnp.float32)]
    return call(functools.partial(plan_kernel, experts, capacity, topk, group), outs, *blocks, name="plan")


def combine_kernel(experts, choices, gates, *refs):
    results, outs = refs[: COLUMNS * experts][::-1], refs[COLUMNS * experts :]
    chip, _, _ = place()
    wide = results[0].shape[1]
    rows = outs[0].shape[0]
    for dy in range(COLUMNS):
        total = None
        for kk in range(gates.shape[0]):
            found = None
            for de in range(experts):
                term = dot(choices[kk * experts + de], results[dy * experts + de][...])
                found = term if found is None else found + term
            term = found * gates[kk][:, :1]
            total = term if total is None else total + term
        total = total.astype(jnp.bfloat16)
        for dz in range(ROWS):
            outs[dz][:, block_of((chip % COLUMNS) ^ dy, wide)] = total[dz * rows : (dz + 1) * rows]


def combine(choices, gates, results):
    experts = len(results) // COLUMNS
    outs = [shape((choices.shape[1] // ROWS, COLUMNS * results[0].shape[1])) for _ in range(ROWS)]
    return call(functools.partial(combine_kernel, experts), outs, choices, gates, *results, name="combine")


def join_kernel(count, *refs):
    chip, _, _ = place()
    blocks, outs, ready = refs[:count], refs[count:-1], refs[-1]
    tokens, wide = outs[0].shape[0], blocks[0].shape[1]
    copies = []
    for at, out in enumerate(outs):
        for dz in range(ROWS):
            block = blocks[dz + at * (count - ROWS)]
            first = at * tokens if count == ROWS else 0
            target = out.at[:, block_of((chip // COLUMNS) ^ dz, wide)]
            copies.append(pltpu.make_async_copy(block.at[first : first + tokens], target, ready.at[at, dz]))
            copies[-1].start()
    for copy in copies:
        copy.wait()


def join(blocks, tokens):
    out = shape((tokens, ROWS * blocks[0].shape[1]))
    count = len(blocks)
    return pl.pallas_call(
        functools.partial(join_kernel, count),
        out_shape=[out, out],
        in_specs=[pl.BlockSpec(memory_space=pltpu.VMEM)] * count,
        out_specs=[pl.BlockSpec(memory_space=pl.ANY)] * 2,
        scratch_shapes=[pltpu.SemaphoreType.DMA((2, ROWS))],
        compiler_params=pltpu.CompilerParams(vmem_limit_bytes=16 * 2**20),
        cost_estimate=pl.CostEstimate(flops=0, bytes_accessed=8 * out.size, transcendentals=0),
        name="join",
    )(*blocks)


def on_device(
    forward_input,
    forward_route,
    forward_gates,
    backward_cotangent,
    backward_route,
    backward_gates,
    gate_up_weight,
    down_weight,
    saved_projections,
):
    sections = lax.axis_size("section")
    experts = lax.axis_size("expert")
    topk = forward_route.shape[2]
    capacity = saved_projections.shape[2] // (GROUP * experts)
    tokens = forward_route.shape[1]

    def to_chip(value, j):
        places = [(k, c) for k in range(CHIPS) for c in range(CORES)]
        pairs = [(k * CORES + c, peer(k, c, j) * CORES + c) for k, c in places]
        return lax.ppermute(value, ("chip", "core"), pairs)

    def to_section(value, dz, by):
        places = [(i, k) for i in range(sections) for k in range(CHIPS)]
        pairs = [(i * CHIPS + k, (i + by) % sections * CHIPS + (k ^ (dz * COLUMNS))) for i, k in places]
        return lax.ppermute(value, ("section", "chip"), pairs)

    def to_expert(block, de):
        if de == 0:
            return block
        return lax.ppermute(block, "expert", [(i, (i + de) % experts) for i in range(experts)])

    def to_core(value):
        return lax.ppermute(value, "core", [(i, i ^ 1) for i in range(CORES)])

    def returned(block, dy, de):
        if dy == 0 and de == 0:
            return block
        places = [(k, e) for k in range(CHIPS) for e in range(experts)]
        pairs = [(k * experts + (e + de) % experts, (k ^ dy) * experts + e) for k, e in places]
        return lax.ppermute(block, ("chip", "expert"), pairs)

    def to_chips(blocks):
        return [blocks[0]] + [to_chip(blocks[dk], dk) for dk in range(1, CHIPS)]

    args = [a[0].T for a in (forward_route, forward_gates, backward_route, backward_gates)]
    gu, down_rows, saved = gate_up_weight[0, 0], down_weight[0, 0], saved_projections[0, 0]
    far = [to_core(gu), to_core(down_rows)]
    tokens_here = to_chips(dispatch(args + [forward_input[0], backward_cotangent[0]], experts))
    others = pick(tokens_here, (*range(1, experts),), experts, capacity, topk, "pick_others")
    rows_here = [to_expert(others[de - 1], de) for de in range(1, experts)]
    rows_here = [*pick(tokens_here, (0,), experts, capacity, topk, "pick_own"), *rows_here]
    near, turned, (mine, theirs) = hold(gu, down_rows, saved, far, experts, capacity)
    parts = [to_chip(part, j) for j, part in zip(FAR_FIRST, up(rows_here, turned, FAR_FIRST, jnp.bfloat16, "up_others"))]
    parts = [*up(rows_here, turned, (0,), jnp.float32, "up_own"), *parts]
    units = act(parts, mine, to_core(theirs))
    others = [to_chip(units, j) for j in range(1, CHIPS)]
    results = down(down_own(units, near, far), others, near, far, experts)
    steps = [(dy, de) for dy in range(COLUMNS) for de in range(experts)][::-1]
    results = [returned(result, *step) for result, step in zip(results, steps)]
    outs = combine(*plan(tokens_here, experts, capacity, topk), results)
    steps = range(ROWS)
    if sections == 2:
        joined = [to_section(out, dz, 1) for out, dz in zip(outs, steps)]
    else:
        joined = [to_section(out[:tokens], dz, 1) for out, dz in zip(outs, steps)]
        joined += [to_section(out[tokens:], dz, -1) for out, dz in zip(outs, steps)]
    next_input, prior_gradient = join(joined, tokens)
    return next_input[None], prior_gradient[None]


def solution(mesh):
    pipes, experts = mesh.devices.shape
    axes = ("section", "chip", "core", "expert")
    mesh = Mesh(mesh.devices.reshape(pipes // GROUP, CHIPS, CORES, experts), axes)
    rows = P(axes[:3], "expert", None)
    weights = P(axes[:3], "expert", None, None)
    return jax.shard_map(
        on_device,
        mesh=mesh,
        in_specs=(rows,) * 6 + (weights,) * 3,
        out_specs=(rows, rows),
        check_vma=False,
    )
```

```python
import functools

import jax
import jax.numpy as jnp
from jax import lax
from jax.experimental import pallas as pl
from jax.experimental.pallas import tpu as pltpu
from jax.sharding import Mesh
from jax.sharding import PartitionSpec as P

GROUP = 8
CORES = 2
CHIPS = GROUP // CORES
COLUMNS = 2
ROWS = CHIPS // COLUMNS
FAR_FIRST = (CHIPS - 1, *range(1, CHIPS - 1))
TILE = 16
NT = (((1,), (1,)), ((), ()))
NN = (((1,), (0,)), ((), ()))
TN = (((0,), (0,)), ((), ()))


def round_up(value, step):
    return (value + step - 1) // step * step


def dot(a, b, dims=NN):
    return lax.dot_general(a, b, dims, preferred_element_type=jnp.float32)


def iota(shape, axis):
    return lax.broadcasted_iota(jnp.int32, shape, axis)


def place():
    return lax.axis_index("chip"), lax.axis_index("core"), lax.axis_index("expert")


def peer(chip, core, j):
    if isinstance(core, int):
        return chip ^ (CHIPS - 1 - j if core == 1 and 0 < j < CHIPS - 1 else j)
    return chip ^ (jnp.where(core == 1, CHIPS - 1 - j, j) if 0 < j < CHIPS - 1 else j)


def block_of(index, size):
    return pl.ds(pl.multiple_of(index * size, size), size)


def pinned(array, memory):
    return array if memory is None else pltpu.with_memory_space_constraint(array, memory)


def call(kernel, outs, *args, scratch=(), flops=0, name=None, far=(), near=()):
    size = sum(a.size * a.dtype.itemsize for a in args)
    size += sum(o.size * o.dtype.itemsize for o in jax.tree.leaves(outs))
    spec = pl.BlockSpec(memory_space=pltpu.VMEM)
    return pl.pallas_call(
        kernel,
        out_shape=outs,
        in_specs=[pl.BlockSpec(memory_space=pl.ANY) if i in far else spec for i in range(len(args))],
        out_specs=jax.tree.map(lambda _: spec, outs),
        scratch_shapes=scratch,
        compiler_params=pltpu.CompilerParams(vmem_limit_bytes=16 * 2**20),
        cost_estimate=pl.CostEstimate(flops=flops, bytes_accessed=size, transcendentals=0),
        name=name,
    )(*(pinned(a, pltpu.HBM if i in far else pltpu.VMEM if i in near else None) for i, a in enumerate(args)))


def shape(dims, dtype=jnp.bfloat16):
    return jax.ShapeDtypeStruct(dims, dtype)


def group_rows(capacity):
    return round_up(ROWS * capacity, 8)


def slot_rows(capacity):
    return COLUMNS * group_rows(capacity)


def first_row(chip, capacity):
    return (chip % COLUMNS) * group_rows(capacity) + (chip // COLUMNS) * capacity


def dispatch_kernel(experts, *refs):
    far, outs, near, ready = refs[:6], refs[6 : 6 + CHIPS], refs[6 + CHIPS : -1], refs[-1]
    chip, core, _ = place()
    tokens, width = far[4].shape
    wide = width // CHIPS
    jobs = [(far[i], near[i]) for i in range(4)]
    for dk in range(CHIPS):
        for at in range(2):
            block = outs[dk].at[at * tokens : (at + 1) * tokens, :wide]
            jobs.append((far[4 + at].at[:, block_of(peer(chip, core, dk), wide)], block))
    copies = [pltpu.make_async_copy(*job, ready.at[i]) for i, job in enumerate(jobs)]
    for copy in copies:
        copy.start()
    for copy in copies[:4]:
        copy.wait()
    for at in range(2):
        route, gate = near[2 * at][...], near[2 * at + 1][...]
        topk = route.shape[0]
        earlier = (iota((tokens, tokens), 0) < iota((tokens, tokens), 1)).astype(jnp.float32)
        rank = jnp.zeros((topk, tokens), jnp.float32)
        for e in range(experts):
            named = (route == e).astype(jnp.float32)
            count = jnp.broadcast_to(jnp.sum(named, axis=0, keepdims=True), (8, tokens))
            rank = rank + named * dot(count, earlier)[:1]
        high = gate.astype(jnp.bfloat16).astype(jnp.float32)
        middle = (gate - high).astype(jnp.bfloat16).astype(jnp.float32)
        low = gate - high - middle
        table = jnp.zeros((128, tokens), jnp.float32)
        for part, value in enumerate((route.astype(jnp.float32), rank, high, middle, low)):
            for kk in range(topk):
                row = jnp.broadcast_to(value[kk : kk + 1], (128, tokens))
                table = jnp.where(iota((128, tokens), 0) == part * topk + kk, row, table)
        same = (iota((tokens, tokens), 0) == iota((tokens, tokens), 1)).astype(jnp.bfloat16)
        note = dot(same, table.astype(jnp.bfloat16), NT).astype(jnp.bfloat16)
        for dk in range(CHIPS):
            outs[dk][at * tokens : (at + 1) * tokens, wide:] = note
    for copy in copies[4:]:
        copy.wait()


def stash(experts, capacity, core, expert, saved, mine, theirs):
    rows = slot_rows(capacity)
    dims = (rows * experts, saved.shape[0])
    row, column = iota(dims, 0), iota(dims, 1)
    for target, ref in ((1 - core, theirs), (core, mine)):
        wanted = jnp.full(dims, -1, jnp.int32)
        for de in range(experts):
            for at in range(CHIPS):
                source = (at * CORES + target) * experts + lax.rem(expert + experts - de, experts)
                low = de * rows + first_row(at, capacity)
                inside = jnp.logical_and(row >= low, row < low + capacity)
                wanted = jnp.where(inside, row + (source * capacity - low), wanted)
        pick = jnp.where(column == wanted, 1.0, 0.0).astype(jnp.bfloat16)
        ref[...] = dot(pick, saved[...]).astype(jnp.bfloat16)


def dispatch(args, experts):
    tokens, wide = args[4].shape[0], args[4].shape[1] // CHIPS
    return call(
        functools.partial(dispatch_kernel, experts),
        [shape((2 * tokens, wide + 128)) for _ in range(CHIPS)],
        *args,
        scratch=[pltpu.VMEM(a.shape, a.dtype) for a in args[:4]] + [pltpu.SemaphoreType.DMA((4 + 2 * CHIPS,))],
        name="dispatch",
        far=range(6),
    )


def pick_kernel(shifts, experts, capacity, topk, *refs):
    blocks, outs = refs[:CHIPS], refs[CHIPS:]
    chip, core, expert = place()
    wide = outs[0].shape[1]
    rows = outs[0].shape[0] // 2
    tokens = blocks[0].shape[0] // 2
    lane = iota((CHIPS * tokens, rows), 1).astype(jnp.float32)
    for at in range(2):
        span = slice(at * tokens, (at + 1) * tokens)
        left = jnp.concatenate([b[span, :wide] for b in blocks], axis=0)
        notes = [b[span, wide:].astype(jnp.float32) for b in blocks]
        for out, de in zip(outs, shifts):
            here = lax.rem(expert + de, experts).astype(jnp.float32)
            choice = jnp.zeros((CHIPS * tokens, rows), jnp.float32)
            for kk in range(topk):
                targets = []
                for j, note in enumerate(notes):
                    route, rank = note[:, kk : kk + 1], note[:, topk + kk : topk + kk + 1]
                    first = first_row(peer(chip, core, j), capacity).astype(jnp.float32)
                    targets.append(jnp.where(route == here, rank + first, -1.0))
                choice += jnp.where(lane == jnp.concatenate(targets, axis=0), 1.0, 0.0)
            picked = dot(choice.astype(jnp.bfloat16), left, TN)
            out[at * rows : (at + 1) * rows] = picked.astype(jnp.bfloat16)


def pick(blocks, shifts, experts, capacity, topk, name):
    wide = blocks[0].shape[1] - 128
    outs = [shape((2 * slot_rows(capacity), wide)) for _ in shifts]
    kernel = functools.partial(pick_kernel, shifts, experts, capacity, topk)
    return call(kernel, outs, *blocks, name=name)


def hold_kernel(experts, capacity, gu, down, saved, gu_far, down_far, *refs):
    gu_near, down_near, gu_turned, down_turned, mine, theirs, near_saved, ready = refs
    _, core, expert = place()
    jobs = ((saved, near_saved), (gu, gu_near), (down, down_near))
    copies = [pltpu.make_async_copy(*job, ready.at[i]) for i, job in enumerate(jobs)]
    for copy in copies:
        copy.start()

    def turn(source, target, first):
        step = source.shape[0] // 8
        for i in range(8):
            span = slice(i * step, (i + 1) * step)
            target[first : first + source.shape[1], span] = source[span, :].T

    half = gu.shape[1]
    turn(gu_far, gu_turned, half)
    turn(down_far, down_turned, half)
    copies[0].wait()
    stash(experts, capacity, core, expert, near_saved, mine, theirs)
    copies[1].wait()
    turn(gu_near, gu_turned, 0)
    copies[2].wait()
    turn(down_near, down_turned, 0)


def hold(gu, down, saved, far, experts, capacity):
    stashed = shape((slot_rows(capacity) * experts, saved.shape[1]))
    turned = [shape((CORES * w.shape[1], w.shape[0])) for w in (gu, down)]
    results = call(
        functools.partial(hold_kernel, experts, capacity),
        [shape(gu.shape), shape(down.shape), *turned, stashed, stashed],
        gu,
        down,
        saved,
        *far,
        scratch=[pltpu.VMEM(saved.shape, saved.dtype), pltpu.SemaphoreType.DMA((3,))],
        name="hold",
        far=range(3),
        near=(3, 4),
    )
    return results[:2], results[2:4], results[4:]


def unit_rows(part, chip, units):
    return pl.ds(pl.multiple_of((part * CHIPS + chip) * units, units), units)


def up_kernel(experts, steps, *refs):
    blocks, turned, outs = refs[:experts], refs[experts : experts + 2], refs[experts + 2 :]
    chip, core, _ = place()
    half = turned[0].shape[0] // CORES
    units = turned[1].shape[1] // CHIPS
    rows = blocks[0].shape[0] // 2

    def left(at):
        sides = [
            jnp.concatenate([b[at * rows : (at + 1) * rows, block_of(side, half)] for b in blocks], axis=0)
            for side in (core, 1 - core)
        ]
        return jnp.concatenate(sides, axis=1)

    lefts = [left(at) for at in range(2)]
    for out, j in zip(outs, steps):
        for part in range(3):
            which, piece = divmod(part, 2)
            span = unit_rows(piece, peer(chip, core, j), units)
            out[:, part * units : (part + 1) * units] = dot(lefts[which], turned[which][:, span]).astype(out.dtype)


def up(blocks, turned, steps, dtype, name):
    experts = len(blocks)
    rows = blocks[0].shape[0] // 2 * experts
    width = (turned[0].shape[1] + turned[1].shape[1]) // CHIPS
    outs = [shape((rows, width), dtype) for _ in steps]
    flops = 2 * rows * width * turned[0].shape[0] * len(steps)
    return call(functools.partial(up_kernel, experts, steps), outs, *blocks, *turned, flops=flops, name=name)


def act_kernel(*refs):
    parts, (mine, theirs, out) = refs[:CHIPS], refs[CHIPS:]
    _, core, _ = place()
    total = parts[0][...]
    for part in parts[1:]:
        total = total + part[...].astype(jnp.float32)
    units = total.shape[1] // 3
    gate_pre, up_pre, hidden_grad = total[:, :units], total[:, units : 2 * units], total[:, 2 * units :]
    out[:, :units] = (gate_pre * jax.nn.sigmoid(gate_pre) * up_pre).astype(jnp.bfloat16)
    half = units // CORES
    own, other = mine[...].astype(jnp.float32), theirs[...].astype(jnp.float32)
    low, high = jnp.where(core == 0, own, other), jnp.where(core == 0, other, own)
    for at, saved in enumerate((low, high)):
        gate_pre, up_pre = saved[:, :half], saved[:, half:]
        sig = jax.nn.sigmoid(gate_pre)
        grad = hidden_grad[:, at * half : (at + 1) * half]
        first = units + at * half
        out[:, first : first + half] = (grad * up_pre * (sig * (1.0 + gate_pre * (1.0 - sig)))).astype(jnp.bfloat16)
        out[:, first + units : first + units + half] = (grad * (gate_pre * sig)).astype(jnp.bfloat16)


def act(parts, mine, theirs):
    return call(act_kernel, shape(parts[0].shape), *parts, mine, theirs, name="act")


DOWN_TERMS = ((1, ((0, 0),)), (0, ((1, 0), (2, 1))))


def down_terms(parts, peers, weights, at, total):
    which, terms = DOWN_TERMS[at]
    weight = weights[which]
    units = weights[1].shape[0] // CHIPS
    for part_ref, chip in zip(parts, peers):
        for piece, part in terms:
            left = part_ref[:, piece * units : (piece + 1) * units]
            term = dot(left, weight[unit_rows(part, chip, units), :])
            total = term if total is None else total + term
    return total


def down_part_kernel(j, part, gu_near, down_near, gu_far, down_far, *refs):
    out = refs[-1]
    chip, core, _ = place()
    for side, weights in enumerate(((gu_near, down_near), (gu_far, down_far))):
        for at in range(2):
            so_far = refs[0][2 * side + at] if len(refs) > 1 else None
            out[2 * side + at] = down_terms((part,), (peer(chip, core, j),), weights, at, so_far)


def down_part(j, part, near, far, *so_far):
    out = shape((4, part.shape[0], near[0].shape[1]), jnp.float32)
    flops = part.shape[0] * (near[0].size + near[1].size)
    kernel = functools.partial(down_part_kernel, j)
    return call(kernel, out, part, *near, *far, *so_far, flops=flops, name="down_part", near=(3, 4))


def down_kernel(experts, so_far, last, *refs):
    sides, outs = (refs[:2], refs[2:4]), refs[4:][::-1]
    chip, core, _ = place()
    half = sides[0][0].shape[1]
    rows = last.shape[0] // experts
    group = rows // COLUMNS
    low = chip % COLUMNS == 0
    for side, column in ((0, core), (1, 1 - core)):
        totals = [
            down_terms((last,), (peer(chip, core, 1),), sides[side], at, so_far[2 * side + at]) for at in range(2)
        ]
        for de in range(experts):
            first = de * rows
            lower = jnp.concatenate([t[first : first + group] for t in totals], axis=0).astype(jnp.bfloat16)
            upper = jnp.concatenate([t[first + group : first + rows] for t in totals], axis=0).astype(jnp.bfloat16)
            outs[de][:, block_of(column, half)] = jnp.where(low, lower, upper)
            outs[experts + de][:, block_of(column, half)] = jnp.where(low, upper, lower)


def down(so_far, last, near, far, experts):
    rows = last.shape[0] // experts
    outs = [shape((2 * rows // COLUMNS, CORES * near[0].shape[1])) for _ in range(COLUMNS * experts)]
    flops = last.shape[0] * (near[0].size + near[1].size)
    kernel = functools.partial(down_kernel, experts)
    return call(kernel, outs, so_far, last, *near, *far, flops=flops, name="down", near=(4, 5))


def plan_kernel(experts, capacity, topk, group, *refs):
    blocks, (choices, gates) = refs[:CHIPS], refs[CHIPS:]
    chip, core, expert = place()
    tokens, wide = blocks[0].shape[0] // 2, blocks[0].shape[1] - 128
    count = 2 * ROWS * tokens
    lane = iota((count, 2 * group), 1).astype(jnp.float32)
    own = blocks[0][:, wide:].astype(jnp.float32)
    other = jnp.where(core == 0, blocks[2][:, wide:].astype(jnp.float32), blocks[1][:, wide:].astype(jnp.float32))
    notes, firsts = [], []
    for dz, note in enumerate((own, other)):
        for at in range(2):
            notes.append(note[at * tokens : (at + 1) * tokens])
            firsts.append((((chip // COLUMNS) ^ dz) * capacity + at * group).astype(jnp.float32))
    for kk in range(topk):
        for de in range(experts):
            here = lax.rem(expert + de, experts).astype(jnp.float32)
            targets = []
            for note, first in zip(notes, firsts):
                route, rank = note[:, kk : kk + 1], note[:, topk + kk : topk + kk + 1]
                targets.append(jnp.where(route == here, rank + first, -1.0))
            choice = jnp.where(lane == jnp.concatenate(targets, axis=0), 1.0, 0.0)
            choices[kk * experts + de] = choice.astype(jnp.bfloat16)
        terms = []
        for note in notes:
            part = [note[:, i * topk + kk : i * topk + kk + 1] for i in (2, 3, 4)]
            terms.append(part[0] + part[1] + part[2])
        gates[kk] = jnp.broadcast_to(jnp.concatenate(terms, axis=0), (count, 128))


def plan(blocks, experts, capacity, topk):
    group = group_rows(capacity)
    count = ROWS * blocks[0].shape[0]
    outs = [shape((topk * experts, count, 2 * group)), shape((topk, count, 128), jnp.float32)]
    return call(functools.partial(plan_kernel, experts, capacity, topk, group), outs, *blocks, name="plan")


def combine_kernel(experts, choices, gates, *refs):
    results, outs = refs[: COLUMNS * experts][::-1], refs[COLUMNS * experts :]
    chip, _, _ = place()
    wide = results[0].shape[1]
    rows = outs[0].shape[0]
    for dy in range(COLUMNS):
        total = None
        for kk in range(gates.shape[0]):
            found = None
            for de in range(experts):
                term = dot(choices[kk * experts + de], results[dy * experts + de][...])
                found = term if found is None else found + term
            term = found * gates[kk][:, :1]
            total = term if total is None else total + term
        total = total.astype(jnp.bfloat16)
        for dz in range(ROWS):
            outs[dz][:, block_of((chip % COLUMNS) ^ dy, wide)] = total[dz * rows : (dz + 1) * rows]


def combine(choices, gates, results):
    experts = len(results) // COLUMNS
    outs = [shape((choices.shape[1] // ROWS, COLUMNS * results[0].shape[1])) for _ in range(ROWS)]
    return call(functools.partial(combine_kernel, experts), outs, choices, gates, *results, name="combine")


def join_kernel(count, *refs):
    chip, _, _ = place()
    blocks, outs, ready = refs[:count], refs[count:-1], refs[-1]
    tokens, wide = outs[0].shape[0], blocks[0].shape[1]
    copies = []
    for at, out in enumerate(outs):
        for dz in range(ROWS):
            block = blocks[dz + at * (count - ROWS)]
            first = at * tokens if count == ROWS else 0
            target = out.at[:, block_of((chip // COLUMNS) ^ dz, wide)]
            copies.append(pltpu.make_async_copy(block.at[first : first + tokens], target, ready.at[at, dz]))
            copies[-1].start()
    for copy in copies:
        copy.wait()


def join(blocks, tokens):
    out = shape((tokens, ROWS * blocks[0].shape[1]))
    count = len(blocks)
    return pl.pallas_call(
        functools.partial(join_kernel, count),
        out_shape=[out, out],
        in_specs=[pl.BlockSpec(memory_space=pltpu.VMEM)] * count,
        out_specs=[pl.BlockSpec(memory_space=pl.ANY)] * 2,
        scratch_shapes=[pltpu.SemaphoreType.DMA((2, ROWS))],
        compiler_params=pltpu.CompilerParams(vmem_limit_bytes=16 * 2**20),
        cost_estimate=pl.CostEstimate(flops=0, bytes_accessed=8 * out.size, transcendentals=0),
        name="join",
    )(*blocks)


def on_device(
    forward_input,
    forward_route,
    forward_gates,
    backward_cotangent,
    backward_route,
    backward_gates,
    gate_up_weight,
    down_weight,
    saved_projections,
):
    sections = lax.axis_size("section")
    experts = lax.axis_size("expert")
    topk = forward_route.shape[2]
    capacity = saved_projections.shape[2] // (GROUP * experts)
    tokens = forward_route.shape[1]

    def to_chip(value, j):
        places = [(k, c) for k in range(CHIPS) for c in range(CORES)]
        pairs = [(k * CORES + c, peer(k, c, j) * CORES + c) for k, c in places]
        return lax.ppermute(value, ("chip", "core"), pairs)

    def to_section(value, dz, by):
        places = [(i, k) for i in range(sections) for k in range(CHIPS)]
        pairs = [(i * CHIPS + k, (i + by) % sections * CHIPS + (k ^ (dz * COLUMNS))) for i, k in places]
        return lax.ppermute(value, ("section", "chip"), pairs)

    def to_expert(block, de):
        if de == 0:
            return block
        return lax.ppermute(block, "expert", [(i, (i + de) % experts) for i in range(experts)])

    def to_core(value):
        return lax.ppermute(value, "core", [(i, i ^ 1) for i in range(CORES)])

    def returned(block, dy, de):
        if dy == 0 and de == 0:
            return block
        places = [(k, e) for k in range(CHIPS) for e in range(experts)]
        pairs = [(k * experts + (e + de) % experts, (k ^ dy) * experts + e) for k, e in places]
        return lax.ppermute(block, ("chip", "expert"), pairs)

    def to_chips(blocks):
        return [blocks[0]] + [to_chip(blocks[dk], dk) for dk in range(1, CHIPS)]

    args = [a[0].T for a in (forward_route, forward_gates, backward_route, backward_gates)]
    gu, down_rows, saved = gate_up_weight[0, 0], down_weight[0, 0], saved_projections[0, 0]
    far = [to_core(gu), to_core(down_rows)]
    tokens_here = to_chips(dispatch(args + [forward_input[0], backward_cotangent[0]], experts))
    others = pick(tokens_here, (*range(1, experts),), experts, capacity, topk, "pick_others")
    rows_here = [to_expert(others[de - 1], de) for de in range(1, experts)]
    rows_here = [*pick(tokens_here, (0,), experts, capacity, topk, "pick_own"), *rows_here]
    near, turned, (mine, theirs) = hold(gu, down_rows, saved, far, experts, capacity)
    parts = [to_chip(part, j) for j, part in zip(FAR_FIRST, up(rows_here, turned, FAR_FIRST, jnp.bfloat16, "up_others"))]
    parts = [*up(rows_here, turned, (0,), jnp.float32, "up_own"), *parts]
    units = act(parts, mine, to_core(theirs))
    others = [to_chip(units, j) for j in range(1, CHIPS)]
    so_far = down_part(0, units, near, far)
    for j in range(CHIPS - 1, 1, -1):
        so_far = down_part(j, others[j - 1], near, far, so_far)
    results = down(so_far, others[0], near, far, experts)
    steps = [(dy, de) for dy in range(COLUMNS) for de in range(experts)][::-1]
    results = [returned(result, *step) for result, step in zip(results, steps)]
    outs = combine(*plan(tokens_here, experts, capacity, topk), results)
    steps = range(ROWS)
    if sections == 2:
        joined = [to_section(out, dz, 1) for out, dz in zip(outs, steps)]
    else:
        joined = [to_section(out[:tokens], dz, 1) for out, dz in zip(outs, steps)]
        joined += [to_section(out[tokens:], dz, -1) for out, dz in zip(outs, steps)]
    next_input, prior_gradient = join(joined, tokens)
    return next_input[None], prior_gradient[None]


def solution(mesh):
    pipes, experts = mesh.devices.shape
    axes = ("section", "chip", "core", "expert")
    mesh = Mesh(mesh.devices.reshape(pipes // GROUP, CHIPS, CORES, experts), axes)
    rows = P(axes[:3], "expert", None)
    weights = P(axes[:3], "expert", None, None)
    return jax.shard_map(
        on_device,
        mesh=mesh,
        in_specs=(rows,) * 6 + (weights,) * 3,
        out_specs=(rows, rows),
        check_vma=False,
    )
```

```python
import functools

import jax
import jax.numpy as jnp
from jax import lax
from jax.experimental import pallas as pl
from jax.experimental.pallas import tpu as pltpu
from jax.sharding import Mesh
from jax.sharding import PartitionSpec as P

GROUP = 8
CORES = 2
CHIPS = GROUP // CORES
COLUMNS = 2
ROWS = CHIPS // COLUMNS
FAR_FIRST = (CHIPS - 1, *range(1, CHIPS - 1))
TILE = 16
NT = (((1,), (1,)), ((), ()))
NN = (((1,), (0,)), ((), ()))
TN = (((0,), (0,)), ((), ()))


def round_up(value, step):
    return (value + step - 1) // step * step


def dot(a, b, dims=NN):
    return lax.dot_general(a, b, dims, preferred_element_type=jnp.float32)


def iota(shape, axis):
    return lax.broadcasted_iota(jnp.int32, shape, axis)


def place():
    return lax.axis_index("chip"), lax.axis_index("core"), lax.axis_index("expert")


def peer(chip, core, j):
    if isinstance(core, int):
        return chip ^ (CHIPS - 1 - j if core == 1 and 0 < j < CHIPS - 1 else j)
    return chip ^ (jnp.where(core == 1, CHIPS - 1 - j, j) if 0 < j < CHIPS - 1 else j)


def block_of(index, size):
    return pl.ds(pl.multiple_of(index * size, size), size)


def pinned(array, memory):
    return array if memory is None else pltpu.with_memory_space_constraint(array, memory)


def call(kernel, outs, *args, scratch=(), flops=0, name=None, far=(), near=()):
    size = sum(a.size * a.dtype.itemsize for a in args)
    size += sum(o.size * o.dtype.itemsize for o in jax.tree.leaves(outs))
    spec = pl.BlockSpec(memory_space=pltpu.VMEM)
    return pl.pallas_call(
        kernel,
        out_shape=outs,
        in_specs=[pl.BlockSpec(memory_space=pl.ANY) if i in far else spec for i in range(len(args))],
        out_specs=jax.tree.map(lambda _: spec, outs),
        scratch_shapes=scratch,
        compiler_params=pltpu.CompilerParams(vmem_limit_bytes=16 * 2**20),
        cost_estimate=pl.CostEstimate(flops=flops, bytes_accessed=size, transcendentals=0),
        name=name,
    )(*(pinned(a, pltpu.HBM if i in far else pltpu.VMEM if i in near else None) for i, a in enumerate(args)))


def shape(dims, dtype=jnp.bfloat16):
    return jax.ShapeDtypeStruct(dims, dtype)


def group_rows(capacity):
    return round_up(ROWS * capacity, 8)


def slot_rows(capacity):
    return COLUMNS * group_rows(capacity)


def first_row(chip, capacity):
    return (chip % COLUMNS) * group_rows(capacity) + (chip // COLUMNS) * capacity


def dispatch_kernel(experts, *refs):
    far, outs, near, ready = refs[:6], refs[6 : 6 + CHIPS], refs[6 + CHIPS : -1], refs[-1]
    chip, core, _ = place()
    tokens, width = far[4].shape
    wide = width // CHIPS
    jobs = [(far[i], near[i]) for i in range(4)]
    for dk in range(CHIPS):
        for at in range(2):
            block = outs[dk].at[at * tokens : (at + 1) * tokens, :wide]
            jobs.append((far[4 + at].at[:, block_of(peer(chip, core, dk), wide)], block))
    copies = [pltpu.make_async_copy(*job, ready.at[i]) for i, job in enumerate(jobs)]
    for copy in copies:
        copy.start()
    for copy in copies[:4]:
        copy.wait()
    for at in range(2):
        route, gate = near[2 * at][...], near[2 * at + 1][...]
        topk = route.shape[0]
        earlier = (iota((tokens, tokens), 0) < iota((tokens, tokens), 1)).astype(jnp.float32)
        rank = jnp.zeros((topk, tokens), jnp.float32)
        for e in range(experts):
            named = (route == e).astype(jnp.float32)
            count = jnp.broadcast_to(jnp.sum(named, axis=0, keepdims=True), (8, tokens))
            rank = rank + named * dot(count, earlier)[:1]
        high = gate.astype(jnp.bfloat16).astype(jnp.float32)
        middle = (gate - high).astype(jnp.bfloat16).astype(jnp.float32)
        low = gate - high - middle
        table = jnp.zeros((128, tokens), jnp.float32)
        for part, value in enumerate((route.astype(jnp.float32), rank, high, middle, low)):
            for kk in range(topk):
                row = jnp.broadcast_to(value[kk : kk + 1], (128, tokens))
                table = jnp.where(iota((128, tokens), 0) == part * topk + kk, row, table)
        same = (iota((tokens, tokens), 0) == iota((tokens, tokens), 1)).astype(jnp.bfloat16)
        note = dot(same, table.astype(jnp.bfloat16), NT).astype(jnp.bfloat16)
        for dk in range(CHIPS):
            outs[dk][at * tokens : (at + 1) * tokens, wide:] = note
    for copy in copies[4:]:
        copy.wait()


def stash(experts, capacity, core, expert, saved, mine, theirs):
    rows = slot_rows(capacity)
    dims = (rows * experts, saved.shape[0])
    row, column = iota(dims, 0), iota(dims, 1)
    for target, ref in ((1 - core, theirs), (core, mine)):
        wanted = jnp.full(dims, -1, jnp.int32)
        for de in range(experts):
            for at in range(CHIPS):
                source = (at * CORES + target) * experts + lax.rem(expert + experts - de, experts)
                low = de * rows + first_row(at, capacity)
                inside = jnp.logical_and(row >= low, row < low + capacity)
                wanted = jnp.where(inside, row + (source * capacity - low), wanted)
        pick = jnp.where(column == wanted, 1.0, 0.0).astype(jnp.bfloat16)
        ref[...] = dot(pick, saved[...]).astype(jnp.bfloat16)


def dispatch(args, experts):
    tokens, wide = args[4].shape[0], args[4].shape[1] // CHIPS
    return call(
        functools.partial(dispatch_kernel, experts),
        [shape((2 * tokens, wide + 128)) for _ in range(CHIPS)],
        *args,
        scratch=[pltpu.VMEM(a.shape, a.dtype) for a in args[:4]] + [pltpu.SemaphoreType.DMA((4 + 2 * CHIPS,))],
        name="dispatch",
        far=range(6),
    )


def pick_kernel(shifts, steps, experts, capacity, topk, *refs):
    blocks, so_far, outs = refs[: len(steps)], refs[len(steps) : -len(shifts)], refs[-len(shifts) :]
    chip, core, expert = place()
    wide = outs[0].shape[1]
    rows = outs[0].shape[0] // 2
    tokens = blocks[0].shape[0] // 2
    lane = iota((len(steps) * tokens, rows), 1).astype(jnp.float32)
    for at in range(2):
        span, target = slice(at * tokens, (at + 1) * tokens), slice(at * rows, (at + 1) * rows)
        left = jnp.concatenate([b[span, :wide] for b in blocks], axis=0)
        notes = [b[span, wide:].astype(jnp.float32) for b in blocks]
        for i, de in enumerate(shifts):
            here = lax.rem(expert + de, experts).astype(jnp.float32)
            choice = jnp.zeros((len(steps) * tokens, rows), jnp.float32)
            for kk in range(topk):
                targets = []
                for j, note in zip(steps, notes):
                    route, rank = note[:, kk : kk + 1], note[:, topk + kk : topk + kk + 1]
                    first = first_row(peer(chip, core, j), capacity).astype(jnp.float32)
                    targets.append(jnp.where(route == here, rank + first, -1.0))
                choice += jnp.where(lane == jnp.concatenate(targets, axis=0), 1.0, 0.0)
            picked = dot(choice.astype(jnp.bfloat16), left, TN)
            if so_far:
                picked = picked + so_far[i][target]
            outs[i][target] = picked.astype(outs[i].dtype)


def pick(blocks, shifts, steps, experts, capacity, topk, name, so_far=(), dtype=jnp.bfloat16):
    wide = blocks[0].shape[1] - 128
    outs = [shape((2 * slot_rows(capacity), wide), dtype) for _ in shifts]
    kernel = functools.partial(pick_kernel, shifts, steps, experts, capacity, topk)
    return call(kernel, outs, *[blocks[j] for j in steps], *so_far, name=name)


def hold_kernel(experts, capacity, gu, down, saved, gu_far, down_far, *refs):
    gu_near, down_near, gu_turned, down_turned, mine, theirs, near_saved, ready = refs
    _, core, expert = place()
    jobs = ((saved, near_saved), (gu, gu_near), (down, down_near))
    copies = [pltpu.make_async_copy(*job, ready.at[i]) for i, job in enumerate(jobs)]
    for copy in copies:
        copy.start()

    def turn(source, target, first):
        step = source.shape[0] // 8
        for i in range(8):
            span = slice(i * step, (i + 1) * step)
            target[first : first + source.shape[1], span] = source[span, :].T

    half = gu.shape[1]
    turn(gu_far, gu_turned, half)
    turn(down_far, down_turned, half)
    copies[0].wait()
    stash(experts, capacity, core, expert, near_saved, mine, theirs)
    copies[1].wait()
    turn(gu_near, gu_turned, 0)
    copies[2].wait()
    turn(down_near, down_turned, 0)


def hold(gu, down, saved, far, experts, capacity):
    stashed = shape((slot_rows(capacity) * experts, saved.shape[1]))
    turned = [shape((CORES * w.shape[1], w.shape[0])) for w in (gu, down)]
    results = call(
        functools.partial(hold_kernel, experts, capacity),
        [shape(gu.shape), shape(down.shape), *turned, stashed, stashed],
        gu,
        down,
        saved,
        *far,
        scratch=[pltpu.VMEM(saved.shape, saved.dtype), pltpu.SemaphoreType.DMA((3,))],
        name="hold",
        far=range(3),
        near=(3, 4),
    )
    return results[:2], results[2:4], results[4:]


def unit_rows(part, chip, units):
    return pl.ds(pl.multiple_of((part * CHIPS + chip) * units, units), units)


def up_kernel(experts, steps, *refs):
    blocks, turned, outs = refs[:experts], refs[experts : experts + 2], refs[experts + 2 :]
    chip, core, _ = place()
    half = turned[0].shape[0] // CORES
    units = turned[1].shape[1] // CHIPS
    rows = blocks[0].shape[0] // 2

    def left(at):
        sides = [
            jnp.concatenate([b[at * rows : (at + 1) * rows, block_of(side, half)] for b in blocks], axis=0)
            for side in (core, 1 - core)
        ]
        return jnp.concatenate(sides, axis=1)

    lefts = [left(at) for at in range(2)]
    for out, j in zip(outs, steps):
        for part in range(3):
            which, piece = divmod(part, 2)
            span = unit_rows(piece, peer(chip, core, j), units)
            out[:, part * units : (part + 1) * units] = dot(lefts[which], turned[which][:, span]).astype(out.dtype)


def up(blocks, turned, steps, dtype, name):
    experts = len(blocks)
    rows = blocks[0].shape[0] // 2 * experts
    width = (turned[0].shape[1] + turned[1].shape[1]) // CHIPS
    outs = [shape((rows, width), dtype) for _ in steps]
    flops = 2 * rows * width * turned[0].shape[0] * len(steps)
    return call(functools.partial(up_kernel, experts, steps), outs, *blocks, *turned, flops=flops, name=name)


def act_kernel(*refs):
    parts, (mine, theirs, out) = refs[:CHIPS], refs[CHIPS:]
    _, core, _ = place()
    total = parts[0][...]
    for part in parts[1:]:
        total = total + part[...].astype(jnp.float32)
    units = total.shape[1] // 3
    gate_pre, up_pre, hidden_grad = total[:, :units], total[:, units : 2 * units], total[:, 2 * units :]
    out[:, :units] = (gate_pre * jax.nn.sigmoid(gate_pre) * up_pre).astype(jnp.bfloat16)
    half = units // CORES
    own, other = mine[...].astype(jnp.float32), theirs[...].astype(jnp.float32)
    low, high = jnp.where(core == 0, own, other), jnp.where(core == 0, other, own)
    for at, saved in enumerate((low, high)):
        gate_pre, up_pre = saved[:, :half], saved[:, half:]
        sig = jax.nn.sigmoid(gate_pre)
        grad = hidden_grad[:, at * half : (at + 1) * half]
        first = units + at * half
        out[:, first : first + half] = (grad * up_pre * (sig * (1.0 + gate_pre * (1.0 - sig)))).astype(jnp.bfloat16)
        out[:, first + units : first + units + half] = (grad * (gate_pre * sig)).astype(jnp.bfloat16)


def act(parts, mine, theirs):
    return call(act_kernel, shape(parts[0].shape), *parts, mine, theirs, name="act")


DOWN_TERMS = ((1, ((0, 0),)), (0, ((1, 0), (2, 1))))


def down_terms(parts, peers, weights, at, total):
    which, terms = DOWN_TERMS[at]
    weight = weights[which]
    units = weights[1].shape[0] // CHIPS
    for part_ref, chip in zip(parts, peers):
        for piece, part in terms:
            left = part_ref[:, piece * units : (piece + 1) * units]
            term = dot(left, weight[unit_rows(part, chip, units), :])
            total = term if total is None else total + term
    return total


def down_part_kernel(j, part, gu_near, down_near, gu_far, down_far, *refs):
    out = refs[-1]
    chip, core, _ = place()
    for side, weights in enumerate(((gu_near, down_near), (gu_far, down_far))):
        for at in range(2):
            so_far = refs[0][2 * side + at] if len(refs) > 1 else None
            out[2 * side + at] = down_terms((part,), (peer(chip, core, j),), weights, at, so_far)


def down_part(j, part, near, far, *so_far):
    out = shape((4, part.shape[0], near[0].shape[1]), jnp.float32)
    flops = part.shape[0] * (near[0].size + near[1].size)
    kernel = functools.partial(down_part_kernel, j)
    return call(kernel, out, part, *near, *far, *so_far, flops=flops, name="down_part", near=(3, 4))


def down_kernel(experts, so_far, last, *refs):
    sides, outs = (refs[:2], refs[2:4]), refs[4:][::-1]
    chip, core, _ = place()
    half = sides[0][0].shape[1]
    rows = last.shape[0] // experts
    group = rows // COLUMNS
    low = chip % COLUMNS == 0
    for side, column in ((0, core), (1, 1 - core)):
        totals = [
            down_terms((last,), (peer(chip, core, 1),), sides[side], at, so_far[2 * side + at]) for at in range(2)
        ]
        for de in range(experts):
            first = de * rows
            lower = jnp.concatenate([t[first : first + group] for t in totals], axis=0).astype(jnp.bfloat16)
            upper = jnp.concatenate([t[first + group : first + rows] for t in totals], axis=0).astype(jnp.bfloat16)
            outs[de][:, block_of(column, half)] = jnp.where(low, lower, upper)
            outs[experts + de][:, block_of(column, half)] = jnp.where(low, upper, lower)


def down(so_far, last, near, far, experts):
    rows = last.shape[0] // experts
    outs = [shape((2 * rows // COLUMNS, CORES * near[0].shape[1])) for _ in range(COLUMNS * experts)]
    flops = last.shape[0] * (near[0].size + near[1].size)
    kernel = functools.partial(down_kernel, experts)
    return call(kernel, outs, so_far, last, *near, *far, flops=flops, name="down", near=(4, 5))


def plan_kernel(experts, capacity, topk, group, *refs):
    blocks, (choices, gates) = refs[:CHIPS], refs[CHIPS:]
    chip, core, expert = place()
    tokens, wide = blocks[0].shape[0] // 2, blocks[0].shape[1] - 128
    count = 2 * ROWS * tokens
    lane = iota((count, 2 * group), 1).astype(jnp.float32)
    own = blocks[0][:, wide:].astype(jnp.float32)
    other = jnp.where(core == 0, blocks[2][:, wide:].astype(jnp.float32), blocks[1][:, wide:].astype(jnp.float32))
    notes, firsts = [], []
    for dz, note in enumerate((own, other)):
        for at in range(2):
            notes.append(note[at * tokens : (at + 1) * tokens])
            firsts.append((((chip // COLUMNS) ^ dz) * capacity + at * group).astype(jnp.float32))
    for kk in range(topk):
        for de in range(experts):
            here = lax.rem(expert + de, experts).astype(jnp.float32)
            targets = []
            for note, first in zip(notes, firsts):
                route, rank = note[:, kk : kk + 1], note[:, topk + kk : topk + kk + 1]
                targets.append(jnp.where(route == here, rank + first, -1.0))
            choice = jnp.where(lane == jnp.concatenate(targets, axis=0), 1.0, 0.0)
            choices[kk * experts + de] = choice.astype(jnp.bfloat16)
        terms = []
        for note in notes:
            part = [note[:, i * topk + kk : i * topk + kk + 1] for i in (2, 3, 4)]
            terms.append(part[0] + part[1] + part[2])
        gates[kk] = jnp.broadcast_to(jnp.concatenate(terms, axis=0), (count, 128))


def plan(blocks, experts, capacity, topk):
    group = group_rows(capacity)
    count = ROWS * blocks[0].shape[0]
    outs = [shape((topk * experts, count, 2 * group)), shape((topk, count, 128), jnp.float32)]
    return call(functools.partial(plan_kernel, experts, capacity, topk, group), outs, *blocks, name="plan")


def found_rows(choices, results, kk, first, experts):
    found = None
    for i, result in enumerate(results):
        term = dot(choices[kk * experts + first + i], result[...])
        found = term if found is None else found + term
    return found


def combine_other_kernel(experts, choices, gates, *refs):
    results, out = refs[:-1][::-1], refs[-1]
    total = None
    for kk in range(gates.shape[0]):
        term = found_rows(choices, results, kk, 0, experts) * gates[kk][:, :1]
        total = term if total is None else total + term
    out[...] = total.astype(jnp.bfloat16)


def combine_own_kernel(experts, choices, result, out):
    for kk in range(out.shape[0]):
        out[kk] = found_rows(choices, [result], kk, 0, experts)


def combine_kernel(experts, choices, gates, other, own, *refs):
    results, outs = refs[: experts - 1][::-1], refs[experts - 1 :]
    chip, _, _ = place()
    wide = other.shape[1]
    rows = outs[0].shape[0]
    total = None
    for kk in range(gates.shape[0]):
        term = (own[kk] + found_rows(choices, results, kk, 1, experts)) * gates[kk][:, :1]
        total = term if total is None else total + term
    total = total.astype(jnp.bfloat16)
    for dz in range(ROWS):
        span = slice(dz * rows, (dz + 1) * rows)
        outs[dz][:, block_of(chip % COLUMNS, wide)] = total[span]
        outs[dz][:, block_of((chip % COLUMNS) ^ 1, wide)] = other[span]


def combine(choices, gates, results):
    experts = len(results) // COLUMNS
    count, wide = choices.shape[1], results[0].shape[1]
    kernel = functools.partial(combine_other_kernel, experts)
    other = call(kernel, shape((count, wide)), choices, gates, *results[:experts], name="combine_other")
    kernel = functools.partial(combine_own_kernel, experts)
    out = shape((gates.shape[0], count, wide), jnp.float32)
    own = call(kernel, out, choices, results[-1], name="combine_own")
    outs = [shape((count // ROWS, COLUMNS * wide)) for _ in range(ROWS)]
    kernel = functools.partial(combine_kernel, experts)
    return call(kernel, outs, choices, gates, other, own, *results[experts:-1], name="combine")


def join_kernel(count, *refs):
    chip, _, _ = place()
    blocks, outs, ready = refs[:count], refs[count:-1], refs[-1]
    tokens, wide = outs[0].shape[0], blocks[0].shape[1]
    copies = []
    for at, out in enumerate(outs):
        for dz in range(ROWS):
            block = blocks[dz + at * (count - ROWS)]
            first = at * tokens if count == ROWS else 0
            target = out.at[:, block_of((chip // COLUMNS) ^ dz, wide)]
            copies.append(pltpu.make_async_copy(block.at[first : first + tokens], target, ready.at[at, dz]))
            copies[-1].start()
    for copy in copies:
        copy.wait()


def join(blocks, tokens):
    out = shape((tokens, ROWS * blocks[0].shape[1]))
    count = len(blocks)
    return pl.pallas_call(
        functools.partial(join_kernel, count),
        out_shape=[out, out],
        in_specs=[pl.BlockSpec(memory_space=pltpu.VMEM)] * count,
        out_specs=[pl.BlockSpec(memory_space=pl.ANY)] * 2,
        scratch_shapes=[pltpu.SemaphoreType.DMA((2, ROWS))],
        compiler_params=pltpu.CompilerParams(vmem_limit_bytes=16 * 2**20),
        cost_estimate=pl.CostEstimate(flops=0, bytes_accessed=8 * out.size, transcendentals=0),
        name="join",
    )(*blocks)


def on_device(
    forward_input,
    forward_route,
    forward_gates,
    backward_cotangent,
    backward_route,
    backward_gates,
    gate_up_weight,
    down_weight,
    saved_projections,
):
    sections = lax.axis_size("section")
    experts = lax.axis_size("expert")
    topk = forward_route.shape[2]
    capacity = saved_projections.shape[2] // (GROUP * experts)
    tokens = forward_route.shape[1]

    def to_chip(value, j):
        places = [(k, c) for k in range(CHIPS) for c in range(CORES)]
        pairs = [(k * CORES + c, peer(k, c, j) * CORES + c) for k, c in places]
        return lax.ppermute(value, ("chip", "core"), pairs)

    def to_section(value, dz, by):
        places = [(i, k) for i in range(sections) for k in range(CHIPS)]
        pairs = [(i * CHIPS + k, (i + by) % sections * CHIPS + (k ^ (dz * COLUMNS))) for i, k in places]
        return lax.ppermute(value, ("section", "chip"), pairs)

    def to_expert(block, de):
        if de == 0:
            return block
        return lax.ppermute(block, "expert", [(i, (i + de) % experts) for i in range(experts)])

    def to_core(value):
        return lax.ppermute(value, "core", [(i, i ^ 1) for i in range(CORES)])

    def returned(block, dy, de):
        if dy == 0 and de == 0:
            return block
        places = [(k, e) for k in range(CHIPS) for e in range(experts)]
        pairs = [(k * experts + (e + de) % experts, (k ^ dy) * experts + e) for k, e in places]
        return lax.ppermute(block, ("chip", "expert"), pairs)

    def to_chips(blocks):
        return [blocks[0]] + [to_chip(blocks[dk], dk) for dk in range(1, CHIPS)]

    args = [a[0].T for a in (forward_route, forward_gates, backward_route, backward_gates)]
    gu, down_rows, saved = gate_up_weight[0, 0], down_weight[0, 0], saved_projections[0, 0]
    far = [to_core(gu), to_core(down_rows)]
    tokens_here = to_chips(dispatch(args + [forward_input[0], backward_cotangent[0]], experts))
    shifts, steps = (*range(1, experts),), (*range(CHIPS),)
    so_far = pick(tokens_here, shifts, steps[:-1], experts, capacity, topk, "pick_near", dtype=jnp.float32)
    others = pick(tokens_here, shifts, steps[-1:], experts, capacity, topk, "pick_far", so_far=so_far)
    rows_here = [to_expert(block, de) for block, de in zip(others, shifts)]
    rows_here = [*pick(tokens_here, (0,), steps, experts, capacity, topk, "pick_own"), *rows_here]
    near, turned, (mine, theirs) = hold(gu, down_rows, saved, far, experts, capacity)
    parts = [to_chip(part, j) for j, part in zip(FAR_FIRST, up(rows_here, turned, FAR_FIRST, jnp.bfloat16, "up_others"))]
    parts = [*up(rows_here, turned, (0,), jnp.float32, "up_own"), *parts]
    units = act(parts, mine, to_core(theirs))
    others = [to_chip(units, j) for j in range(1, CHIPS)]
    so_far = down_part(0, units, near, far)
    for j in range(CHIPS - 1, 1, -1):
        so_far = down_part(j, others[j - 1], near, far, so_far)
    results = down(so_far, others[0], near, far, experts)
    steps = [(dy, de) for dy in range(COLUMNS) for de in range(experts)][::-1]
    results = [returned(result, *step) for result, step in zip(results, steps)]
    outs = combine(*plan(tokens_here, experts, capacity, topk), results)
    steps = range(ROWS)
    if sections == 2:
        joined = [to_section(out, dz, 1) for out, dz in zip(outs, steps)]
    else:
        joined = [to_section(out[:tokens], dz, 1) for out, dz in zip(outs, steps)]
        joined += [to_section(out[tokens:], dz, -1) for out, dz in zip(outs, steps)]
    next_input, prior_gradient = join(joined, tokens)
    return next_input[None], prior_gradient[None]


def solution(mesh):
    pipes, experts = mesh.devices.shape
    axes = ("section", "chip", "core", "expert")
    mesh = Mesh(mesh.devices.reshape(pipes // GROUP, CHIPS, CORES, experts), axes)
    rows = P(axes[:3], "expert", None)
    weights = P(axes[:3], "expert", None, None)
    return jax.shard_map(
        on_device,
        mesh=mesh,
        in_specs=(rows,) * 6 + (weights,) * 3,
        out_specs=(rows, rows),
        check_vma=False,
    )
```

```python
import functools

import jax
import jax.numpy as jnp
from jax import lax
from jax.experimental import pallas as pl
from jax.experimental.pallas import tpu as pltpu
from jax.sharding import Mesh
from jax.sharding import PartitionSpec as P

GROUP = 8
CORES = 2
CHIPS = GROUP // CORES
COLUMNS = 2
ROWS = CHIPS // COLUMNS
FAR_FIRST = (CHIPS - 1, *range(1, CHIPS - 1))
TILE = 16
NT = (((1,), (1,)), ((), ()))
NN = (((1,), (0,)), ((), ()))
TN = (((0,), (0,)), ((), ()))


def round_up(value, step):
    return (value + step - 1) // step * step


def dot(a, b, dims=NN):
    return lax.dot_general(a, b, dims, preferred_element_type=jnp.float32)


def iota(shape, axis):
    return lax.broadcasted_iota(jnp.int32, shape, axis)


def place():
    return lax.axis_index("chip"), lax.axis_index("core"), lax.axis_index("expert")


def peer(chip, core, j):
    if isinstance(core, int):
        return chip ^ (CHIPS - 1 - j if core == 0 and 0 < j < CHIPS - 1 else j)
    return chip ^ (jnp.where(core == 0, CHIPS - 1 - j, j) if 0 < j < CHIPS - 1 else j)


def block_of(index, size):
    return pl.ds(pl.multiple_of(index * size, size), size)


def pinned(array, memory):
    return array if memory is None else pltpu.with_memory_space_constraint(array, memory)


def call(kernel, outs, *args, scratch=(), flops=0, name=None, far=(), near=()):
    size = sum(a.size * a.dtype.itemsize for a in args)
    size += sum(o.size * o.dtype.itemsize for o in jax.tree.leaves(outs))
    spec = pl.BlockSpec(memory_space=pltpu.VMEM)
    return pl.pallas_call(
        kernel,
        out_shape=outs,
        in_specs=[pl.BlockSpec(memory_space=pl.ANY) if i in far else spec for i in range(len(args))],
        out_specs=jax.tree.map(lambda _: spec, outs),
        scratch_shapes=scratch,
        compiler_params=pltpu.CompilerParams(vmem_limit_bytes=16 * 2**20),
        cost_estimate=pl.CostEstimate(flops=flops, bytes_accessed=size, transcendentals=0),
        name=name,
    )(*(pinned(a, pltpu.HBM if i in far else pltpu.VMEM if i in near else None) for i, a in enumerate(args)))


def shape(dims, dtype=jnp.bfloat16):
    return jax.ShapeDtypeStruct(dims, dtype)


def group_rows(capacity):
    return round_up(ROWS * capacity, 8)


def slot_rows(capacity):
    return COLUMNS * group_rows(capacity)


def first_row(chip, capacity):
    return (chip % COLUMNS) * group_rows(capacity) + (chip // COLUMNS) * capacity


def dispatch_kernel(experts, *refs):
    far, outs, near, ready = refs[:6], refs[6 : 6 + CHIPS], refs[6 + CHIPS : -1], refs[-1]
    chip, core, _ = place()
    tokens, width = far[4].shape
    wide = width // CHIPS
    jobs = [(far[i], near[i]) for i in range(4)]
    for dk in range(CHIPS):
        for at in range(2):
            block = outs[dk].at[at * tokens : (at + 1) * tokens, :wide]
            jobs.append((far[4 + at].at[:, block_of(peer(chip, core, dk), wide)], block))
    copies = [pltpu.make_async_copy(*job, ready.at[i]) for i, job in enumerate(jobs)]
    for copy in copies:
        copy.start()
    for copy in copies[:4]:
        copy.wait()
    for at in range(2):
        route, gate = near[2 * at][...], near[2 * at + 1][...]
        topk = route.shape[0]
        earlier = (iota((tokens, tokens), 0) < iota((tokens, tokens), 1)).astype(jnp.float32)
        rank = jnp.zeros((topk, tokens), jnp.float32)
        for e in range(experts):
            named = (route == e).astype(jnp.float32)
            count = jnp.broadcast_to(jnp.sum(named, axis=0, keepdims=True), (8, tokens))
            rank = rank + named * dot(count, earlier)[:1]
        high = gate.astype(jnp.bfloat16).astype(jnp.float32)
        middle = (gate - high).astype(jnp.bfloat16).astype(jnp.float32)
        low = gate - high - middle
        table = jnp.zeros((128, tokens), jnp.float32)
        for part, value in enumerate((route.astype(jnp.float32), rank, high, middle, low)):
            for kk in range(topk):
                row = jnp.broadcast_to(value[kk : kk + 1], (128, tokens))
                table = jnp.where(iota((128, tokens), 0) == part * topk + kk, row, table)
        same = (iota((tokens, tokens), 0) == iota((tokens, tokens), 1)).astype(jnp.bfloat16)
        note = dot(same, table.astype(jnp.bfloat16), NT).astype(jnp.bfloat16)
        for dk in range(CHIPS):
            outs[dk][at * tokens : (at + 1) * tokens, wide:] = note
    for copy in copies[4:]:
        copy.wait()


def stash(experts, capacity, core, expert, saved, mine, theirs):
    rows = slot_rows(capacity)
    dims = (rows * experts, saved.shape[0])
    row, column = iota(dims, 0), iota(dims, 1)
    for target, ref in ((1 - core, theirs), (core, mine)):
        wanted = jnp.full(dims, -1, jnp.int32)
        for de in range(experts):
            for at in range(CHIPS):
                source = (at * CORES + target) * experts + lax.rem(expert + experts - de, experts)
                low = de * rows + first_row(at, capacity)
                inside = jnp.logical_and(row >= low, row < low + capacity)
                wanted = jnp.where(inside, row + (source * capacity - low), wanted)
        pick = jnp.where(column == wanted, 1.0, 0.0).astype(jnp.bfloat16)
        ref[...] = dot(pick, saved[...]).astype(jnp.bfloat16)


def dispatch(args, experts):
    tokens, wide = args[4].shape[0], args[4].shape[1] // CHIPS
    return call(
        functools.partial(dispatch_kernel, experts),
        [shape((2 * tokens, wide + 128)) for _ in range(CHIPS)],
        *args,
        scratch=[pltpu.VMEM(a.shape, a.dtype) for a in args[:4]] + [pltpu.SemaphoreType.DMA((4 + 2 * CHIPS,))],
        name="dispatch",
        far=range(6),
    )


def pick_kernel(shifts, steps, experts, capacity, topk, *refs):
    blocks, so_far, outs = refs[: len(steps)], refs[len(steps) : -len(shifts)], refs[-len(shifts) :]
    chip, core, expert = place()
    wide = outs[0].shape[1]
    rows = outs[0].shape[0] // 2
    tokens = blocks[0].shape[0] // 2
    lane = iota((len(steps) * tokens, rows), 1).astype(jnp.float32)
    for at in range(2):
        span, target = slice(at * tokens, (at + 1) * tokens), slice(at * rows, (at + 1) * rows)
        left = jnp.concatenate([b[span, :wide] for b in blocks], axis=0)
        notes = [b[span, wide:].astype(jnp.float32) for b in blocks]
        for i, de in enumerate(shifts):
            here = lax.rem(expert + de, experts).astype(jnp.float32)
            choice = jnp.zeros((len(steps) * tokens, rows), jnp.float32)
            for kk in range(topk):
                targets = []
                for j, note in zip(steps, notes):
                    route, rank = note[:, kk : kk + 1], note[:, topk + kk : topk + kk + 1]
                    first = first_row(peer(chip, core, j), capacity).astype(jnp.float32)
                    targets.append(jnp.where(route == here, rank + first, -1.0))
                choice += jnp.where(lane == jnp.concatenate(targets, axis=0), 1.0, 0.0)
            picked = dot(choice.astype(jnp.bfloat16), left, TN)
            if so_far:
                picked = picked + so_far[i][target]
            outs[i][target] = picked.astype(outs[i].dtype)


def pick(blocks, shifts, steps, experts, capacity, topk, name, so_far=(), dtype=jnp.bfloat16):
    wide = blocks[0].shape[1] - 128
    outs = [shape((2 * slot_rows(capacity), wide), dtype) for _ in shifts]
    kernel = functools.partial(pick_kernel, shifts, steps, experts, capacity, topk)
    return call(kernel, outs, *[blocks[j] for j in steps], *so_far, name=name)


def hold_kernel(experts, capacity, gu, down, saved, gu_far, down_far, *refs):
    gu_near, down_near, gu_turned, down_turned, mine, theirs, near_saved, ready = refs
    _, core, expert = place()
    jobs = ((saved, near_saved), (gu, gu_near), (down, down_near))
    copies = [pltpu.make_async_copy(*job, ready.at[i]) for i, job in enumerate(jobs)]
    for copy in copies:
        copy.start()

    def turn(source, target, first):
        step = source.shape[0] // 8
        for i in range(8):
            span = slice(i * step, (i + 1) * step)
            target[first : first + source.shape[1], span] = source[span, :].T

    half = gu.shape[1]
    turn(gu_far, gu_turned, half)
    turn(down_far, down_turned, half)
    copies[0].wait()
    stash(experts, capacity, core, expert, near_saved, mine, theirs)
    copies[1].wait()
    turn(gu_near, gu_turned, 0)
    copies[2].wait()
    turn(down_near, down_turned, 0)


def hold(gu, down, saved, far, experts, capacity):
    stashed = shape((slot_rows(capacity) * experts, saved.shape[1]))
    turned = [shape((CORES * w.shape[1], w.shape[0])) for w in (gu, down)]
    results = call(
        functools.partial(hold_kernel, experts, capacity),
        [shape(gu.shape), shape(down.shape), *turned, stashed, stashed],
        gu,
        down,
        saved,
        *far,
        scratch=[pltpu.VMEM(saved.shape, saved.dtype), pltpu.SemaphoreType.DMA((3,))],
        name="hold",
        far=range(3),
        near=(3, 4),
    )
    return results[:2], results[2:4], results[4:]


def unit_rows(part, chip, units):
    return pl.ds(pl.multiple_of((part * CHIPS + chip) * units, units), units)


def up_kernel(experts, steps, *refs):
    blocks, turned, outs = refs[:experts], refs[experts : experts + 2], refs[experts + 2 :]
    chip, core, _ = place()
    half = turned[0].shape[0] // CORES
    units = turned[1].shape[1] // CHIPS
    rows = blocks[0].shape[0] // 2

    def left(at):
        sides = [
            jnp.concatenate([b[at * rows : (at + 1) * rows, block_of(side, half)] for b in blocks], axis=0)
            for side in (core, 1 - core)
        ]
        return jnp.concatenate(sides, axis=1)

    lefts = [left(at) for at in range(2)]
    for out, j in zip(outs, steps):
        for part in range(3):
            which, piece = divmod(part, 2)
            span = unit_rows(piece, peer(chip, core, j), units)
            out[:, part * units : (part + 1) * units] = dot(lefts[which], turned[which][:, span]).astype(out.dtype)


def up(blocks, turned, steps, dtype, name):
    experts = len(blocks)
    rows = blocks[0].shape[0] // 2 * experts
    width = (turned[0].shape[1] + turned[1].shape[1]) // CHIPS
    outs = [shape((rows, width), dtype) for _ in steps]
    flops = 2 * rows * width * turned[0].shape[0] * len(steps)
    return call(functools.partial(up_kernel, experts, steps), outs, *blocks, *turned, flops=flops, name=name)


def act_kernel(*refs):
    parts, (mine, theirs, out) = refs[:CHIPS], refs[CHIPS:]
    _, core, _ = place()
    total = parts[0][...]
    for part in parts[1:]:
        total = total + part[...].astype(jnp.float32)
    units = total.shape[1] // 3
    gate_pre, up_pre, hidden_grad = total[:, :units], total[:, units : 2 * units], total[:, 2 * units :]
    out[:, :units] = (gate_pre * jax.nn.sigmoid(gate_pre) * up_pre).astype(jnp.bfloat16)
    half = units // CORES
    own, other = mine[...].astype(jnp.float32), theirs[...].astype(jnp.float32)
    low, high = jnp.where(core == 0, own, other), jnp.where(core == 0, other, own)
    for at, saved in enumerate((low, high)):
        gate_pre, up_pre = saved[:, :half], saved[:, half:]
        sig = jax.nn.sigmoid(gate_pre)
        grad = hidden_grad[:, at * half : (at + 1) * half]
        first = units + at * half
        out[:, first : first + half] = (grad * up_pre * (sig * (1.0 + gate_pre * (1.0 - sig)))).astype(jnp.bfloat16)
        out[:, first + units : first + units + half] = (grad * (gate_pre * sig)).astype(jnp.bfloat16)


def act(parts, mine, theirs):
    return call(act_kernel, shape(parts[0].shape), *parts, mine, theirs, name="act")


DOWN_TERMS = ((1, ((0, 0),)), (0, ((1, 0), (2, 1))))


def down_terms(parts, peers, weights, at, total):
    which, terms = DOWN_TERMS[at]
    weight = weights[which]
    units = weights[1].shape[0] // CHIPS
    for part_ref, chip in zip(parts, peers):
        for piece, part in terms:
            left = part_ref[:, piece * units : (piece + 1) * units]
            term = dot(left, weight[unit_rows(part, chip, units), :])
            total = term if total is None else total + term
    return total


def down_part_kernel(j, part, gu_near, down_near, gu_far, down_far, *refs):
    out = refs[-1]
    chip, core, _ = place()
    for side, weights in enumerate(((gu_near, down_near), (gu_far, down_far))):
        for at in range(2):
            so_far = refs[0][2 * side + at] if len(refs) > 1 else None
            out[2 * side + at] = down_terms((part,), (peer(chip, core, j),), weights, at, so_far)


def down_part(j, part, near, far, *so_far):
    out = shape((4, part.shape[0], near[0].shape[1]), jnp.float32)
    flops = part.shape[0] * (near[0].size + near[1].size)
    kernel = functools.partial(down_part_kernel, j)
    return call(kernel, out, part, *near, *far, *so_far, flops=flops, name="down_part", near=(3, 4))


def down_kernel(experts, so_far, last, *refs):
    sides, outs = (refs[:2], refs[2:4]), refs[4:][::-1]
    chip, core, _ = place()
    half = sides[0][0].shape[1]
    rows = last.shape[0] // experts
    group = rows // COLUMNS
    low = chip % COLUMNS == 0
    for side, column in ((0, core), (1, 1 - core)):
        totals = [
            down_terms((last,), (peer(chip, core, 1),), sides[side], at, so_far[2 * side + at]) for at in range(2)
        ]
        for de in range(experts):
            first = de * rows
            lower = jnp.concatenate([t[first : first + group] for t in totals], axis=0).astype(jnp.bfloat16)
            upper = jnp.concatenate([t[first + group : first + rows] for t in totals], axis=0).astype(jnp.bfloat16)
            outs[de][:, block_of(column, half)] = jnp.where(low, lower, upper)
            outs[experts + de][:, block_of(column, half)] = jnp.where(low, upper, lower)


def down(so_far, last, near, far, experts):
    rows = last.shape[0] // experts
    outs = [shape((2 * rows // COLUMNS, CORES * near[0].shape[1])) for _ in range(COLUMNS * experts)]
    flops = last.shape[0] * (near[0].size + near[1].size)
    kernel = functools.partial(down_kernel, experts)
    return call(kernel, outs, so_far, last, *near, *far, flops=flops, name="down", near=(4, 5))


def plan_kernel(experts, capacity, topk, group, *refs):
    blocks, (choices, gates) = refs[:CHIPS], refs[CHIPS:]
    chip, core, expert = place()
    tokens, wide = blocks[0].shape[0] // 2, blocks[0].shape[1] - 128
    count = 2 * ROWS * tokens
    lane = iota((count, 2 * group), 1).astype(jnp.float32)
    own = blocks[0][:, wide:].astype(jnp.float32)
    other = jnp.where(core == 0, blocks[1][:, wide:].astype(jnp.float32), blocks[2][:, wide:].astype(jnp.float32))
    notes, firsts = [], []
    for dz, note in enumerate((own, other)):
        for at in range(2):
            notes.append(note[at * tokens : (at + 1) * tokens])
            firsts.append((((chip // COLUMNS) ^ dz) * capacity + at * group).astype(jnp.float32))
    for kk in range(topk):
        for de in range(experts):
            here = lax.rem(expert + de, experts).astype(jnp.float32)
            targets = []
            for note, first in zip(notes, firsts):
                route, rank = note[:, kk : kk + 1], note[:, topk + kk : topk + kk + 1]
                targets.append(jnp.where(route == here, rank + first, -1.0))
            choice = jnp.where(lane == jnp.concatenate(targets, axis=0), 1.0, 0.0)
            choices[kk * experts + de] = choice.astype(jnp.bfloat16)
        terms = []
        for note in notes:
            part = [note[:, i * topk + kk : i * topk + kk + 1] for i in (2, 3, 4)]
            terms.append(part[0] + part[1] + part[2])
        gates[kk] = jnp.broadcast_to(jnp.concatenate(terms, axis=0), (count, 128))


def plan(blocks, experts, capacity, topk):
    group = group_rows(capacity)
    count = ROWS * blocks[0].shape[0]
    outs = [shape((topk * experts, count, 2 * group)), shape((topk, count, 128), jnp.float32)]
    return call(functools.partial(plan_kernel, experts, capacity, topk, group), outs, *blocks, name="plan")


def found_rows(choices, results, kk, first, experts):
    found = None
    for i, result in enumerate(results):
        term = dot(choices[kk * experts + first + i], result[...])
        found = term if found is None else found + term
    return found


def combine_other_kernel(experts, choices, gates, *refs):
    results, out = refs[:-1][::-1], refs[-1]
    total = None
    for kk in range(gates.shape[0]):
        term = found_rows(choices, results, kk, 0, experts) * gates[kk][:, :1]
        total = term if total is None else total + term
    out[...] = total.astype(jnp.bfloat16)


def combine_own_kernel(experts, choices, result, out):
    for kk in range(out.shape[0]):
        out[kk] = found_rows(choices, [result], kk, 0, experts)


def combine_kernel(experts, choices, gates, other, own, *refs):
    results, outs = refs[: experts - 1][::-1], refs[experts - 1 :]
    chip, _, _ = place()
    wide = other.shape[1]
    rows = outs[0].shape[0]
    total = None
    for kk in range(gates.shape[0]):
        term = (own[kk] + found_rows(choices, results, kk, 1, experts)) * gates[kk][:, :1]
        total = term if total is None else total + term
    total = total.astype(jnp.bfloat16)
    for dz in range(ROWS):
        span = slice(dz * rows, (dz + 1) * rows)
        outs[dz][:, block_of(chip % COLUMNS, wide)] = total[span]
        outs[dz][:, block_of((chip % COLUMNS) ^ 1, wide)] = other[span]


def combine(choices, gates, results):
    experts = len(results) // COLUMNS
    count, wide = choices.shape[1], results[0].shape[1]
    kernel = functools.partial(combine_other_kernel, experts)
    other = call(kernel, shape((count, wide)), choices, gates, *results[:experts], name="combine_other")
    kernel = functools.partial(combine_own_kernel, experts)
    out = shape((gates.shape[0], count, wide), jnp.float32)
    own = call(kernel, out, choices, results[-1], name="combine_own")
    outs = [shape((count // ROWS, COLUMNS * wide)) for _ in range(ROWS)]
    kernel = functools.partial(combine_kernel, experts)
    return call(kernel, outs, choices, gates, other, own, *results[experts:-1], name="combine")


def join_kernel(count, *refs):
    chip, _, _ = place()
    blocks, outs, ready = refs[:count], refs[count:-1], refs[-1]
    tokens, wide = outs[0].shape[0], blocks[0].shape[1]
    copies = []
    for at, out in enumerate(outs):
        for dz in range(ROWS):
            block = blocks[dz + at * (count - ROWS)]
            first = at * tokens if count == ROWS else 0
            target = out.at[:, block_of((chip // COLUMNS) ^ dz, wide)]
            copies.append(pltpu.make_async_copy(block.at[first : first + tokens], target, ready.at[at, dz]))
            copies[-1].start()
    for copy in copies:
        copy.wait()


def join(blocks, tokens):
    out = shape((tokens, ROWS * blocks[0].shape[1]))
    count = len(blocks)
    return pl.pallas_call(
        functools.partial(join_kernel, count),
        out_shape=[out, out],
        in_specs=[pl.BlockSpec(memory_space=pltpu.VMEM)] * count,
        out_specs=[pl.BlockSpec(memory_space=pl.ANY)] * 2,
        scratch_shapes=[pltpu.SemaphoreType.DMA((2, ROWS))],
        compiler_params=pltpu.CompilerParams(vmem_limit_bytes=16 * 2**20),
        cost_estimate=pl.CostEstimate(flops=0, bytes_accessed=8 * out.size, transcendentals=0),
        name="join",
    )(*blocks)


def on_device(
    forward_input,
    forward_route,
    forward_gates,
    backward_cotangent,
    backward_route,
    backward_gates,
    gate_up_weight,
    down_weight,
    saved_projections,
):
    sections = lax.axis_size("section")
    experts = lax.axis_size("expert")
    topk = forward_route.shape[2]
    capacity = saved_projections.shape[2] // (GROUP * experts)
    tokens = forward_route.shape[1]

    def to_chip(value, j):
        places = [(k, c) for k in range(CHIPS) for c in range(CORES)]
        pairs = [(k * CORES + c, peer(k, c, j) * CORES + c) for k, c in places]
        return lax.ppermute(value, ("chip", "core"), pairs)

    def to_section(value, dz, by):
        places = [(i, k) for i in range(sections) for k in range(CHIPS)]
        pairs = [(i * CHIPS + k, (i + by) % sections * CHIPS + (k ^ (dz * COLUMNS))) for i, k in places]
        return lax.ppermute(value, ("section", "chip"), pairs)

    def to_expert(block, de):
        if de == 0:
            return block
        return lax.ppermute(block, "expert", [(i, (i + de) % experts) for i in range(experts)])

    def to_core(value):
        return lax.ppermute(value, "core", [(i, i ^ 1) for i in range(CORES)])

    def returned(block, dy, de):
        if dy == 0 and de == 0:
            return block
        places = [(k, e) for k in range(CHIPS) for e in range(experts)]
        pairs = [(k * experts + (e + de) % experts, (k ^ dy) * experts + e) for k, e in places]
        return lax.ppermute(block, ("chip", "expert"), pairs)

    def to_chips(blocks):
        return [blocks[0]] + [to_chip(blocks[dk], dk) for dk in range(1, CHIPS)]

    args = [a[0].T for a in (forward_route, forward_gates, backward_route, backward_gates)]
    gu, down_rows, saved = gate_up_weight[0, 0], down_weight[0, 0], saved_projections[0, 0]
    far = [to_core(gu), to_core(down_rows)]
    tokens_here = to_chips(dispatch(args + [forward_input[0], backward_cotangent[0]], experts))
    shifts, steps = (*range(1, experts),), (*range(CHIPS),)
    so_far = pick(tokens_here, shifts, steps[:-1], experts, capacity, topk, "pick_near", dtype=jnp.float32)
    others = pick(tokens_here, shifts, steps[-1:], experts, capacity, topk, "pick_far", so_far=so_far)
    rows_here = [to_expert(block, de) for block, de in zip(others, shifts)]
    rows_here = [*pick(tokens_here, (0,), steps, experts, capacity, topk, "pick_own"), *rows_here]
    near, turned, (mine, theirs) = hold(gu, down_rows, saved, far, experts, capacity)
    parts = [to_chip(part, j) for j, part in zip(FAR_FIRST, up(rows_here, turned, FAR_FIRST, jnp.bfloat16, "up_others"))]
    parts = [*up(rows_here, turned, (0,), jnp.float32, "up_own"), *parts]
    units = act(parts, mine, to_core(theirs))
    others = [to_chip(units, j) for j in range(1, CHIPS)]
    so_far = down_part(0, units, near, far)
    for j in range(CHIPS - 1, 1, -1):
        so_far = down_part(j, others[j - 1], near, far, so_far)
    results = down(so_far, others[0], near, far, experts)
    steps = [(dy, de) for dy in range(COLUMNS) for de in range(experts)][::-1]
    results = [returned(result, *step) for result, step in zip(results, steps)]
    outs = combine(*plan(tokens_here, experts, capacity, topk), results)
    steps = range(ROWS)
    if sections == 2:
        joined = [to_section(out, dz, 1) for out, dz in zip(outs, steps)]
    else:
        joined = [to_section(out[:tokens], dz, 1) for out, dz in zip(outs, steps)]
        joined += [to_section(out[tokens:], dz, -1) for out, dz in zip(outs, steps)]
    next_input, prior_gradient = join(joined, tokens)
    return next_input[None], prior_gradient[None]


def solution(mesh):
    pipes, experts = mesh.devices.shape
    axes = ("section", "chip", "core", "expert")
    mesh = Mesh(mesh.devices.reshape(pipes // GROUP, CHIPS, CORES, experts), axes)
    rows = P(axes[:3], "expert", None)
    weights = P(axes[:3], "expert", None, None)
    return jax.shard_map(
        on_device,
        mesh=mesh,
        in_specs=(rows,) * 6 + (weights,) * 3,
        out_specs=(rows, rows),
        check_vma=False,
    )
```
